32 devices in a mesh: dp: 4 (over y, x), expert: 8 (over z, core).
Axes of the slice: x: 2, y: 2, z: 4, core: 2. Of those that a mesh axis runs over, the one named last changes fastest.
Arguments:
- tokens: bfloat16 [5120, 2048], P(('dp', 'expert')), may hold values from -6 to 6
- teacher: bfloat16 [5120, 2048], P(('dp', 'expert')), may hold values from -6 to 6
- routes: int32 [5120, 8], P(('dp', 'expert')), may hold values from 0 to 31, all different within a row; in each aligned block of 160 rows (0 to 159, 160 to 319, ...) at most 50 rows name the same one
- cont_lengths: int32 [32], replicated, may hold values from 1 to 128, as said below
- query_weight: bfloat16 [2048, 4096], P('dp'), may hold values from -0.125 to 0.125
- key_projection: bfloat16 [2048, 512], P('dp'), may hold values from -0.125 to 0.125
- value_projection: bfloat16 [2048, 512], P('dp'), may hold values from -0.125 to 0.125
- output_weight: bfloat16 [4096, 2048], P('dp'), may hold values from -0.75 to 0.75
- router_weight: bfloat16 [2048, 32], replicated, may hold values from -0.0625 to 0.0625
- gate_weight: bfloat16 [32, 2048, 768], P(('dp', 'expert')), may hold values from -0.125 to 0.125
- up_weight: bfloat16 [32, 2048, 768], P(('dp', 'expert')), may hold values from -0.125 to 0.125
- down_weight: bfloat16 [32, 768, 2048], P(('dp', 'expert')), may hold values from -0.625 to 0.625
- input_gain: float32 [2048], replicated, may hold values from 0.5 to 1.5
- post_gain: float32 [2048], replicated, may hold values from 0.5 to 1.5
- query_gain: float32 [128], replicated, may hold values from 0.5 to 1.5
- key_gain: float32 [128], replicated, may hold values from 0.5 to 1.5
Outputs:
- layer_out: float32 [5120, 2048], P(('dp', 'expert'))
- loss: float32 [], replicated
- tokens_grad: float32 [5120, 2048], P(('dp', 'expert'))
- query_grad: float32 [2048, 4096], P(('dp', 'expert'))
- key_grad: float32 [2048, 512], P(('dp', 'expert'))
- value_grad: float32 [2048, 512], P(('dp', 'expert'))
- output_grad: float32 [4096, 2048], P(('dp', 'expert'))
- router_grad: float32 [2048, 32], replicated
- gate_grad: float32 [32, 2048, 768], P(('dp', 'expert'))
- up_grad: float32 [32, 2048, 768], P(('dp', 'expert'))
- down_grad: float32 [32, 768, 2048], P(('dp', 'expert'))
- input_gain_grad: float32 [2048], replicated
- post_gain_grad: float32 [2048], replicated
- query_gain_grad: float32 [128], replicated
- key_gain_grad: float32 [128], replicated
The draws below stay inside these ranges and needn't reach their ends.
Inputs may be any that keep to these rules, and one draw needn't show every extreme that they name: `routes`: each row names 8 different experts; within the rows of one device (aligned blocks of 160 rows) no expert is named by more than 50 rows, a bound that some block reaches. `cont_lengths`: at least one continuation fills all 128 slots.
All inputs are finite; a program needn't handle non-finite values.
Results may differ from the reference program's by a relative error of at most 0.015.
Values may be sent and summed in bfloat16 or wider, within the bound.
A program may use at most 384 MiB of HBM per device.

```python
import math
import jax
import jax.numpy as jnp
import numpy as np
from jax import lax

MODEL_SIZE = 2048
QUERY_HEADS = 32
KEY_VALUE_HEADS = 4
HEAD_SIZE = 128
FF = 768
TOPK = 8
PROMPT_PER_RANK = 32
CMAX = 128
TOK_DEV = 160
PROMPT_TOKENS = 256
TOKEN_SLOTS = 5120
NCONT = 32
EXPERTS = 32
CAP = 50
N_DP = 4
N_EXPERT = 8
DEVICES = 32


def draw_cont_lengths(key, part):
    length_key, index_key = jax.random.split(jax.random.fold_in(key, 11))
    lengths = jax.random.randint(length_key, (NCONT,), 1, CMAX + 1, dtype=jnp.int32)
    full_index = jax.random.randint(index_key, (), 0, NCONT, dtype=jnp.int32)
    return jnp.where(jnp.arange(NCONT, dtype=jnp.int32) == full_index, CMAX, lengths).astype(jnp.int32)


def shard_levels(own_key, dims, cuts, least, high):
    gain = 1.0
    for axis_at, shards_of in cuts:
        draws = jax.random.uniform(jax.random.fold_in(jax.random.fold_in(own_key, 6), axis_at), (shards_of,), jnp.float32, least / len(cuts), high / len(cuts))
        gain = gain * jnp.repeat(jnp.exp(draws), dims[axis_at] // shards_of).reshape((-1,) + (1,) * (len(dims) - 1 - axis_at))
    return gain


def routed_block(rng, own, number, rows, count, top, bound, slope):
    order = jax.random.permutation(rng, count)
    heavy_load, usual = load_shares(count, rows * top, bound, slope, True), load_shares(count, rows * top, bound, slope, False)
    places = jnp.arange(count)

    def named(tallies, offset_by):
        used = int((tallies > 0).sum())
        fixed = max(1, used // 4)
        passed = fixed + (places - fixed + offset_by * (used - fixed)) % max(1, count - fixed)
        return jnp.zeros((count,), jnp.int32).at[order[jnp.where(places < fixed, places, passed)]].set(jnp.asarray(tallies, jnp.int32))

    tallies = jnp.where(number % 4 == 0, named(heavy_load, number // 4), named(usual, number - number // 4 - 1))
    mixed = jax.random.permutation(jax.random.fold_in(own, 3), count)
    source_of, sink = mixed[0:count // 2 * 2:2], mixed[1:count // 2 * 2:2]
    room = jnp.minimum(tallies[source_of] - 1, bound - tallies[sink]) // 2
    room = jnp.where((source_of == order[0]) | (sink == order[0]) | (tallies[sink] == 0), 0, jnp.maximum(room, 0))
    passed = jax.random.randint(jax.random.fold_in(own, 4), (count // 2,), 0, 1 << 20) % (room + 1)
    tallies = tallies.at[source_of].add(-passed).at[sink].add(passed)
    items = jnp.searchsorted(jnp.cumsum(tallies), jnp.arange(rows * top), side="right").astype(jnp.int32)
    table = items.reshape(top, rows).T
    table = table[jax.random.permutation(jax.random.fold_in(own, 1), rows)]
    offset_by = jax.random.randint(jax.random.fold_in(own, 2), (rows, 1), 0, top)
    return jnp.take_along_axis(table, (jnp.arange(top)[None, :] + offset_by) % top, axis=1)


def load_shares(number_of, total, bound, lean, full):
    loads = [(1 << 20) // math.isqrt(grade ** lean) + 1 for grade in range(1, number_of + 1)]
    largest = bound if full else min(bound, max(-(-total // number_of), total * loads[0] // sum(loads)))
    least = 1 if total - largest >= number_of - 1 else 0
    given, rest = [largest] + [least] * (number_of - 1), total - largest - least * (number_of - 1)
    while rest > 0:
        candidates = [i for i in range(1, number_of) if given[i] < largest] or [i for i in range(1, number_of) if given[i] < bound]
        mass, left = sum([loads[i] for i in candidates]), rest
        for i in candidates:
            addition = min(bound - given[i], max(1, left * loads[i] // mass), rest)
            given[i] = given[i] + addition
            rest = rest - addition
    return np.array(given)


def scatter_about(key, dims, scale, reach, shards=(), kind=jnp.bfloat16):
    factor_of = shard_levels(key, dims, shards, -0.22, 0.18) if shards else 1.0
    entries = jax.random.normal(key, dims, jnp.float32) * scale * factor_of
    return jnp.minimum(jnp.maximum(entries, -reach), reach).astype(kind)


def setup_inputs(seed: int = 0) -> dict:
    key_of = jax.random.split(jax.random.key(seed), 17)
    tokens = scatter_about(key_of[0], (TOKEN_SLOTS, MODEL_SIZE), 1.0, 6.0, ((0, 32),))
    teacher = scatter_about(key_of[1], (TOKEN_SLOTS, MODEL_SIZE), 1.0, 6.0, ((0, 32),))
    routes_keys = jax.random.split(jax.random.fold_in(key_of[2], 1), TOKEN_SLOTS // TOK_DEV)
    routes_turns = jax.random.permutation(jax.random.fold_in(key_of[2], 3), TOKEN_SLOTS // TOK_DEV)
    routes = jax.vmap(lambda own, number: routed_block(jax.random.fold_in(key_of[2], 2), own, number, TOK_DEV, EXPERTS, TOPK, CAP, 2))(routes_keys, routes_turns).reshape((TOKEN_SLOTS, TOPK))
    cont_lengths = draw_cont_lengths(jax.random.fold_in(key_of[16], 71), 0)
    query_weight = scatter_about(key_of[4], (MODEL_SIZE, QUERY_HEADS * HEAD_SIZE), MODEL_SIZE ** -0.5, 0.125, ((0, 4),))
    key_projection = scatter_about(key_of[5], (MODEL_SIZE, KEY_VALUE_HEADS * HEAD_SIZE), MODEL_SIZE ** -0.5, 0.125, ((0, 4),))
    value_projection = scatter_about(key_of[6], (MODEL_SIZE, KEY_VALUE_HEADS * HEAD_SIZE), MODEL_SIZE ** -0.5, 0.125, ((0, 4),))
    output_weight = scatter_about(key_of[7], (QUERY_HEADS * HEAD_SIZE, MODEL_SIZE), (QUERY_HEADS * HEAD_SIZE // 64) ** -0.5, 0.75, ((0, 4),))
    router_weight = scatter_about(key_of[8], (MODEL_SIZE, EXPERTS), (4 * MODEL_SIZE) ** -0.5, 0.0625)
    gate_weight = scatter_about(key_of[9], (EXPERTS, MODEL_SIZE, FF), MODEL_SIZE ** -0.5, 0.125, ((0, 32),))
    up_weight = scatter_about(key_of[10], (EXPERTS, MODEL_SIZE, FF), MODEL_SIZE ** -0.5, 0.125, ((0, 32),))
    down_weight = scatter_about(key_of[11], (EXPERTS, FF, MODEL_SIZE), (FF // 8) ** -0.5, 0.625, ((0, 32),))
    input_gain = jnp.clip(1.0 + 0.1 * jax.random.normal(key_of[12], (MODEL_SIZE,), jnp.float32), 0.5, 1.5)
    post_gain = jnp.clip(1.0 + 0.1 * jax.random.normal(key_of[13], (MODEL_SIZE,), jnp.float32), 0.5, 1.5)
    query_gain = jnp.clip(1.0 + 0.1 * jax.random.normal(key_of[14], (HEAD_SIZE,), jnp.float32), 0.5, 1.5)
    key_gain = jnp.clip(1.0 + 0.1 * jax.random.normal(key_of[15], (HEAD_SIZE,), jnp.float32), 0.5, 1.5)
    return {"tokens": tokens, "teacher": teacher, "routes": routes, "cont_lengths": cont_lengths, "query_weight": query_weight, "key_projection": key_projection, "value_projection": value_projection, "output_weight": output_weight, "router_weight": router_weight, "gate_weight": gate_weight, "up_weight": up_weight, "down_weight": down_weight, "input_gain": input_gain, "post_gain": post_gain, "query_gain": query_gain, "key_gain": key_gain}


norm_eps = 1e-06
rope_base = 1000000.0

@jax.custom_vjp
def lower_precision(v):
    return lax.optimization_barrier(v.astype(jnp.bfloat16)).astype(jnp.float32)

@jax.custom_vjp
def low_back(v):
    return v

def low_keep(v):
    return (lower_precision(v), None)

def low_pass(kept, grad):
    return (grad,)

def back_keep(v):
    return (v, None)

def back_low(kept, grad):
    return (lower_precision(grad),)
lower_precision.defvjp(low_keep, low_pass)
low_back.defvjp(back_keep, back_low)

def matmul(left_side, right_side):
    return jnp.dot(left_side, right_side, precision=lax.Precision.HIGHEST, preferred_element_type=jnp.float32)

def root_mean_scale(value_rows, gain_vec):
    return value_rows * lax.rsqrt(lax.optimization_barrier(jnp.mean(value_rows * value_rows, axis=-1, keepdims=True)) + norm_eps) * gain_vec

def rotary_apply(value_rows, token_positions):
    head_width = value_rows.shape[-1]
    half_width = head_width // 2
    frequency = rope_base ** (-(jnp.arange(half_width, dtype=jnp.float32) * 2.0) / head_width)
    angles = token_positions.astype(jnp.float32)[:, None] * frequency[None, :]
    cosine = jnp.concatenate([jnp.cos(angles), jnp.cos(angles)], axis=-1)[:, None, :]
    sine_table = jnp.concatenate([jnp.sin(angles), jnp.sin(angles)], axis=-1)[:, None, :]
    turned = jnp.concatenate([-value_rows[..., half_width:], value_rows[..., :half_width]], axis=-1)
    return value_rows * cosine + turned * sine_table

def slot_layout(cont_lengths):
    dp_ids = jnp.arange(N_DP, dtype=jnp.int32)[:, None, None]
    owner_ids = jnp.arange(N_EXPERT, dtype=jnp.int32)[None, :, None]
    slot_ids = jnp.arange(TOK_DEV, dtype=jnp.int32)[None, None, :]
    piece_index = owner_ids % 2 * N_DP + dp_ids
    token_positions = jnp.where(slot_ids < PROMPT_PER_RANK, piece_index * PROMPT_PER_RANK + slot_ids, PROMPT_TOKENS + slot_ids - PROMPT_PER_RANK)
    own_length = cont_lengths.reshape(N_DP, N_EXPERT)[:, :, None]
    valid_slot = (slot_ids < PROMPT_PER_RANK) | (slot_ids - PROMPT_PER_RANK < own_length)
    return (token_positions.reshape(TOKEN_SLOTS).astype(jnp.int32), valid_slot.reshape(TOKEN_SLOTS))

def expert_slots(routes, valid_slot):
    row_total = TOK_DEV * TOPK
    expert_ids = routes.reshape(DEVICES, row_total).astype(jnp.int32)
    live_rows = jnp.repeat(valid_slot.reshape(DEVICES, TOK_DEV), TOPK, axis=1)
    all_experts = jnp.arange(EXPERTS, dtype=jnp.int32)[None, None, :]
    hit_table = ((expert_ids[:, :, None] == all_experts) & live_rows[:, :, None]).astype(jnp.int32)
    earlier = (jnp.cumsum(hit_table, axis=1) - hit_table).astype(jnp.int32)
    position_in = lax.optimization_barrier(jnp.sum(earlier * hit_table, axis=2)).astype(jnp.int32)
    sender = jnp.arange(DEVICES, dtype=jnp.int32)[:, None]
    room_size = DEVICES * CAP
    slot_index = jnp.where(live_rows, expert_ids * room_size + sender * CAP + position_in, EXPERTS * room_size).astype(jnp.int32)
    token_row = (sender * TOK_DEV + jnp.arange(row_total, dtype=jnp.int32)[None, :] // TOPK).astype(jnp.int32)
    source_row = jnp.full((EXPERTS * room_size + 1,), TOKEN_SLOTS, jnp.int32)
    source_row = source_row.at[slot_index.reshape(-1)].set(token_row.reshape(-1))
    return (slot_index.reshape(TOKEN_SLOTS, TOPK), source_row[:EXPERTS * room_size])

def group_attention(queries, key_rows, value_rows, lengths):
    key_value_group = QUERY_HEADS // KEY_VALUE_HEADS
    score_scale = HEAD_SIZE ** (-0.5)
    conts = queries.shape[0]
    prompt_q = queries[:, :PROMPT_PER_RANK].reshape(PROMPT_TOKENS, QUERY_HEADS, HEAD_SIZE)
    prompt_key_rows = jnp.repeat(key_rows[:, :PROMPT_PER_RANK].reshape(PROMPT_TOKENS, KEY_VALUE_HEADS, HEAD_SIZE), key_value_group, axis=1)
    prompt_value_rows = jnp.repeat(value_rows[:, :PROMPT_PER_RANK].reshape(PROMPT_TOKENS, KEY_VALUE_HEADS, HEAD_SIZE), key_value_group, axis=1)
    cont_q = queries[:, PROMPT_PER_RANK:]
    cont_k = jnp.repeat(key_rows[:, PROMPT_PER_RANK:], key_value_group, axis=2)
    cont_v = jnp.repeat(value_rows[:, PROMPT_PER_RANK:], key_value_group, axis=2)
    first_scores = low_back(score_scale * jnp.einsum('qhd,khd->hqk', prompt_q, prompt_key_rows, precision=lax.Precision.HIGHEST))
    order_ids = jnp.arange(PROMPT_TOKENS, dtype=jnp.int32)
    causal = order_ids[:, None] >= order_ids[None, :]
    first_probs = jax.nn.softmax(jnp.where(causal[None], first_scores, -jnp.inf), axis=-1)
    prompt_out = jnp.einsum('hqk,khd->qhd', lower_precision(first_probs), prompt_value_rows, precision=lax.Precision.HIGHEST)
    both_keys = jnp.concatenate([jnp.broadcast_to(prompt_key_rows[None], (conts, PROMPT_TOKENS, QUERY_HEADS, HEAD_SIZE)), cont_k], axis=1)
    both_values = jnp.concatenate([jnp.broadcast_to(prompt_value_rows[None], (conts, PROMPT_TOKENS, QUERY_HEADS, HEAD_SIZE)), cont_v], axis=1)
    second_scores = low_back(score_scale * jnp.einsum('cqhd,ckhd->chqk', cont_q, both_keys, precision=lax.Precision.HIGHEST))
    key_ids = jnp.arange(PROMPT_TOKENS + CMAX, dtype=jnp.int32)[None, None, :]
    query_ids = jnp.arange(CMAX, dtype=jnp.int32)[None, :, None]
    seen = (key_ids < PROMPT_TOKENS) | (key_ids - PROMPT_TOKENS <= query_ids) & (key_ids - PROMPT_TOKENS < lengths[:, None, None])
    second_probs = jax.nn.softmax(jnp.where(seen[:, None], second_scores, -jnp.inf), axis=-1)
    cont_out = jnp.einsum('chqk,ckhd->cqhd', lower_precision(second_probs), both_values, precision=lax.Precision.HIGHEST)
    return (prompt_out, cont_out)

def attend(queries, key_rows, value_rows, cont_lengths):
    groups = N_EXPERT // 2

    def arrange(array):
        heads = array.shape[1]
        shaped = array.reshape(N_DP, groups, 2, TOK_DEV, heads, HEAD_SIZE)
        return shaped.transpose(1, 2, 0, 3, 4, 5).reshape(groups, 2 * N_DP, TOK_DEV, heads, HEAD_SIZE)
    lengths = cont_lengths.reshape(N_DP, groups, 2).transpose(1, 2, 0).reshape(groups, 2 * N_DP)

    def one_group(carry, block):
        prompt_out, cont_out = jax.checkpoint(group_attention)(*block)
        joined = jnp.concatenate([prompt_out.reshape(2 * N_DP, PROMPT_PER_RANK, QUERY_HEADS, HEAD_SIZE), cont_out], axis=1)
        return (carry, joined)
    unused, outputs = lax.scan(one_group, jnp.zeros((), jnp.float32), (arrange(queries), arrange(key_rows), arrange(value_rows), lengths))
    outputs = outputs.reshape(groups, 2, N_DP, TOK_DEV, QUERY_HEADS, HEAD_SIZE).transpose(2, 0, 1, 3, 4, 5)
    return outputs.reshape(TOKEN_SLOTS, QUERY_HEADS * HEAD_SIZE)

def expert_block(operands):
    rows_in, gate_mat, up_mat, down_mat = operands
    gate_pre = low_back(matmul(rows_in, gate_mat))
    up_pre = low_back(matmul(rows_in, up_mat))
    hidden_units = lower_precision(jax.nn.silu(gate_pre) * up_pre)
    return lower_precision(matmul(hidden_units, down_mat))

def reference(tokens, teacher, routes, cont_lengths, query_weight, key_projection, value_projection, output_weight, router_weight, gate_weight, up_weight, down_weight, input_gain, post_gain, query_gain, key_gain):
    token_positions, valid_slot = slot_layout(cont_lengths)
    slot_index, source_row = expert_slots(routes, valid_slot)

    def forward(tokens_float, query_mat, key_mat, value_mat, output_mat, router_mat, gate_mats, up_mats, down_mats, input_vec, post_vec, query_vec, key_gain_vector):
        normed = lower_precision(root_mean_scale(tokens_float, input_vec))
        query_lin = low_back(matmul(normed, query_mat))
        key_linear = low_back(matmul(normed, key_mat))
        value_linear = low_back(matmul(normed, value_mat))
        queries = lower_precision(rotary_apply(root_mean_scale(query_lin.reshape(TOKEN_SLOTS, QUERY_HEADS, HEAD_SIZE), query_vec), token_positions))
        key_rows = lower_precision(rotary_apply(root_mean_scale(key_linear.reshape(TOKEN_SLOTS, KEY_VALUE_HEADS, HEAD_SIZE), key_gain_vector), token_positions))
        value_rows = lower_precision(value_linear).reshape(TOKEN_SLOTS, KEY_VALUE_HEADS, HEAD_SIZE)
        attended = lower_precision(low_back(attend(queries, key_rows, value_rows, cont_lengths)))
        state = tokens_float + low_back(matmul(attended, output_mat))
        mixed = lower_precision(root_mean_scale(state, post_vec))
        logits = low_back(matmul(mixed, router_mat))
        gates = jax.nn.softmax(jnp.take_along_axis(logits, routes, axis=1), axis=-1)
        mixed_pad = jnp.concatenate([mixed, jnp.zeros((1, MODEL_SIZE), jnp.float32)], axis=0)
        expert_in = low_back(mixed_pad[source_row]).reshape(EXPERTS, DEVICES * CAP, MODEL_SIZE)
        expert_out = lax.map(jax.checkpoint(expert_block), (expert_in, gate_mats, up_mats, down_mats))
        out_pad = jnp.concatenate([expert_out.reshape(EXPERTS * DEVICES * CAP, MODEL_SIZE), jnp.zeros((1, MODEL_SIZE), jnp.float32)], axis=0)
        copies = low_back(out_pad[slot_index])
        return state + lax.optimization_barrier(jnp.sum(gates[:, :, None] * copies, axis=1))
    params = tuple((array.astype(jnp.float32) for array in (tokens, query_weight, key_projection, value_projection, output_weight, router_weight, gate_weight, up_weight, down_weight, input_gain, post_gain, query_gain, key_gain)))
    layer_out, backward = jax.vjp(forward, *params)
    live = valid_slot.astype(jnp.float32)[:, None]
    diff = (layer_out - teacher.astype(jnp.float32)) * live
    valid_count = (DEVICES * PROMPT_PER_RANK + jnp.sum(cont_lengths)).astype(jnp.float32)
    loss = jnp.sum(diff * diff) / (valid_count * MODEL_SIZE)
    grads = backward(2.0 * TOKEN_SLOTS * diff / valid_count)
    return (layer_out, loss, grads[0], grads[1], grads[2], grads[3], grads[4], grads[5], grads[6], grads[7], grads[8], grads[9], grads[10], grads[11], grads[12])
```

```python
import functools

import jax
import jax.numpy as jnp
from jax import lax
from jax.experimental import pallas as pl
from jax.experimental.pallas import tpu as pltpu
from jax.sharding import PartitionSpec as P

CMAX = 128
norm_eps = 1e-06
rope_base = 1000000.0
MESH = pl.DeviceIdType.MESH
F32 = jnp.float32
BF16 = jnp.bfloat16
VMEM_SPEC = pl.BlockSpec(memory_space=pltpu.VMEM)
ANY_SPEC = pl.BlockSpec(memory_space=pl.ANY)
VMEM_LIMIT = 56 * 1024 * 1024


def params(collective_id=None):
    return pltpu.CompilerParams(
        collective_id=collective_id,
        has_side_effects=collective_id is not None,
        vmem_limit_bytes=VMEM_LIMIT,
    )


def greet(devices):
    barrier = pltpu.get_barrier_semaphore()
    for device in devices:
        pl.semaphore_signal(barrier, inc=1, device_id=device, device_id_type=MESH)
    pl.semaphore_wait(barrier, len(devices))


def remote(src, dst, send_sem, recv_sem, device):
    return pltpu.make_async_remote_copy(
        src_ref=src,
        dst_ref=dst,
        send_sem=send_sem,
        recv_sem=recv_sem,
        device_id=device,
        device_id_type=MESH,
    )


def aligned(index, size):
    return pl.ds(pl.multiple_of(index * size, size), size)


def dot_nn(a, b):
    return lax.dot_general(a, b, (((1,), (0,)), ((), ())), preferred_element_type=F32)


def dot_nt(a, b):
    return lax.dot_general(a, b, (((1,), (1,)), ((), ())), preferred_element_type=F32)


def dot_tn(a, b):
    return lax.dot_general(a, b, (((0,), (0,)), ((), ())), preferred_element_type=F32)


PEER_MASKS = (3, 1, 2)


def qkv_kernel(tok, normed, wq, wk, wv, lin, cols, send, recv, asend, arecv, ssem, rsem):
    r, e = lax.axis_index("dp"), lax.axis_index("expert")
    peers = [r ^ m for m in PEER_MASKS]
    width = wq.shape[0]
    qg = wq.shape[1] // 4
    kg = wk.shape[1] // 4
    rows = cols.shape[0]
    greet([(p, e) for p in peers])
    first = []
    for i, p in enumerate(peers):
        copy = remote(
            normed.at[:, aligned(p, width)], cols.at[aligned(r, tok), :],
            asend.at[i], arecv.at[i], (p, e),
        )
        copy.start()
        first.append(copy)
    cols[aligned(r, tok), :] = normed[:, aligned(r, width)]
    for copy in first:
        copy.wait()

    def products(p, dst):
        def chunk(c, carry):
            t = aligned(c, tok)
            x = cols[t, :]
            dst[t, :qg] = dot_nn(x, wq[:, aligned(p, qg)]).astype(dst.dtype)
            dst[t, qg : qg + kg] = dot_nn(x, wk[:, aligned(p, kg)]).astype(dst.dtype)
            dst[t, qg + kg :] = dot_nn(x, wv[:, aligned(p, kg)]).astype(dst.dtype)
            return carry

        lax.fori_loop(0, rows // tok, chunk, 0)

    second = []
    for i, p in enumerate(peers):
        products(p, send.at[i])
        copy = remote(send.at[i], recv.at[i], ssem.at[i], rsem.at[i], (p, e))
        copy.start()
        second.append(copy)
    products(r, lin)
    for i in (1, 2, 0):
        second[i].wait()

    def total(c, carry):
        t = aligned(c, 32)
        lin[t, :] = lin[t, :] + (
            recv[0, t, :].astype(F32) + recv[1, t, :].astype(F32) + recv[2, t, :].astype(F32)
        )
        return carry

    lax.fori_loop(0, rows // 32, total, 0)


def project_qkv(normed, wq, wk, wv):
    tok = normed.shape[0]
    rows = 4 * tok
    group = (wq.shape[1] + wk.shape[1] + wv.shape[1]) // 4
    return pl.pallas_call(
        functools.partial(qkv_kernel, tok),
        out_shape=(
            jax.ShapeDtypeStruct((rows, group), F32),
            jax.ShapeDtypeStruct((rows, wq.shape[0]), BF16),
        ),
        in_specs=[VMEM_SPEC] * 4,
        out_specs=(VMEM_SPEC, VMEM_SPEC),
        scratch_shapes=[
            pltpu.VMEM((3, rows, group), BF16),
            pltpu.VMEM((3, rows, group), BF16),
        ]
        + [pltpu.SemaphoreType.DMA((3,))] * 4,
        compiler_params=params(1),
        name="qkv_exchange",
    )(normed, wq, wk, wv)


def out_kernel(attn, wo, total, send, recv, ssem, rsem):
    r, e = lax.axis_index("dp"), lax.axis_index("expert")
    peers = [r ^ m for m in PEER_MASKS]
    tok = total.shape[0]
    width = total.shape[1]
    step = width // 4
    greet([(p, e) for p in peers])

    def products(p, dst):
        def chunk(c, carry):
            n = aligned(c, step)
            dst[:, n] = dot_nn(attn[aligned(p, tok), :], wo[:, n]).astype(dst.dtype)
            return carry

        lax.fori_loop(0, width // step, chunk, 0)

    copies = []
    for i, p in enumerate(peers):
        products(p, send.at[i])
        copy = remote(send.at[i], recv.at[i], ssem.at[i], rsem.at[i], (p, e))
        copy.start()
        copies.append(copy)
    products(r, total)
    for i in (1, 2, 0):
        copies[i].wait()

    def add(c, carry):
        t = aligned(c, 32)
        total[t, :] = total[t, :] + (
            recv[0, t, :].astype(F32) + recv[1, t, :].astype(F32) + recv[2, t, :].astype(F32)
        )
        return carry

    lax.fori_loop(0, tok // 32, add, 0)


def project_out(attn, wo):
    tok = attn.shape[0] // 4
    return pl.pallas_call(
        out_kernel,
        out_shape=jax.ShapeDtypeStruct((tok, wo.shape[1]), F32),
        in_specs=[VMEM_SPEC] * 2,
        out_specs=VMEM_SPEC,
        scratch_shapes=[
            pltpu.VMEM((3, tok, wo.shape[1]), BF16),
            pltpu.VMEM((3, tok, wo.shape[1]), BF16),
        ]
        + [pltpu.SemaphoreType.DMA((3,))] * 2,
        compiler_params=params(2),
        name="out_exchange",
    )(attn, wo)


def dgrad_kernel(mine, wq, wk, wv, cols_t, normal, grads, blocks, dsum, dsend, drecv, ssem, rsem, bsend, brecv):
    r, e = lax.axis_index("dp"), lax.axis_index("expert")
    rows = mine.shape[0]
    tok = rows // 4
    half = rows // 2
    qg = wq.shape[1] // 4
    kg = wk.shape[1] // 4
    width = wq.shape[0]
    peers = [r ^ m for m in PEER_MASKS]
    near, far, diag = r ^ 1, r ^ 2, r ^ 3
    greet([(p, e) for p in peers])
    low, high = pl.ds(0, half), pl.ds(half, half)
    first_near = remote(mine.at[low], blocks.at[0, low], ssem.at[0], rsem.at[0], (near, e))
    first_far = remote(mine.at[high], blocks.at[1, high], ssem.at[1], rsem.at[1], (far, e))
    second_near = remote(mine.at[high], blocks.at[0, high], ssem.at[2], rsem.at[2], (near, e))
    second_far = remote(mine.at[low], blocks.at[1, low], ssem.at[3], rsem.at[3], (far, e))
    pass_far = remote(blocks.at[0, low], blocks.at[2, low], ssem.at[4], rsem.at[4], (far, e))
    pass_near = remote(blocks.at[1, high], blocks.at[2, high], ssem.at[5], rsem.at[5], (near, e))
    for copy in (first_near, first_far, second_near, second_far):
        copy.start()

    def products(p, src, start):
        def chunk(c, carry):
            t = aligned(c, tok)
            x = src[t, :]
            value = (
                dot_nt(x[:, :qg], wq[:, aligned(p, qg)])
                + dot_nt(x[:, qg : qg + kg], wk[:, aligned(p, kg)])
                + dot_nt(x[:, qg + kg :], wv[:, aligned(p, kg)])
            )
            if start:
                dsum[t, :] = value
            else:
                dsum[t, :] = dsum[t, :] + value
            return carry

        lax.fori_loop(0, 4, chunk, 0)

        def outer(c, carry):
            n = aligned(c, 128)
            grads[aligned(p, width), n] = dot_nn(cols_t[...], src[:, n]).astype(BF16)
            return carry

        lax.fori_loop(0, (qg + 2 * kg) // 128, outer, 0)

    products(r, mine, True)
    first_near.wait()
    pass_far.start()
    first_far.wait()
    pass_near.start()
    second_near.wait()
    products(near, blocks.at[0], False)
    second_far.wait()
    products(far, blocks.at[1], False)
    pass_far.wait()
    pass_near.wait()
    products(diag, blocks.at[2], False)
    back = []
    for i, p in enumerate(peers):
        dsend[i] = dsum[aligned(p, tok), :].astype(BF16)
        copy = remote(dsend.at[i], drecv.at[i], bsend.at[i], brecv.at[i], (p, e))
        copy.start()
        back.append(copy)
    normal[:, aligned(r, width)] = dsum[aligned(r, tok), :]
    for i, p in enumerate(peers):
        back[i].wait()
        normal[:, aligned(p, width)] = drecv[i].astype(F32)


def grad_qkv(mine, wq, wk, wv, cols_t):
    rows, group = mine.shape
    tok = rows // 4
    width = wq.shape[0]
    return pl.pallas_call(
        dgrad_kernel,
        out_shape=(
            jax.ShapeDtypeStruct((tok, 4 * width), F32),
            jax.ShapeDtypeStruct((4 * width, group), BF16),
        ),
        in_specs=[VMEM_SPEC] * 5,
        out_specs=(VMEM_SPEC, VMEM_SPEC),
        scratch_shapes=[
            pltpu.VMEM((3, rows, group), BF16),
            pltpu.VMEM((rows, width), F32),
            pltpu.VMEM((3, tok, width), BF16),
            pltpu.VMEM((3, tok, width), BF16),
            pltpu.SemaphoreType.DMA((6,)),
            pltpu.SemaphoreType.DMA((6,)),
            pltpu.SemaphoreType.DMA((3,)),
            pltpu.SemaphoreType.DMA((3,)),
        ],
        compiler_params=params(4),
        name="dqkv_exchange",
    )(mine, wq, wk, wv, cols_t)


def branch_kernel(mine, wo, attn_t, d_attn, grads, full, ssem, rsem):
    r, e = lax.axis_index("dp"), lax.axis_index("expert")
    tok = mine.shape[0]
    half = tok // 2
    peers = [r ^ m for m in PEER_MASKS]
    near, far, diag = r ^ 1, r ^ 2, r ^ 3
    greet([(p, e) for p in peers])

    def part(q, which):
        return pl.ds(pl.multiple_of(q * tok + which * half, half), half)

    low, high = pl.ds(0, half), pl.ds(half, half)
    first_near = remote(mine.at[low], full.at[part(r, 0)], ssem.at[0], rsem.at[0], (near, e))
    first_far = remote(mine.at[high], full.at[part(r, 1)], ssem.at[1], rsem.at[1], (far, e))
    second_near = remote(mine.at[high], full.at[part(r, 1)], ssem.at[2], rsem.at[2], (near, e))
    second_far = remote(mine.at[low], full.at[part(r, 0)], ssem.at[3], rsem.at[3], (far, e))
    pass_far = remote(full.at[part(near, 0)], full.at[part(near, 0)], ssem.at[4], rsem.at[4], (far, e))
    pass_near = remote(full.at[part(far, 1)], full.at[part(far, 1)], ssem.at[5], rsem.at[5], (near, e))
    for copy in (first_near, first_far, second_near, second_far):
        copy.start()
    full[aligned(r, tok), :] = mine[...]
    heads = wo.shape[0]
    step = heads // 4

    def products(q):
        def chunk(c, carry):
            n = aligned(c, step)
            d_attn[aligned(q, tok), n] = dot_nt(full[aligned(q, tok), :], wo[n, :]).astype(BF16)
            return carry

        lax.fori_loop(0, 4, chunk, 0)

    products(r)
    first_near.wait()
    pass_far.start()
    first_far.wait()
    pass_near.start()
    second_near.wait()
    products(near)
    second_far.wait()
    products(far)
    pass_far.wait()
    pass_near.wait()
    products(diag)

    def outer(c, carry):
        n = aligned(c, 256)
        grads[:, n] = dot_nn(attn_t[...], full[:, n]).astype(BF16)
        return carry

    lax.fori_loop(0, mine.shape[1] // 256, outer, 0)


def grad_branch(mine, wo, attn_t):
    tok, width = mine.shape
    return pl.pallas_call(
        branch_kernel,
        out_shape=(
            jax.ShapeDtypeStruct((4 * tok, wo.shape[0]), BF16),
            jax.ShapeDtypeStruct((wo.shape[0], width), BF16),
        ),
        in_specs=[VMEM_SPEC] * 3,
        out_specs=(VMEM_SPEC, VMEM_SPEC),
        scratch_shapes=[
            pltpu.VMEM((4 * tok, width), BF16),
            pltpu.SemaphoreType.DMA((6,)),
            pltpu.SemaphoreType.DMA((6,)),
        ],
        compiler_params=params(3),
        name="branch_exchange",
    )(mine, wo, attn_t)


def owner_sum_kernel(n_owner, n_arrays, *refs):
    arrays = refs[:n_arrays]
    outs = refs[n_arrays : 2 * n_arrays]
    scratch = refs[2 * n_arrays :]
    pair_in = scratch[:n_arrays]
    send = scratch[n_arrays : 2 * n_arrays]
    recv = scratch[2 * n_arrays : 3 * n_arrays]
    psend, precv, zsend, zrecv = scratch[3 * n_arrays :]
    r, e = lax.axis_index("dp"), lax.axis_index("expert")
    n_z = n_owner // 2
    z, core = e // 2, e % 2
    targets = [lax.rem(z + j, n_z) for j in range(n_z)]
    order = list(range(1, n_z)) + [0]
    order = order[1:2] + order[:1] + order[2:] if n_z > 2 else order
    greet([(r, e ^ 1)] + [(r, targets[j] * 2 + core) for j in range(1, n_z)])
    pair = {}
    for j in order:
        for a in range(n_arrays):
            copy = remote(
                arrays[a].at[targets[j] * 2 + (1 - core)], pair_in[a].at[j],
                psend.at[a, j], precv.at[a, j], (r, e ^ 1),
            )
            copy.start()
            pair[a, j] = copy
    moves = []
    for j in order:
        for a in range(n_arrays):
            pair[a, j].wait()
            own = arrays[a][targets[j] * 2 + core].astype(F32) + pair_in[a][j].astype(F32)
            if j == 0:
                outs[a][...] = own
            else:
                send[a][j - 1] = own.astype(BF16)
                copy = remote(
                    send[a].at[j - 1], recv[a].at[j - 1],
                    zsend.at[a, j - 1], zrecv.at[a, j - 1], (r, targets[j] * 2 + core),
                )
                copy.start()
                moves.append(copy)
    for copy in moves:
        copy.wait()
    for a in range(n_arrays):
        value = outs[a][...]
        for j in range(n_z - 1):
            value = value + recv[a][j].astype(F32)
        outs[a][...] = value


def owner_sums(arrays, n_owner, collective_id):
    n = len(arrays)
    n_z = n_owner // 2
    shapes = [a.shape[1:] for a in arrays]
    return pl.pallas_call(
        functools.partial(owner_sum_kernel, n_owner, n),
        out_shape=tuple(jax.ShapeDtypeStruct(s, F32) for s in shapes),
        in_specs=[VMEM_SPEC] * n,
        out_specs=(VMEM_SPEC,) * n,
        scratch_shapes=[pltpu.VMEM((n_z, *s), BF16) for s in shapes]
        + [pltpu.VMEM((n_z - 1, *s), BF16) for s in shapes]
        + [pltpu.VMEM((n_z - 1, *s), BF16) for s in shapes]
        + [pltpu.SemaphoreType.DMA((n, n_z))] * 2
        + [pltpu.SemaphoreType.DMA((n, n_z - 1))] * 2,
        compiler_params=params(collective_id),
        name="owner_sums",
    )(*arrays)


def masks_of(block, own_length, slots, prompt_block, prompt_len, column, keys):
    slot = lax.broadcasted_iota(jnp.int32, (slots, keys), 0)
    key = lax.broadcasted_iota(jnp.int32, (slots, keys), 1)
    is_prompt = slot < prompt_block
    position = (column * 4 + block) * prompt_block + slot
    sees_prompt = (key < prompt_len) & (jnp.logical_not(is_prompt) | (key <= position))
    cont = key - prompt_len
    sees_cont = (
        (key >= prompt_len)
        & jnp.logical_not(is_prompt)
        & (cont <= slot - prompt_block)
        & (cont < own_length)
    )
    return sees_prompt | sees_cont


def attention_fwd_kernel(prompt_len, lengths, lin, gain, cos, sin, keys, values, queries, attn):
    block = pl.program_id(0)
    slots = lin.shape[0]
    head = gain.shape[1]
    allowed = masks_of(
        block, lengths[block], slots, slots - CMAX, prompt_len, lengths[4], keys.shape[1]
    )
    scale = head ** (-0.5)
    k, v = keys[0], values[0]
    c, s, g = cos[0], sin[0], gain[...]
    for h in range(lin.shape[1] // head):
        part = slice(h * head, (h + 1) * head)
        x = lin[:, part]
        x = x * lax.rsqrt(jnp.mean(x * x, axis=-1, keepdims=True) + norm_eps) * g
        q = (x * c + pltpu.roll(x, head // 2, 1) * s).astype(BF16)
        queries[:, part] = q
        score = jnp.where(allowed, dot_nt(q, k) * scale, -jnp.inf)
        peak = jnp.max(score, axis=-1, keepdims=True)
        exponent = jnp.exp(score - peak)
        low = (exponent * (1.0 / jnp.sum(exponent, axis=-1, keepdims=True))).astype(BF16)
        attn[:, part] = dot_nn(low, v).astype(BF16)


def attention_fwd(lengths, lin, gain, cos, sin, keys, values, prompt_len):
    blocks, total_keys, head = keys.shape
    slots = lin.shape[0] // blocks
    width = lin.shape[1] - 2 * head
    row = pl.BlockSpec((slots, width), lambda i, *_: (i, 0))
    table = pl.BlockSpec((1, slots, head), lambda i, *_: (i, 0, 0))
    kv = pl.BlockSpec((1, total_keys, head), lambda i, *_: (i, 0, 0))
    one = pl.BlockSpec((1, head), lambda i, *_: (0, 0))
    return pl.pallas_call(
        functools.partial(attention_fwd_kernel, prompt_len),
        grid_spec=pltpu.PrefetchScalarGridSpec(
            num_scalar_prefetch=1,
            grid=(blocks,),
            in_specs=[row, one, table, table, kv, kv],
            out_specs=[row, row],
        ),
        out_shape=(
            jax.ShapeDtypeStruct((lin.shape[0], width), BF16),
            jax.ShapeDtypeStruct((lin.shape[0], width), BF16),
        ),
        compiler_params=params(),
        name="attention_fwd",
    )(lengths, lin, gain, cos, sin, keys, values)


def attention_bwd_kernel(
    prompt_len, lengths, lin, queries, d_attn, gain, cos, sin, keys, values, d_lin, d_keys, d_values, d_gain
):
    block = pl.program_id(0)
    slots = lin.shape[0]
    head = gain.shape[1]
    allowed = masks_of(
        block, lengths[block], slots, slots - CMAX, prompt_len, lengths[4], keys.shape[1]
    )
    scale = head ** (-0.5)
    k, v = keys[0], values[0]
    c, s, g = cos[0], sin[0], gain[...]
    key_total = jnp.zeros(k.shape, F32)
    value_total = jnp.zeros(v.shape, F32)
    gain_total = jnp.zeros((8, head), F32)
    for h in range(lin.shape[1] // head):
        part = slice(h * head, (h + 1) * head)
        q = queries[:, part]
        score = jnp.where(allowed, dot_nt(q, k) * scale, -jnp.inf)
        peak = jnp.max(score, axis=-1, keepdims=True)
        exponent = jnp.exp(score - peak)
        probs = exponent * (1.0 / jnp.sum(exponent, axis=-1, keepdims=True))
        d_out = d_attn[:, part]
        d_probs = dot_nt(d_out, v)
        inner = jnp.sum(probs * d_probs, axis=-1, keepdims=True)
        d_score = (probs * (d_probs - inner)).astype(BF16)
        key_total = key_total + dot_tn(d_score, q)
        value_total = value_total + dot_tn(probs.astype(BF16), d_out)
        d_q = dot_nn(d_score, k) * scale
        turned = d_q * c + pltpu.roll(d_q * s, head // 2, 1)
        x = lin[:, part]
        inverse = lax.rsqrt(jnp.mean(x * x, axis=-1, keepdims=True) + norm_eps)
        unit = x * inverse
        pairs = turned * unit
        for j in range(slots // 8):
            gain_total = gain_total + pairs[j * 8 : (j + 1) * 8]
        weighted = turned * g
        d_lin[:, part] = (
            inverse * (weighted - unit * jnp.mean(weighted * unit, axis=-1, keepdims=True))
        ).astype(BF16)
    d_keys[0] = key_total * scale
    d_values[0] = value_total
    d_gain[0] = gain_total


def attention_bwd(lengths, lin, queries, d_attn, gain, cos, sin, keys, values, prompt_len):
    blocks, total_keys, head = keys.shape
    slots = lin.shape[0] // blocks
    width = lin.shape[1] - 2 * head
    row = pl.BlockSpec((slots, width), lambda i, *_: (i, 0))
    table = pl.BlockSpec((1, slots, head), lambda i, *_: (i, 0, 0))
    kv = pl.BlockSpec((1, total_keys, head), lambda i, *_: (i, 0, 0))
    one = pl.BlockSpec((1, head), lambda i, *_: (0, 0))
    return pl.pallas_call(
        functools.partial(attention_bwd_kernel, prompt_len),
        grid_spec=pltpu.PrefetchScalarGridSpec(
            num_scalar_prefetch=1,
            grid=(blocks,),
            in_specs=[row, row, row, one, table, table, kv, kv],
            out_specs=[row, kv, kv, pl.BlockSpec((1, 8, head), lambda i, *_: (i, 0, 0))],
        ),
        out_shape=(
            jax.ShapeDtypeStruct((lin.shape[0], width), BF16),
            jax.ShapeDtypeStruct(keys.shape, F32),
            jax.ShapeDtypeStruct(values.shape, F32),
            jax.ShapeDtypeStruct((blocks, 8, head), F32),
        ),
        compiler_params=params(),
        name="attention_bwd",
    )(lengths, lin, queries, d_attn, gain, cos, sin, keys, values)


def partner(shard, axis, bit):
    return lax.ppermute(shard, axis, [(i, i ^ 1 << bit) for i in range(lax.axis_size(axis))])


def root_mean_scale(value_rows, gain_vec):
    return (
        value_rows
        * lax.rsqrt(jnp.mean(value_rows * value_rows, axis=-1, keepdims=True) + norm_eps)
        * gain_vec
    )


def contract(left_side, right_side, left_dim, right_dim):
    return lax.dot_general(
        left_side,
        right_side,
        (((left_dim,), (right_dim,)), ((), ())),
        preferred_element_type=F32,
    )


def head_rope(linear, gain_vec, cos, sin):
    value = root_mean_scale(linear, gain_vec)
    half = value.shape[-1] // 2
    return value * cos + jnp.roll(value, half, axis=-1) * sin


def body(
    tokens,
    teacher,
    routes,
    cont_lengths,
    query_weight,
    key_projection,
    value_projection,
    output_weight,
    router_weight,
    gate_weight,
    up_weight,
    down_weight,
    input_gain,
    post_gain,
    query_gain,
    key_gain,
):
    n_dp = lax.axis_size("dp")
    n_owner = lax.axis_size("expert")
    devices = n_dp * n_owner
    rank_dp = lax.axis_index("dp")
    rank_owner = lax.axis_index("expert")
    flat_rank = rank_dp * n_owner + rank_owner
    column = rank_owner % 2
    first_column = column == 0
    tok_dev, model_width = tokens.shape
    top_count = routes.shape[1]
    head_dim = query_gain.shape[0]
    kv_width = key_projection.shape[1]
    query_width = query_weight.shape[1]
    query_group = query_width // n_dp
    assert n_dp == 4 and kv_width == n_dp * head_dim
    ffn_width = gate_weight.shape[2]
    prompt_block = tok_dev - CMAX
    half_prompt = n_dp * prompt_block
    prompt_len = 2 * half_prompt
    capacity = max(2, tok_dev * top_count * 5 // (4 * devices))
    slots_all = devices * tok_dev
    slot_ids = jnp.arange(tok_dev, dtype=jnp.int32)
    own_length = cont_lengths[flat_rank]
    valid_slot = (slot_ids < prompt_block) | (slot_ids - prompt_block < own_length)
    valid_count = (devices * prompt_block + jnp.sum(cont_lengths)).astype(F32)
    tokens_float = tokens.astype(F32)
    normed_float, first_norm_back = jax.vjp(root_mean_scale, tokens_float, input_gain)
    normed = normed_float.astype(BF16)

    block_ids = jnp.arange(n_dp, dtype=jnp.int32)[:, None]
    positions = jnp.where(
        slot_ids[None] < prompt_block,
        (column * n_dp + block_ids) * prompt_block + slot_ids[None],
        prompt_len + slot_ids[None] - prompt_block,
    )
    half_head = head_dim // 2
    frequency = rope_base ** (-(jnp.arange(half_head, dtype=F32) * 2.0) / head_dim)
    angles = positions.astype(F32)[:, :, None] * frequency
    cos_half, sin_half = jnp.cos(angles), jnp.sin(angles)
    cos = jnp.concatenate([cos_half, cos_half], axis=-1)
    sin = jnp.concatenate([-sin_half, sin_half], axis=-1)
    lengths = jnp.concatenate(
        [lax.dynamic_index_in_dim(cont_lengths.reshape(n_dp, n_owner), rank_owner, 1, False), column[None]]
    ).astype(jnp.int32)

    lin, normed_cols = project_qkv(normed, query_weight, key_projection, value_projection)
    key_lin = lin[:, query_group : query_group + head_dim].reshape(n_dp, tok_dev, head_dim)
    keys_float, key_back = jax.vjp(lambda a, b: head_rope(a, b, cos, sin), key_lin, key_gain)
    keys_own = keys_float.astype(BF16)
    values_own = lin[:, query_group + head_dim :].reshape(n_dp, tok_dev, head_dim).astype(BF16)
    column_kv = jnp.stack([keys_own[:, :prompt_block], values_own[:, :prompt_block]]).reshape(
        2, half_prompt, head_dim
    )
    other_kv = partner(column_kv, "expert", 0)
    full_kv = jnp.where(
        first_column,
        jnp.concatenate([column_kv, other_kv], axis=1),
        jnp.concatenate([other_kv, column_kv], axis=1),
    )
    spread = jnp.broadcast_to(full_kv[:, None], (2, n_dp, prompt_len, head_dim))
    all_keys = jnp.concatenate([spread[0], keys_own[:, prompt_block:]], axis=1)
    all_values = jnp.concatenate([spread[1], values_own[:, prompt_block:]], axis=1)
    query_gain_row = query_gain[None]
    queries, attended = attention_fwd(
        lengths, lin, query_gain_row, cos, sin, all_keys, all_values, prompt_len
    )
    state = tokens_float + project_out(attended, output_weight)
    mixed_float, second_norm_back = jax.vjp(root_mean_scale, state, post_gain)
    mixed = mixed_float.astype(BF16)
    logits = jnp.dot(mixed, router_weight, preferred_element_type=jnp.float32)
    gates = jax.nn.softmax(jnp.take_along_axis(logits, routes, axis=1), axis=-1)
    rows_total = tok_dev * top_count
    expert_ids = routes.reshape(rows_total)
    live_rows = jnp.repeat(valid_slot, top_count)
    expert_range = jnp.arange(devices, dtype=jnp.int32)
    hit_table = ((expert_ids[:, None] == expert_range[None, :]) & live_rows[:, None]).astype(
        jnp.int32
    )
    earlier = jnp.cumsum(hit_table, axis=0) - hit_table
    position_in = jnp.sum(earlier * hit_table, axis=1)
    slot_index = jnp.where(live_rows, expert_ids * capacity + position_in, devices * capacity)
    row_of_slot = (
        jnp.full((devices * capacity + 1,), rows_total, jnp.int32)
        .at[slot_index]
        .set(jnp.arange(rows_total, dtype=jnp.int32))[: devices * capacity]
    )
    token_of_slot = jnp.where(row_of_slot < rows_total, row_of_slot // top_count, tok_dev)
    mixed_pad = jnp.concatenate([mixed, jnp.zeros((1, model_width), jnp.bfloat16)], axis=0)
    send_rows = mixed_pad[token_of_slot].reshape(devices, capacity, model_width)
    arrived = lax.all_to_all(send_rows, ("dp", "expert"), split_axis=0, concat_axis=0, tiled=True)
    sources = arrived.shape[0]
    items = arrived.shape[1]
    flat_in = arrived.reshape(sources * items, model_width)
    gate_pre = jnp.dot(flat_in, gate_weight[0], preferred_element_type=jnp.float32)
    up_pre = jnp.dot(flat_in, up_weight[0], preferred_element_type=jnp.float32)
    hidden_units = (jax.nn.silu(gate_pre) * up_pre).astype(jnp.bfloat16)
    produced = jnp.dot(hidden_units, down_weight[0], preferred_element_type=jnp.float32).astype(
        jnp.bfloat16
    )
    produced, gate_pre, up_pre, hidden_units, arrived = (
        produced.reshape(sources, items, model_width),
        gate_pre.reshape(sources, items, ffn_width),
        up_pre.reshape(sources, items, ffn_width),
        hidden_units.reshape(sources, items, ffn_width),
        arrived,
    )
    returned = lax.all_to_all(produced, ("dp", "expert"), split_axis=0, concat_axis=0, tiled=True)
    returned_pad = jnp.concatenate(
        [
            returned.reshape(devices * capacity, model_width),
            jnp.zeros((1, model_width), jnp.bfloat16),
        ],
        axis=0,
    )
    copies = returned_pad[slot_index].reshape(tok_dev, top_count, model_width)
    layer_out = state + jnp.sum(gates[:, :, None] * copies, axis=1)
    live_tokens = valid_slot.astype(jnp.float32)[:, None]
    diff = (layer_out - teacher.astype(jnp.float32)) * live_tokens
    local_square = jnp.sum(diff * diff)
    d_out = 2.0 * slots_all * diff / valid_count
    d_gates = jnp.sum(d_out[:, None, :] * copies, axis=-1)
    d_chosen = gates * (d_gates - jnp.sum(gates * d_gates, axis=-1, keepdims=True))
    d_logits = jnp.sum(
        jnp.where(routes[:, :, None] == expert_range[None, None, :], d_chosen[:, :, None], 0.0),
        axis=1,
    ).astype(jnp.bfloat16)
    d_copies = (
        (gates[:, :, None] * d_out[:, None, :])
        .astype(jnp.bfloat16)
        .reshape(rows_total, model_width)
    )
    d_copies_pad = jnp.concatenate([d_copies, jnp.zeros((1, model_width), jnp.bfloat16)], axis=0)
    d_send = d_copies_pad[row_of_slot].reshape(devices, capacity, model_width)
    d_arrived = lax.all_to_all(d_send, ("dp", "expert"), split_axis=0, concat_axis=0, tiled=True)
    flat_d = d_arrived.reshape(-1, model_width)
    flat_in = arrived.reshape(-1, model_width)
    flat_gate = gate_pre.reshape(-1, ffn_width)
    flat_up = up_pre.reshape(-1, ffn_width)
    flat_hidden = hidden_units.reshape(-1, ffn_width)
    d_hidden = contract(flat_d, down_weight[0], 1, 1)
    sigmoid_gate = jax.nn.sigmoid(flat_gate)
    d_gate = (d_hidden * flat_up * sigmoid_gate * (1.0 + flat_gate * (1.0 - sigmoid_gate))).astype(
        jnp.bfloat16
    )
    d_up = (d_hidden * flat_gate * sigmoid_gate).astype(jnp.bfloat16)
    down_grad = contract(flat_hidden, flat_d, 0, 0)[None]
    gate_grad = contract(flat_in, d_gate, 0, 0)[None]
    up_grad = contract(flat_in, d_up, 0, 0)[None]
    d_in = (contract(d_gate, gate_weight[0], 1, 1) + contract(d_up, up_weight[0], 1, 1)).astype(
        jnp.bfloat16
    )
    d_returned = lax.all_to_all(
        d_in.reshape(devices, capacity, model_width),
        ("dp", "expert"),
        split_axis=0,
        concat_axis=0,
        tiled=True,
    )
    d_returned_pad = jnp.concatenate(
        [
            d_returned.reshape(devices * capacity, model_width),
            jnp.zeros((1, model_width), jnp.bfloat16),
        ],
        axis=0,
    )
    d_mixed = jnp.sum(
        d_returned_pad[slot_index].reshape(tok_dev, top_count, model_width),
        axis=1,
        dtype=jnp.float32,
    )
    d_mixed = d_mixed + contract(d_logits, router_weight, 1, 1)
    router_local = contract(mixed, d_logits, 0, 0)
    d_state_norm, d_post_gain = second_norm_back(d_mixed)
    d_state = d_out + d_state_norm
    d_branch = d_state.astype(BF16)
    d_attended, out_part = grad_branch(d_branch, output_weight, attended.T)
    d_query_lin, d_keys, d_values, gain_parts = attention_bwd(
        lengths, lin, queries, d_attended, query_gain_row, cos, sin, all_keys, all_values, prompt_len
    )
    d_query_gain = jnp.sum(gain_parts, axis=(0, 1))
    prompt_grads = jnp.stack(
        [jnp.sum(d_keys[:, :prompt_len], axis=0), jnp.sum(d_values[:, :prompt_len], axis=0)]
    )
    mine_part = jnp.where(first_column, prompt_grads[:, :half_prompt], prompt_grads[:, half_prompt:])
    their_part = jnp.where(first_column, prompt_grads[:, half_prompt:], prompt_grads[:, :half_prompt])
    own_prompt = (mine_part + partner(their_part, "expert", 0)).reshape(
        2, n_dp, prompt_block, head_dim
    )
    d_key_post = jnp.concatenate([own_prompt[0], d_keys[:, prompt_len:]], axis=1)
    d_value_lin = jnp.concatenate([own_prompt[1], d_values[:, prompt_len:]], axis=1)
    d_key_float, d_key_gain = key_back(d_key_post)
    rows = n_dp * tok_dev
    d_lin = jnp.concatenate(
        [
            d_query_lin,
            d_key_float.astype(BF16).reshape(rows, head_dim),
            d_value_lin.astype(BF16).reshape(rows, head_dim),
        ],
        axis=1,
    )
    d_normed, qkv_part = grad_qkv(
        d_lin, query_weight, key_projection, value_projection, normed_cols.T
    )
    d_tokens_norm, d_input_gain = first_norm_back(d_normed)
    tokens_grad = d_state + d_tokens_norm
    width = query_weight.shape[0]
    group = d_lin.shape[1]
    rows_here = width // n_owner
    by_owner = (
        qkv_part.reshape(n_dp, n_owner, rows_here, group)
        .transpose(1, 0, 2, 3)
        .reshape(n_owner, n_dp * rows_here, group)
    )
    qkv_rows, output_grad = owner_sums(
        [by_owner, out_part.reshape(n_owner, -1, model_width)], n_owner, 5
    )
    qkv_rows = qkv_rows.reshape(n_dp, rows_here, group)

    def columns(start, size):
        return qkv_rows[:, :, start : start + size].transpose(1, 0, 2).reshape(rows_here, n_dp * size)

    query_grad = columns(0, query_group)
    key_grad = columns(query_group, head_dim)
    value_grad = columns(query_group + head_dim, head_dim)
    total_square, input_gain_grad, post_gain_grad, query_gain_grad, key_gain_grad, router_grad = (
        lax.psum(
            (local_square, d_input_gain, d_post_gain, d_query_gain, d_key_gain, router_local),
            ("dp", "expert"),
        )
    )
    loss = total_square / (valid_count * model_width)
    return (
        layer_out,
        loss,
        tokens_grad,
        query_grad,
        key_grad,
        value_grad,
        output_grad,
        router_grad,
        gate_grad,
        up_grad,
        down_grad,
        input_gain_grad,
        post_gain_grad,
        query_gain_grad,
        key_gain_grad,
    )


def solution(mesh):
    in_specs = (
        P(("dp", "expert"), None),
        P(("dp", "expert"), None),
        P(("dp", "expert"), None),
        P(),
        P("dp", None),
        P("dp", None),
        P("dp", None),
        P("dp", None),
        P(),
        P(("dp", "expert"), None, None),
        P(("dp", "expert"), None, None),
        P(("dp", "expert"), None, None),
        P(),
        P(),
        P(),
        P(),
    )
    out_specs = (
        P(("dp", "expert"), None),
        P(),
        P(("dp", "expert"), None),
        P(("dp", "expert"), None),
        P(("dp", "expert"), None),
        P(("dp", "expert"), None),
        P(("dp", "expert"), None),
        P(),
        P(("dp", "expert"), None, None),
        P(("dp", "expert"), None, None),
        P(("dp", "expert"), None, None),
        P(),
        P(),
        P(),
        P(),
    )
    return jax.shard_map(body, mesh=mesh, in_specs=in_specs, out_specs=out_specs, check_vma=False)
```

```python
import functools

import jax
import jax.numpy as jnp
from jax import lax
from jax.experimental import pallas as pl
from jax.experimental.pallas import tpu as pltpu
from jax.sharding import PartitionSpec as P

CMAX = 128
norm_eps = 1e-06
rope_base = 1000000.0
MESH = pl.DeviceIdType.MESH
F32 = jnp.float32
BF16 = jnp.bfloat16
VMEM_SPEC = pl.BlockSpec(memory_space=pltpu.VMEM)
ANY_SPEC = pl.BlockSpec(memory_space=pl.ANY)
VMEM_LIMIT = 56 * 1024 * 1024


def params(collective_id=None):
    return pltpu.CompilerParams(
        collective_id=collective_id,
        has_side_effects=collective_id is not None,
        vmem_limit_bytes=VMEM_LIMIT,
    )


def greet(devices):
    barrier = pltpu.get_barrier_semaphore()
    for device in devices:
        pl.semaphore_signal(barrier, inc=1, device_id=device, device_id_type=MESH)
    pl.semaphore_wait(barrier, len(devices))


def remote(src, dst, send_sem, recv_sem, device):
    return pltpu.make_async_remote_copy(
        src_ref=src,
        dst_ref=dst,
        send_sem=send_sem,
        recv_sem=recv_sem,
        device_id=device,
        device_id_type=MESH,
    )


def aligned(index, size):
    return pl.ds(pl.multiple_of(index * size, size), size)


def dot_nn(a, b):
    return lax.dot_general(a, b, (((1,), (0,)), ((), ())), preferred_element_type=F32)


def dot_nt(a, b):
    return lax.dot_general(a, b, (((1,), (1,)), ((), ())), preferred_element_type=F32)


def dot_tn(a, b):
    return lax.dot_general(a, b, (((0,), (0,)), ((), ())), preferred_element_type=F32)


PEER_MASKS = (3, 1, 2)


def qkv_kernel(tok, normed, wq, wk, wv, lin, cols, send, recv, asend, arecv, ssem, rsem):
    r, e = lax.axis_index("dp"), lax.axis_index("expert")
    peers = [r ^ m for m in PEER_MASKS]
    width = wq.shape[0]
    qg = wq.shape[1] // 4
    kg = wk.shape[1] // 4
    rows = cols.shape[0]
    greet([(p, e) for p in peers])
    first = []
    for i, p in enumerate(peers):
        copy = remote(
            normed.at[:, aligned(p, width)], cols.at[aligned(r, tok), :],
            asend.at[i], arecv.at[i], (p, e),
        )
        copy.start()
        first.append(copy)
    cols[aligned(r, tok), :] = normed[:, aligned(r, width)]
    for copy in first:
        copy.wait()

    def products(p, dst):
        def chunk(c, carry):
            t = aligned(c, tok)
            x = cols[t, :]
            dst[t, :qg] = dot_nn(x, wq[:, aligned(p, qg)]).astype(dst.dtype)
            dst[t, qg : qg + kg] = dot_nn(x, wk[:, aligned(p, kg)]).astype(dst.dtype)
            dst[t, qg + kg :] = dot_nn(x, wv[:, aligned(p, kg)]).astype(dst.dtype)
            return carry

        lax.fori_loop(0, rows // tok, chunk, 0)

    second = []
    for i, p in enumerate(peers):
        products(p, send.at[i])
        copy = remote(send.at[i], recv.at[i], ssem.at[i], rsem.at[i], (p, e))
        copy.start()
        second.append(copy)
    products(r, lin)
    for i in (1, 2, 0):
        second[i].wait()

    def total(c, carry):
        t = aligned(c, 32)
        lin[t, :] = lin[t, :] + (
            recv[0, t, :].astype(F32) + recv[1, t, :].astype(F32) + recv[2, t, :].astype(F32)
        )
        return carry

    lax.fori_loop(0, rows // 32, total, 0)


def project_qkv(normed, wq, wk, wv):
    tok = normed.shape[0]
    rows = 4 * tok
    group = (wq.shape[1] + wk.shape[1] + wv.shape[1]) // 4
    return pl.pallas_call(
        functools.partial(qkv_kernel, tok),
        out_shape=(
            jax.ShapeDtypeStruct((rows, group), F32),
            jax.ShapeDtypeStruct((rows, wq.shape[0]), BF16),
        ),
        in_specs=[VMEM_SPEC] * 4,
        out_specs=(VMEM_SPEC, VMEM_SPEC),
        scratch_shapes=[
            pltpu.VMEM((3, rows, group), BF16),
            pltpu.VMEM((3, rows, group), BF16),
        ]
        + [pltpu.SemaphoreType.DMA((3,))] * 4,
        compiler_params=params(1),
        name="qkv_exchange",
    )(normed, wq, wk, wv)


def out_kernel(attn, wo, total, send, recv, ssem, rsem):
    r, e = lax.axis_index("dp"), lax.axis_index("expert")
    peers = [r ^ m for m in PEER_MASKS]
    tok = total.shape[0]
    width = total.shape[1]
    step = width // 4
    greet([(p, e) for p in peers])

    def products(p, dst):
        def chunk(c, carry):
            n = aligned(c, step)
            dst[:, n] = dot_nn(attn[aligned(p, tok), :], wo[:, n]).astype(dst.dtype)
            return carry

        lax.fori_loop(0, width // step, chunk, 0)

    copies = []
    for i, p in enumerate(peers):
        products(p, send.at[i])
        copy = remote(send.at[i], recv.at[i], ssem.at[i], rsem.at[i], (p, e))
        copy.start()
        copies.append(copy)
    products(r, total)
    for i in (1, 2, 0):
        copies[i].wait()

    def add(c, carry):
        t = aligned(c, 32)
        total[t, :] = total[t, :] + (
            recv[0, t, :].astype(F32) + recv[1, t, :].astype(F32) + recv[2, t, :].astype(F32)
        )
        return carry

    lax.fori_loop(0, tok // 32, add, 0)


def project_out(attn, wo):
    tok = attn.shape[0] // 4
    return pl.pallas_call(
        out_kernel,
        out_shape=jax.ShapeDtypeStruct((tok, wo.shape[1]), F32),
        in_specs=[VMEM_SPEC] * 2,
        out_specs=VMEM_SPEC,
        scratch_shapes=[
            pltpu.VMEM((3, tok, wo.shape[1]), BF16),
            pltpu.VMEM((3, tok, wo.shape[1]), BF16),
        ]
        + [pltpu.SemaphoreType.DMA((3,))] * 2,
        compiler_params=params(2),
        name="out_exchange",
    )(attn, wo)


def dgrad_kernel(mine, wq, wk, wv, cols_t, normal, grads, blocks, dsum, dsend, drecv, ssem, rsem, bsend, brecv):
    r, e = lax.axis_index("dp"), lax.axis_index("expert")
    rows = mine.shape[0]
    tok = rows // 4
    half = rows // 2
    qg = wq.shape[1] // 4
    kg = wk.shape[1] // 4
    width = wq.shape[0]
    peers = [r ^ m for m in PEER_MASKS]
    near, far, diag = r ^ 1, r ^ 2, r ^ 3
    greet([(p, e) for p in peers])
    low, high = pl.ds(0, half), pl.ds(half, half)
    first_near = remote(mine.at[low], blocks.at[0, low], ssem.at[0], rsem.at[0], (near, e))
    first_far = remote(mine.at[high], blocks.at[1, high], ssem.at[1], rsem.at[1], (far, e))
    second_near = remote(mine.at[high], blocks.at[0, high], ssem.at[2], rsem.at[2], (near, e))
    second_far = remote(mine.at[low], blocks.at[1, low], ssem.at[3], rsem.at[3], (far, e))
    pass_far = remote(blocks.at[0, low], blocks.at[2, low], ssem.at[4], rsem.at[4], (far, e))
    pass_near = remote(blocks.at[1, high], blocks.at[2, high], ssem.at[5], rsem.at[5], (near, e))
    for copy in (first_near, first_far, second_near, second_far):
        copy.start()

    def products(p, src, start):
        def chunk(c, carry):
            t = aligned(c, tok)
            x = src[t, :]
            value = (
                dot_nt(x[:, :qg], wq[:, aligned(p, qg)])
                + dot_nt(x[:, qg : qg + kg], wk[:, aligned(p, kg)])
                + dot_nt(x[:, qg + kg :], wv[:, aligned(p, kg)])
            )
            if start:
                dsum[t, :] = value
            else:
                dsum[t, :] = dsum[t, :] + value
            return carry

        lax.fori_loop(0, 4, chunk, 0)

        def outer(c, carry):
            n = aligned(c, 128)
            grads[aligned(p, width), n] = dot_nn(cols_t[...], src[:, n]).astype(BF16)
            return carry

        lax.fori_loop(0, (qg + 2 * kg) // 128, outer, 0)

    products(r, mine, True)
    first_near.wait()
    pass_far.start()
    first_far.wait()
    pass_near.start()
    second_near.wait()
    products(near, blocks.at[0], False)
    second_far.wait()
    products(far, blocks.at[1], False)
    pass_far.wait()
    pass_near.wait()
    products(diag, blocks.at[2], False)
    back = []
    for i, p in enumerate(peers):
        dsend[i] = dsum[aligned(p, tok), :].astype(BF16)
        copy = remote(dsend.at[i], drecv.at[i], bsend.at[i], brecv.at[i], (p, e))
        copy.start()
        back.append(copy)
    normal[:, aligned(r, width)] = dsum[aligned(r, tok), :]
    for i, p in enumerate(peers):
        back[i].wait()
        normal[:, aligned(p, width)] = drecv[i].astype(F32)


def grad_qkv(mine, wq, wk, wv, cols_t):
    rows, group = mine.shape
    tok = rows // 4
    width = wq.shape[0]
    return pl.pallas_call(
        dgrad_kernel,
        out_shape=(
            jax.ShapeDtypeStruct((tok, 4 * width), F32),
            jax.ShapeDtypeStruct((4 * width, group), BF16),
        ),
        in_specs=[VMEM_SPEC] * 5,
        out_specs=(VMEM_SPEC, VMEM_SPEC),
        scratch_shapes=[
            pltpu.VMEM((3, rows, group), BF16),
            pltpu.VMEM((rows, width), F32),
            pltpu.VMEM((3, tok, width), BF16),
            pltpu.VMEM((3, tok, width), BF16),
            pltpu.SemaphoreType.DMA((6,)),
            pltpu.SemaphoreType.DMA((6,)),
            pltpu.SemaphoreType.DMA((3,)),
            pltpu.SemaphoreType.DMA((3,)),
        ],
        compiler_params=params(4),
        name="dqkv_exchange",
    )(mine, wq, wk, wv, cols_t)


def branch_kernel(mine, wo, attn_t, d_attn, grads, full, ssem, rsem):
    r, e = lax.axis_index("dp"), lax.axis_index("expert")
    tok = mine.shape[0]
    half = tok // 2
    peers = [r ^ m for m in PEER_MASKS]
    near, far, diag = r ^ 1, r ^ 2, r ^ 3
    greet([(p, e) for p in peers])

    def part(q, which):
        return pl.ds(pl.multiple_of(q * tok + which * half, half), half)

    low, high = pl.ds(0, half), pl.ds(half, half)
    first_near = remote(mine.at[low], full.at[part(r, 0)], ssem.at[0], rsem.at[0], (near, e))
    first_far = remote(mine.at[high], full.at[part(r, 1)], ssem.at[1], rsem.at[1], (far, e))
    second_near = remote(mine.at[high], full.at[part(r, 1)], ssem.at[2], rsem.at[2], (near, e))
    second_far = remote(mine.at[low], full.at[part(r, 0)], ssem.at[3], rsem.at[3], (far, e))
    pass_far = remote(full.at[part(near, 0)], full.at[part(near, 0)], ssem.at[4], rsem.at[4], (far, e))
    pass_near = remote(full.at[part(far, 1)], full.at[part(far, 1)], ssem.at[5], rsem.at[5], (near, e))
    for copy in (first_near, first_far, second_near, second_far):
        copy.start()
    full[aligned(r, tok), :] = mine[...]
    heads = wo.shape[0]
    step = heads // 4

    def products(q):
        def chunk(c, carry):
            n = aligned(c, step)
            d_attn[aligned(q, tok), n] = dot_nt(full[aligned(q, tok), :], wo[n, :]).astype(BF16)
            return carry

        lax.fori_loop(0, 4, chunk, 0)

    products(r)
    first_near.wait()
    pass_far.start()
    first_far.wait()
    pass_near.start()
    second_near.wait()
    products(near)
    second_far.wait()
    products(far)
    pass_far.wait()
    pass_near.wait()
    products(diag)

    def outer(c, carry):
        n = aligned(c, 256)
        grads[:, n] = dot_nn(attn_t[...], full[:, n]).astype(BF16)
        return carry

    lax.fori_loop(0, mine.shape[1] // 256, outer, 0)


def grad_branch(mine, wo, attn_t):
    tok, width = mine.shape
    return pl.pallas_call(
        branch_kernel,
        out_shape=(
            jax.ShapeDtypeStruct((4 * tok, wo.shape[0]), BF16),
            jax.ShapeDtypeStruct((wo.shape[0], width), BF16),
        ),
        in_specs=[VMEM_SPEC] * 3,
        out_specs=(VMEM_SPEC, VMEM_SPEC),
        scratch_shapes=[
            pltpu.VMEM((4 * tok, width), BF16),
            pltpu.SemaphoreType.DMA((6,)),
            pltpu.SemaphoreType.DMA((6,)),
        ],
        compiler_params=params(3),
        name="branch_exchange",
    )(mine, wo, attn_t)


def owner_sum_kernel(n_owner, n_arrays, *refs):
    arrays = refs[:n_arrays]
    outs = refs[n_arrays : 2 * n_arrays]
    scratch = refs[2 * n_arrays :]
    pair_in = scratch[:n_arrays]
    send = scratch[n_arrays : 2 * n_arrays]
    recv = scratch[2 * n_arrays : 3 * n_arrays]
    psend, precv, zsend, zrecv = scratch[3 * n_arrays :]
    r, e = lax.axis_index("dp"), lax.axis_index("expert")
    n_z = n_owner // 2
    z, core = e // 2, e % 2
    targets = [lax.rem(z + j, n_z) for j in range(n_z)]
    order = list(range(1, n_z)) + [0]
    order = order[1:2] + order[:1] + order[2:] if n_z > 2 else order
    greet([(r, e ^ 1)] + [(r, targets[j] * 2 + core) for j in range(1, n_z)])
    pair = {}
    for j in order:
        for a in range(n_arrays):
            copy = remote(
                arrays[a].at[targets[j] * 2 + (1 - core)], pair_in[a].at[j],
                psend.at[a, j], precv.at[a, j], (r, e ^ 1),
            )
            copy.start()
            pair[a, j] = copy
    moves = []
    for j in order:
        for a in range(n_arrays):
            pair[a, j].wait()
            own = arrays[a][targets[j] * 2 + core].astype(F32) + pair_in[a][j].astype(F32)
            if j == 0:
                outs[a][...] = own
            else:
                send[a][j - 1] = own.astype(BF16)
                copy = remote(
                    send[a].at[j - 1], recv[a].at[j - 1],
                    zsend.at[a, j - 1], zrecv.at[a, j - 1], (r, targets[j] * 2 + core),
                )
                copy.start()
                moves.append(copy)
    for copy in moves:
        copy.wait()
    for a in range(n_arrays):
        value = outs[a][...]
        for j in range(n_z - 1):
            value = value + recv[a][j].astype(F32)
        outs[a][...] = value


def owner_sums(arrays, n_owner, collective_id):
    n = len(arrays)
    n_z = n_owner // 2
    shapes = [a.shape[1:] for a in arrays]
    return pl.pallas_call(
        functools.partial(owner_sum_kernel, n_owner, n),
        out_shape=tuple(jax.ShapeDtypeStruct(s, F32) for s in shapes),
        in_specs=[VMEM_SPEC] * n,
        out_specs=(VMEM_SPEC,) * n,
        scratch_shapes=[pltpu.VMEM((n_z, *s), BF16) for s in shapes]
        + [pltpu.VMEM((n_z - 1, *s), BF16) for s in shapes]
        + [pltpu.VMEM((n_z - 1, *s), BF16) for s in shapes]
        + [pltpu.SemaphoreType.DMA((n, n_z))] * 2
        + [pltpu.SemaphoreType.DMA((n, n_z - 1))] * 2,
        compiler_params=params(collective_id),
        name="owner_sums",
    )(*arrays)


def masks_of(block, own_length, slots, prompt_block, prompt_len, column, keys):
    slot = lax.broadcasted_iota(jnp.int32, (slots, keys), 0)
    key = lax.broadcasted_iota(jnp.int32, (slots, keys), 1)
    is_prompt = slot < prompt_block
    position = (column * 4 + block) * prompt_block + slot
    sees_prompt = (key < prompt_len) & (jnp.logical_not(is_prompt) | (key <= position))
    cont = key - prompt_len
    sees_cont = (
        (key >= prompt_len)
        & jnp.logical_not(is_prompt)
        & (cont <= slot - prompt_block)
        & (cont < own_length)
    )
    return sees_prompt | sees_cont


def attention_fwd_kernel(prompt_len, lengths, lin, gain, cos, sin, keys, values, queries, attn):
    block = pl.program_id(0)
    slots = lin.shape[0]
    head = gain.shape[1]
    allowed = masks_of(
        block, lengths[block], slots, slots - CMAX, prompt_len, lengths[4], keys.shape[1]
    )
    scale = head ** (-0.5)
    k, v = keys[0], values[0]
    c, s, g = cos[0], sin[0], gain[...]
    for h in range(lin.shape[1] // head):
        part = slice(h * head, (h + 1) * head)
        x = lin[:, part]
        x = x * lax.rsqrt(jnp.mean(x * x, axis=-1, keepdims=True) + norm_eps) * g
        q = (x * c + pltpu.roll(x, head // 2, 1) * s).astype(BF16)
        queries[:, part] = q
        score = jnp.where(allowed, dot_nt(q, k) * scale, -jnp.inf)
        peak = jnp.max(score, axis=-1, keepdims=True)
        exponent = jnp.exp(score - peak)
        low = (exponent * (1.0 / jnp.sum(exponent, axis=-1, keepdims=True))).astype(BF16)
        attn[:, part] = dot_nn(low, v).astype(BF16)


def attention_fwd(lengths, lin, gain, cos, sin, keys, values, prompt_len):
    blocks, total_keys, head = keys.shape
    slots = lin.shape[0] // blocks
    width = lin.shape[1] - 2 * head
    row = pl.BlockSpec((slots, width), lambda i, *_: (i, 0))
    table = pl.BlockSpec((1, slots, head), lambda i, *_: (i, 0, 0))
    kv = pl.BlockSpec((1, total_keys, head), lambda i, *_: (i, 0, 0))
    one = pl.BlockSpec((1, head), lambda i, *_: (0, 0))
    return pl.pallas_call(
        functools.partial(attention_fwd_kernel, prompt_len),
        grid_spec=pltpu.PrefetchScalarGridSpec(
            num_scalar_prefetch=1,
            grid=(blocks,),
            in_specs=[row, one, table, table, kv, kv],
            out_specs=[row, row],
        ),
        out_shape=(
            jax.ShapeDtypeStruct((lin.shape[0], width), BF16),
            jax.ShapeDtypeStruct((lin.shape[0], width), BF16),
        ),
        compiler_params=params(),
        name="attention_fwd",
    )(lengths, lin, gain, cos, sin, keys, values)


def attention_bwd_kernel(
    prompt_len, lengths, lin, queries, d_attn, gain, cos, sin, keys, values, d_lin, d_keys, d_values, d_gain
):
    block = pl.program_id(0)
    slots = lin.shape[0]
    head = gain.shape[1]
    allowed = masks_of(
        block, lengths[block], slots, slots - CMAX, prompt_len, lengths[4], keys.shape[1]
    )
    scale = head ** (-0.5)
    k, v = keys[0], values[0]
    c, s, g = cos[0], sin[0], gain[...]
    key_total = jnp.zeros(k.shape, F32)
    value_total = jnp.zeros(v.shape, F32)
    gain_total = jnp.zeros((8, head), F32)
    for h in range(lin.shape[1] // head):
        part = slice(h * head, (h + 1) * head)
        q = queries[:, part]
        score = jnp.where(allowed, dot_nt(q, k) * scale, -jnp.inf)
        peak = jnp.max(score, axis=-1, keepdims=True)
        exponent = jnp.exp(score - peak)
        probs = exponent * (1.0 / jnp.sum(exponent, axis=-1, keepdims=True))
        d_out = d_attn[:, part]
        d_probs = dot_nt(d_out, v)
        inner = jnp.sum(probs * d_probs, axis=-1, keepdims=True)
        d_score = (probs * (d_probs - inner)).astype(BF16)
        key_total = key_total + dot_tn(d_score, q)
        value_total = value_total + dot_tn(probs.astype(BF16), d_out)
        d_q = dot_nn(d_score, k) * scale
        turned = d_q * c + pltpu.roll(d_q * s, head // 2, 1)
        x = lin[:, part]
        inverse = lax.rsqrt(jnp.mean(x * x, axis=-1, keepdims=True) + norm_eps)
        unit = x * inverse
        pairs = turned * unit
        for j in range(slots // 8):
            gain_total = gain_total + pairs[j * 8 : (j + 1) * 8]
        weighted = turned * g
        d_lin[:, part] = (
            inverse * (weighted - unit * jnp.mean(weighted * unit, axis=-1, keepdims=True))
        ).astype(BF16)
    d_keys[0] = key_total * scale
    d_values[0] = value_total
    d_gain[0] = gain_total


def attention_bwd(lengths, lin, queries, d_attn, gain, cos, sin, keys, values, prompt_len):
    blocks, total_keys, head = keys.shape
    slots = lin.shape[0] // blocks
    width = lin.shape[1] - 2 * head
    row = pl.BlockSpec((slots, width), lambda i, *_: (i, 0))
    table = pl.BlockSpec((1, slots, head), lambda i, *_: (i, 0, 0))
    kv = pl.BlockSpec((1, total_keys, head), lambda i, *_: (i, 0, 0))
    one = pl.BlockSpec((1, head), lambda i, *_: (0, 0))
    return pl.pallas_call(
        functools.partial(attention_bwd_kernel, prompt_len),
        grid_spec=pltpu.PrefetchScalarGridSpec(
            num_scalar_prefetch=1,
            grid=(blocks,),
            in_specs=[row, row, row, one, table, table, kv, kv],
            out_specs=[row, kv, kv, pl.BlockSpec((1, 8, head), lambda i, *_: (i, 0, 0))],
        ),
        out_shape=(
            jax.ShapeDtypeStruct((lin.shape[0], width), BF16),
            jax.ShapeDtypeStruct(keys.shape, F32),
            jax.ShapeDtypeStruct(values.shape, F32),
            jax.ShapeDtypeStruct((blocks, 8, head), F32),
        ),
        compiler_params=params(),
        name="attention_bwd",
    )(lengths, lin, queries, d_attn, gain, cos, sin, keys, values)


def partner(shard, axis, bit):
    return lax.ppermute(shard, axis, [(i, i ^ 1 << bit) for i in range(lax.axis_size(axis))])


def root_mean_scale(value_rows, gain_vec):
    return (
        value_rows
        * lax.rsqrt(jnp.mean(value_rows * value_rows, axis=-1, keepdims=True) + norm_eps)
        * gain_vec
    )


def contract(left_side, right_side, left_dim, right_dim):
    return lax.dot_general(
        left_side,
        right_side,
        (((left_dim,), (right_dim,)), ((), ())),
        preferred_element_type=F32,
    )


def plane_order(z):
    upper, odd = z // 2, z % 2
    return [z, z + 1 - 2 * upper, 2 + upper - 2 * odd, 3 - 3 * upper]


def world(with_diag):
    r, e = lax.axis_index("dp"), lax.axis_index("expert")
    z, core = e // 2, e % 2
    near, far = r ^ 1, r ^ 2
    devices = [(near, e), (far, e), (r, e ^ 1)]
    devices += [(r, lax.rem(z + j, 4) * 2 + core) for j in (1, 2, 3)]
    return r, e, z, core, near, far, devices


def gather_world(mine, buf, zs, zr, ps, pr, ds, dr, before, group):
    r, e, z, core, near, far, greeted = world(True)
    half = mine.shape[0] // 2
    low, high = pl.ds(0, half), pl.ds(half, half)
    order = plane_order(z)
    greet(greeted)

    def slot(q, b, c):
        return q * 8 + b * 2 + c

    buf[slot(r, z, core)] = mine[...]
    diag = r ^ 3
    plane, pairs, lines = {}, {}, []

    def hand(k, i, q):
        at = slot(q, order[k], core)
        copy = remote(buf.at[at], buf.at[at], ds.at[k, i], dr.at[k, i], (r, e ^ 1))
        copy.start()
        pairs[k, i] = copy

    def issue(k):
        b = order[k]
        at = slot(r, b, core)
        for side, cond, to in (
            (0, (b <= z) & (z < 3), jnp.minimum(z + 1, 3)),
            (1, (b >= z) & (z > 0), jnp.maximum(z - 1, 0)),
        ):
            copy = remote(buf.at[at], buf.at[at], zs.at[k, side], zr.at[b], (r, to * 2 + core))
            lines.append((cond, copy))

            @pl.when(cond)
            def _():
                copy.start()

        mine_at, near_at, far_at = at, slot(near, b, core), slot(far, b, core)
        for i, (src, part, p) in enumerate(
            (
                (mine_at, low, near),
                (mine_at, high, far),
                (mine_at, high, near),
                (mine_at, low, far),
                (near_at, low, far),
                (far_at, high, near),
            )
        ):
            plane[k, i] = remote(
                buf.at[src, part], buf.at[src, part], ps.at[k, i], pr.at[k, i], (p, e)
            )
        for i in range(4):
            plane[k, i].start()
        hand(k, 0, r)

    def line_wait(k):
        b = order[k]
        at = slot(r, b, core)
        remote(buf.at[at], buf.at[at], zs.at[k, 0], zr.at[b], (r, e ^ 1)).wait_recv()
        issue(k)

    def passes(k):
        plane[k, 0].wait_recv()
        plane[k, 4].start()
        plane[k, 1].wait_recv()
        plane[k, 5].start()

    def finish(k):
        plane[k, 2].wait_recv()
        hand(k, 1, near)
        plane[k, 3].wait_recv()
        hand(k, 2, far)

    def corner(k):
        plane[k, 4].wait_recv()
        plane[k, 5].wait_recv()
        hand(k, 3, diag)

    def ready(k):
        for i in range(4):
            pairs[k, i].wait_recv()
        group(k, order[k])

    issue(0)
    passes(0)
    line_wait(1)
    finish(0)
    passes(1)
    line_wait(2)
    corner(0)
    finish(1)
    before(0, order[0])
    ready(0)
    passes(2)
    line_wait(3)
    corner(1)
    finish(2)
    before(1, order[1])
    ready(1)
    passes(3)
    corner(2)
    finish(3)
    before(2, order[2])
    ready(2)
    before(3, order[3])
    corner(3)
    ready(3)
    for copy in plane.values():
        copy.wait_send()
    for copy in pairs.values():
        copy.wait_send()
    for cond, copy in lines:

        @pl.when(cond)
        def _():
            copy.wait_send()


GATHER_SEMS = [
    pltpu.SemaphoreType.DMA((4, 2)),
    pltpu.SemaphoreType.DMA((4,)),
    pltpu.SemaphoreType.DMA((4, 6)),
    pltpu.SemaphoreType.DMA((4, 6)),
    pltpu.SemaphoreType.DMA((4, 4)),
    pltpu.SemaphoreType.DMA((4, 4)),
]


def selector(pos, source, room):
    row = pos[source]
    ids = lax.broadcasted_iota(jnp.int32, (room, row.shape[1]), 0)
    return jnp.where(ids == row, 1.0, 0.0).astype(BF16)


def experts_fwd_kernel(
    mine, pos, wg, wu, wd, x_out, y_out, gate_out,
    buf, wg_v, wu_v, wd_v, x_v, y_v, hid_v, gate_v, local, zs, zr, ps, pr, ds, dr,
):
    model = wg.shape[0]
    room = x_v.shape[0] // 8
    me = lax.axis_index("dp") * 8 + lax.axis_index("expert")
    loads = [
        pltpu.make_async_copy(a, b, local.at[i])
        for i, (a, b) in enumerate(((wg, wg_v), (wu, wu_v), (wd, wd_v)))
    ]
    for copy in loads:
        copy.start()

    def before(k, b):
        if k == 0:
            for copy in loads:
                copy.wait()

    def group(k, b):
        def pick(j, carry):
            s = j // 2 * 8 + b * 2 + j % 2
            rows = aligned(j, room)
            sel = selector(pos, s, room)
            for c in range(4):
                n = slice(c * model // 4, (c + 1) * model // 4)
                x_v[rows, n] = dot_nn(sel, buf[s, :, n]).astype(BF16)
            extra = dot_nn(sel, buf[s, :, model:])
            lane = lax.broadcasted_iota(jnp.int32, extra.shape, 1)
            hit = (lane == me) | (lane == me + 64)
            gate = jnp.sum(jnp.where(hit, extra, 0.0), axis=-1, keepdims=True)
            gate_v[rows, :] = jnp.broadcast_to(gate, extra.shape)
            return carry

        lax.fori_loop(0, 8, pick, 0)

        def first(c, carry):
            n = aligned(c, 256)
            g = dot_nn(x_v[...], wg_v[:, n])
            u = dot_nn(x_v[...], wu_v[:, n])
            hid_v[:, n] = (g / (1.0 + jnp.exp(-g)) * u).astype(BF16)
            return carry

        lax.fori_loop(0, wg.shape[1] // 256, first, 0)

        def second(c, carry):
            n = aligned(c, 256)
            o = dot_nn(hid_v[...], wd_v[:, n]).astype(BF16).astype(F32)
            y_v[:, n] = (o * gate_v[:, :1]).astype(BF16)
            return carry

        lax.fori_loop(0, model // 256, second, 0)
        outs = [
            pltpu.make_async_copy(a, o.at[b], local.at[i])
            for i, (a, o) in enumerate(((x_v, x_out), (y_v, y_out), (gate_v, gate_out)))
        ]
        for copy in outs:
            copy.start()
        for copy in outs:
            copy.wait()

    gather_world(mine, buf, zs, zr, ps, pr, ds, dr, before, group)


def experts_fwd(mine, pos, wg, wu, wd, room):
    rows, width = mine.shape
    model, ff = wg.shape
    group = 8 * room
    return pl.pallas_call(
        experts_fwd_kernel,
        out_shape=(
            jax.ShapeDtypeStruct((4, group, model), BF16),
            jax.ShapeDtypeStruct((4, group, model), BF16),
            jax.ShapeDtypeStruct((4, group, 128), F32),
        ),
        in_specs=[VMEM_SPEC, VMEM_SPEC, ANY_SPEC, ANY_SPEC, ANY_SPEC],
        out_specs=(ANY_SPEC,) * 3,
        scratch_shapes=[
            pltpu.VMEM((32, rows, width), BF16),
            pltpu.VMEM((model, ff), BF16),
            pltpu.VMEM((model, ff), BF16),
            pltpu.VMEM((ff, model), BF16),
            pltpu.VMEM((group, model), BF16),
            pltpu.VMEM((group, model), BF16),
            pltpu.VMEM((group, ff), BF16),
            pltpu.VMEM((group, 128), F32),
            pltpu.SemaphoreType.DMA((3,)),
        ]
        + GATHER_SEMS,
        compiler_params=params(6),
        name="experts_fwd",
    )(mine, pos, wg, wu, wd)


def experts_bwd_kernel(
    mine, pos, x_in, gate_in, wg, wu, wd, y_out, d_copy_out, hid_out, dg_out, du_out,
    buf, wg_v, wu_v, wd_v, x_v, gate_v, g_v, u_v, o_v, y_v, d_copy_v, hid_v, dg_v, du_v,
    local, zs, zr, ps, pr, ds, dr,
):
    model, ff = wg.shape
    room = x_v.shape[0] // 8
    me = lax.axis_index("dp") * 8 + lax.axis_index("expert")
    loads = [
        pltpu.make_async_copy(a, b, local.at[i])
        for i, (a, b) in enumerate(((wg, wg_v), (wu, wu_v), (wd, wd_v)))
    ]
    for copy in loads:
        copy.start()

    def before(k, b):
        if k == 0:
            for copy in loads:
                copy.wait()
        ins = [
            pltpu.make_async_copy(x_in.at[b], x_v, local.at[3]),
            pltpu.make_async_copy(gate_in.at[b], gate_v, local.at[4]),
        ]
        for copy in ins:
            copy.start()
        for copy in ins:
            copy.wait()

        def first(c, carry):
            n = aligned(c, 256)
            g = dot_nn(x_v[...], wg_v[:, n])
            u = dot_nn(x_v[...], wu_v[:, n])
            g_v[:, n] = g
            u_v[:, n] = u
            hid_v[:, n] = (g / (1.0 + jnp.exp(-g)) * u).astype(BF16)
            return carry

        lax.fori_loop(0, ff // 256, first, 0)

        def second(c, carry):
            n = aligned(c, 256)
            o_v[:, n] = dot_nn(hid_v[...], wd_v[:, n]).astype(BF16)
            return carry

        lax.fori_loop(0, model // 256, second, 0)

    def group(k, b):
        def pick(j, carry):
            s = j // 2 * 8 + b * 2 + j % 2
            rows = aligned(j, room)
            sel = selector(pos, s, room)
            gate = gate_v[rows, :1]
            inner = jnp.zeros((room, 1), F32)
            for c in range(4):
                n = slice(c * model // 4, (c + 1) * model // 4)
                picked = dot_nn(sel, buf[s, :, n])
                d_copy_v[rows, n] = (gate * picked).astype(BF16)
                inner = inner + jnp.sum(picked * o_v[rows, n].astype(F32), axis=-1, keepdims=True)
            top = inner.astype(BF16).astype(F32)
            rest = inner - top
            lane = lax.broadcasted_iota(jnp.int32, (room, 128), 1)
            extra = jnp.where(lane == me, top, 0.0) + jnp.where(lane == me + 64, rest, 0.0)
            y_v[rows, model:] = extra.astype(BF16)
            return carry

        lax.fori_loop(0, 8, pick, 0)

        def third(c, carry):
            n = aligned(c, 256)
            d_hidden = dot_nt(d_copy_v[...], wd_v[n, :])
            g, u = g_v[:, n], u_v[:, n]
            s = 1.0 / (1.0 + jnp.exp(-g))
            dg_v[:, n] = (d_hidden * u * s * (1.0 + g * (1.0 - s))).astype(BF16)
            du_v[:, n] = (d_hidden * g * s).astype(BF16)
            return carry

        lax.fori_loop(0, ff // 256, third, 0)

        def fourth(c, carry):
            n = aligned(c, 256)
            y_v[:, n] = (dot_nt(dg_v[...], wg_v[n, :]) + dot_nt(du_v[...], wu_v[n, :])).astype(BF16)
            return carry

        lax.fori_loop(0, model // 256, fourth, 0)
        outs = [
            pltpu.make_async_copy(a, o.at[b], local.at[i])
            for i, (a, o) in enumerate(
                (
                    (y_v, y_out),
                    (d_copy_v, d_copy_out),
                    (hid_v, hid_out),
                    (dg_v, dg_out),
                    (du_v, du_out),
                )
            )
        ]
        for copy in outs:
            copy.start()
        for copy in outs:
            copy.wait()

    gather_world(mine, buf, zs, zr, ps, pr, ds, dr, before, group)


def experts_bwd(mine, pos, x_in, gate_in, wg, wu, wd, room):
    rows, width = mine.shape
    model, ff = wg.shape
    group = 8 * room
    return pl.pallas_call(
        experts_bwd_kernel,
        out_shape=(
            jax.ShapeDtypeStruct((4, group, model + 128), BF16),
            jax.ShapeDtypeStruct((4, group, model), BF16),
            jax.ShapeDtypeStruct((4, group, ff), BF16),
            jax.ShapeDtypeStruct((4, group, ff), BF16),
            jax.ShapeDtypeStruct((4, group, ff), BF16),
        ),
        in_specs=[VMEM_SPEC, VMEM_SPEC] + [ANY_SPEC] * 5,
        out_specs=(ANY_SPEC,) * 5,
        scratch_shapes=[
            pltpu.VMEM((32, rows, width), BF16),
            pltpu.VMEM((model, ff), BF16),
            pltpu.VMEM((model, ff), BF16),
            pltpu.VMEM((ff, model), BF16),
            pltpu.VMEM((group, model), BF16),
            pltpu.VMEM((group, 128), F32),
            pltpu.VMEM((group, ff), F32),
            pltpu.VMEM((group, ff), F32),
            pltpu.VMEM((group, model), BF16),
            pltpu.VMEM((group, model + 128), BF16),
            pltpu.VMEM((group, model), BF16),
            pltpu.VMEM((group, ff), BF16),
            pltpu.VMEM((group, ff), BF16),
            pltpu.VMEM((group, ff), BF16),
            pltpu.SemaphoreType.DMA((5,)),
        ]
        + GATHER_SEMS,
        compiler_params=params(7),
        name="experts_bwd",
    )(mine, pos, x_in, gate_in, wg, wu, wd)


def sum_world_kernel(
    y, pos, out, psend, pair, half_near, half_far, full_near, full_far, lines,
    ds, dr, hs, hr, fs, fr, zs, zr,
):
    r, e, z, core, near, far, greeted = world(True)
    rows, width = out.shape
    room = y.shape[2]
    half = rows // 2
    low, high = pl.ds(0, half), pl.ds(half, half)
    order = plane_order(z)[::-1]
    diag = r ^ 3
    who = [r, near, far, diag]
    body_width = width // 512 * 512
    greet(greeted)

    def for_columns(fn):
        def step(c, carry):
            fn(aligned(c, 512))
            return carry

        lax.fori_loop(0, body_width // 512, step, 0)
        if width > body_width:
            fn(pl.ds(body_width, width - body_width))

    def scattered(sel, q, b, c, n):
        return dot_tn(sel, y[b, q * 2 + c, :, n])

    pairs, halves, fulls, moves = {}, {}, {}, []

    def stage_a(k):
        b = order[k]
        for i in (3, 1, 2, 0):
            at = k * 4 + i
            sel = selector(pos, who[i] * 8 + b * 2 + (1 - core), room)

            def fill(n):
                psend[at, :, n] = scattered(sel, who[i], b, 1 - core, n).astype(BF16)

            for_columns(fill)
            copy = remote(psend.at[at], pair.at[at], ds.at[at], dr.at[at], (r, e ^ 1))
            copy.start()
            pairs[at] = copy
        for i in (3, 1, 2, 0):
            at = k * 4 + i
            sel = selector(pos, who[i] * 8 + b * 2 + core, room)
            pairs[at].wait_recv()

            def add(n):
                value = scattered(sel, who[i], b, core, n) + pair[at, :, n].astype(F32)
                pair[at, :, n] = value.astype(BF16)

            for_columns(add)
            if i == 3:
                for side, (part, dst, p) in enumerate(
                    ((low, half_near, near), (high, half_far, far))
                ):
                    copy = remote(
                        pair.at[at, part], dst.at[k], hs.at[k, side], hr.at[k, side], (p, e)
                    )
                    copy.start()
                    halves[k, side] = copy

    def stage_b(k):
        for side, (i, part, src, dst, p) in enumerate(
            (
                (2, low, half_near, full_far, far),
                (1, high, half_far, full_near, near),
            )
        ):
            at = k * 4 + i
            halves[k, side].wait_recv()

            def add(n):
                value = pair[at, part, n].astype(F32) + src[k, :, n].astype(F32)
                pair[at, part, n] = value.astype(BF16)

            for_columns(add)
            copy = remote(pair.at[at], dst.at[k], fs.at[k, side], fr.at[k, side], (p, e))
            copy.start()
            fulls[k, side] = copy

    def stage_c(k):
        b = order[k]
        at = k * 4
        fulls[k, 0].wait_recv()
        fulls[k, 1].wait_recv()

        def add(n):
            out[:, n] = (
                pair[at, :, n].astype(F32)
                + full_near[k, :, n].astype(F32)
                + full_far[k, :, n].astype(F32)
            )

        for_columns(add)
        for side, cond in ((0, (b >= z) & (z > 0)), (1, (b <= z) & (z < 3))):

            @pl.when(cond)
            def _():
                remote(
                    lines.at[side, b], lines.at[side, b], zs.at[side, k], zr.at[side, b], (r, e ^ 1)
                ).wait_recv()

                def more(n):
                    out[:, n] = out[:, n] + lines[side, b, :, n].astype(F32)

                for_columns(more)

        if k < 3:

            def keep(n):
                pair[at, :, n] = out[:, n].astype(BF16)

            for_columns(keep)
            for side, cond, to in (
                (0, b > z, jnp.minimum(z + 1, 3)),
                (1, b < z, jnp.maximum(z - 1, 0)),
            ):
                copy = remote(
                    pair.at[at], lines.at[side, b], zs.at[side, k], zr.at[side, b], (r, to * 2 + core)
                )
                moves.append((cond, copy))

                @pl.when(cond)
                def _():
                    copy.start()

    stage_a(0)
    stage_a(1)
    stage_b(0)
    stage_a(2)
    stage_b(1)
    stage_c(0)
    stage_a(3)
    stage_b(2)
    stage_c(1)
    stage_b(3)
    stage_c(2)
    stage_c(3)
    for copies in (pairs, halves, fulls):
        for copy in copies.values():
            copy.wait_send()
    for cond, copy in moves:

        @pl.when(cond)
        def _():
            copy.wait_send()


def sum_world(y, pos, rows, collective_id):
    groups, per, room, width = y.shape

    def blocks(n, size):
        return pltpu.VMEM((n, size, width), BF16)

    return pl.pallas_call(
        sum_world_kernel,
        out_shape=jax.ShapeDtypeStruct((rows, width), F32),
        in_specs=[VMEM_SPEC, VMEM_SPEC],
        out_specs=VMEM_SPEC,
        scratch_shapes=[
            blocks(16, rows),
            blocks(16, rows),
            blocks(4, rows // 2),
            blocks(4, rows // 2),
            blocks(4, rows),
            blocks(4, rows),
            pltpu.VMEM((2, 4, rows, width), BF16),
            pltpu.SemaphoreType.DMA((16,)),
            pltpu.SemaphoreType.DMA((16,)),
            pltpu.SemaphoreType.DMA((4, 2)),
            pltpu.SemaphoreType.DMA((4, 2)),
            pltpu.SemaphoreType.DMA((4, 2)),
            pltpu.SemaphoreType.DMA((4, 2)),
            pltpu.SemaphoreType.DMA((2, 4)),
            pltpu.SemaphoreType.DMA((2, 4)),
        ],
        compiler_params=params(collective_id),
        name="sum_world",
    )(y, pos)


def experts_by_all_to_all(
    mixed, state, teacher, routes, valid_slot, valid_count, router_weight, gate_weight, up_weight, down_weight,
    devices, capacity, slots_all,
):
    tok_dev, model_width = mixed.shape
    top_count = routes.shape[1]
    ffn_width = gate_weight.shape[2]
    logits = jnp.dot(mixed, router_weight, preferred_element_type=jnp.float32)
    gates = jax.nn.softmax(jnp.take_along_axis(logits, routes, axis=1), axis=-1)
    rows_total = tok_dev * top_count
    expert_ids = routes.reshape(rows_total)
    live_rows = jnp.repeat(valid_slot, top_count)
    expert_range = jnp.arange(devices, dtype=jnp.int32)
    hit_table = ((expert_ids[:, None] == expert_range[None, :]) & live_rows[:, None]).astype(
        jnp.int32
    )
    earlier = jnp.cumsum(hit_table, axis=0) - hit_table
    position_in = jnp.sum(earlier * hit_table, axis=1)
    slot_index = jnp.where(live_rows, expert_ids * capacity + position_in, devices * capacity)
    row_of_slot = (
        jnp.full((devices * capacity + 1,), rows_total, jnp.int32)
        .at[slot_index]
        .set(jnp.arange(rows_total, dtype=jnp.int32))[: devices * capacity]
    )
    token_of_slot = jnp.where(row_of_slot < rows_total, row_of_slot // top_count, tok_dev)
    mixed_pad = jnp.concatenate([mixed, jnp.zeros((1, model_width), jnp.bfloat16)], axis=0)
    send_rows = mixed_pad[token_of_slot].reshape(devices, capacity, model_width)
    arrived = lax.all_to_all(send_rows, ("dp", "expert"), split_axis=0, concat_axis=0, tiled=True)
    sources = arrived.shape[0]
    items = arrived.shape[1]
    flat_in = arrived.reshape(sources * items, model_width)
    gate_pre = jnp.dot(flat_in, gate_weight[0], preferred_element_type=jnp.float32)
    up_pre = jnp.dot(flat_in, up_weight[0], preferred_element_type=jnp.float32)
    hidden_units = (jax.nn.silu(gate_pre) * up_pre).astype(jnp.bfloat16)
    produced = jnp.dot(hidden_units, down_weight[0], preferred_element_type=jnp.float32).astype(
        jnp.bfloat16
    )
    produced, gate_pre, up_pre, hidden_units, arrived = (
        produced.reshape(sources, items, model_width),
        gate_pre.reshape(sources, items, ffn_width),
        up_pre.reshape(sources, items, ffn_width),
        hidden_units.reshape(sources, items, ffn_width),
        arrived,
    )
    returned = lax.all_to_all(produced, ("dp", "expert"), split_axis=0, concat_axis=0, tiled=True)
    returned_pad = jnp.concatenate(
        [
            returned.reshape(devices * capacity, model_width),
            jnp.zeros((1, model_width), jnp.bfloat16),
        ],
        axis=0,
    )
    copies = returned_pad[slot_index].reshape(tok_dev, top_count, model_width)
    layer_out = state + jnp.sum(gates[:, :, None] * copies, axis=1)
    live_tokens = valid_slot.astype(jnp.float32)[:, None]
    diff = (layer_out - teacher.astype(jnp.float32)) * live_tokens
    local_square = jnp.sum(diff * diff)
    d_out = 2.0 * slots_all * diff / valid_count
    d_gates = jnp.sum(d_out[:, None, :] * copies, axis=-1)
    d_chosen = gates * (d_gates - jnp.sum(gates * d_gates, axis=-1, keepdims=True))
    d_logits = jnp.sum(
        jnp.where(routes[:, :, None] == expert_range[None, None, :], d_chosen[:, :, None], 0.0),
        axis=1,
    ).astype(jnp.bfloat16)
    d_copies = (
        (gates[:, :, None] * d_out[:, None, :])
        .astype(jnp.bfloat16)
        .reshape(rows_total, model_width)
    )
    d_copies_pad = jnp.concatenate([d_copies, jnp.zeros((1, model_width), jnp.bfloat16)], axis=0)
    d_send = d_copies_pad[row_of_slot].reshape(devices, capacity, model_width)
    d_arrived = lax.all_to_all(d_send, ("dp", "expert"), split_axis=0, concat_axis=0, tiled=True)
    flat_d = d_arrived.reshape(-1, model_width)
    flat_in = arrived.reshape(-1, model_width)
    flat_gate = gate_pre.reshape(-1, ffn_width)
    flat_up = up_pre.reshape(-1, ffn_width)
    flat_hidden = hidden_units.reshape(-1, ffn_width)
    d_hidden = contract(flat_d, down_weight[0], 1, 1)
    sigmoid_gate = jax.nn.sigmoid(flat_gate)
    d_gate = (d_hidden * flat_up * sigmoid_gate * (1.0 + flat_gate * (1.0 - sigmoid_gate))).astype(
        jnp.bfloat16
    )
    d_up = (d_hidden * flat_gate * sigmoid_gate).astype(jnp.bfloat16)
    down_grad = contract(flat_hidden, flat_d, 0, 0)[None]
    gate_grad = contract(flat_in, d_gate, 0, 0)[None]
    up_grad = contract(flat_in, d_up, 0, 0)[None]
    d_in = (contract(d_gate, gate_weight[0], 1, 1) + contract(d_up, up_weight[0], 1, 1)).astype(
        jnp.bfloat16
    )
    d_returned = lax.all_to_all(
        d_in.reshape(devices, capacity, model_width),
        ("dp", "expert"),
        split_axis=0,
        concat_axis=0,
        tiled=True,
    )
    d_returned_pad = jnp.concatenate(
        [
            d_returned.reshape(devices * capacity, model_width),
            jnp.zeros((1, model_width), jnp.bfloat16),
        ],
        axis=0,
    )
    d_mixed = jnp.sum(
        d_returned_pad[slot_index].reshape(tok_dev, top_count, model_width),
        axis=1,
        dtype=jnp.float32,
    )
    d_mixed = d_mixed + contract(d_logits, router_weight, 1, 1)
    router_local = contract(mixed, d_logits, 0, 0)
    return layer_out, d_out, d_mixed, local_square, router_local, gate_grad, up_grad, down_grad


def experts_by_gather(
    mixed, state, teacher, routes, cont_lengths, valid_slot, valid_count, router_weight,
    gate_weight, up_weight, down_weight, devices, capacity, slots_all, flat_rank,
):
    tok_dev, model_width = mixed.shape
    room = -(-capacity // 16) * 16
    expert_range = jnp.arange(devices, dtype=jnp.int32)
    slot_ids = jnp.arange(tok_dev, dtype=jnp.int32)
    prompt_block = tok_dev - CMAX
    routes_all = lax.all_gather(routes, ("dp", "expert"), axis=0, tiled=False)
    valid_all = (slot_ids[None] < prompt_block) | (slot_ids[None] - prompt_block < cont_lengths[:, None])
    named = jnp.any(routes_all == flat_rank, axis=-1) & valid_all
    upto = (slot_ids[:, None] <= slot_ids[None]).astype(F32)
    place = jnp.dot(named.astype(F32), upto, preferred_element_type=F32).astype(jnp.int32) - 1
    pos = jnp.where(named, place, -1)[:, None, :]

    logits = jnp.dot(mixed, router_weight, preferred_element_type=F32)
    chosen = jnp.any(routes[:, :, None] == expert_range[None, None], axis=1)
    gates = jax.nn.softmax(jnp.where(chosen, logits, -jnp.inf), axis=-1)
    gates_high = gates.astype(BF16)
    gates_low = (gates - gates_high.astype(F32)).astype(BF16)
    gap = jnp.zeros((tok_dev, 64 - devices), BF16)
    payload = jnp.concatenate([mixed, gates_high, gap, gates_low, gap], axis=1)
    x_rows, y_rows, slot_gates = experts_fwd(
        payload, pos, gate_weight[0], up_weight[0], down_weight[0], room
    )
    layer_out = state + sum_world(y_rows.reshape(4, 8, room, model_width), pos, tok_dev, 8)
    live_tokens = valid_slot.astype(F32)[:, None]
    diff = (layer_out - teacher.astype(F32)) * live_tokens
    local_square = jnp.sum(diff * diff)
    d_out = 2.0 * slots_all * diff / valid_count
    d_rows, d_copy, hidden, d_gate, d_up = experts_bwd(
        d_out.astype(BF16), pos, x_rows, slot_gates, gate_weight[0], up_weight[0], down_weight[0], room
    )
    back = sum_world(d_rows.reshape(4, 8, room, model_width + 128), pos, tok_dev, 9)

    def flat(a):
        return a.reshape(4 * 8 * room, a.shape[-1])

    down_grad = contract(flat(hidden), flat(d_copy), 0, 0)[None]
    gate_grad = contract(flat(x_rows), flat(d_gate), 0, 0)[None]
    up_grad = contract(flat(x_rows), flat(d_up), 0, 0)[None]
    d_gates = back[:, model_width : model_width + devices] + back[:, model_width + 64 : model_width + 64 + devices]
    d_logits = (gates * (d_gates - jnp.sum(gates * d_gates, axis=-1, keepdims=True))).astype(BF16)
    d_mixed = back[:, :model_width] + contract(d_logits, router_weight, 1, 1)
    router_local = contract(mixed, d_logits, 0, 0)
    return layer_out, d_out, d_mixed, local_square, router_local, gate_grad, up_grad, down_grad


def head_rope(linear, gain_vec, cos, sin):
    value = root_mean_scale(linear, gain_vec)
    half = value.shape[-1] // 2
    return value * cos + jnp.roll(value, half, axis=-1) * sin


def body(
    tokens,
    teacher,
    routes,
    cont_lengths,
    query_weight,
    key_projection,
    value_projection,
    output_weight,
    router_weight,
    gate_weight,
    up_weight,
    down_weight,
    input_gain,
    post_gain,
    query_gain,
    key_gain,
):
    n_dp = lax.axis_size("dp")
    n_owner = lax.axis_size("expert")
    devices = n_dp * n_owner
    rank_dp = lax.axis_index("dp")
    rank_owner = lax.axis_index("expert")
    flat_rank = rank_dp * n_owner + rank_owner
    column = rank_owner % 2
    first_column = column == 0
    tok_dev, model_width = tokens.shape
    top_count = routes.shape[1]
    head_dim = query_gain.shape[0]
    kv_width = key_projection.shape[1]
    query_width = query_weight.shape[1]
    query_group = query_width // n_dp
    assert n_dp == 4 and kv_width == n_dp * head_dim
    prompt_block = tok_dev - CMAX
    half_prompt = n_dp * prompt_block
    prompt_len = 2 * half_prompt
    capacity = max(2, tok_dev * top_count * 5 // (4 * devices))
    slots_all = devices * tok_dev
    slot_ids = jnp.arange(tok_dev, dtype=jnp.int32)
    own_length = cont_lengths[flat_rank]
    valid_slot = (slot_ids < prompt_block) | (slot_ids - prompt_block < own_length)
    valid_count = (devices * prompt_block + jnp.sum(cont_lengths)).astype(F32)
    tokens_float = tokens.astype(F32)
    normed_float, first_norm_back = jax.vjp(root_mean_scale, tokens_float, input_gain)
    normed = normed_float.astype(BF16)

    block_ids = jnp.arange(n_dp, dtype=jnp.int32)[:, None]
    positions = jnp.where(
        slot_ids[None] < prompt_block,
        (column * n_dp + block_ids) * prompt_block + slot_ids[None],
        prompt_len + slot_ids[None] - prompt_block,
    )
    half_head = head_dim // 2
    frequency = rope_base ** (-(jnp.arange(half_head, dtype=F32) * 2.0) / head_dim)
    angles = positions.astype(F32)[:, :, None] * frequency
    cos_half, sin_half = jnp.cos(angles), jnp.sin(angles)
    cos = jnp.concatenate([cos_half, cos_half], axis=-1)
    sin = jnp.concatenate([-sin_half, sin_half], axis=-1)
    lengths = jnp.concatenate(
        [lax.dynamic_index_in_dim(cont_lengths.reshape(n_dp, n_owner), rank_owner, 1, False), column[None]]
    ).astype(jnp.int32)

    lin, normed_cols = project_qkv(normed, query_weight, key_projection, value_projection)
    key_lin = lin[:, query_group : query_group + head_dim].reshape(n_dp, tok_dev, head_dim)
    keys_float, key_back = jax.vjp(lambda a, b: head_rope(a, b, cos, sin), key_lin, key_gain)
    keys_own = keys_float.astype(BF16)
    values_own = lin[:, query_group + head_dim :].reshape(n_dp, tok_dev, head_dim).astype(BF16)
    column_kv = jnp.stack([keys_own[:, :prompt_block], values_own[:, :prompt_block]]).reshape(
        2, half_prompt, head_dim
    )
    other_kv = partner(column_kv, "expert", 0)
    full_kv = jnp.where(
        first_column,
        jnp.concatenate([column_kv, other_kv], axis=1),
        jnp.concatenate([other_kv, column_kv], axis=1),
    )
    spread = jnp.broadcast_to(full_kv[:, None], (2, n_dp, prompt_len, head_dim))
    all_keys = jnp.concatenate([spread[0], keys_own[:, prompt_block:]], axis=1)
    all_values = jnp.concatenate([spread[1], values_own[:, prompt_block:]], axis=1)
    query_gain_row = query_gain[None]
    queries, attended = attention_fwd(
        lengths, lin, query_gain_row, cos, sin, all_keys, all_values, prompt_len
    )
    state = tokens_float + project_out(attended, output_weight)
    mixed_float, second_norm_back = jax.vjp(root_mean_scale, state, post_gain)
    mixed = mixed_float.astype(BF16)
    sizes = (devices, capacity, slots_all)
    weights = (router_weight, gate_weight, up_weight, down_weight)
    if n_dp == 4 and n_owner == 8:
        moe = experts_by_gather(
            mixed, state, teacher, routes, cont_lengths, valid_slot, valid_count, *weights, *sizes, flat_rank
        )
    else:
        moe = experts_by_all_to_all(
            mixed, state, teacher, routes, valid_slot, valid_count, *weights, *sizes
        )
    layer_out, d_out, d_mixed, local_square, router_local, gate_grad, up_grad, down_grad = moe
    d_state_norm, d_post_gain = second_norm_back(d_mixed)
    d_state = d_out + d_state_norm
    d_branch = d_state.astype(BF16)
    d_attended, out_part = grad_branch(d_branch, output_weight, attended.T)
    d_query_lin, d_keys, d_values, gain_parts = attention_bwd(
        lengths, lin, queries, d_attended, query_gain_row, cos, sin, all_keys, all_values, prompt_len
    )
    d_query_gain = jnp.sum(gain_parts, axis=(0, 1))
    prompt_grads = jnp.stack(
        [jnp.sum(d_keys[:, :prompt_len], axis=0), jnp.sum(d_values[:, :prompt_len], axis=0)]
    )
    mine_part = jnp.where(first_column, prompt_grads[:, :half_prompt], prompt_grads[:, half_prompt:])
    their_part = jnp.where(first_column, prompt_grads[:, half_prompt:], prompt_grads[:, :half_prompt])
    own_prompt = (mine_part + partner(their_part, "expert", 0)).reshape(
        2, n_dp, prompt_block, head_dim
    )
    d_key_post = jnp.concatenate([own_prompt[0], d_keys[:, prompt_len:]], axis=1)
    d_value_lin = jnp.concatenate([own_prompt[1], d_values[:, prompt_len:]], axis=1)
    d_key_float, d_key_gain = key_back(d_key_post)
    rows = n_dp * tok_dev
    d_lin = jnp.concatenate(
        [
            d_query_lin,
            d_key_float.astype(BF16).reshape(rows, head_dim),
            d_value_lin.astype(BF16).reshape(rows, head_dim),
        ],
        axis=1,
    )
    d_normed, qkv_part = grad_qkv(
        d_lin, query_weight, key_projection, value_projection, normed_cols.T
    )
    d_tokens_norm, d_input_gain = first_norm_back(d_normed)
    tokens_grad = d_state + d_tokens_norm
    width = query_weight.shape[0]
    group = d_lin.shape[1]
    rows_here = width // n_owner
    by_owner = (
        qkv_part.reshape(n_dp, n_owner, rows_here, group)
        .transpose(1, 0, 2, 3)
        .reshape(n_owner, n_dp * rows_here, group)
    )
    qkv_rows, output_grad = owner_sums(
        [by_owner, out_part.reshape(n_owner, -1, model_width)], n_owner, 5
    )
    qkv_rows = qkv_rows.reshape(n_dp, rows_here, group)

    def columns(start, size):
        return qkv_rows[:, :, start : start + size].transpose(1, 0, 2).reshape(rows_here, n_dp * size)

    query_grad = columns(0, query_group)
    key_grad = columns(query_group, head_dim)
    value_grad = columns(query_group + head_dim, head_dim)
    total_square, input_gain_grad, post_gain_grad, query_gain_grad, key_gain_grad, router_grad = (
        lax.psum(
            (local_square, d_input_gain, d_post_gain, d_query_gain, d_key_gain, router_local),
            ("dp", "expert"),
        )
    )
    loss = total_square / (valid_count * model_width)
    return (
        layer_out,
        loss,
        tokens_grad,
        query_grad,
        key_grad,
        value_grad,
        output_grad,
        router_grad,
        gate_grad,
        up_grad,
        down_grad,
        input_gain_grad,
        post_gain_grad,
        query_gain_grad,
        key_gain_grad,
    )


def solution(mesh):
    in_specs = (
        P(("dp", "expert"), None),
        P(("dp", "expert"), None),
        P(("dp", "expert"), None),
        P(),
        P("dp", None),
        P("dp", None),
        P("dp", None),
        P("dp", None),
        P(),
        P(("dp", "expert"), None, None),
        P(("dp", "expert"), None, None),
        P(("dp", "expert"), None, None),
        P(),
        P(),
        P(),
        P(),
    )
    out_specs = (
        P(("dp", "expert"), None),
        P(),
        P(("dp", "expert"), None),
        P(("dp", "expert"), None),
        P(("dp", "expert"), None),
        P(("dp", "expert"), None),
        P(("dp", "expert"), None),
        P(),
        P(("dp", "expert"), None, None),
        P(("dp", "expert"), None, None),
        P(("dp", "expert"), None, None),
        P(),
        P(),
        P(),
        P(),
    )
    return jax.shard_map(body, mesh=mesh, in_specs=in_specs, out_specs=out_specs, check_vma=False)
```

```python
import functools

import jax
import jax.numpy as jnp
from jax import lax
from jax.experimental import pallas as pl
from jax.experimental.pallas import tpu as pltpu
from jax.sharding import PartitionSpec as P

CMAX = 128
norm_eps = 1e-06
rope_base = 1000000.0
MESH = pl.DeviceIdType.MESH
F32 = jnp.float32
BF16 = jnp.bfloat16
VMEM_SPEC = pl.BlockSpec(memory_space=pltpu.VMEM)
ANY_SPEC = pl.BlockSpec(memory_space=pl.ANY)
VMEM_LIMIT = 56 * 1024 * 1024


def params(collective_id=None):
    return pltpu.CompilerParams(
        collective_id=collective_id,
        has_side_effects=collective_id is not None,
        vmem_limit_bytes=VMEM_LIMIT,
    )


def greet(devices):
    barrier = pltpu.get_barrier_semaphore()
    for device in devices:
        pl.semaphore_signal(barrier, inc=1, device_id=device, device_id_type=MESH)
    pl.semaphore_wait(barrier, len(devices))


def remote(src, dst, send_sem, recv_sem, device):
    return pltpu.make_async_remote_copy(
        src_ref=src,
        dst_ref=dst,
        send_sem=send_sem,
        recv_sem=recv_sem,
        device_id=device,
        device_id_type=MESH,
    )


def aligned(index, size):
    return pl.ds(pl.multiple_of(index * size, size), size)


def dot_nn(a, b):
    return lax.dot_general(a, b, (((1,), (0,)), ((), ())), preferred_element_type=F32)


def dot_nt(a, b):
    return lax.dot_general(a, b, (((1,), (1,)), ((), ())), preferred_element_type=F32)


def dot_tn(a, b):
    return lax.dot_general(a, b, (((0,), (0,)), ((), ())), preferred_element_type=F32)


PEER_MASKS = (3, 1, 2)


def relay_sum(r, e, products, own, mine, send, half_in, full_in, hs, hr, fs, fr, step):
    near, far, diag = r ^ 1, r ^ 2, r ^ 3
    rows = mine.shape[0]
    half = rows // 2
    low, high = pl.ds(0, half), pl.ds(half, half)
    products(diag, send.at[2])
    relays = [
        remote(send.at[2, low], half_in.at[0], hs.at[0], hr.at[0], (near, e)),
        remote(send.at[2, high], half_in.at[1], hs.at[1], hr.at[1], (far, e)),
    ]
    for copy in relays:
        copy.start()
    parts = ((0, low, near), (1, high, far), (0, high, near), (1, low, far))
    fulls = [
        remote(send.at[i, part], full_in.at[i, part], fs.at[n], fr.at[n], (p, e))
        for n, (i, part, p) in enumerate(parts)
    ]
    products(near, send.at[0])
    fulls[0].start()
    products(far, send.at[1])
    fulls[1].start()
    for i, start, slot, n in ((1, 0, 0, 3), (0, half, 1, 2)):
        relays[slot].wait_recv()

        def add(c, carry):
            t = pl.ds(pl.multiple_of(start + c * step, step), step)
            value = send[i, t, :].astype(F32) + half_in[slot, aligned(c, step), :].astype(F32)
            send[i, t, :] = value.astype(BF16)
            return carry

        lax.fori_loop(0, half // step, add, 0)
        fulls[n].start()
    own()
    for copy in fulls:
        copy.wait_recv()

    def total(c, carry):
        t = aligned(c, step)
        mine[t, :] = mine[t, :] + (full_in[0, t, :].astype(F32) + full_in[1, t, :].astype(F32))
        return carry

    lax.fori_loop(0, rows // step, total, 0)
    for copy in relays + fulls:
        copy.wait_send()


def relay_scratch(rows, width):
    return [
        pltpu.VMEM((3, rows, width), BF16),
        pltpu.VMEM((2, rows // 2, width), BF16),
        pltpu.VMEM((2, rows, width), BF16),
        pltpu.SemaphoreType.DMA((2,)),
        pltpu.SemaphoreType.DMA((2,)),
        pltpu.SemaphoreType.DMA((4,)),
        pltpu.SemaphoreType.DMA((4,)),
    ]


def qkv_kernel(tok, normed, wq, wk, wv, lin, cols, asend, arecv, *relay):
    r, e = lax.axis_index("dp"), lax.axis_index("expert")
    peers = [r ^ m for m in PEER_MASKS]
    width = wq.shape[0]
    qg = wq.shape[1] // 4
    kg = wk.shape[1] // 4
    rows = cols.shape[0]
    greet([(p, e) for p in peers])
    first = []
    for i, p in enumerate(peers):
        copy = remote(
            normed.at[:, aligned(p, width)], cols.at[aligned(r, tok), :],
            asend.at[i], arecv.at[i], (p, e),
        )
        copy.start()
        first.append(copy)
    cols[aligned(r, tok), :] = normed[:, aligned(r, width)]
    for copy in first:
        copy.wait()

    def products(p, dst):
        def chunk(c, carry):
            t = aligned(c, tok)
            x = cols[t, :]
            dst[t, :qg] = dot_nn(x, wq[:, aligned(p, qg)]).astype(dst.dtype)
            dst[t, qg : qg + kg] = dot_nn(x, wk[:, aligned(p, kg)]).astype(dst.dtype)
            dst[t, qg + kg :] = dot_nn(x, wv[:, aligned(p, kg)]).astype(dst.dtype)
            return carry

        lax.fori_loop(0, rows // tok, chunk, 0)

    relay_sum(r, e, products, lambda: products(r, lin), lin, *relay, 32)


def project_qkv(normed, wq, wk, wv):
    tok = normed.shape[0]
    rows = 4 * tok
    group = (wq.shape[1] + wk.shape[1] + wv.shape[1]) // 4
    return pl.pallas_call(
        functools.partial(qkv_kernel, tok),
        out_shape=(
            jax.ShapeDtypeStruct((rows, group), F32),
            jax.ShapeDtypeStruct((rows, wq.shape[0]), BF16),
        ),
        in_specs=[VMEM_SPEC] * 4,
        out_specs=(VMEM_SPEC, VMEM_SPEC),
        scratch_shapes=[pltpu.SemaphoreType.DMA((3,))] * 2 + relay_scratch(rows, group),
        compiler_params=params(1),
        name="qkv_exchange",
    )(normed, wq, wk, wv)


def out_kernel(attn, wo, total, *relay):
    r, e = lax.axis_index("dp"), lax.axis_index("expert")
    tok, width = total.shape
    step = width // 4
    greet([(r ^ m, e) for m in PEER_MASKS])

    def products(p, dst):
        def chunk(c, carry):
            n = aligned(c, step)
            dst[:, n] = dot_nn(attn[aligned(p, tok), :], wo[:, n]).astype(dst.dtype)
            return carry

        lax.fori_loop(0, width // step, chunk, 0)

    relay_sum(r, e, products, lambda: products(r, total), total, *relay, 16)


def project_out(attn, wo):
    tok = attn.shape[0] // 4
    return pl.pallas_call(
        out_kernel,
        out_shape=jax.ShapeDtypeStruct((tok, wo.shape[1]), F32),
        in_specs=[VMEM_SPEC] * 2,
        out_specs=VMEM_SPEC,
        scratch_shapes=relay_scratch(tok, wo.shape[1]),
        compiler_params=params(2),
        name="out_exchange",
    )(attn, wo)


def dgrad_kernel(
    mine, wq, wk, wv, cols_t, out_part, normal, grads, out_grad,
    blocks, dsum, dsend, drecv, ssem, rsem, bsend, brecv, *scratch,
):
    r, e = lax.axis_index("dp"), lax.axis_index("expert")
    rows = mine.shape[0]
    tok = rows // 4
    half = rows // 2
    qg = wq.shape[1] // 4
    kg = wk.shape[1] // 4
    width = wq.shape[0]
    peers = [r ^ m for m in PEER_MASKS]
    near, far, diag = r ^ 1, r ^ 2, r ^ 3
    pair_in, send, recv, *sems = scratch
    begin, middle, finish = owner_sum([out_part], [out_grad], [pair_in], [send], [recv], *sems)
    greet([(p, e) for p in peers] + [(r, e ^ 1)] + owner_peers())
    begin()
    low, high = pl.ds(0, half), pl.ds(half, half)
    first_near = remote(mine.at[low], blocks.at[0, low], ssem.at[0], rsem.at[0], (near, e))
    first_far = remote(mine.at[high], blocks.at[1, high], ssem.at[1], rsem.at[1], (far, e))
    second_near = remote(mine.at[high], blocks.at[0, high], ssem.at[2], rsem.at[2], (near, e))
    second_far = remote(mine.at[low], blocks.at[1, low], ssem.at[3], rsem.at[3], (far, e))
    pass_far = remote(blocks.at[0, low], blocks.at[2, low], ssem.at[4], rsem.at[4], (far, e))
    pass_near = remote(blocks.at[1, high], blocks.at[2, high], ssem.at[5], rsem.at[5], (near, e))
    for copy in (first_near, first_far, second_near, second_far):
        copy.start()

    def products(p, src, start):
        def chunk(c, carry):
            t = aligned(c, tok)
            x = src[t, :]
            value = (
                dot_nt(x[:, :qg], wq[:, aligned(p, qg)])
                + dot_nt(x[:, qg : qg + kg], wk[:, aligned(p, kg)])
                + dot_nt(x[:, qg + kg :], wv[:, aligned(p, kg)])
            )
            if start:
                dsum[t, :] = value
            else:
                dsum[t, :] = dsum[t, :] + value
            return carry

        lax.fori_loop(0, 4, chunk, 0)

        def outer(c, carry):
            n = aligned(c, 128)
            grads[aligned(p, width), n] = dot_nn(cols_t[...], src[:, n]).astype(BF16)
            return carry

        lax.fori_loop(0, (qg + 2 * kg) // 128, outer, 0)

    middle()
    products(r, mine, True)
    first_near.wait()
    pass_far.start()
    first_far.wait()
    pass_near.start()
    second_near.wait()
    products(near, blocks.at[0], False)
    second_far.wait()
    products(far, blocks.at[1], False)
    pass_far.wait()
    pass_near.wait()
    products(diag, blocks.at[2], False)
    back = []
    for i, p in enumerate(peers):
        dsend[i] = dsum[aligned(p, tok), :].astype(BF16)
        copy = remote(dsend.at[i], drecv.at[i], bsend.at[i], brecv.at[i], (p, e))
        copy.start()
        back.append(copy)
    normal[:, aligned(r, width)] = dsum[aligned(r, tok), :]
    for i, p in enumerate(peers):
        back[i].wait()
        normal[:, aligned(p, width)] = drecv[i].astype(F32)
    finish()


def grad_qkv(mine, wq, wk, wv, cols_t, out_part):
    rows, group = mine.shape
    tok = rows // 4
    width = wq.shape[0]
    return pl.pallas_call(
        dgrad_kernel,
        out_shape=(
            jax.ShapeDtypeStruct((tok, 4 * width), F32),
            jax.ShapeDtypeStruct((4 * width, group), BF16),
            jax.ShapeDtypeStruct(out_part.shape[1:], F32),
        ),
        in_specs=[VMEM_SPEC] * 6,
        out_specs=(VMEM_SPEC,) * 3,
        scratch_shapes=[
            pltpu.VMEM((3, rows, group), BF16),
            pltpu.VMEM((rows, width), F32),
            pltpu.VMEM((3, tok, width), BF16),
            pltpu.VMEM((3, tok, width), BF16),
            pltpu.SemaphoreType.DMA((6,)),
            pltpu.SemaphoreType.DMA((6,)),
            pltpu.SemaphoreType.DMA((3,)),
            pltpu.SemaphoreType.DMA((3,)),
        ]
        + owner_scratch([out_part]),
        compiler_params=params(4),
        name="dqkv_exchange",
    )(mine, wq, wk, wv, cols_t, out_part)


def branch_kernel(mine, wo, attn_t, d_attn, grads, full, ssem, rsem):
    r, e = lax.axis_index("dp"), lax.axis_index("expert")
    tok = mine.shape[0]
    half = tok // 2
    peers = [r ^ m for m in PEER_MASKS]
    near, far, diag = r ^ 1, r ^ 2, r ^ 3
    greet([(p, e) for p in peers])

    def part(q, which):
        return pl.ds(pl.multiple_of(q * tok + which * half, half), half)

    low, high = pl.ds(0, half), pl.ds(half, half)
    first_near = remote(mine.at[low], full.at[part(r, 0)], ssem.at[0], rsem.at[0], (near, e))
    first_far = remote(mine.at[high], full.at[part(r, 1)], ssem.at[1], rsem.at[1], (far, e))
    second_near = remote(mine.at[high], full.at[part(r, 1)], ssem.at[2], rsem.at[2], (near, e))
    second_far = remote(mine.at[low], full.at[part(r, 0)], ssem.at[3], rsem.at[3], (far, e))
    pass_far = remote(full.at[part(near, 0)], full.at[part(near, 0)], ssem.at[4], rsem.at[4], (far, e))
    pass_near = remote(full.at[part(far, 1)], full.at[part(far, 1)], ssem.at[5], rsem.at[5], (near, e))
    for copy in (first_near, first_far, second_near, second_far):
        copy.start()
    full[aligned(r, tok), :] = mine[...]
    heads = wo.shape[0]
    step = heads // 4

    def products(q):
        def chunk(c, carry):
            n = aligned(c, step)
            d_attn[aligned(q, tok), n] = dot_nt(full[aligned(q, tok), :], wo[n, :]).astype(BF16)
            return carry

        lax.fori_loop(0, 4, chunk, 0)

    products(r)
    first_near.wait()
    pass_far.start()
    first_far.wait()
    pass_near.start()
    second_near.wait()
    products(near)
    second_far.wait()
    products(far)
    pass_far.wait()
    pass_near.wait()
    products(diag)

    def outer(c, carry):
        n = aligned(c, 256)
        grads[:, n] = dot_nn(attn_t[...], full[:, n]).astype(BF16)
        return carry

    lax.fori_loop(0, mine.shape[1] // 256, outer, 0)


def grad_branch(mine, wo, attn_t):
    tok, width = mine.shape
    return pl.pallas_call(
        branch_kernel,
        out_shape=(
            jax.ShapeDtypeStruct((4 * tok, wo.shape[0]), BF16),
            jax.ShapeDtypeStruct((wo.shape[0], width), BF16),
        ),
        in_specs=[VMEM_SPEC] * 3,
        out_specs=(VMEM_SPEC, VMEM_SPEC),
        scratch_shapes=[
            pltpu.VMEM((4 * tok, width), BF16),
            pltpu.SemaphoreType.DMA((6,)),
            pltpu.SemaphoreType.DMA((6,)),
        ],
        compiler_params=params(3),
        name="branch_exchange",
    )(mine, wo, attn_t)


def owner_order(n_z):
    order = list(range(1, n_z)) + [0]
    return order[1:2] + order[:1] + order[2:] if n_z > 2 else order


def owner_sum(arrays, outs, pair_in, send, recv, psend, precv, zsend, zrecv):
    r, e = lax.axis_index("dp"), lax.axis_index("expert")
    n_z = arrays[0].shape[0] // 2
    z, core = e // 2, e % 2
    targets = [lax.rem(z + j, n_z) for j in range(n_z)]
    order = owner_order(n_z)
    n_arrays = len(arrays)
    pair, moves = {}, []

    def begin():
        for j in order:
            for a in range(n_arrays):
                copy = remote(
                    arrays[a].at[targets[j] * 2 + (1 - core)], pair_in[a].at[j],
                    psend.at[a, j], precv.at[a, j], (r, e ^ 1),
                )
                copy.start()
                pair[a, j] = copy

    def middle():
        for j in order:
            for a in range(n_arrays):
                pair[a, j].wait()
                own = arrays[a][targets[j] * 2 + core].astype(F32) + pair_in[a][j].astype(F32)
                if j == 0:
                    outs[a][...] = own
                else:
                    send[a][j - 1] = own.astype(BF16)
                    copy = remote(
                        send[a].at[j - 1], recv[a].at[j - 1],
                        zsend.at[a, j - 1], zrecv.at[a, j - 1], (r, targets[j] * 2 + core),
                    )
                    copy.start()
                    moves.append(copy)

    def finish():
        for copy in moves:
            copy.wait()
        for a in range(n_arrays):
            value = outs[a][...]
            for j in range(n_z - 1):
                value = value + recv[a][j].astype(F32)
            outs[a][...] = value

    return begin, middle, finish


def owner_scratch(arrays):
    n_z = arrays[0].shape[0] // 2
    n = len(arrays)
    shapes = [a.shape[1:] for a in arrays]
    return (
        [pltpu.VMEM((n_z, *s), BF16) for s in shapes]
        + [pltpu.VMEM((n_z - 1, *s), BF16) for s in shapes]
        + [pltpu.VMEM((n_z - 1, *s), BF16) for s in shapes]
        + [pltpu.SemaphoreType.DMA((n, n_z))] * 2
        + [pltpu.SemaphoreType.DMA((n, n_z - 1))] * 2
    )


def owner_peers():
    r, e = lax.axis_index("dp"), lax.axis_index("expert")
    n_z = lax.axis_size("expert") // 2
    return [(r, lax.rem(e // 2 + j, n_z) * 2 + e % 2) for j in range(1, n_z)]


def last_sums_kernel(grads, small, grads_out, small_out, *scratch):
    r, e = lax.axis_index("dp"), lax.axis_index("expert")
    z, core = e // 2, e % 2
    n_z = grads.shape[0] // 2
    pair_in, send, recv, psend, precv, zsend, zrecv = scratch[:7]
    first_in, piece, line_in, s1, r1, s2, r2, s3, r3 = scratch[7:]
    begin, middle, finish = owner_sum(
        [grads], [grads_out], [pair_in], [send], [recv], psend, precv, zsend, zrecv
    )
    others = [(m // 2, m % 2) for m in range(1, 8)]
    plane = [(r ^ a, e ^ c) for a, c in others]
    greet(plane + owner_peers())
    begin()
    firsts = []
    for i, (a, c) in enumerate(others):
        copy = remote(
            small.at[(r ^ a) * 2 + (core ^ c)], first_in.at[i], s1.at[i], r1.at[i], plane[i]
        )
        copy.start()
        firsts.append(copy)
    middle()
    for copy in firsts:
        copy.wait()
    mine = r * 2 + core
    value = small[mine]
    for i in range(7):
        value = value + first_in[i]
    piece[0] = value
    seconds = []
    for j in range(1, n_z):
        copy = remote(
            piece.at[0], line_in.at[j - 1], s2.at[j - 1], r2.at[j - 1], owner_peers()[j - 1]
        )
        copy.start()
        seconds.append(copy)
    for copy in seconds:
        copy.wait()
    value = piece[0]
    for j in range(n_z - 1):
        value = value + line_in[j]
    small_out[mine] = value
    thirds = []
    for i, (a, c) in enumerate(others):
        copy = remote(small_out.at[mine], small_out.at[mine], s3.at[i], r3.at[i], plane[i])
        copy.start()
        thirds.append(copy)
    finish()
    for copy in thirds:
        copy.wait()


def last_sums(grads, small):
    n_z = grads.shape[0] // 2
    piece = small.shape[1:]
    return pl.pallas_call(
        last_sums_kernel,
        out_shape=(
            jax.ShapeDtypeStruct(grads.shape[1:], F32),
            jax.ShapeDtypeStruct(small.shape, F32),
        ),
        in_specs=[VMEM_SPEC] * 2,
        out_specs=(VMEM_SPEC,) * 2,
        scratch_shapes=owner_scratch([grads])
        + [
            pltpu.VMEM((7, *piece), F32),
            pltpu.VMEM((1, *piece), F32),
            pltpu.VMEM((n_z - 1, *piece), F32),
            pltpu.SemaphoreType.DMA((7,)),
            pltpu.SemaphoreType.DMA((7,)),
            pltpu.SemaphoreType.DMA((n_z - 1,)),
            pltpu.SemaphoreType.DMA((n_z - 1,)),
            pltpu.SemaphoreType.DMA((7,)),
            pltpu.SemaphoreType.DMA((7,)),
        ],
        compiler_params=params(5),
        name="last_sums",
    )(grads, small)


def masks_of(block, own_length, slots, prompt_block, prompt_len, column, keys):
    slot = lax.broadcasted_iota(jnp.int32, (slots, keys), 0)
    key = lax.broadcasted_iota(jnp.int32, (slots, keys), 1)
    is_prompt = slot < prompt_block
    position = (column * 4 + block) * prompt_block + slot
    sees_prompt = (key < prompt_len) & (jnp.logical_not(is_prompt) | (key <= position))
    cont = key - prompt_len
    sees_cont = (
        (key >= prompt_len)
        & jnp.logical_not(is_prompt)
        & (cont <= slot - prompt_block)
        & (cont < own_length)
    )
    return sees_prompt | sees_cont


def attention_fwd_kernel(prompt_len, lengths, lin, gain, cos, sin, keys, values, queries, attn):
    block = pl.program_id(0)
    slots = lin.shape[0]
    head = gain.shape[1]
    allowed = masks_of(
        block, lengths[block], slots, slots - CMAX, prompt_len, lengths[4], keys.shape[1]
    )
    scale = head ** (-0.5)
    k, v = keys[0], values[0]
    c, s, g = cos[0], sin[0], gain[...]
    for h in range(lin.shape[1] // head):
        part = slice(h * head, (h + 1) * head)
        x = lin[:, part]
        x = x * lax.rsqrt(jnp.mean(x * x, axis=-1, keepdims=True) + norm_eps) * g
        q = (x * c + pltpu.roll(x, head // 2, 1) * s).astype(BF16)
        queries[:, part] = q
        score = jnp.where(allowed, dot_nt(q, k) * scale, -jnp.inf)
        peak = jnp.max(score, axis=-1, keepdims=True)
        exponent = jnp.exp(score - peak)
        low = (exponent * (1.0 / jnp.sum(exponent, axis=-1, keepdims=True))).astype(BF16)
        attn[:, part] = dot_nn(low, v).astype(BF16)


def attention_fwd(lengths, lin, gain, cos, sin, keys, values, prompt_len):
    blocks, total_keys, head = keys.shape
    slots = lin.shape[0] // blocks
    width = lin.shape[1] - 2 * head
    row = pl.BlockSpec((slots, width), lambda i, *_: (i, 0))
    table = pl.BlockSpec((1, slots, head), lambda i, *_: (i, 0, 0))
    kv = pl.BlockSpec((1, total_keys, head), lambda i, *_: (i, 0, 0))
    one = pl.BlockSpec((1, head), lambda i, *_: (0, 0))
    return pl.pallas_call(
        functools.partial(attention_fwd_kernel, prompt_len),
        grid_spec=pltpu.PrefetchScalarGridSpec(
            num_scalar_prefetch=1,
            grid=(blocks,),
            in_specs=[row, one, table, table, kv, kv],
            out_specs=[row, row],
        ),
        out_shape=(
            jax.ShapeDtypeStruct((lin.shape[0], width), BF16),
            jax.ShapeDtypeStruct((lin.shape[0], width), BF16),
        ),
        compiler_params=params(),
        name="attention_fwd",
    )(lengths, lin, gain, cos, sin, keys, values)


def attention_bwd_kernel(
    prompt_len, lengths, lin, queries, d_attn, gain, cos, sin, keys, values, d_lin, d_keys, d_values, d_gain
):
    block = pl.program_id(0)
    slots = lin.shape[0]
    head = gain.shape[1]
    allowed = masks_of(
        block, lengths[block], slots, slots - CMAX, prompt_len, lengths[4], keys.shape[1]
    )
    scale = head ** (-0.5)
    k, v = keys[0], values[0]
    c, s, g = cos[0], sin[0], gain[...]
    key_total = jnp.zeros(k.shape, F32)
    value_total = jnp.zeros(v.shape, F32)
    gain_total = jnp.zeros((8, head), F32)
    for h in range(lin.shape[1] // head):
        part = slice(h * head, (h + 1) * head)
        q = queries[:, part]
        score = jnp.where(allowed, dot_nt(q, k) * scale, -jnp.inf)
        peak = jnp.max(score, axis=-1, keepdims=True)
        exponent = jnp.exp(score - peak)
        probs = exponent * (1.0 / jnp.sum(exponent, axis=-1, keepdims=True))
        d_out = d_attn[:, part]
        d_probs = dot_nt(d_out, v)
        inner = jnp.sum(probs * d_probs, axis=-1, keepdims=True)
        d_score = (probs * (d_probs - inner)).astype(BF16)
        key_total = key_total + dot_tn(d_score, q)
        value_total = value_total + dot_tn(probs.astype(BF16), d_out)
        d_q = dot_nn(d_score, k) * scale
        turned = d_q * c + pltpu.roll(d_q * s, head // 2, 1)
        x = lin[:, part]
        inverse = lax.rsqrt(jnp.mean(x * x, axis=-1, keepdims=True) + norm_eps)
        unit = x * inverse
        pairs = turned * unit
        for j in range(slots // 8):
            gain_total = gain_total + pairs[j * 8 : (j + 1) * 8]
        weighted = turned * g
        d_lin[:, part] = (
            inverse * (weighted - unit * jnp.mean(weighted * unit, axis=-1, keepdims=True))
        ).astype(BF16)
    d_keys[0] = key_total * scale
    d_values[0] = value_total
    d_gain[0] = gain_total


def attention_bwd(lengths, lin, queries, d_attn, gain, cos, sin, keys, values, prompt_len):
    blocks, total_keys, head = keys.shape
    slots = lin.shape[0] // blocks
    width = lin.shape[1] - 2 * head
    row = pl.BlockSpec((slots, width), lambda i, *_: (i, 0))
    table = pl.BlockSpec((1, slots, head), lambda i, *_: (i, 0, 0))
    kv = pl.BlockSpec((1, total_keys, head), lambda i, *_: (i, 0, 0))
    one = pl.BlockSpec((1, head), lambda i, *_: (0, 0))
    return pl.pallas_call(
        functools.partial(attention_bwd_kernel, prompt_len),
        grid_spec=pltpu.PrefetchScalarGridSpec(
            num_scalar_prefetch=1,
            grid=(blocks,),
            in_specs=[row, row, row, one, table, table, kv, kv],
            out_specs=[row, kv, kv, pl.BlockSpec((1, 8, head), lambda i, *_: (i, 0, 0))],
        ),
        out_shape=(
            jax.ShapeDtypeStruct((lin.shape[0], width), BF16),
            jax.ShapeDtypeStruct(keys.shape, F32),
            jax.ShapeDtypeStruct(values.shape, F32),
            jax.ShapeDtypeStruct((blocks, 8, head), F32),
        ),
        compiler_params=params(),
        name="attention_bwd",
    )(lengths, lin, queries, d_attn, gain, cos, sin, keys, values)


def partner(shard, axis, bit):
    return lax.ppermute(shard, axis, [(i, i ^ 1 << bit) for i in range(lax.axis_size(axis))])


def root_mean_scale(value_rows, gain_vec):
    return (
        value_rows
        * lax.rsqrt(jnp.mean(value_rows * value_rows, axis=-1, keepdims=True) + norm_eps)
        * gain_vec
    )


def contract(left_side, right_side, left_dim, right_dim):
    return lax.dot_general(
        left_side,
        right_side,
        (((left_dim,), (right_dim,)), ((), ())),
        preferred_element_type=F32,
    )


def plane_order(z):
    upper, odd = z // 2, z % 2
    return [z, z + 1 - 2 * upper, 2 + upper - 2 * odd, 3 - 3 * upper]


def world(with_diag):
    r, e = lax.axis_index("dp"), lax.axis_index("expert")
    z, core = e // 2, e % 2
    near, far = r ^ 1, r ^ 2
    devices = [(near, e), (far, e), (r, e ^ 1)]
    devices += [(r, lax.rem(z + j, 4) * 2 + core) for j in (1, 2, 3)]
    return r, e, z, core, near, far, devices


def gather_world(mine, buf, zs, zr, ps, pr, ds, dr, before, group):
    r, e, z, core, near, far, greeted = world(True)
    half = mine.shape[0] // 2
    low, high = pl.ds(0, half), pl.ds(half, half)
    order = plane_order(z)
    greet(greeted)

    def slot(q, b, c):
        return q * 8 + b * 2 + c

    buf[slot(r, z, core)] = mine[...]
    diag = r ^ 3
    plane, pairs, lines = {}, {}, []

    def hand(k, i, q):
        at = slot(q, order[k], core)
        copy = remote(buf.at[at], buf.at[at], ds.at[k, i], dr.at[k, i], (r, e ^ 1))
        copy.start()
        pairs[k, i] = copy

    def issue(k):
        b = order[k]
        at = slot(r, b, core)
        for side, cond, to in (
            (0, (b <= z) & (z < 3), jnp.minimum(z + 1, 3)),
            (1, (b >= z) & (z > 0), jnp.maximum(z - 1, 0)),
        ):
            copy = remote(buf.at[at], buf.at[at], zs.at[k, side], zr.at[b], (r, to * 2 + core))
            lines.append((cond, copy))

            @pl.when(cond)
            def _():
                copy.start()

        mine_at, near_at, far_at = at, slot(near, b, core), slot(far, b, core)
        for i, (src, part, p) in enumerate(
            (
                (mine_at, low, near),
                (mine_at, high, far),
                (mine_at, high, near),
                (mine_at, low, far),
                (near_at, low, far),
                (far_at, high, near),
            )
        ):
            plane[k, i] = remote(
                buf.at[src, part], buf.at[src, part], ps.at[k, i], pr.at[k, i], (p, e)
            )
        for i in range(4):
            plane[k, i].start()
        hand(k, 0, r)

    def line_wait(k):
        b = order[k]
        at = slot(r, b, core)
        remote(buf.at[at], buf.at[at], zs.at[k, 0], zr.at[b], (r, e ^ 1)).wait_recv()
        issue(k)

    def passes(k):
        plane[k, 0].wait_recv()
        plane[k, 4].start()
        plane[k, 1].wait_recv()
        plane[k, 5].start()

    def finish(k):
        plane[k, 2].wait_recv()
        hand(k, 1, near)
        plane[k, 3].wait_recv()
        hand(k, 2, far)

    def corner(k):
        plane[k, 4].wait_recv()
        plane[k, 5].wait_recv()
        hand(k, 3, diag)

    def ready(k):
        for i in range(4):
            pairs[k, i].wait_recv()
        group(k, order[k])

    issue(0)
    passes(0)
    line_wait(1)
    finish(0)
    passes(1)
    line_wait(2)
    corner(0)
    finish(1)
    before(0, order[0])
    ready(0)
    passes(2)
    line_wait(3)
    corner(1)
    finish(2)
    before(1, order[1])
    ready(1)
    passes(3)
    corner(2)
    finish(3)
    before(2, order[2])
    ready(2)
    before(3, order[3])
    corner(3)
    ready(3)
    for copy in plane.values():
        copy.wait_send()
    for copy in pairs.values():
        copy.wait_send()
    for cond, copy in lines:

        @pl.when(cond)
        def _():
            copy.wait_send()


GATHER_SEMS = [
    pltpu.SemaphoreType.DMA((4, 2)),
    pltpu.SemaphoreType.DMA((4,)),
    pltpu.SemaphoreType.DMA((4, 6)),
    pltpu.SemaphoreType.DMA((4, 6)),
    pltpu.SemaphoreType.DMA((4, 4)),
    pltpu.SemaphoreType.DMA((4, 4)),
]


def selector(pos, source, room):
    row = pos[source]
    ids = lax.broadcasted_iota(jnp.int32, (room, row.shape[1]), 0).astype(F32)
    return jnp.where(ids == row, 1.0, 0.0).astype(BF16)


def start_all(copies):
    for copy in copies:
        copy.start()
    return copies


def wait_all(copies):
    for copy in copies:
        copy.wait()
    copies.clear()


def experts_fwd_kernel(
    mine, wg, wu, wd, pos, x_out, y_out, g_out, u_out, o_out, hid_out, gate_out,
    buf, wg_v, wu_v, wd_v, x_v, y_v, g_v, u_v, o_v, hid_v, gate_v, local, zs, zr, ps, pr, ds, dr,
):
    model = wg.shape[0]
    rows_in = mine.shape[0]
    room = x_v.shape[0] // 8
    me = lax.axis_index("dp") * 8 + lax.axis_index("expert")
    loads = start_all(
        [
            pltpu.make_async_copy(a, b, local.at[i])
            for i, (a, b) in enumerate(((wg, wg_v), (wu, wu_v), (wd, wd_v)))
        ]
    )
    leaving = []

    def leave(b, pairs):
        leaving.extend(
            start_all([pltpu.make_async_copy(v, o.at[b], local.at[i]) for i, v, o in pairs])
        )

    def before(k, b):
        wait_all(loads)

    def group(k, b):
        wait_all(leaving)
        upto = jnp.where(
            lax.broadcasted_iota(jnp.int32, (rows_in, rows_in), 0)
            <= lax.broadcasted_iota(jnp.int32, (rows_in, rows_in), 1),
            1.0,
            0.0,
        ).astype(BF16)
        is_me = jnp.where(lax.broadcasted_iota(jnp.int32, (16, 128), 1) == me, 1.0, 0.0).astype(BF16)

        def pick(j, carry):
            s = j // 2 * 8 + b * 2 + j % 2
            rows = aligned(j, room)
            named = jnp.where(dot_nt(is_me, buf[s, :, model:]) > 0.0, 1.0, 0.0)
            place = dot_nn(named.astype(BF16), upto) * named - 1.0
            pos[s] = place[:1]
            ids = lax.broadcasted_iota(jnp.int32, (room, rows_in), 0).astype(F32)
            sel = jnp.where(ids == place[:1], 1.0, 0.0).astype(BF16)
            for c in range(4):
                n = slice(c * model // 4, (c + 1) * model // 4)
                x_v[rows, n] = dot_nn(sel, buf[s, :, n]).astype(BF16)
            extra = dot_nn(sel, buf[s, :, model:])
            lane = lax.broadcasted_iota(jnp.int32, extra.shape, 1)
            hit = (lane == me) | (lane == me + 64)
            gate = jnp.sum(jnp.where(hit, extra, 0.0), axis=-1, keepdims=True)
            gate_v[rows, :] = jnp.broadcast_to(gate, extra.shape)
            return carry

        lax.fori_loop(0, 8, pick, 0)
        leave(b, ((0, x_v, x_out), (1, gate_v, gate_out)))

        def first(c, carry):
            n = aligned(c, 256)
            g = dot_nn(x_v[...], wg_v[:, n])
            u = dot_nn(x_v[...], wu_v[:, n])
            g_v[:, n] = g.astype(BF16)
            u_v[:, n] = u.astype(BF16)
            hid_v[:, n] = (g / (1.0 + jnp.exp(-g)) * u).astype(BF16)
            return carry

        lax.fori_loop(0, wg.shape[1] // 256, first, 0)
        leave(b, ((2, g_v, g_out), (3, u_v, u_out), (4, hid_v, hid_out)))

        def second(c, carry):
            n = aligned(c, 256)
            o = dot_nn(hid_v[...], wd_v[:, n]).astype(BF16)
            o_v[:, n] = o
            y_v[:, n] = (o.astype(F32) * gate_v[:, :1]).astype(BF16)
            return carry

        lax.fori_loop(0, model // 256, second, 0)
        leave(b, ((5, o_v, o_out), (6, y_v, y_out)))
        if k == 3:
            wait_all(leaving)

    gather_world(mine, buf, zs, zr, ps, pr, ds, dr, before, group)


def experts_fwd(mine, wg, wu, wd, room):
    rows, width = mine.shape
    model, ff = wg.shape
    group = 8 * room
    wide = jax.ShapeDtypeStruct((4, group, model), BF16)
    thin = jax.ShapeDtypeStruct((4, group, ff), BF16)
    pos, x, y, g, u, o, hidden, gates = pl.pallas_call(
        experts_fwd_kernel,
        out_shape=(
            jax.ShapeDtypeStruct((32, 1, rows), F32),
            wide,
            wide,
            thin,
            thin,
            wide,
            thin,
            jax.ShapeDtypeStruct((4, group, 128), F32),
        ),
        in_specs=[VMEM_SPEC, ANY_SPEC, ANY_SPEC, ANY_SPEC],
        out_specs=(VMEM_SPEC,) + (ANY_SPEC,) * 7,
        scratch_shapes=[
            pltpu.VMEM((32, rows, width), BF16),
            pltpu.VMEM((model, ff), BF16),
            pltpu.VMEM((model, ff), BF16),
            pltpu.VMEM((ff, model), BF16),
            pltpu.VMEM((group, model), BF16),
            pltpu.VMEM((group, model), BF16),
            pltpu.VMEM((group, ff), BF16),
            pltpu.VMEM((group, ff), BF16),
            pltpu.VMEM((group, model), BF16),
            pltpu.VMEM((group, ff), BF16),
            pltpu.VMEM((group, 128), F32),
            pltpu.SemaphoreType.DMA((7,)),
        ]
        + GATHER_SEMS,
        compiler_params=params(6),
        name="experts_fwd",
    )(mine, wg, wu, wd)
    return pos, x, y, (g, u, o, hidden, gates)


def experts_bwd_kernel(
    mine, pos, g_in, u_in, o_in, gate_in, wg, wu, wd, y_out, d_copy_out, dg_out, du_out,
    buf, wg_v, wu_v, wd_v, g_v, u_v, o_v, gate_v, y_v, d_copy_v, dg_v, du_v,
    local, ins, zs, zr, ps, pr, ds, dr,
):
    model, ff = wg.shape
    room = d_copy_v.shape[0] // 8
    z = lax.axis_index("expert") // 2
    me = lax.axis_index("dp") * 8 + lax.axis_index("expert")
    loads = start_all(
        [
            pltpu.make_async_copy(a, b, local.at[i])
            for i, (a, b) in enumerate(((wg, wg_v), (wu, wu_v), (wd, wd_v)))
        ]
    )
    leaving, coming = [], {}

    def fetch(k):
        b = plane_order(z)[k]
        at = k % 2
        coming[k] = start_all(
            [
                pltpu.make_async_copy(a.at[b], v.at[at], ins.at[at, i])
                for i, (a, v) in enumerate(
                    ((g_in, g_v), (u_in, u_v), (o_in, o_v), (gate_in, gate_v))
                )
            ]
        )

    fetch(0)

    def leave(b, pairs):
        leaving.extend(
            start_all([pltpu.make_async_copy(v, o.at[b], local.at[i]) for i, v, o in pairs])
        )

    def before(k, b):
        wait_all(loads)
        wait_all(coming[k])
        if k < 3:
            fetch(k + 1)

    def group(k, b):
        at = k % 2
        wait_all(leaving)

        def pick(j, carry):
            s = j // 2 * 8 + b * 2 + j % 2
            rows = aligned(j, room)
            sel = selector(pos, s, room)
            gate = gate_v[at, rows, :1]
            inner = jnp.zeros((room, 1), F32)
            for c in range(4):
                n = slice(c * model // 4, (c + 1) * model // 4)
                picked = dot_nn(sel, buf[s, :, n])
                d_copy_v[rows, n] = (gate * picked).astype(BF16)
                inner = inner + jnp.sum(
                    picked * o_v[at, rows, n].astype(F32), axis=-1, keepdims=True
                )
            top = inner.astype(BF16).astype(F32)
            rest = inner - top
            lane = lax.broadcasted_iota(jnp.int32, (room, 128), 1)
            extra = jnp.where(lane == me, top, 0.0) + jnp.where(lane == me + 64, rest, 0.0)
            y_v[rows, model:] = extra.astype(BF16)
            return carry

        lax.fori_loop(0, 8, pick, 0)
        leave(b, ((0, d_copy_v, d_copy_out),))

        def third(c, carry):
            n = aligned(c, 256)
            d_hidden = dot_nt(d_copy_v[...], wd_v[n, :])
            g, u = g_v[at, :, n].astype(F32), u_v[at, :, n].astype(F32)
            s = 1.0 / (1.0 + jnp.exp(-g))
            dg_v[:, n] = (d_hidden * u * s * (1.0 + g * (1.0 - s))).astype(BF16)
            du_v[:, n] = (d_hidden * g * s).astype(BF16)
            return carry

        lax.fori_loop(0, ff // 256, third, 0)
        leave(b, ((1, dg_v, dg_out), (2, du_v, du_out)))

        def fourth(c, carry):
            n = aligned(c, 256)
            y_v[:, n] = (dot_nt(dg_v[...], wg_v[n, :]) + dot_nt(du_v[...], wu_v[n, :])).astype(BF16)
            return carry

        lax.fori_loop(0, model // 256, fourth, 0)
        leave(b, ((3, y_v, y_out),))
        if k == 3:
            wait_all(leaving)

    gather_world(mine, buf, zs, zr, ps, pr, ds, dr, before, group)


def experts_bwd(mine, pos, kept, wg, wu, wd, room):
    rows, width = mine.shape
    model, ff = wg.shape
    group = 8 * room
    return pl.pallas_call(
        experts_bwd_kernel,
        out_shape=(
            jax.ShapeDtypeStruct((4, group, model + 128), BF16),
            jax.ShapeDtypeStruct((4, group, model), BF16),
            jax.ShapeDtypeStruct((4, group, ff), BF16),
            jax.ShapeDtypeStruct((4, group, ff), BF16),
        ),
        in_specs=[VMEM_SPEC, VMEM_SPEC] + [ANY_SPEC] * 7,
        out_specs=(ANY_SPEC,) * 4,
        scratch_shapes=[
            pltpu.VMEM((32, rows, width), BF16),
            pltpu.VMEM((model, ff), BF16),
            pltpu.VMEM((model, ff), BF16),
            pltpu.VMEM((ff, model), BF16),
            pltpu.VMEM((2, group, ff), BF16),
            pltpu.VMEM((2, group, ff), BF16),
            pltpu.VMEM((2, group, model), BF16),
            pltpu.VMEM((2, group, 128), F32),
            pltpu.VMEM((group, model + 128), BF16),
            pltpu.VMEM((group, model), BF16),
            pltpu.VMEM((group, ff), BF16),
            pltpu.VMEM((group, ff), BF16),
            pltpu.SemaphoreType.DMA((4,)),
            pltpu.SemaphoreType.DMA((2, 4)),
        ]
        + GATHER_SEMS,
        compiler_params=params(7),
        name="experts_bwd",
    )(mine, pos, *kept, wg, wu, wd)


def sum_world_kernel(
    y, pos, out, psend, pair, half_near, half_far, full_near, full_far, lines,
    ds, dr, hs, hr, fs, fr, zs, zr,
):
    r, e, z, core, near, far, greeted = world(True)
    rows, width = out.shape
    room = y.shape[2]
    half = rows // 2
    low, high = pl.ds(0, half), pl.ds(half, half)
    order = plane_order(z)[::-1]
    diag = r ^ 3
    who = [r, near, far, diag]
    body_width = width // 512 * 512
    greet(greeted)

    def for_columns(fn):
        def step(c, carry):
            fn(aligned(c, 512))
            return carry

        lax.fori_loop(0, body_width // 512, step, 0)
        if width > body_width:
            fn(pl.ds(body_width, width - body_width))

    def scattered(sel, q, b, c, n):
        return dot_tn(sel, y[b, q * 2 + c, :, n])

    pairs, halves, fulls, moves = {}, {}, {}, []

    def stage_a(k):
        b = order[k]
        for i in (3, 1, 2, 0):
            at = k * 4 + i
            sel = selector(pos, who[i] * 8 + b * 2 + (1 - core), room)

            def fill(n):
                psend[at, :, n] = scattered(sel, who[i], b, 1 - core, n).astype(BF16)

            for_columns(fill)
            copy = remote(psend.at[at], pair.at[at], ds.at[at], dr.at[at], (r, e ^ 1))
            copy.start()
            pairs[at] = copy
        for i in (3, 1, 2, 0):
            at = k * 4 + i
            sel = selector(pos, who[i] * 8 + b * 2 + core, room)
            pairs[at].wait_recv()

            def add(n):
                value = scattered(sel, who[i], b, core, n) + pair[at, :, n].astype(F32)
                pair[at, :, n] = value.astype(BF16)

            for_columns(add)
            if i == 3:
                for side, (part, dst, p) in enumerate(
                    ((low, half_near, near), (high, half_far, far))
                ):
                    copy = remote(
                        pair.at[at, part], dst.at[k], hs.at[k, side], hr.at[k, side], (p, e)
                    )
                    copy.start()
                    halves[k, side] = copy

    def stage_b(k):
        for side, (i, part, src, dst, p) in enumerate(
            (
                (2, low, half_near, full_far, far),
                (1, high, half_far, full_near, near),
            )
        ):
            at = k * 4 + i
            halves[k, side].wait_recv()

            def add(n):
                value = pair[at, part, n].astype(F32) + src[k, :, n].astype(F32)
                pair[at, part, n] = value.astype(BF16)

            for_columns(add)
            copy = remote(pair.at[at], dst.at[k], fs.at[k, side], fr.at[k, side], (p, e))
            copy.start()
            fulls[k, side] = copy

    def stage_c(k):
        b = order[k]
        at = k * 4
        fulls[k, 0].wait_recv()
        fulls[k, 1].wait_recv()

        def add(n):
            out[:, n] = (
                pair[at, :, n].astype(F32)
                + full_near[k, :, n].astype(F32)
                + full_far[k, :, n].astype(F32)
            )

        for_columns(add)
        for side, cond in ((0, (b >= z) & (z > 0)), (1, (b <= z) & (z < 3))):

            @pl.when(cond)
            def _():
                remote(
                    lines.at[side, b], lines.at[side, b], zs.at[side, k], zr.at[side, b], (r, e ^ 1)
                ).wait_recv()

                def more(n):
                    out[:, n] = out[:, n] + lines[side, b, :, n].astype(F32)

                for_columns(more)

        if k < 3:

            def keep(n):
                pair[at, :, n] = out[:, n].astype(BF16)

            for_columns(keep)
            for side, cond, to in (
                (0, b > z, jnp.minimum(z + 1, 3)),
                (1, b < z, jnp.maximum(z - 1, 0)),
            ):
                copy = remote(
                    pair.at[at], lines.at[side, b], zs.at[side, k], zr.at[side, b], (r, to * 2 + core)
                )
                moves.append((cond, copy))

                @pl.when(cond)
                def _():
                    copy.start()

    stage_a(0)
    stage_a(1)
    stage_b(0)
    stage_a(2)
    stage_b(1)
    stage_c(0)
    stage_a(3)
    stage_b(2)
    stage_c(1)
    stage_b(3)
    stage_c(2)
    stage_c(3)
    for copies in (pairs, halves, fulls):
        for copy in copies.values():
            copy.wait_send()
    for cond, copy in moves:

        @pl.when(cond)
        def _():
            copy.wait_send()


def sum_world(y, pos, rows, collective_id):
    groups, per, room, width = y.shape

    def blocks(n, size):
        return pltpu.VMEM((n, size, width), BF16)

    return pl.pallas_call(
        sum_world_kernel,
        out_shape=jax.ShapeDtypeStruct((rows, width), F32),
        in_specs=[VMEM_SPEC, VMEM_SPEC],
        out_specs=VMEM_SPEC,
        scratch_shapes=[
            blocks(16, rows),
            blocks(16, rows),
            blocks(4, rows // 2),
            blocks(4, rows // 2),
            blocks(4, rows),
            blocks(4, rows),
            pltpu.VMEM((2, 4, rows, width), BF16),
            pltpu.SemaphoreType.DMA((16,)),
            pltpu.SemaphoreType.DMA((16,)),
            pltpu.SemaphoreType.DMA((4, 2)),
            pltpu.SemaphoreType.DMA((4, 2)),
            pltpu.SemaphoreType.DMA((4, 2)),
            pltpu.SemaphoreType.DMA((4, 2)),
            pltpu.SemaphoreType.DMA((2, 4)),
            pltpu.SemaphoreType.DMA((2, 4)),
        ],
        compiler_params=params(collective_id),
        name="sum_world",
    )(y, pos)


def experts_by_all_to_all(
    mixed, state, teacher, routes, valid_slot, valid_count, router_weight, gate_weight, up_weight, down_weight,
    devices, capacity, slots_all,
):
    tok_dev, model_width = mixed.shape
    top_count = routes.shape[1]
    ffn_width = gate_weight.shape[2]
    logits = jnp.dot(mixed, router_weight, preferred_element_type=jnp.float32)
    gates = jax.nn.softmax(jnp.take_along_axis(logits, routes, axis=1), axis=-1)
    rows_total = tok_dev * top_count
    expert_ids = routes.reshape(rows_total)
    live_rows = jnp.repeat(valid_slot, top_count)
    expert_range = jnp.arange(devices, dtype=jnp.int32)
    hit_table = ((expert_ids[:, None] == expert_range[None, :]) & live_rows[:, None]).astype(
        jnp.int32
    )
    earlier = jnp.cumsum(hit_table, axis=0) - hit_table
    position_in = jnp.sum(earlier * hit_table, axis=1)
    slot_index = jnp.where(live_rows, expert_ids * capacity + position_in, devices * capacity)
    row_of_slot = (
        jnp.full((devices * capacity + 1,), rows_total, jnp.int32)
        .at[slot_index]
        .set(jnp.arange(rows_total, dtype=jnp.int32))[: devices * capacity]
    )
    token_of_slot = jnp.where(row_of_slot < rows_total, row_of_slot // top_count, tok_dev)
    mixed_pad = jnp.concatenate([mixed, jnp.zeros((1, model_width), jnp.bfloat16)], axis=0)
    send_rows = mixed_pad[token_of_slot].reshape(devices, capacity, model_width)
    arrived = lax.all_to_all(send_rows, ("dp", "expert"), split_axis=0, concat_axis=0, tiled=True)
    sources = arrived.shape[0]
    items = arrived.shape[1]
    flat_in = arrived.reshape(sources * items, model_width)
    gate_pre = jnp.dot(flat_in, gate_weight[0], preferred_element_type=jnp.float32)
    up_pre = jnp.dot(flat_in, up_weight[0], preferred_element_type=jnp.float32)
    hidden_units = (jax.nn.silu(gate_pre) * up_pre).astype(jnp.bfloat16)
    produced = jnp.dot(hidden_units, down_weight[0], preferred_element_type=jnp.float32).astype(
        jnp.bfloat16
    )
    produced, gate_pre, up_pre, hidden_units, arrived = (
        produced.reshape(sources, items, model_width),
        gate_pre.reshape(sources, items, ffn_width),
        up_pre.reshape(sources, items, ffn_width),
        hidden_units.reshape(sources, items, ffn_width),
        arrived,
    )
    returned = lax.all_to_all(produced, ("dp", "expert"), split_axis=0, concat_axis=0, tiled=True)
    returned_pad = jnp.concatenate(
        [
            returned.reshape(devices * capacity, model_width),
            jnp.zeros((1, model_width), jnp.bfloat16),
        ],
        axis=0,
    )
    copies = returned_pad[slot_index].reshape(tok_dev, top_count, model_width)
    layer_out = state + jnp.sum(gates[:, :, None] * copies, axis=1)
    live_tokens = valid_slot.astype(jnp.float32)[:, None]
    diff = (layer_out - teacher.astype(jnp.float32)) * live_tokens
    local_square = jnp.sum(diff * diff)
    d_out = 2.0 * slots_all * diff / valid_count
    d_gates = jnp.sum(d_out[:, None, :] * copies, axis=-1)
    d_chosen = gates * (d_gates - jnp.sum(gates * d_gates, axis=-1, keepdims=True))
    d_logits = jnp.sum(
        jnp.where(routes[:, :, None] == expert_range[None, None, :], d_chosen[:, :, None], 0.0),
        axis=1,
    ).astype(jnp.bfloat16)
    d_copies = (
        (gates[:, :, None] * d_out[:, None, :])
        .astype(jnp.bfloat16)
        .reshape(rows_total, model_width)
    )
    d_copies_pad = jnp.concatenate([d_copies, jnp.zeros((1, model_width), jnp.bfloat16)], axis=0)
    d_send = d_copies_pad[row_of_slot].reshape(devices, capacity, model_width)
    d_arrived = lax.all_to_all(d_send, ("dp", "expert"), split_axis=0, concat_axis=0, tiled=True)
    flat_d = d_arrived.reshape(-1, model_width)
    flat_in = arrived.reshape(-1, model_width)
    flat_gate = gate_pre.reshape(-1, ffn_width)
    flat_up = up_pre.reshape(-1, ffn_width)
    flat_hidden = hidden_units.reshape(-1, ffn_width)
    d_hidden = contract(flat_d, down_weight[0], 1, 1)
    sigmoid_gate = jax.nn.sigmoid(flat_gate)
    d_gate = (d_hidden * flat_up * sigmoid_gate * (1.0 + flat_gate * (1.0 - sigmoid_gate))).astype(
        jnp.bfloat16
    )
    d_up = (d_hidden * flat_gate * sigmoid_gate).astype(jnp.bfloat16)
    down_grad = contract(flat_hidden, flat_d, 0, 0)[None]
    gate_grad = contract(flat_in, d_gate, 0, 0)[None]
    up_grad = contract(flat_in, d_up, 0, 0)[None]
    d_in = (contract(d_gate, gate_weight[0], 1, 1) + contract(d_up, up_weight[0], 1, 1)).astype(
        jnp.bfloat16
    )
    d_returned = lax.all_to_all(
        d_in.reshape(devices, capacity, model_width),
        ("dp", "expert"),
        split_axis=0,
        concat_axis=0,
        tiled=True,
    )
    d_returned_pad = jnp.concatenate(
        [
            d_returned.reshape(devices * capacity, model_width),
            jnp.zeros((1, model_width), jnp.bfloat16),
        ],
        axis=0,
    )
    d_mixed = jnp.sum(
        d_returned_pad[slot_index].reshape(tok_dev, top_count, model_width),
        axis=1,
        dtype=jnp.float32,
    )
    d_mixed = d_mixed + contract(d_logits, router_weight, 1, 1)
    router_local = contract(mixed, d_logits, 0, 0)
    return layer_out, d_out, d_mixed, local_square, router_local, gate_grad, up_grad, down_grad


def experts_by_gather(
    mixed, state, teacher, routes, valid_slot, valid_count, router_weight,
    gate_weight, up_weight, down_weight, devices, capacity, slots_all,
):
    tok_dev, model_width = mixed.shape
    room = -(-capacity // 16) * 16
    expert_range = jnp.arange(devices, dtype=jnp.int32)
    logits = jnp.dot(mixed, router_weight, preferred_element_type=F32)
    chosen = jnp.any(routes[:, :, None] == expert_range[None, None], axis=1)
    gates = jax.nn.softmax(jnp.where(chosen, logits, -jnp.inf), axis=-1)
    live_gates = jnp.where(valid_slot[:, None], gates, 0.0)
    gates_high = live_gates.astype(BF16)
    gates_low = (live_gates - gates_high.astype(F32)).astype(BF16)
    gap = jnp.zeros((tok_dev, 64 - devices), BF16)
    payload = jnp.concatenate([mixed, gates_high, gap, gates_low, gap], axis=1)
    pos, x_rows, y_rows, kept = experts_fwd(
        payload, gate_weight[0], up_weight[0], down_weight[0], room
    )
    layer_out = state + sum_world(y_rows.reshape(4, 8, room, model_width), pos, tok_dev, 8)
    live_tokens = valid_slot.astype(F32)[:, None]
    diff = (layer_out - teacher.astype(F32)) * live_tokens
    local_square = jnp.sum(diff * diff)
    d_out = 2.0 * slots_all * diff / valid_count
    hidden = kept[3]
    d_rows, d_copy, d_gate, d_up = experts_bwd(
        d_out.astype(BF16), pos, kept[:3] + kept[4:], gate_weight[0], up_weight[0], down_weight[0], room
    )
    back = sum_world(d_rows.reshape(4, 8, room, model_width + 128), pos, tok_dev, 9)

    def flat(a):
        return a.reshape(4 * 8 * room, a.shape[-1])

    down_grad = contract(flat(hidden), flat(d_copy), 0, 0)[None]
    gate_grad = contract(flat(x_rows), flat(d_gate), 0, 0)[None]
    up_grad = contract(flat(x_rows), flat(d_up), 0, 0)[None]
    d_gates = back[:, model_width : model_width + devices] + back[:, model_width + 64 : model_width + 64 + devices]
    d_logits = (gates * (d_gates - jnp.sum(gates * d_gates, axis=-1, keepdims=True))).astype(BF16)
    d_mixed = back[:, :model_width] + contract(d_logits, router_weight, 1, 1)
    router_local = contract(mixed, d_logits, 0, 0)
    return layer_out, d_out, d_mixed, local_square, router_local, gate_grad, up_grad, down_grad


def head_rope(linear, gain_vec, cos, sin):
    value = root_mean_scale(linear, gain_vec)
    half = value.shape[-1] // 2
    return value * cos + jnp.roll(value, half, axis=-1) * sin


def body(
    tokens,
    teacher,
    routes,
    cont_lengths,
    query_weight,
    key_projection,
    value_projection,
    output_weight,
    router_weight,
    gate_weight,
    up_weight,
    down_weight,
    input_gain,
    post_gain,
    query_gain,
    key_gain,
):
    n_dp = lax.axis_size("dp")
    n_owner = lax.axis_size("expert")
    devices = n_dp * n_owner
    rank_dp = lax.axis_index("dp")
    rank_owner = lax.axis_index("expert")
    flat_rank = rank_dp * n_owner + rank_owner
    column = rank_owner % 2
    first_column = column == 0
    tok_dev, model_width = tokens.shape
    top_count = routes.shape[1]
    head_dim = query_gain.shape[0]
    kv_width = key_projection.shape[1]
    query_width = query_weight.shape[1]
    query_group = query_width // n_dp
    assert n_dp == 4 and kv_width == n_dp * head_dim
    prompt_block = tok_dev - CMAX
    half_prompt = n_dp * prompt_block
    prompt_len = 2 * half_prompt
    capacity = max(2, tok_dev * top_count * 5 // (4 * devices))
    slots_all = devices * tok_dev
    slot_ids = jnp.arange(tok_dev, dtype=jnp.int32)
    own_length = cont_lengths[flat_rank]
    valid_slot = (slot_ids < prompt_block) | (slot_ids - prompt_block < own_length)
    valid_count = (devices * prompt_block + jnp.sum(cont_lengths)).astype(F32)
    tokens_float = tokens.astype(F32)
    normed_float, first_norm_back = jax.vjp(root_mean_scale, tokens_float, input_gain)
    normed = normed_float.astype(BF16)

    block_ids = jnp.arange(n_dp, dtype=jnp.int32)[:, None]
    positions = jnp.where(
        slot_ids[None] < prompt_block,
        (column * n_dp + block_ids) * prompt_block + slot_ids[None],
        prompt_len + slot_ids[None] - prompt_block,
    )
    half_head = head_dim // 2
    frequency = rope_base ** (-(jnp.arange(half_head, dtype=F32) * 2.0) / head_dim)
    angles = positions.astype(F32)[:, :, None] * frequency
    cos_half, sin_half = jnp.cos(angles), jnp.sin(angles)
    cos = jnp.concatenate([cos_half, cos_half], axis=-1)
    sin = jnp.concatenate([-sin_half, sin_half], axis=-1)
    lengths = jnp.concatenate(
        [lax.dynamic_index_in_dim(cont_lengths.reshape(n_dp, n_owner), rank_owner, 1, False), column[None]]
    ).astype(jnp.int32)

    lin, normed_cols = project_qkv(normed, query_weight, key_projection, value_projection)
    key_lin = lin[:, query_group : query_group + head_dim].reshape(n_dp, tok_dev, head_dim)
    keys_float, key_back = jax.vjp(lambda a, b: head_rope(a, b, cos, sin), key_lin, key_gain)
    keys_own = keys_float.astype(BF16)
    values_own = lin[:, query_group + head_dim :].reshape(n_dp, tok_dev, head_dim).astype(BF16)
    column_kv = jnp.stack([keys_own[:, :prompt_block], values_own[:, :prompt_block]]).reshape(
        2, half_prompt, head_dim
    )
    other_kv = partner(column_kv, "expert", 0)
    full_kv = jnp.where(
        first_column,
        jnp.concatenate([column_kv, other_kv], axis=1),
        jnp.concatenate([other_kv, column_kv], axis=1),
    )
    spread = jnp.broadcast_to(full_kv[:, None], (2, n_dp, prompt_len, head_dim))
    all_keys = jnp.concatenate([spread[0], keys_own[:, prompt_block:]], axis=1)
    all_values = jnp.concatenate([spread[1], values_own[:, prompt_block:]], axis=1)
    query_gain_row = query_gain[None]
    queries, attended = attention_fwd(
        lengths, lin, query_gain_row, cos, sin, all_keys, all_values, prompt_len
    )
    state = tokens_float + project_out(attended, output_weight)
    mixed_float, second_norm_back = jax.vjp(root_mean_scale, state, post_gain)
    mixed = mixed_float.astype(BF16)
    sizes = (devices, capacity, slots_all)
    weights = (router_weight, gate_weight, up_weight, down_weight)
    if n_dp == 4 and n_owner == 8:
        moe = experts_by_gather(
            mixed, state, teacher, routes, valid_slot, valid_count, *weights, *sizes
        )
    else:
        moe = experts_by_all_to_all(
            mixed, state, teacher, routes, valid_slot, valid_count, *weights, *sizes
        )
    layer_out, d_out, d_mixed, local_square, router_local, gate_grad, up_grad, down_grad = moe
    d_state_norm, d_post_gain = second_norm_back(d_mixed)
    d_state = d_out + d_state_norm
    d_branch = d_state.astype(BF16)
    d_attended, out_part = grad_branch(d_branch, output_weight, attended.T)
    d_query_lin, d_keys, d_values, gain_parts = attention_bwd(
        lengths, lin, queries, d_attended, query_gain_row, cos, sin, all_keys, all_values, prompt_len
    )
    d_query_gain = jnp.sum(gain_parts, axis=(0, 1))
    prompt_grads = jnp.stack(
        [jnp.sum(d_keys[:, :prompt_len], axis=0), jnp.sum(d_values[:, :prompt_len], axis=0)]
    )
    mine_part = jnp.where(first_column, prompt_grads[:, :half_prompt], prompt_grads[:, half_prompt:])
    their_part = jnp.where(first_column, prompt_grads[:, half_prompt:], prompt_grads[:, :half_prompt])
    own_prompt = (mine_part + partner(their_part, "expert", 0)).reshape(
        2, n_dp, prompt_block, head_dim
    )
    d_key_post = jnp.concatenate([own_prompt[0], d_keys[:, prompt_len:]], axis=1)
    d_value_lin = jnp.concatenate([own_prompt[1], d_values[:, prompt_len:]], axis=1)
    d_key_float, d_key_gain = key_back(d_key_post)
    rows = n_dp * tok_dev
    d_lin = jnp.concatenate(
        [
            d_query_lin,
            d_key_float.astype(BF16).reshape(rows, head_dim),
            d_value_lin.astype(BF16).reshape(rows, head_dim),
        ],
        axis=1,
    )
    d_normed, qkv_part, output_grad = grad_qkv(
        d_lin, query_weight, key_projection, value_projection, normed_cols.T,
        out_part.reshape(n_owner, -1, model_width),
    )
    d_tokens_norm, d_input_gain = first_norm_back(d_normed)
    tokens_grad = d_state + d_tokens_norm
    width = query_weight.shape[0]
    group = d_lin.shape[1]
    rows_here = width // n_owner
    by_owner = (
        qkv_part.reshape(n_dp, n_owner, rows_here, group)
        .transpose(1, 0, 2, 3)
        .reshape(n_owner, n_dp * rows_here, group)
    )
    small_parts = (
        router_local, d_input_gain, d_post_gain, d_query_gain, d_key_gain, local_square[None]
    )
    small = jnp.concatenate([a.reshape(-1) for a in small_parts])
    piece_rows = -(-small.shape[0] // (8 * 8 * 128)) * 8
    small = jnp.pad(small, (0, 8 * piece_rows * 128 - small.shape[0]))
    qkv_rows, small_sums = last_sums(by_owner, small.reshape(8, piece_rows, 128))
    small_sums = small_sums.reshape(-1)
    starts = [0]
    for a in small_parts:
        starts.append(starts[-1] + a.size)
    router_grad, input_gain_grad, post_gain_grad, query_gain_grad, key_gain_grad, total_square = (
        small_sums[i:j].reshape(a.shape) for a, i, j in zip(small_parts, starts, starts[1:])
    )
    loss = total_square[0] / (valid_count * model_width)
    qkv_rows = qkv_rows.reshape(n_dp, rows_here, group)

    def columns(start, size):
        return qkv_rows[:, :, start : start + size].transpose(1, 0, 2).reshape(rows_here, n_dp * size)

    query_grad = columns(0, query_group)
    key_grad = columns(query_group, head_dim)
    value_grad = columns(query_group + head_dim, head_dim)
    return (
        layer_out,
        loss,
        tokens_grad,
        query_grad,
        key_grad,
        value_grad,
        output_grad,
        router_grad,
        gate_grad,
        up_grad,
        down_grad,
        input_gain_grad,
        post_gain_grad,
        query_gain_grad,
        key_gain_grad,
    )


def solution(mesh):
    in_specs = (
        P(("dp", "expert"), None),
        P(("dp", "expert"), None),
        P(("dp", "expert"), None),
        P(),
        P("dp", None),
        P("dp", None),
        P("dp", None),
        P("dp", None),
        P(),
        P(("dp", "expert"), None, None),
        P(("dp", "expert"), None, None),
        P(("dp", "expert"), None, None),
        P(),
        P(),
        P(),
        P(),
    )
    out_specs = (
        P(("dp", "expert"), None),
        P(),
        P(("dp", "expert"), None),
        P(("dp", "expert"), None),
        P(("dp", "expert"), None),
        P(("dp", "expert"), None),
        P(("dp", "expert"), None),
        P(),
        P(("dp", "expert"), None, None),
        P(("dp", "expert"), None, None),
        P(("dp", "expert"), None, None),
        P(),
        P(),
        P(),
        P(),
    )
    return jax.shard_map(body, mesh=mesh, in_specs=in_specs, out_specs=out_specs, check_vma=False)
```

```python
import functools

import jax
import jax.numpy as jnp
from jax import lax
from jax.experimental import pallas as pl
from jax.experimental.pallas import tpu as pltpu
from jax.sharding import PartitionSpec as P

CMAX = 128
norm_eps = 1e-06
rope_base = 1000000.0
MESH = pl.DeviceIdType.MESH
F32 = jnp.float32
BF16 = jnp.bfloat16
VMEM_SPEC = pl.BlockSpec(memory_space=pltpu.VMEM)
ANY_SPEC = pl.BlockSpec(memory_space=pl.ANY)
VMEM_LIMIT = 56 * 1024 * 1024


def params(collective_id=None):
    return pltpu.CompilerParams(
        collective_id=collective_id,
        has_side_effects=collective_id is not None,
        vmem_limit_bytes=VMEM_LIMIT,
    )


def greet(devices):
    barrier = pltpu.get_barrier_semaphore()
    for device in devices:
        pl.semaphore_signal(barrier, inc=1, device_id=device, device_id_type=MESH)
    pl.semaphore_wait(barrier, len(devices))


def remote(src, dst, send_sem, recv_sem, device):
    return pltpu.make_async_remote_copy(
        src_ref=src,
        dst_ref=dst,
        send_sem=send_sem,
        recv_sem=recv_sem,
        device_id=device,
        device_id_type=MESH,
    )


def aligned(index, size):
    return pl.ds(pl.multiple_of(index * size, size), size)


def dot_nn(a, b):
    return lax.dot_general(a, b, (((1,), (0,)), ((), ())), preferred_element_type=F32)


def dot_nt(a, b):
    return lax.dot_general(a, b, (((1,), (1,)), ((), ())), preferred_element_type=F32)


def dot_tn(a, b):
    return lax.dot_general(a, b, (((0,), (0,)), ((), ())), preferred_element_type=F32)


PEER_MASKS = (3, 1, 2)


def relay_sum(r, e, products, own, mine, send, half_in, full_in, hs, hr, fs, fr, step):
    near, far, diag = r ^ 1, r ^ 2, r ^ 3
    rows = mine.shape[0]
    half = rows // 2
    low, high = pl.ds(0, half), pl.ds(half, half)
    products(diag, send.at[2])
    relays = [
        remote(send.at[2, low], half_in.at[0], hs.at[0], hr.at[0], (near, e)),
        remote(send.at[2, high], half_in.at[1], hs.at[1], hr.at[1], (far, e)),
    ]
    for copy in relays:
        copy.start()
    parts = ((0, low, near), (1, high, far), (0, high, near), (1, low, far))
    fulls = [
        remote(send.at[i, part], full_in.at[i, part], fs.at[n], fr.at[n], (p, e))
        for n, (i, part, p) in enumerate(parts)
    ]
    products(near, send.at[0])
    fulls[0].start()
    products(far, send.at[1])
    fulls[1].start()
    for i, start, slot, n in ((1, 0, 0, 3), (0, half, 1, 2)):
        relays[slot].wait_recv()

        def add(c, carry):
            t = pl.ds(pl.multiple_of(start + c * step, step), step)
            value = send[i, t, :].astype(F32) + half_in[slot, aligned(c, step), :].astype(F32)
            send[i, t, :] = value.astype(BF16)
            return carry

        lax.fori_loop(0, half // step, add, 0)
        fulls[n].start()
    own()
    for copy in fulls:
        copy.wait_recv()

    def total(c, carry):
        t = aligned(c, step)
        mine[t, :] = mine[t, :] + (full_in[0, t, :].astype(F32) + full_in[1, t, :].astype(F32))
        return carry

    lax.fori_loop(0, rows // step, total, 0)
    for copy in relays + fulls:
        copy.wait_send()


def relay_scratch(rows, width):
    return [
        pltpu.VMEM((3, rows, width), BF16),
        pltpu.VMEM((2, rows // 2, width), BF16),
        pltpu.VMEM((2, rows, width), BF16),
        pltpu.SemaphoreType.DMA((2,)),
        pltpu.SemaphoreType.DMA((2,)),
        pltpu.SemaphoreType.DMA((4,)),
        pltpu.SemaphoreType.DMA((4,)),
    ]


def qkv_kernel(tok, normed, wq, wk, wv, lin, cols_t, cols, asend, arecv, *relay):
    r, e = lax.axis_index("dp"), lax.axis_index("expert")
    peers = [r ^ m for m in PEER_MASKS]
    width = wq.shape[0]
    qg = wq.shape[1] // 4
    kg = wk.shape[1] // 4
    rows = cols.shape[0]
    greet([(p, e) for p in peers])
    first = []
    for i, p in enumerate(peers):
        copy = remote(
            normed.at[:, aligned(p, width)], cols.at[aligned(r, tok), :],
            asend.at[i], arecv.at[i], (p, e),
        )
        copy.start()
        first.append(copy)
    cols[aligned(r, tok), :] = normed[:, aligned(r, width)]
    for copy in first:
        copy.wait()

    def products(p, dst):
        def chunk(c, carry):
            t = aligned(c, tok)
            x = cols[t, :]
            dst[t, :qg] = dot_nn(x, wq[:, aligned(p, qg)]).astype(dst.dtype)
            dst[t, qg : qg + kg] = dot_nn(x, wk[:, aligned(p, kg)]).astype(dst.dtype)
            dst[t, qg + kg :] = dot_nn(x, wv[:, aligned(p, kg)]).astype(dst.dtype)
            return carry

        lax.fori_loop(0, rows // tok, chunk, 0)

    def own():
        products(r, lin)
        cols_t[...] = cols[...].T

    relay_sum(r, e, products, own, lin, *relay, 32)


def project_qkv(normed, wq, wk, wv):
    tok = normed.shape[0]
    rows = 4 * tok
    group = (wq.shape[1] + wk.shape[1] + wv.shape[1]) // 4
    return pl.pallas_call(
        functools.partial(qkv_kernel, tok),
        out_shape=(
            jax.ShapeDtypeStruct((rows, group), F32),
            jax.ShapeDtypeStruct((wq.shape[0], rows), BF16),
        ),
        in_specs=[VMEM_SPEC] * 4,
        out_specs=(VMEM_SPEC, VMEM_SPEC),
        scratch_shapes=[pltpu.VMEM((rows, wq.shape[0]), BF16)]
        + [pltpu.SemaphoreType.DMA((3,))] * 2
        + relay_scratch(rows, group),
        compiler_params=params(1),
        name="qkv_exchange",
    )(normed, wq, wk, wv)


def out_kernel(attn, wo, total, *relay):
    r, e = lax.axis_index("dp"), lax.axis_index("expert")
    tok, width = total.shape
    step = width // 4
    greet([(r ^ m, e) for m in PEER_MASKS])

    def products(p, dst):
        def chunk(c, carry):
            n = aligned(c, step)
            dst[:, n] = dot_nn(attn[aligned(p, tok), :], wo[:, n]).astype(dst.dtype)
            return carry

        lax.fori_loop(0, width // step, chunk, 0)

    relay_sum(r, e, products, lambda: products(r, total), total, *relay, 16)


def project_out(attn, wo):
    tok = attn.shape[0] // 4
    return pl.pallas_call(
        out_kernel,
        out_shape=jax.ShapeDtypeStruct((tok, wo.shape[1]), F32),
        in_specs=[VMEM_SPEC] * 2,
        out_specs=VMEM_SPEC,
        scratch_shapes=relay_scratch(tok, wo.shape[1]),
        compiler_params=params(2),
        name="out_exchange",
    )(attn, wo)


def dgrad_kernel(
    mine, wq, wk, wv, cols_t, out_part, normal, grads, out_grad,
    blocks, dsum, dsend, drecv, ssem, rsem, bsend, brecv, *scratch,
):
    r, e = lax.axis_index("dp"), lax.axis_index("expert")
    rows = mine.shape[0]
    tok = rows // 4
    half = rows // 2
    qg = wq.shape[1] // 4
    kg = wk.shape[1] // 4
    width = wq.shape[0]
    peers = [r ^ m for m in PEER_MASKS]
    near, far, diag = r ^ 1, r ^ 2, r ^ 3
    pair_in, send, recv, *sems = scratch
    begin, middle, finish = owner_sum([out_part], [out_grad], [pair_in], [send], [recv], *sems)
    greet([(p, e) for p in peers] + [(r, e ^ 1)] + owner_peers())
    begin()
    low, high = pl.ds(0, half), pl.ds(half, half)
    first_near = remote(mine.at[low], blocks.at[0, low], ssem.at[0], rsem.at[0], (near, e))
    first_far = remote(mine.at[high], blocks.at[1, high], ssem.at[1], rsem.at[1], (far, e))
    second_near = remote(mine.at[high], blocks.at[0, high], ssem.at[2], rsem.at[2], (near, e))
    second_far = remote(mine.at[low], blocks.at[1, low], ssem.at[3], rsem.at[3], (far, e))
    pass_far = remote(blocks.at[0, low], blocks.at[2, low], ssem.at[4], rsem.at[4], (far, e))
    pass_near = remote(blocks.at[1, high], blocks.at[2, high], ssem.at[5], rsem.at[5], (near, e))
    for copy in (first_near, first_far, second_near, second_far):
        copy.start()

    def products(p, src, start):
        def chunk(c, carry):
            t = aligned(c, tok)
            x = src[t, :]
            value = (
                dot_nt(x[:, :qg], wq[:, aligned(p, qg)])
                + dot_nt(x[:, qg : qg + kg], wk[:, aligned(p, kg)])
                + dot_nt(x[:, qg + kg :], wv[:, aligned(p, kg)])
            )
            if start:
                dsum[t, :] = value
            else:
                dsum[t, :] = dsum[t, :] + value
            return carry

        lax.fori_loop(0, 4, chunk, 0)

        def outer(c, carry):
            n = aligned(c, 128)
            grads[aligned(p, width), n] = dot_nn(cols_t[...], src[:, n]).astype(BF16)
            return carry

        lax.fori_loop(0, (qg + 2 * kg) // 128, outer, 0)

    middle()
    products(r, mine, True)
    first_near.wait()
    pass_far.start()
    first_far.wait()
    pass_near.start()
    second_near.wait()
    products(near, blocks.at[0], False)
    second_far.wait()
    products(far, blocks.at[1], False)
    pass_far.wait()
    pass_near.wait()
    products(diag, blocks.at[2], False)
    back = []
    for i, p in enumerate(peers):
        dsend[i] = dsum[aligned(p, tok), :].astype(BF16)
        copy = remote(dsend.at[i], drecv.at[i], bsend.at[i], brecv.at[i], (p, e))
        copy.start()
        back.append(copy)
    normal[:, aligned(r, width)] = dsum[aligned(r, tok), :]
    for i, p in enumerate(peers):
        back[i].wait()
        normal[:, aligned(p, width)] = drecv[i].astype(F32)
    finish()


def grad_qkv(mine, wq, wk, wv, cols_t, out_part):
    rows, group = mine.shape
    tok = rows // 4
    width = wq.shape[0]
    return pl.pallas_call(
        dgrad_kernel,
        out_shape=(
            jax.ShapeDtypeStruct((tok, 4 * width), F32),
            jax.ShapeDtypeStruct((4 * width, group), BF16),
            jax.ShapeDtypeStruct(out_part.shape[1:], F32),
        ),
        in_specs=[VMEM_SPEC] * 6,
        out_specs=(VMEM_SPEC,) * 3,
        scratch_shapes=[
            pltpu.VMEM((3, rows, group), BF16),
            pltpu.VMEM((rows, width), F32),
            pltpu.VMEM((3, tok, width), BF16),
            pltpu.VMEM((3, tok, width), BF16),
            pltpu.SemaphoreType.DMA((6,)),
            pltpu.SemaphoreType.DMA((6,)),
            pltpu.SemaphoreType.DMA((3,)),
            pltpu.SemaphoreType.DMA((3,)),
        ]
        + owner_scratch([out_part]),
        compiler_params=params(4),
        name="dqkv_exchange",
    )(mine, wq, wk, wv, cols_t, out_part)


def branch_kernel(mine, wo, attn, d_attn, grads, full, attn_t, ssem, rsem):
    r, e = lax.axis_index("dp"), lax.axis_index("expert")
    tok = mine.shape[0]
    half = tok // 2
    peers = [r ^ m for m in PEER_MASKS]
    near, far, diag = r ^ 1, r ^ 2, r ^ 3
    greet([(p, e) for p in peers])

    def part(q, which):
        return pl.ds(pl.multiple_of(q * tok + which * half, half), half)

    low, high = pl.ds(0, half), pl.ds(half, half)
    first_near = remote(mine.at[low], full.at[part(r, 0)], ssem.at[0], rsem.at[0], (near, e))
    first_far = remote(mine.at[high], full.at[part(r, 1)], ssem.at[1], rsem.at[1], (far, e))
    second_near = remote(mine.at[high], full.at[part(r, 1)], ssem.at[2], rsem.at[2], (near, e))
    second_far = remote(mine.at[low], full.at[part(r, 0)], ssem.at[3], rsem.at[3], (far, e))
    pass_far = remote(full.at[part(near, 0)], full.at[part(near, 0)], ssem.at[4], rsem.at[4], (far, e))
    pass_near = remote(full.at[part(far, 1)], full.at[part(far, 1)], ssem.at[5], rsem.at[5], (near, e))
    for copy in (first_near, first_far, second_near, second_far):
        copy.start()
    full[aligned(r, tok), :] = mine[...]
    attn_t[...] = attn[...].T
    heads = wo.shape[0]
    step = heads // 4

    def products(q):
        def chunk(c, carry):
            n = aligned(c, step)
            d_attn[aligned(q, tok), n] = dot_nt(full[aligned(q, tok), :], wo[n, :]).astype(BF16)
            return carry

        lax.fori_loop(0, 4, chunk, 0)

    products(r)
    first_near.wait()
    pass_far.start()
    first_far.wait()
    pass_near.start()
    second_near.wait()
    products(near)
    second_far.wait()
    products(far)
    pass_far.wait()
    pass_near.wait()
    products(diag)

    def outer(c, carry):
        n = aligned(c, 256)
        grads[:, n] = dot_nn(attn_t[...], full[:, n]).astype(BF16)
        return carry

    lax.fori_loop(0, mine.shape[1] // 256, outer, 0)


def grad_branch(mine, wo, attn):
    tok, width = mine.shape
    return pl.pallas_call(
        branch_kernel,
        out_shape=(
            jax.ShapeDtypeStruct((4 * tok, wo.shape[0]), BF16),
            jax.ShapeDtypeStruct((wo.shape[0], width), BF16),
        ),
        in_specs=[VMEM_SPEC] * 3,
        out_specs=(VMEM_SPEC, VMEM_SPEC),
        scratch_shapes=[
            pltpu.VMEM((4 * tok, width), BF16),
            pltpu.VMEM((wo.shape[0], 4 * tok), BF16),
            pltpu.SemaphoreType.DMA((6,)),
            pltpu.SemaphoreType.DMA((6,)),
        ],
        compiler_params=params(3),
        name="branch_exchange",
    )(mine, wo, attn)


def owner_order(n_z):
    order = list(range(1, n_z)) + [0]
    return order[1:2] + order[:1] + order[2:] if n_z > 2 else order


def owner_sum(arrays, outs, pair_in, send, recv, psend, precv, zsend, zrecv):
    r, e = lax.axis_index("dp"), lax.axis_index("expert")
    n_z = arrays[0].shape[0] // 2
    z, core = e // 2, e % 2
    targets = [lax.rem(z + j, n_z) for j in range(n_z)]
    order = owner_order(n_z)
    n_arrays = len(arrays)
    pair, moves = {}, []

    def begin():
        for j in order:
            for a in range(n_arrays):
                copy = remote(
                    arrays[a].at[targets[j] * 2 + (1 - core)], pair_in[a].at[j],
                    psend.at[a, j], precv.at[a, j], (r, e ^ 1),
                )
                copy.start()
                pair[a, j] = copy

    def middle():
        for j in order:
            for a in range(n_arrays):
                pair[a, j].wait()
                own = arrays[a][targets[j] * 2 + core].astype(F32) + pair_in[a][j].astype(F32)
                if j == 0:
                    outs[a][...] = own
                else:
                    send[a][j - 1] = own.astype(BF16)
                    copy = remote(
                        send[a].at[j - 1], recv[a].at[j - 1],
                        zsend.at[a, j - 1], zrecv.at[a, j - 1], (r, targets[j] * 2 + core),
                    )
                    copy.start()
                    moves.append(copy)

    def finish():
        for copy in moves:
            copy.wait()
        for a in range(n_arrays):
            value = outs[a][...]
            for j in range(n_z - 1):
                value = value + recv[a][j].astype(F32)
            outs[a][...] = value

    return begin, middle, finish


def owner_scratch(arrays):
    n_z = arrays[0].shape[0] // 2
    n = len(arrays)
    shapes = [a.shape[1:] for a in arrays]
    return (
        [pltpu.VMEM((n_z, *s), BF16) for s in shapes]
        + [pltpu.VMEM((n_z - 1, *s), BF16) for s in shapes]
        + [pltpu.VMEM((n_z - 1, *s), BF16) for s in shapes]
        + [pltpu.SemaphoreType.DMA((n, n_z))] * 2
        + [pltpu.SemaphoreType.DMA((n, n_z - 1))] * 2
    )


def owner_peers():
    r, e = lax.axis_index("dp"), lax.axis_index("expert")
    n_z = lax.axis_size("expert") // 2
    return [(r, lax.rem(e // 2 + j, n_z) * 2 + e % 2) for j in range(1, n_z)]


def last_sums_kernel(grads, small, grads_out, small_out, *scratch):
    r, e = lax.axis_index("dp"), lax.axis_index("expert")
    z, core = e // 2, e % 2
    n_z = grads.shape[0] // 2
    pair_in, send, recv, psend, precv, zsend, zrecv = scratch[:7]
    first_in, piece, line_in, s1, r1, s2, r2, s3, r3 = scratch[7:]
    begin, middle, finish = owner_sum(
        [grads], [grads_out], [pair_in], [send], [recv], psend, precv, zsend, zrecv
    )
    others = [(m // 2, m % 2) for m in range(1, 8)]
    plane = [(r ^ a, e ^ c) for a, c in others]
    greet(plane + owner_peers())
    begin()
    firsts = []
    for i, (a, c) in enumerate(others):
        copy = remote(
            small.at[(r ^ a) * 2 + (core ^ c)], first_in.at[i], s1.at[i], r1.at[i], plane[i]
        )
        copy.start()
        firsts.append(copy)
    middle()
    for copy in firsts:
        copy.wait()
    mine = r * 2 + core
    value = small[mine]
    for i in range(7):
        value = value + first_in[i]
    piece[0] = value
    seconds = []
    for j in range(1, n_z):
        copy = remote(
            piece.at[0], line_in.at[j - 1], s2.at[j - 1], r2.at[j - 1], owner_peers()[j - 1]
        )
        copy.start()
        seconds.append(copy)
    for copy in seconds:
        copy.wait()
    value = piece[0]
    for j in range(n_z - 1):
        value = value + line_in[j]
    small_out[mine] = value
    thirds = []
    for i, (a, c) in enumerate(others):
        copy = remote(small_out.at[mine], small_out.at[mine], s3.at[i], r3.at[i], plane[i])
        copy.start()
        thirds.append(copy)
    finish()
    for copy in thirds:
        copy.wait()


def last_sums(grads, small):
    n_z = grads.shape[0] // 2
    piece = small.shape[1:]
    return pl.pallas_call(
        last_sums_kernel,
        out_shape=(
            jax.ShapeDtypeStruct(grads.shape[1:], F32),
            jax.ShapeDtypeStruct(small.shape, F32),
        ),
        in_specs=[VMEM_SPEC] * 2,
        out_specs=(VMEM_SPEC,) * 2,
        scratch_shapes=owner_scratch([grads])
        + [
            pltpu.VMEM((7, *piece), F32),
            pltpu.VMEM((1, *piece), F32),
            pltpu.VMEM((n_z - 1, *piece), F32),
            pltpu.SemaphoreType.DMA((7,)),
            pltpu.SemaphoreType.DMA((7,)),
            pltpu.SemaphoreType.DMA((n_z - 1,)),
            pltpu.SemaphoreType.DMA((n_z - 1,)),
            pltpu.SemaphoreType.DMA((7,)),
            pltpu.SemaphoreType.DMA((7,)),
        ],
        compiler_params=params(5),
        name="last_sums",
    )(grads, small)


def line_sum(block, out, pair_in, work, lines, ps, pr, zs, zr):
    r, e = lax.axis_index("dp"), lax.axis_index("expert")
    z, core = e // 2, e % 2
    order = plane_order(z)[::-1]
    right = jnp.minimum(z + 1, 3) * 2 + core
    left = jnp.maximum(z - 1, 0) * 2 + core
    pairs, moves = [], []

    def begin():
        for k in range(4):
            copy = remote(
                block(order[k] * 2 + (1 - core)), pair_in.at[k], ps.at[k], pr.at[k], (r, e ^ 1)
            )
            copy.start()
            pairs.append(copy)

    def move(k, side, cond, to, add):
        b = order[k]
        copy = remote(work.at[k], lines.at[side, b], zs.at[side, k], zr.at[side, b], (r, to))
        moves.append((cond, copy))

        @pl.when(cond)
        def _():
            if add:
                copy.wait_recv()
                value = work[k].astype(F32) + lines[side, b].astype(F32)
                work[k] = value.astype(BF16)
            copy.start()

    def first():
        for k in range(4):
            pairs[k].wait_recv()
            value = block(order[k] * 2 + core)[...].astype(F32) + pair_in[k].astype(F32)
            if k == 3:
                out[...] = value
            else:
                work[k] = value.astype(BF16)
        ends(0)

    def ends(k):
        move(k, 0, z == 0, right, False)
        move(k, 1, z == 3, left, False)

    def inner(k):
        inside = (z > 0) & (z < 3)
        move(k, 0, inside & (order[k] > z), right, True)
        move(k, 1, inside & (order[k] < z), left, True)
        if k < 2:
            ends(k + 1)

    def last():
        for side, cond in ((0, z > 0), (1, z < 3)):

            @pl.when(cond)
            def _():
                at = lines.at[side, z]
                remote(at, at, zs.at[side, 3], zr.at[side, z], (r, e ^ 1)).wait_recv()
                out[...] = out[...] + lines[side, z].astype(F32)

        for copy in pairs:
            copy.wait_send()
        for cond, copy in moves:

            @pl.when(cond)
            def _():
                copy.wait_send()

    return begin, first, inner, last


LINE_SEMS = [
    pltpu.SemaphoreType.DMA((4,)),
    pltpu.SemaphoreType.DMA((4,)),
    pltpu.SemaphoreType.DMA((2, 4)),
    pltpu.SemaphoreType.DMA((2, 4)),
]


def dgrad_line_kernel(
    mine, wq, wk, wv, cols_t, out_part, small, unit_rows, normal, qkv_sum, out_sum, small_out,
    grads, blocks, dsum, dsend, drecv, opair, owork, olines, qpair, qwork, qlines,
    small_v, first_in, piece, line_in, ssem, rsem, bsend, brecv, s1, r1, s2, r2, s3, r3, *sems,
):
    r, e = lax.axis_index("dp"), lax.axis_index("expert")
    z, core = e // 2, e % 2
    rows = mine.shape[0]
    tok = rows // 4
    half = rows // 2
    qg = wq.shape[1] // 4
    kg = wk.shape[1] // 4
    width = wq.shape[0]
    share = width // 8
    peers = [r ^ m for m in PEER_MASKS]
    near, far, diag = r ^ 1, r ^ 2, r ^ 3
    order = (r, near, far, diag)
    out_begin, out_first, out_inner, out_last = line_sum(
        lambda o: out_part.at[o], out_sum, opair, owork, olines, *sems[:4]
    )
    units = [
        line_sum(
            lambda o, p=p: grads.at[o, p], qkv_sum.at[p], qpair.at[i], qwork.at[i], qlines.at[i],
            *(sem.at[i] for sem in sems[4:]),
        )
        for i, p in enumerate(order)
    ]
    line_peers = [(r, lax.rem(z + j, 4) * 2 + core) for j in (1, 2, 3)]
    others = [(m // 2, m % 2) for m in (6, 7, 2, 3, 4, 5, 1)]
    plane = [(r ^ a, e ^ c) for a, c in others]
    greet(plane + line_peers)
    low, high = pl.ds(0, half), pl.ds(half, half)
    first_near = remote(mine.at[low], blocks.at[0, low], ssem.at[0], rsem.at[0], (near, e))
    first_far = remote(mine.at[high], blocks.at[1, high], ssem.at[1], rsem.at[1], (far, e))
    second_near = remote(mine.at[high], blocks.at[0, high], ssem.at[2], rsem.at[2], (near, e))
    second_far = remote(mine.at[low], blocks.at[1, low], ssem.at[3], rsem.at[3], (far, e))
    pass_far = remote(blocks.at[0, low], blocks.at[2, low], ssem.at[4], rsem.at[4], (far, e))
    pass_near = remote(blocks.at[1, high], blocks.at[2, high], ssem.at[5], rsem.at[5], (near, e))
    for copy in (first_near, first_far, second_near, second_far):
        copy.start()
    out_begin()

    def outer(p, src):
        def step(c, carry):
            n = aligned(c, 256)
            value = dot_nn(cols_t[...], src[:, n]).astype(BF16)
            for o in range(8):
                grads[o, p, :, n] = value[o * share : (o + 1) * share]
            return carry

        lax.fori_loop(0, (qg + 2 * kg) // 256, step, 0)

    def inner(p, src, start):
        def chunk(c, carry):
            t = aligned(c, tok)
            x = src[t, :]
            value = (
                dot_nt(x[:, :qg], wq[:, aligned(p, qg)])
                + dot_nt(x[:, qg : qg + kg], wk[:, aligned(p, kg)])
                + dot_nt(x[:, qg + kg :], wv[:, aligned(p, kg)])
            )
            if start:
                dsum[t, :] = value
            else:
                dsum[t, :] = dsum[t, :] + value
            return carry

        lax.fori_loop(0, 4, chunk, 0)

    def begin(i):
        units[i][0]()

    def first(i):
        units[i][1]()

    def onward(i, k):
        units[i][2](k)

    outer(r, mine)
    begin(0)
    out_first()
    inner(r, mine, True)
    first_near.wait()
    pass_far.start()
    first_far.wait()
    pass_near.start()
    out_inner(0)
    first(0)
    out_inner(1)
    onward(0, 0)
    second_near.wait()
    outer(near, blocks.at[0])
    begin(1)
    second_far.wait()
    outer(far, blocks.at[1])
    begin(2)
    out_inner(2)
    onward(0, 1)
    first(1)
    inner(near, blocks.at[0], False)
    onward(0, 2)
    onward(1, 0)
    first(2)
    inner(far, blocks.at[1], False)
    onward(1, 1)
    pass_far.wait()
    pass_near.wait()
    outer(diag, blocks.at[2])
    begin(3)
    inner(diag, blocks.at[2], False)
    back = []
    for i, p in enumerate(peers):
        dsend[i] = dsum[aligned(p, tok), :].astype(BF16)
        copy = remote(dsend.at[i], drecv.at[i], bsend.at[i], brecv.at[i], (p, e))
        copy.start()
        back.append(copy)
    onward(1, 2)
    onward(2, 0)
    first(3)
    onward(2, 1)
    onward(3, 0)
    normal[:, aligned(r, width)] = dsum[aligned(r, tok), :]
    for i, p in enumerate(peers):
        back[i].wait()
        normal[:, aligned(p, width)] = drecv[i].astype(F32)
    at_small = small.shape[1]
    small_v[:, :at_small] = small[...]
    small_v[:, at_small:] = jnp.zeros((8, 8, 128), F32)
    per = 4 * width // 8
    for i in range(8):
        n = slice(i * per, (i + 1) * per)
        gain = jnp.sum(normal[:, n] * unit_rows[:, n], axis=0, keepdims=True)
        for c in range(per // 128):
            small_v[i, at_small + c : at_small + c + 1] = gain[:, c * 128 : (c + 1) * 128]
    firsts = []
    for i, (a, c) in enumerate(others):
        copy = remote(
            small_v.at[(r ^ a) * 2 + (core ^ c)], first_in.at[i], s1.at[i], r1.at[i], plane[i]
        )
        copy.start()
        firsts.append(copy)
    onward(2, 2)
    onward(3, 1)
    for copy in firsts:
        copy.wait()
    me = r * 2 + core
    value = small_v[me]
    for i in range(7):
        value = value + first_in[i]
    piece[0] = value
    seconds = []
    for j in range(3):
        copy = remote(piece.at[0], line_in.at[j], s2.at[j], r2.at[j], line_peers[j])
        copy.start()
        seconds.append(copy)
    onward(3, 2)
    for copy in seconds:
        copy.wait()
    small_out[me] = piece[0] + line_in[0] + line_in[1] + line_in[2]
    thirds = []
    for i in range(7):
        copy = remote(small_out.at[me], small_out.at[me], s3.at[i], r3.at[i], plane[i])
        copy.start()
        thirds.append(copy)
    out_last()
    for unit in units:
        unit[3]()
    for copy in thirds:
        copy.wait()


def grad_qkv_line(mine, wq, wk, wv, cols_t, out_part, small, unit_rows):
    rows, group = mine.shape
    tok = rows // 4
    width = wq.shape[0]
    piece = (width // 8, group)
    out_piece = out_part.shape[1:]
    small_shape = (8, small.shape[1] + 8, 128)
    return pl.pallas_call(
        dgrad_line_kernel,
        out_shape=(
            jax.ShapeDtypeStruct((tok, 4 * width), F32),
            jax.ShapeDtypeStruct((4, *piece), F32),
            jax.ShapeDtypeStruct(out_piece, F32),
            jax.ShapeDtypeStruct(small_shape, F32),
        ),
        in_specs=[VMEM_SPEC] * 8,
        out_specs=(VMEM_SPEC,) * 4,
        scratch_shapes=[
            pltpu.VMEM((8, 4, *piece), BF16),
            pltpu.VMEM((3, rows, group), BF16),
            pltpu.VMEM((rows, width), F32),
            pltpu.VMEM((3, tok, width), BF16),
            pltpu.VMEM((3, tok, width), BF16),
            pltpu.VMEM((4, *out_piece), BF16),
            pltpu.VMEM((3, *out_piece), BF16),
            pltpu.VMEM((2, 4, *out_piece), BF16),
            pltpu.VMEM((4, 4, *piece), BF16),
            pltpu.VMEM((4, 3, *piece), BF16),
            pltpu.VMEM((4, 2, 4, *piece), BF16),
            pltpu.VMEM(small_shape, F32),
            pltpu.VMEM((7, *small_shape[1:]), F32),
            pltpu.VMEM((1, *small_shape[1:]), F32),
            pltpu.VMEM((3, *small_shape[1:]), F32),
            pltpu.SemaphoreType.DMA((6,)),
            pltpu.SemaphoreType.DMA((6,)),
        ]
        + [pltpu.SemaphoreType.DMA((n,)) for n in (3, 3, 7, 7, 3, 3, 7, 7)]
        + LINE_SEMS
        + [
            pltpu.SemaphoreType.DMA((4, 4)),
            pltpu.SemaphoreType.DMA((4, 4)),
            pltpu.SemaphoreType.DMA((4, 2, 4)),
            pltpu.SemaphoreType.DMA((4, 2, 4)),
        ],
        compiler_params=params(10),
        name="dqkv_line_exchange",
    )(mine, wq, wk, wv, cols_t, out_part, small, unit_rows)


def masks_of(block, own_length, slots, prompt_block, prompt_len, column, keys):
    slot = lax.broadcasted_iota(jnp.int32, (slots, keys), 0)
    key = lax.broadcasted_iota(jnp.int32, (slots, keys), 1)
    is_prompt = slot < prompt_block
    position = (column * 4 + block) * prompt_block + slot
    sees_prompt = (key < prompt_len) & (jnp.logical_not(is_prompt) | (key <= position))
    cont = key - prompt_len
    sees_cont = (
        (key >= prompt_len)
        & jnp.logical_not(is_prompt)
        & (cont <= slot - prompt_block)
        & (cont < own_length)
    )
    return sees_prompt | sees_cont


def attention_fwd_kernel(prompt_len, lengths, lin, gain, cos, sin, keys, values, queries, attn):
    block = pl.program_id(0)
    slots = lin.shape[0]
    head = gain.shape[1]
    allowed = masks_of(
        block, lengths[block], slots, slots - CMAX, prompt_len, lengths[4], keys.shape[1]
    )
    scale = head ** (-0.5)
    k, v = keys[0], values[0]
    c, s, g = cos[0], sin[0], gain[...]
    for h in range(lin.shape[1] // head):
        part = slice(h * head, (h + 1) * head)
        x = lin[:, part]
        x = x * lax.rsqrt(jnp.mean(x * x, axis=-1, keepdims=True) + norm_eps) * g
        q = (x * c + pltpu.roll(x, head // 2, 1) * s).astype(BF16)
        queries[:, part] = q
        score = jnp.where(allowed, dot_nt(q, k) * scale, -jnp.inf)
        peak = jnp.max(score, axis=-1, keepdims=True)
        exponent = jnp.exp(score - peak)
        low = (exponent * (1.0 / jnp.sum(exponent, axis=-1, keepdims=True))).astype(BF16)
        attn[:, part] = dot_nn(low, v).astype(BF16)


def attention_fwd(lengths, lin, gain, cos, sin, keys, values, prompt_len):
    blocks, total_keys, head = keys.shape
    slots = lin.shape[0] // blocks
    width = lin.shape[1] - 2 * head
    row = pl.BlockSpec((slots, width), lambda i, *_: (i, 0))
    table = pl.BlockSpec((1, slots, head), lambda i, *_: (i, 0, 0))
    kv = pl.BlockSpec((1, total_keys, head), lambda i, *_: (i, 0, 0))
    one = pl.BlockSpec((1, head), lambda i, *_: (0, 0))
    return pl.pallas_call(
        functools.partial(attention_fwd_kernel, prompt_len),
        grid_spec=pltpu.PrefetchScalarGridSpec(
            num_scalar_prefetch=1,
            grid=(blocks,),
            in_specs=[row, one, table, table, kv, kv],
            out_specs=[row, row],
        ),
        out_shape=(
            jax.ShapeDtypeStruct((lin.shape[0], width), BF16),
            jax.ShapeDtypeStruct((lin.shape[0], width), BF16),
        ),
        compiler_params=params(),
        name="attention_fwd",
    )(lengths, lin, gain, cos, sin, keys, values)


def attention_bwd_kernel(
    prompt_len, lengths, lin, queries, d_attn, gain, cos, sin, keys, values, d_lin, d_keys, d_values, d_gain
):
    block = pl.program_id(0)
    slots = lin.shape[0]
    head = gain.shape[1]
    allowed = masks_of(
        block, lengths[block], slots, slots - CMAX, prompt_len, lengths[4], keys.shape[1]
    )
    scale = head ** (-0.5)
    k, v = keys[0], values[0]
    c, s, g = cos[0], sin[0], gain[...]
    key_total = jnp.zeros(k.shape, F32)
    value_total = jnp.zeros(v.shape, F32)
    gain_total = jnp.zeros((8, head), F32)
    for h in range(lin.shape[1] // head):
        part = slice(h * head, (h + 1) * head)
        q = queries[:, part]
        score = jnp.where(allowed, dot_nt(q, k) * scale, -jnp.inf)
        peak = jnp.max(score, axis=-1, keepdims=True)
        exponent = jnp.exp(score - peak)
        probs = exponent * (1.0 / jnp.sum(exponent, axis=-1, keepdims=True))
        d_out = d_attn[:, part]
        d_probs = dot_nt(d_out, v)
        inner = jnp.sum(probs * d_probs, axis=-1, keepdims=True)
        d_score = (probs * (d_probs - inner)).astype(BF16)
        key_total = key_total + dot_tn(d_score, q)
        value_total = value_total + dot_tn(probs.astype(BF16), d_out)
        d_q = dot_nn(d_score, k) * scale
        turned = d_q * c + pltpu.roll(d_q * s, head // 2, 1)
        x = lin[:, part]
        inverse = lax.rsqrt(jnp.mean(x * x, axis=-1, keepdims=True) + norm_eps)
        unit = x * inverse
        pairs = turned * unit
        for j in range(slots // 8):
            gain_total = gain_total + pairs[j * 8 : (j + 1) * 8]
        weighted = turned * g
        d_lin[:, part] = (
            inverse * (weighted - unit * jnp.mean(weighted * unit, axis=-1, keepdims=True))
        ).astype(BF16)
    d_keys[0] = key_total * scale
    d_values[0] = value_total
    d_gain[0] = gain_total


def attention_bwd(lengths, lin, queries, d_attn, gain, cos, sin, keys, values, prompt_len):
    blocks, total_keys, head = keys.shape
    slots = lin.shape[0] // blocks
    width = lin.shape[1] - 2 * head
    row = pl.BlockSpec((slots, width), lambda i, *_: (i, 0))
    table = pl.BlockSpec((1, slots, head), lambda i, *_: (i, 0, 0))
    kv = pl.BlockSpec((1, total_keys, head), lambda i, *_: (i, 0, 0))
    one = pl.BlockSpec((1, head), lambda i, *_: (0, 0))
    return pl.pallas_call(
        functools.partial(attention_bwd_kernel, prompt_len),
        grid_spec=pltpu.PrefetchScalarGridSpec(
            num_scalar_prefetch=1,
            grid=(blocks,),
            in_specs=[row, row, row, one, table, table, kv, kv],
            out_specs=[row, kv, kv, pl.BlockSpec((1, 8, head), lambda i, *_: (i, 0, 0))],
        ),
        out_shape=(
            jax.ShapeDtypeStruct((lin.shape[0], width), BF16),
            jax.ShapeDtypeStruct(keys.shape, F32),
            jax.ShapeDtypeStruct(values.shape, F32),
            jax.ShapeDtypeStruct((blocks, 8, head), F32),
        ),
        compiler_params=params(),
        name="attention_bwd",
    )(lengths, lin, queries, d_attn, gain, cos, sin, keys, values)


def partner(shard, axis, bit):
    return lax.ppermute(shard, axis, [(i, i ^ 1 << bit) for i in range(lax.axis_size(axis))])


def root_mean_scale(value_rows, gain_vec):
    return (
        value_rows
        * lax.rsqrt(jnp.mean(value_rows * value_rows, axis=-1, keepdims=True) + norm_eps)
        * gain_vec
    )


def contract(left_side, right_side, left_dim, right_dim):
    return lax.dot_general(
        left_side,
        right_side,
        (((left_dim,), (right_dim,)), ((), ())),
        preferred_element_type=F32,
    )


def plane_order(z):
    upper, odd = z // 2, z % 2
    return [z, z + 1 - 2 * upper, 2 + upper - 2 * odd, 3 - 3 * upper]


def world(with_diag):
    r, e = lax.axis_index("dp"), lax.axis_index("expert")
    z, core = e // 2, e % 2
    near, far = r ^ 1, r ^ 2
    devices = [(near, e), (far, e), (r, e ^ 1)]
    devices += [(r, lax.rem(z + j, 4) * 2 + core) for j in (1, 2, 3)]
    return r, e, z, core, near, far, devices


def gather_world(mine, buf, zs, zr, ps, pr, ds, dr, before, group, done):
    r, e, z, core, near, far, greeted = world(True)
    half = mine.shape[0] // 2
    low, high = pl.ds(0, half), pl.ds(half, half)
    order = plane_order(z)
    greet(greeted)

    def slot(q, b, c):
        return q * 8 + b * 2 + c

    buf[slot(r, z, core)] = mine[...]
    diag = r ^ 3
    plane, pairs, lines = {}, {}, []

    def hand(k, i, q):
        at = slot(q, order[k], core)
        copy = remote(buf.at[at], buf.at[at], ds.at[k, i], dr.at[k, i], (r, e ^ 1))
        copy.start()
        pairs[k, i] = copy

    def issue(k):
        b = order[k]
        at = slot(r, b, core)
        for side, cond, to in (
            (0, (b <= z) & (z < 3), jnp.minimum(z + 1, 3)),
            (1, (b >= z) & (z > 0), jnp.maximum(z - 1, 0)),
        ):
            copy = remote(buf.at[at], buf.at[at], zs.at[k, side], zr.at[b], (r, to * 2 + core))
            lines.append((cond, copy))

            @pl.when(cond)
            def _():
                copy.start()

        mine_at, near_at, far_at = at, slot(near, b, core), slot(far, b, core)
        for i, (src, part, p) in enumerate(
            (
                (mine_at, low, near),
                (mine_at, high, far),
                (mine_at, high, near),
                (mine_at, low, far),
                (near_at, low, far),
                (far_at, high, near),
            )
        ):
            plane[k, i] = remote(
                buf.at[src, part], buf.at[src, part], ps.at[k, i], pr.at[k, i], (p, e)
            )
        for i in range(4):
            plane[k, i].start()
        hand(k, 0, r)

    def line_wait(k):
        b = order[k]
        at = slot(r, b, core)
        remote(buf.at[at], buf.at[at], zs.at[k, 0], zr.at[b], (r, e ^ 1)).wait_recv()
        issue(k)

    def passes(k):
        plane[k, 0].wait_recv()
        plane[k, 4].start()
        plane[k, 1].wait_recv()
        plane[k, 5].start()

    def finish(k):
        plane[k, 2].wait_recv()
        hand(k, 1, near)
        plane[k, 3].wait_recv()
        hand(k, 2, far)

    def corner(k):
        plane[k, 4].wait_recv()
        plane[k, 5].wait_recv()
        hand(k, 3, diag)

    def ready(k):
        before(k)
        for i in range(4):
            pairs[k, i].wait_recv()
        group(k, order[k])

    issue(0)
    passes(0)
    line_wait(1)
    finish(0)
    passes(1)
    line_wait(2)
    corner(0)
    finish(1)
    ready(0)
    passes(2)
    line_wait(3)
    corner(1)
    finish(2)
    ready(1)
    passes(3)
    corner(2)
    finish(3)
    ready(2)
    corner(3)
    ready(3)
    done()
    for copy in plane.values():
        copy.wait_send()
    for copy in pairs.values():
        copy.wait_send()
    for cond, copy in lines:

        @pl.when(cond)
        def _():
            copy.wait_send()


GATHER_SEMS = [
    pltpu.SemaphoreType.DMA((4, 2)),
    pltpu.SemaphoreType.DMA((4,)),
    pltpu.SemaphoreType.DMA((4, 6)),
    pltpu.SemaphoreType.DMA((4, 6)),
    pltpu.SemaphoreType.DMA((4, 4)),
    pltpu.SemaphoreType.DMA((4, 4)),
]


def selector(pos, source, room):
    row = pos[source]
    ids = lax.broadcasted_iota(jnp.int32, (room, row.shape[1]), 0).astype(F32)
    return jnp.where(ids == row, 1.0, 0.0).astype(BF16)


def start_all(copies):
    for copy in copies:
        copy.start()
    return copies


def wait_all(copies):
    for copy in copies:
        copy.wait()
    copies.clear()


def experts_fwd_kernel(
    mine, wg, wu, wd, pos, x_out, y_out, g_out, u_out, o_out, hid_out, gate_out,
    buf, wg_v, wu_v, wd_v, x_v, y_v, g_v, u_v, o_v, hid_v, gate_v, local, *sems,
):
    model = wg.shape[0]
    rows_in = mine.shape[0]
    room = x_v.shape[0] // 8
    me = lax.axis_index("dp") * 8 + lax.axis_index("expert")
    loads = start_all(
        [
            pltpu.make_async_copy(a, b, local.at[i])
            for i, (a, b) in enumerate(((wg, wg_v), (wu, wu_v), (wd, wd_v)))
        ]
    )
    leaving = []

    def leave(b, pairs):
        leaving.extend(
            start_all([pltpu.make_async_copy(v, o.at[b], local.at[i]) for i, v, o in pairs])
        )

    def before(k):
        wait_all(loads)

    upto = jnp.where(
        lax.broadcasted_iota(jnp.int32, (rows_in, rows_in), 0)
        <= lax.broadcasted_iota(jnp.int32, (rows_in, rows_in), 1),
        1.0,
        0.0,
    ).astype(BF16)
    is_me = jnp.where(lax.broadcasted_iota(jnp.int32, (16, 128), 1) == me, 1.0, 0.0).astype(BF16)

    def pick_one(b, j):
        s = j // 2 * 8 + b * 2 + j % 2
        rows = aligned(j, room)
        named = jnp.where(dot_nt(is_me, buf[s, :, model:]) > 0.0, 1.0, 0.0)
        place = dot_nn(named.astype(BF16), upto) * named - 1.0
        pos[s] = place[:1]
        ids = lax.broadcasted_iota(jnp.int32, (room, rows_in), 0).astype(F32)
        sel = jnp.where(ids == place[:1], 1.0, 0.0).astype(BF16)
        for c in range(4):
            n = slice(c * model // 4, (c + 1) * model // 4)
            x_v[rows, n] = dot_nn(sel, buf[s, :, n]).astype(BF16)
        extra = dot_nn(sel, buf[s, :, model:])
        lane = lax.broadcasted_iota(jnp.int32, extra.shape, 1)
        hit = (lane == me) | (lane == me + 64)
        gate = jnp.sum(jnp.where(hit, extra, 0.0), axis=-1, keepdims=True)
        gate_v[rows, :] = jnp.broadcast_to(gate, extra.shape)

    def group(k, b):
        wait_all(leaving)

        def four(j, carry):
            for i in range(4):
                pick_one(b, j * 4 + i)
            return carry

        lax.fori_loop(0, 2, four, 0)
        leave(b, ((0, x_v, x_out), (1, gate_v, gate_out)))

        def first(c, carry):
            n = aligned(c, 256)
            g = dot_nn(x_v[...], wg_v[:, n])
            u = dot_nn(x_v[...], wu_v[:, n])
            g_v[:, n] = g.astype(BF16)
            u_v[:, n] = u.astype(BF16)
            hid_v[:, n] = (g / (1.0 + jnp.exp(-g)) * u).astype(BF16)
            return carry

        lax.fori_loop(0, wg.shape[1] // 256, first, 0)
        leave(b, ((2, g_v, g_out), (3, u_v, u_out), (4, hid_v, hid_out)))

        def second(c, carry):
            n = aligned(c, 256)
            o = dot_nn(hid_v[...], wd_v[:, n]).astype(BF16)
            o_v[:, n] = o
            y_v[:, n] = (o.astype(F32) * gate_v[:, :1]).astype(BF16)
            return carry

        lax.fori_loop(0, model // 256, second, 0)
        leave(b, ((5, o_v, o_out), (6, y_v, y_out)))

    gather_world(mine, buf, *sems, before, group, lambda: wait_all(leaving))


def experts_fwd(mine, wg, wu, wd, room):
    rows, width = mine.shape
    model, ff = wg.shape
    group = 8 * room
    wide = jax.ShapeDtypeStruct((4, group, model), BF16)
    thin = jax.ShapeDtypeStruct((4, group, ff), BF16)
    pos, x, y, g, u, o, hidden, gates = pl.pallas_call(
        experts_fwd_kernel,
        out_shape=(
            jax.ShapeDtypeStruct((32, 1, rows), F32),
            wide,
            wide,
            thin,
            thin,
            wide,
            thin,
            jax.ShapeDtypeStruct((4, group, 128), F32),
        ),
        in_specs=[VMEM_SPEC, ANY_SPEC, ANY_SPEC, ANY_SPEC],
        out_specs=(VMEM_SPEC,) + (ANY_SPEC,) * 7,
        scratch_shapes=[
            pltpu.VMEM((32, rows, width), BF16),
            pltpu.VMEM((model, ff), BF16),
            pltpu.VMEM((model, ff), BF16),
            pltpu.VMEM((ff, model), BF16),
            pltpu.VMEM((group, model), BF16),
            pltpu.VMEM((group, model), BF16),
            pltpu.VMEM((group, ff), BF16),
            pltpu.VMEM((group, ff), BF16),
            pltpu.VMEM((group, model), BF16),
            pltpu.VMEM((group, ff), BF16),
            pltpu.VMEM((group, 128), F32),
            pltpu.SemaphoreType.DMA((7,)),
        ]
        + GATHER_SEMS,
        compiler_params=params(6),
        name="experts_fwd",
    )(mine, wg, wu, wd)
    return pos, x, y, (g, u, o, hidden, gates)


def experts_bwd_kernel(
    mine, pos, g_in, u_in, o_in, gate_in, wg, wu, wd, y_out, d_copy_out, dg_out, du_out,
    buf, wg_v, wu_v, wd_v, g_v, u_v, o_v, gate_v, y_v, d_copy_v, dg_v, du_v,
    local, ins, *sems,
):
    model, ff = wg.shape
    room = d_copy_v.shape[0] // 8
    z = lax.axis_index("expert") // 2
    me = lax.axis_index("dp") * 8 + lax.axis_index("expert")
    loads = start_all(
        [
            pltpu.make_async_copy(a, b, local.at[i])
            for i, (a, b) in enumerate(((wg, wg_v), (wu, wu_v), (wd, wd_v)))
        ]
    )
    leaving, coming = [], {}

    def fetch(k):
        b = plane_order(z)[k]
        at = k % 2
        coming[k] = start_all(
            [
                pltpu.make_async_copy(a.at[b], v.at[at], ins.at[at, i])
                for i, (a, v) in enumerate(
                    ((g_in, g_v), (u_in, u_v), (o_in, o_v), (gate_in, gate_v))
                )
            ]
        )

    fetch(0)

    def leave(b, pairs):
        leaving.extend(
            start_all([pltpu.make_async_copy(v, o.at[b], local.at[i]) for i, v, o in pairs])
        )

    def before(k):
        wait_all(loads)
        wait_all(coming[k])
        if k < 3:
            fetch(k + 1)

    def pick_one(b, j, at):
        s = j // 2 * 8 + b * 2 + j % 2
        rows = aligned(j, room)
        sel = selector(pos, s, room)
        gate = gate_v[at, rows, :1]
        inner = jnp.zeros((room, 1), F32)
        for c in range(4):
            n = slice(c * model // 4, (c + 1) * model // 4)
            picked = dot_nn(sel, buf[s, :, n])
            d_copy_v[rows, n] = (gate * picked).astype(BF16)
            inner = inner + jnp.sum(picked * o_v[at, rows, n].astype(F32), axis=-1, keepdims=True)
        top = inner.astype(BF16).astype(F32)
        rest = inner - top
        lane = lax.broadcasted_iota(jnp.int32, (room, 128), 1)
        extra = jnp.where(lane == me, top, 0.0) + jnp.where(lane == me + 64, rest, 0.0)
        y_v[rows, model:] = extra.astype(BF16)

    def group(k, b):
        at = k % 2
        wait_all(leaving)

        def four(j, carry):
            for i in range(4):
                pick_one(b, j * 4 + i, at)
            return carry

        lax.fori_loop(0, 2, four, 0)
        leave(b, ((0, d_copy_v, d_copy_out),))

        def third(c, carry):
            n = aligned(c, 256)
            d_hidden = dot_nt(d_copy_v[...], wd_v[n, :])
            g, u = g_v[at, :, n].astype(F32), u_v[at, :, n].astype(F32)
            s = 1.0 / (1.0 + jnp.exp(-g))
            dg_v[:, n] = (d_hidden * u * s * (1.0 + g * (1.0 - s))).astype(BF16)
            du_v[:, n] = (d_hidden * g * s).astype(BF16)
            return carry

        lax.fori_loop(0, ff // 256, third, 0)
        leave(b, ((1, dg_v, dg_out), (2, du_v, du_out)))

        def fourth(c, carry):
            n = aligned(c, 256)
            y_v[:, n] = (
                dot_nt(dg_v[...], wg_v[n, :]) + dot_nt(du_v[...], wu_v[n, :])
            ).astype(BF16)
            return carry

        lax.fori_loop(0, model // 256, fourth, 0)
        leave(b, ((3, y_v, y_out),))

    gather_world(mine, buf, *sems, before, group, lambda: wait_all(leaving))


def experts_bwd(mine, pos, kept, wg, wu, wd, room):
    rows, width = mine.shape
    model, ff = wg.shape
    group = 8 * room
    return pl.pallas_call(
        experts_bwd_kernel,
        out_shape=(
            jax.ShapeDtypeStruct((4, group, model + 128), BF16),
            jax.ShapeDtypeStruct((4, group, model), BF16),
            jax.ShapeDtypeStruct((4, group, ff), BF16),
            jax.ShapeDtypeStruct((4, group, ff), BF16),
        ),
        in_specs=[VMEM_SPEC, VMEM_SPEC] + [ANY_SPEC] * 7,
        out_specs=(ANY_SPEC,) * 4,
        scratch_shapes=[
            pltpu.VMEM((32, rows, width), BF16),
            pltpu.VMEM((model, ff), BF16),
            pltpu.VMEM((model, ff), BF16),
            pltpu.VMEM((ff, model), BF16),
            pltpu.VMEM((2, group, ff), BF16),
            pltpu.VMEM((2, group, ff), BF16),
            pltpu.VMEM((2, group, model), BF16),
            pltpu.VMEM((2, group, 128), F32),
            pltpu.VMEM((group, model + 128), BF16),
            pltpu.VMEM((group, model), BF16),
            pltpu.VMEM((group, ff), BF16),
            pltpu.VMEM((group, ff), BF16),
            pltpu.SemaphoreType.DMA((4,)),
            pltpu.SemaphoreType.DMA((2, 4)),
        ]
        + GATHER_SEMS,
        compiler_params=params(7),
        name="experts_bwd",
    )(mine, pos, *kept, wg, wu, wd)


def sum_world_kernel(
    y, pos, out, psend, pair, half_near, half_far, full_near, full_far, lines,
    ds, dr, hs, hr, fs, fr, zs, zr,
):
    r, e, z, core, near, far, greeted = world(True)
    rows, width = out.shape
    room = y.shape[2]
    half = rows // 2
    low, high = pl.ds(0, half), pl.ds(half, half)
    order = plane_order(z)[::-1]
    diag = r ^ 3
    who = [r, near, far, diag]
    body_width = width // 512 * 512
    greet(greeted)

    def for_columns(fn):
        def step(c, carry):
            fn(aligned(c, 512))
            return carry

        lax.fori_loop(0, body_width // 512, step, 0)
        if width > body_width:
            fn(pl.ds(body_width, width - body_width))

    def scattered(sel, q, b, c, n):
        return dot_tn(sel, y[b, q * 2 + c, :, n])

    pairs, halves, fulls, moves = {}, {}, {}, []

    def stage_a(k):
        b = order[k]
        for i in (3, 1, 2, 0):
            at = k * 4 + i
            sel = selector(pos, who[i] * 8 + b * 2 + (1 - core), room)

            def fill(n):
                psend[at, :, n] = scattered(sel, who[i], b, 1 - core, n).astype(BF16)

            for_columns(fill)
            copy = remote(psend.at[at], pair.at[at], ds.at[at], dr.at[at], (r, e ^ 1))
            copy.start()
            pairs[at] = copy
        for i in (3, 1, 2, 0):
            at = k * 4 + i
            sel = selector(pos, who[i] * 8 + b * 2 + core, room)
            pairs[at].wait_recv()

            def add(n):
                value = scattered(sel, who[i], b, core, n) + pair[at, :, n].astype(F32)
                pair[at, :, n] = value.astype(BF16)

            for_columns(add)
            if i == 3:
                for side, (part, dst, p) in enumerate(
                    ((low, half_near, near), (high, half_far, far))
                ):
                    copy = remote(
                        pair.at[at, part], dst.at[k], hs.at[k, side], hr.at[k, side], (p, e)
                    )
                    copy.start()
                    halves[k, side] = copy

    def stage_b(k):
        for side, (i, part, src, dst, p) in enumerate(
            (
                (2, low, half_near, full_far, far),
                (1, high, half_far, full_near, near),
            )
        ):
            at = k * 4 + i
            halves[k, side].wait_recv()

            def add(n):
                value = pair[at, part, n].astype(F32) + src[k, :, n].astype(F32)
                pair[at, part, n] = value.astype(BF16)

            for_columns(add)
            copy = remote(pair.at[at], dst.at[k], fs.at[k, side], fr.at[k, side], (p, e))
            copy.start()
            fulls[k, side] = copy

    def stage_c(k):
        b = order[k]
        at = k * 4
        fulls[k, 0].wait_recv()
        fulls[k, 1].wait_recv()

        def add(n):
            out[:, n] = (
                pair[at, :, n].astype(F32)
                + full_near[k, :, n].astype(F32)
                + full_far[k, :, n].astype(F32)
            )

        for_columns(add)
        for side, cond in ((0, (b >= z) & (z > 0)), (1, (b <= z) & (z < 3))):

            @pl.when(cond)
            def _():
                remote(
                    lines.at[side, b], lines.at[side, b], zs.at[side, k], zr.at[side, b], (r, e ^ 1)
                ).wait_recv()

                def more(n):
                    out[:, n] = out[:, n] + lines[side, b, :, n].astype(F32)

                for_columns(more)

        if k < 3:

            def keep(n):
                pair[at, :, n] = out[:, n].astype(BF16)

            for_columns(keep)
            for side, cond, to in (
                (0, b > z, jnp.minimum(z + 1, 3)),
                (1, b < z, jnp.maximum(z - 1, 0)),
            ):
                copy = remote(
                    pair.at[at], lines.at[side, b], zs.at[side, k], zr.at[side, b], (r, to * 2 + core)
                )
                moves.append((cond, copy))

                @pl.when(cond)
                def _():
                    copy.start()

    stage_a(0)
    stage_a(1)
    stage_b(0)
    stage_a(2)
    stage_b(1)
    stage_c(0)
    stage_a(3)
    stage_b(2)
    stage_c(1)
    stage_b(3)
    stage_c(2)
    stage_c(3)
    for copies in (pairs, halves, fulls):
        for copy in copies.values():
            copy.wait_send()
    for cond, copy in moves:

        @pl.when(cond)
        def _():
            copy.wait_send()


def sum_world(y, pos, rows, collective_id):
    groups, per, room, width = y.shape

    def blocks(n, size):
        return pltpu.VMEM((n, size, width), BF16)

    return pl.pallas_call(
        sum_world_kernel,
        out_shape=jax.ShapeDtypeStruct((rows, width), F32),
        in_specs=[VMEM_SPEC, VMEM_SPEC],
        out_specs=VMEM_SPEC,
        scratch_shapes=[
            blocks(16, rows),
            blocks(16, rows),
            blocks(4, rows // 2),
            blocks(4, rows // 2),
            blocks(4, rows),
            blocks(4, rows),
            pltpu.VMEM((2, 4, rows, width), BF16),
            pltpu.SemaphoreType.DMA((16,)),
            pltpu.SemaphoreType.DMA((16,)),
            pltpu.SemaphoreType.DMA((4, 2)),
            pltpu.SemaphoreType.DMA((4, 2)),
            pltpu.SemaphoreType.DMA((4, 2)),
            pltpu.SemaphoreType.DMA((4, 2)),
            pltpu.SemaphoreType.DMA((2, 4)),
            pltpu.SemaphoreType.DMA((2, 4)),
        ],
        compiler_params=params(collective_id),
        name="sum_world",
    )(y, pos)


def experts_by_all_to_all(
    mixed, state, teacher, routes, valid_slot, valid_count, router_weight, gate_weight, up_weight, down_weight,
    devices, capacity, slots_all,
):
    tok_dev, model_width = mixed.shape
    top_count = routes.shape[1]
    ffn_width = gate_weight.shape[2]
    logits = jnp.dot(mixed, router_weight, preferred_element_type=jnp.float32)
    gates = jax.nn.softmax(jnp.take_along_axis(logits, routes, axis=1), axis=-1)
    rows_total = tok_dev * top_count
    expert_ids = routes.reshape(rows_total)
    live_rows = jnp.repeat(valid_slot, top_count)
    expert_range = jnp.arange(devices, dtype=jnp.int32)
    hit_table = ((expert_ids[:, None] == expert_range[None, :]) & live_rows[:, None]).astype(
        jnp.int32
    )
    earlier = jnp.cumsum(hit_table, axis=0) - hit_table
    position_in = jnp.sum(earlier * hit_table, axis=1)
    slot_index = jnp.where(live_rows, expert_ids * capacity + position_in, devices * capacity)
    row_of_slot = (
        jnp.full((devices * capacity + 1,), rows_total, jnp.int32)
        .at[slot_index]
        .set(jnp.arange(rows_total, dtype=jnp.int32))[: devices * capacity]
    )
    token_of_slot = jnp.where(row_of_slot < rows_total, row_of_slot // top_count, tok_dev)
    mixed_pad = jnp.concatenate([mixed, jnp.zeros((1, model_width), jnp.bfloat16)], axis=0)
    send_rows = mixed_pad[token_of_slot].reshape(devices, capacity, model_width)
    arrived = lax.all_to_all(send_rows, ("dp", "expert"), split_axis=0, concat_axis=0, tiled=True)
    sources = arrived.shape[0]
    items = arrived.shape[1]
    flat_in = arrived.reshape(sources * items, model_width)
    gate_pre = jnp.dot(flat_in, gate_weight[0], preferred_element_type=jnp.float32)
    up_pre = jnp.dot(flat_in, up_weight[0], preferred_element_type=jnp.float32)
    hidden_units = (jax.nn.silu(gate_pre) * up_pre).astype(jnp.bfloat16)
    produced = jnp.dot(hidden_units, down_weight[0], preferred_element_type=jnp.float32).astype(
        jnp.bfloat16
    )
    produced, gate_pre, up_pre, hidden_units, arrived = (
        produced.reshape(sources, items, model_width),
        gate_pre.reshape(sources, items, ffn_width),
        up_pre.reshape(sources, items, ffn_width),
        hidden_units.reshape(sources, items, ffn_width),
        arrived,
    )
    returned = lax.all_to_all(produced, ("dp", "expert"), split_axis=0, concat_axis=0, tiled=True)
    returned_pad = jnp.concatenate(
        [
            returned.reshape(devices * capacity, model_width),
            jnp.zeros((1, model_width), jnp.bfloat16),
        ],
        axis=0,
    )
    copies = returned_pad[slot_index].reshape(tok_dev, top_count, model_width)
    layer_out = state + jnp.sum(gates[:, :, None] * copies, axis=1)
    live_tokens = valid_slot.astype(jnp.float32)[:, None]
    diff = (layer_out - teacher.astype(jnp.float32)) * live_tokens
    local_square = jnp.sum(diff * diff)
    d_out = 2.0 * slots_all * diff / valid_count
    d_gates = jnp.sum(d_out[:, None, :] * copies, axis=-1)
    d_chosen = gates * (d_gates - jnp.sum(gates * d_gates, axis=-1, keepdims=True))
    d_logits = jnp.sum(
        jnp.where(routes[:, :, None] == expert_range[None, None, :], d_chosen[:, :, None], 0.0),
        axis=1,
    ).astype(jnp.bfloat16)
    d_copies = (
        (gates[:, :, None] * d_out[:, None, :])
        .astype(jnp.bfloat16)
        .reshape(rows_total, model_width)
    )
    d_copies_pad = jnp.concatenate([d_copies, jnp.zeros((1, model_width), jnp.bfloat16)], axis=0)
    d_send = d_copies_pad[row_of_slot].reshape(devices, capacity, model_width)
    d_arrived = lax.all_to_all(d_send, ("dp", "expert"), split_axis=0, concat_axis=0, tiled=True)
    flat_d = d_arrived.reshape(-1, model_width)
    flat_in = arrived.reshape(-1, model_width)
    flat_gate = gate_pre.reshape(-1, ffn_width)
    flat_up = up_pre.reshape(-1, ffn_width)
    flat_hidden = hidden_units.reshape(-1, ffn_width)
    d_hidden = contract(flat_d, down_weight[0], 1, 1)
    sigmoid_gate = jax.nn.sigmoid(flat_gate)
    d_gate = (d_hidden * flat_up * sigmoid_gate * (1.0 + flat_gate * (1.0 - sigmoid_gate))).astype(
        jnp.bfloat16
    )
    d_up = (d_hidden * flat_gate * sigmoid_gate).astype(jnp.bfloat16)
    down_grad = contract(flat_hidden, flat_d, 0, 0)[None]
    gate_grad = contract(flat_in, d_gate, 0, 0)[None]
    up_grad = contract(flat_in, d_up, 0, 0)[None]
    d_in = (contract(d_gate, gate_weight[0], 1, 1) + contract(d_up, up_weight[0], 1, 1)).astype(
        jnp.bfloat16
    )
    d_returned = lax.all_to_all(
        d_in.reshape(devices, capacity, model_width),
        ("dp", "expert"),
        split_axis=0,
        concat_axis=0,
        tiled=True,
    )
    d_returned_pad = jnp.concatenate(
        [
            d_returned.reshape(devices * capacity, model_width),
            jnp.zeros((1, model_width), jnp.bfloat16),
        ],
        axis=0,
    )
    d_mixed = jnp.sum(
        d_returned_pad[slot_index].reshape(tok_dev, top_count, model_width),
        axis=1,
        dtype=jnp.float32,
    )
    d_mixed = d_mixed + contract(d_logits, router_weight, 1, 1)
    router_local = contract(mixed, d_logits, 0, 0)
    return layer_out, d_out, d_mixed, local_square, router_local, gate_grad, up_grad, down_grad


def experts_by_gather(
    mixed, state, teacher, routes, valid_slot, valid_count, router_weight,
    gate_weight, up_weight, down_weight, devices, capacity, slots_all,
):
    tok_dev, model_width = mixed.shape
    room = -(-capacity // 16) * 16
    expert_range = jnp.arange(devices, dtype=jnp.int32)
    logits = jnp.dot(mixed, router_weight, preferred_element_type=F32)
    chosen = jnp.any(routes[:, :, None] == expert_range[None, None], axis=1)
    gates = jax.nn.softmax(jnp.where(chosen, logits, -jnp.inf), axis=-1)
    live_gates = jnp.where(valid_slot[:, None], gates, 0.0)
    gates_high = live_gates.astype(BF16)
    gates_low = (live_gates - gates_high.astype(F32)).astype(BF16)
    gap = jnp.zeros((tok_dev, 64 - devices), BF16)
    payload = jnp.concatenate([mixed, gates_high, gap, gates_low, gap], axis=1)
    pos, x_rows, y_rows, kept = experts_fwd(
        payload, gate_weight[0], up_weight[0], down_weight[0], room
    )
    layer_out = state + sum_world(y_rows.reshape(4, 8, room, model_width), pos, tok_dev, 8)
    live_tokens = valid_slot.astype(F32)[:, None]
    diff = (layer_out - teacher.astype(F32)) * live_tokens
    local_square = jnp.sum(diff * diff)
    d_out = 2.0 * slots_all * diff / valid_count
    hidden = kept[3]
    d_rows, d_copy, d_gate, d_up = experts_bwd(
        d_out.astype(BF16), pos, kept[:3] + kept[4:], gate_weight[0], up_weight[0], down_weight[0], room
    )
    back = sum_world(d_rows.reshape(4, 8, room, model_width + 128), pos, tok_dev, 9)

    def flat(a):
        return a.reshape(4 * 8 * room, a.shape[-1])

    down_grad = contract(flat(hidden), flat(d_copy), 0, 0)[None]
    gate_grad = contract(flat(x_rows), flat(d_gate), 0, 0)[None]
    up_grad = contract(flat(x_rows), flat(d_up), 0, 0)[None]
    d_gates = back[:, model_width : model_width + devices] + back[:, model_width + 64 : model_width + 64 + devices]
    d_logits = (gates * (d_gates - jnp.sum(gates * d_gates, axis=-1, keepdims=True))).astype(BF16)
    d_mixed = back[:, :model_width] + contract(d_logits, router_weight, 1, 1)
    router_local = contract(mixed, d_logits, 0, 0)
    return layer_out, d_out, d_mixed, local_square, router_local, gate_grad, up_grad, down_grad


def head_rope(linear, gain_vec, cos, sin):
    value = root_mean_scale(linear, gain_vec)
    half = value.shape[-1] // 2
    return value * cos + jnp.roll(value, half, axis=-1) * sin


def body(
    tokens,
    teacher,
    routes,
    cont_lengths,
    query_weight,
    key_projection,
    value_projection,
    output_weight,
    router_weight,
    gate_weight,
    up_weight,
    down_weight,
    input_gain,
    post_gain,
    query_gain,
    key_gain,
):
    n_dp = lax.axis_size("dp")
    n_owner = lax.axis_size("expert")
    devices = n_dp * n_owner
    rank_dp = lax.axis_index("dp")
    rank_owner = lax.axis_index("expert")
    flat_rank = rank_dp * n_owner + rank_owner
    column = rank_owner % 2
    first_column = column == 0
    tok_dev, model_width = tokens.shape
    top_count = routes.shape[1]
    head_dim = query_gain.shape[0]
    kv_width = key_projection.shape[1]
    query_width = query_weight.shape[1]
    query_group = query_width // n_dp
    assert n_dp == 4 and kv_width == n_dp * head_dim
    prompt_block = tok_dev - CMAX
    half_prompt = n_dp * prompt_block
    prompt_len = 2 * half_prompt
    capacity = max(2, tok_dev * top_count * 5 // (4 * devices))
    slots_all = devices * tok_dev
    slot_ids = jnp.arange(tok_dev, dtype=jnp.int32)
    own_length = cont_lengths[flat_rank]
    valid_slot = (slot_ids < prompt_block) | (slot_ids - prompt_block < own_length)
    valid_count = (devices * prompt_block + jnp.sum(cont_lengths)).astype(F32)
    tokens_float = tokens.astype(F32)
    normed_float, first_norm_back = jax.vjp(root_mean_scale, tokens_float, input_gain)
    normed = normed_float.astype(BF16)

    block_ids = jnp.arange(n_dp, dtype=jnp.int32)[:, None]
    positions = jnp.where(
        slot_ids[None] < prompt_block,
        (column * n_dp + block_ids) * prompt_block + slot_ids[None],
        prompt_len + slot_ids[None] - prompt_block,
    )
    half_head = head_dim // 2
    frequency = rope_base ** (-(jnp.arange(half_head, dtype=F32) * 2.0) / head_dim)
    angles = positions.astype(F32)[:, :, None] * frequency
    cos_half, sin_half = jnp.cos(angles), jnp.sin(angles)
    cos = jnp.concatenate([cos_half, cos_half], axis=-1)
    sin = jnp.concatenate([-sin_half, sin_half], axis=-1)
    lengths = jnp.concatenate(
        [lax.dynamic_index_in_dim(cont_lengths.reshape(n_dp, n_owner), rank_owner, 1, False), column[None]]
    ).astype(jnp.int32)

    lin, normed_cols_t = project_qkv(normed, query_weight, key_projection, value_projection)
    key_lin = lin[:, query_group : query_group + head_dim].reshape(n_dp, tok_dev, head_dim)
    keys_float, key_back = jax.vjp(lambda a, b: head_rope(a, b, cos, sin), key_lin, key_gain)
    keys_own = keys_float.astype(BF16)
    values_own = lin[:, query_group + head_dim :].reshape(n_dp, tok_dev, head_dim).astype(BF16)
    column_kv = jnp.stack([keys_own[:, :prompt_block], values_own[:, :prompt_block]]).reshape(
        2, half_prompt, head_dim
    )
    other_kv = partner(column_kv, "expert", 0)
    full_kv = jnp.where(
        first_column,
        jnp.concatenate([column_kv, other_kv], axis=1),
        jnp.concatenate([other_kv, column_kv], axis=1),
    )
    spread = jnp.broadcast_to(full_kv[:, None], (2, n_dp, prompt_len, head_dim))
    all_keys = jnp.concatenate([spread[0], keys_own[:, prompt_block:]], axis=1)
    all_values = jnp.concatenate([spread[1], values_own[:, prompt_block:]], axis=1)
    query_gain_row = query_gain[None]
    queries, attended = attention_fwd(
        lengths, lin, query_gain_row, cos, sin, all_keys, all_values, prompt_len
    )
    state = tokens_float + project_out(attended, output_weight)
    mixed_float, second_norm_back = jax.vjp(root_mean_scale, state, post_gain)
    mixed = mixed_float.astype(BF16)
    sizes = (devices, capacity, slots_all)
    weights = (router_weight, gate_weight, up_weight, down_weight)
    if n_dp == 4 and n_owner == 8:
        moe = experts_by_gather(
            mixed, state, teacher, routes, valid_slot, valid_count, *weights, *sizes
        )
    else:
        moe = experts_by_all_to_all(
            mixed, state, teacher, routes, valid_slot, valid_count, *weights, *sizes
        )
    layer_out, d_out, d_mixed, local_square, router_local, gate_grad, up_grad, down_grad = moe
    d_state_norm, d_post_gain = second_norm_back(d_mixed)
    d_state = d_out + d_state_norm
    d_branch = d_state.astype(BF16)
    d_attended, out_part = grad_branch(d_branch, output_weight, attended)
    d_query_lin, d_keys, d_values, gain_parts = attention_bwd(
        lengths, lin, queries, d_attended, query_gain_row, cos, sin, all_keys, all_values, prompt_len
    )
    d_query_gain = jnp.sum(gain_parts, axis=(0, 1))
    prompt_grads = jnp.stack(
        [jnp.sum(d_keys[:, :prompt_len], axis=0), jnp.sum(d_values[:, :prompt_len], axis=0)]
    )
    mine_part = jnp.where(first_column, prompt_grads[:, :half_prompt], prompt_grads[:, half_prompt:])
    their_part = jnp.where(first_column, prompt_grads[:, half_prompt:], prompt_grads[:, :half_prompt])
    own_prompt = (mine_part + partner(their_part, "expert", 0)).reshape(
        2, n_dp, prompt_block, head_dim
    )
    d_key_post = jnp.concatenate([own_prompt[0], d_keys[:, prompt_len:]], axis=1)
    d_value_lin = jnp.concatenate([own_prompt[1], d_values[:, prompt_len:]], axis=1)
    d_key_float, d_key_gain = key_back(d_key_post)
    rows = n_dp * tok_dev
    d_lin = jnp.concatenate(
        [
            d_query_lin,
            d_key_float.astype(BF16).reshape(rows, head_dim),
            d_value_lin.astype(BF16).reshape(rows, head_dim),
        ],
        axis=1,
    )
    small_parts = [router_local, d_post_gain, d_query_gain, d_key_gain, local_square[None]]
    width = query_weight.shape[0]
    group = d_lin.shape[1]
    rows_here = width // n_owner
    by_line = n_dp == 4 and n_owner == 8

    def packed(parts):
        small = jnp.concatenate([a.reshape(-1) for a in parts])
        piece_rows = -(-small.shape[0] // (8 * 8 * 128)) * 8
        small = jnp.pad(small, (0, 8 * piece_rows * 128 - small.shape[0]))
        return small.reshape(8, piece_rows, 128)

    dqkv_operands = (
        d_lin, query_weight, key_projection, value_projection, normed_cols_t,
        out_part.reshape(n_owner, -1, model_width),
    )
    if by_line:
        small = packed(small_parts)
        unit_rows = tokens_float * lax.rsqrt(
            jnp.mean(tokens_float * tokens_float, axis=-1, keepdims=True) + norm_eps
        )
        d_normed, qkv_rows, output_grad, small_out = grad_qkv_line(*dqkv_operands, small, unit_rows)
        input_gain_grad = small_out[:, small.shape[1] : small.shape[1] + model_width // 1024].reshape(-1)
        small = small_out[:, : small.shape[1]]
    else:
        d_normed, qkv_part, output_grad = grad_qkv(*dqkv_operands)
    d_tokens_norm, d_input_gain = first_norm_back(d_normed)
    tokens_grad = d_state + d_tokens_norm
    if not by_line:
        small_parts.append(d_input_gain)
        by_owner = (
            qkv_part.reshape(n_dp, n_owner, rows_here, group)
            .transpose(1, 0, 2, 3)
            .reshape(n_owner, n_dp * rows_here, group)
        )
        qkv_rows, small = last_sums(by_owner, packed(small_parts))
    qkv_rows = qkv_rows.reshape(n_dp, rows_here, group)

    def columns(start, size):
        return qkv_rows[:, :, start : start + size].transpose(1, 0, 2).reshape(rows_here, n_dp * size)

    query_grad = columns(0, query_group)
    key_grad = columns(query_group, head_dim)
    value_grad = columns(query_group + head_dim, head_dim)
    small = small.reshape(-1)
    starts = [0]
    for a in small_parts:
        starts.append(starts[-1] + a.size)
    sums = [small[i:j].reshape(a.shape) for a, i, j in zip(small_parts, starts, starts[1:])]
    router_grad, post_gain_grad, query_gain_grad, key_gain_grad, total_square = sums[:5]
    if not by_line:
        input_gain_grad = sums[5]
    loss = total_square[0] / (valid_count * model_width)
    return (
        layer_out,
        loss,
        tokens_grad,
        query_grad,
        key_grad,
        value_grad,
        output_grad,
        router_grad,
        gate_grad,
        up_grad,
        down_grad,
        input_gain_grad,
        post_gain_grad,
        query_gain_grad,
        key_gain_grad,
    )


def solution(mesh):
    in_specs = (
        P(("dp", "expert"), None),
        P(("dp", "expert"), None),
        P(("dp", "expert"), None),
        P(),
        P("dp", None),
        P("dp", None),
        P("dp", None),
        P("dp", None),
        P(),
        P(("dp", "expert"), None, None),
        P(("dp", "expert"), None, None),
        P(("dp", "expert"), None, None),
        P(),
        P(),
        P(),
        P(),
    )
    out_specs = (
        P(("dp", "expert"), None),
        P(),
        P(("dp", "expert"), None),
        P(("dp", "expert"), None),
        P(("dp", "expert"), None),
        P(("dp", "expert"), None),
        P(("dp", "expert"), None),
        P(),
        P(("dp", "expert"), None, None),
        P(("dp", "expert"), None, None),
        P(("dp", "expert"), None, None),
        P(),
        P(),
        P(),
        P(),
    )
    return jax.shard_map(body, mesh=mesh, in_specs=in_specs, out_specs=out_specs, check_vma=False)
```

```python
import functools

import jax
import jax.numpy as jnp
from jax import lax
from jax.experimental import pallas as pl
from jax.experimental.pallas import tpu as pltpu
from jax.sharding import PartitionSpec as P

CMAX = 128
norm_eps = 1e-06
rope_base = 1000000.0
MESH = pl.DeviceIdType.MESH
F32 = jnp.float32
BF16 = jnp.bfloat16
VMEM_SPEC = pl.BlockSpec(memory_space=pltpu.VMEM)
ANY_SPEC = pl.BlockSpec(memory_space=pl.ANY)
VMEM_LIMIT = 56 * 1024 * 1024


def params(collective_id=None):
    return pltpu.CompilerParams(
        collective_id=collective_id,
        has_side_effects=collective_id is not None,
        vmem_limit_bytes=VMEM_LIMIT,
    )


def greet(devices):
    barrier = pltpu.get_barrier_semaphore()
    for device in devices:
        pl.semaphore_signal(barrier, inc=1, device_id=device, device_id_type=MESH)
    pl.semaphore_wait(barrier, len(devices))


def remote(src, dst, send_sem, recv_sem, device):
    return pltpu.make_async_remote_copy(
        src_ref=src,
        dst_ref=dst,
        send_sem=send_sem,
        recv_sem=recv_sem,
        device_id=device,
        device_id_type=MESH,
    )


def aligned(index, size):
    return pl.ds(pl.multiple_of(index * size, size), size)


def dot_nn(a, b):
    return lax.dot_general(a, b, (((1,), (0,)), ((), ())), preferred_element_type=F32)


def dot_nt(a, b):
    return lax.dot_general(a, b, (((1,), (1,)), ((), ())), preferred_element_type=F32)


def dot_tn(a, b):
    return lax.dot_general(a, b, (((0,), (0,)), ((), ())), preferred_element_type=F32)


PEER_MASKS = (3, 1, 2)


def relay_sum(r, e, products, own, mine, send, half_in, full_in, hs, hr, fs, fr, step):
    near, far, diag = r ^ 1, r ^ 2, r ^ 3
    rows = mine.shape[0]
    half = rows // 2
    low, high = pl.ds(0, half), pl.ds(half, half)
    products(diag, send.at[2])
    relays = [
        remote(send.at[2, low], half_in.at[0], hs.at[0], hr.at[0], (near, e)),
        remote(send.at[2, high], half_in.at[1], hs.at[1], hr.at[1], (far, e)),
    ]
    for copy in relays:
        copy.start()
    parts = ((0, low, near), (1, high, far), (0, high, near), (1, low, far))
    fulls = [
        remote(send.at[i, part], full_in.at[i, part], fs.at[n], fr.at[n], (p, e))
        for n, (i, part, p) in enumerate(parts)
    ]
    products(near, send.at[0])
    fulls[0].start()
    products(far, send.at[1])
    fulls[1].start()
    for i, start, slot, n in ((1, 0, 0, 3), (0, half, 1, 2)):
        relays[slot].wait_recv()

        def add(c, carry):
            t = pl.ds(pl.multiple_of(start + c * step, step), step)
            value = send[i, t, :].astype(F32) + half_in[slot, aligned(c, step), :].astype(F32)
            send[i, t, :] = value.astype(BF16)
            return carry

        lax.fori_loop(0, half // step, add, 0)
        fulls[n].start()
    own()
    for copy in fulls:
        copy.wait_recv()

    def total(c, carry):
        t = aligned(c, step)
        mine[t, :] = mine[t, :] + (full_in[0, t, :].astype(F32) + full_in[1, t, :].astype(F32))
        return carry

    lax.fori_loop(0, rows // step, total, 0)
    for copy in relays + fulls:
        copy.wait_send()


def relay_scratch(rows, width):
    return [
        pltpu.VMEM((3, rows, width), BF16),
        pltpu.VMEM((2, rows // 2, width), BF16),
        pltpu.VMEM((2, rows, width), BF16),
        pltpu.SemaphoreType.DMA((2,)),
        pltpu.SemaphoreType.DMA((2,)),
        pltpu.SemaphoreType.DMA((4,)),
        pltpu.SemaphoreType.DMA((4,)),
    ]


def qkv_kernel(tok, normed, wq, wk, wv, lin, cols_t, cols, asend, arecv, *relay):
    r, e = lax.axis_index("dp"), lax.axis_index("expert")
    peers = [r ^ m for m in PEER_MASKS]
    width = wq.shape[0]
    qg = wq.shape[1] // 4
    kg = wk.shape[1] // 4
    rows = cols.shape[0]
    greet([(p, e) for p in peers])
    first = []
    for i, p in enumerate(peers):
        copy = remote(
            normed.at[:, aligned(p, width)], cols.at[aligned(r, tok), :],
            asend.at[i], arecv.at[i], (p, e),
        )
        copy.start()
        first.append(copy)
    cols[aligned(r, tok), :] = normed[:, aligned(r, width)]
    for copy in first:
        copy.wait()

    def products(p, dst):
        def chunk(c, carry):
            columns = pl.ds(pl.multiple_of(p * qg + c * 256, 256), 256)
            dst[:, aligned(c, 256)] = dot_nn(cols[...], wq[:, columns]).astype(dst.dtype)
            return carry

        lax.fori_loop(0, qg // 256, chunk, 0)
        dst[:, qg : qg + kg] = dot_nn(cols[...], wk[:, aligned(p, kg)]).astype(dst.dtype)
        dst[:, qg + kg :] = dot_nn(cols[...], wv[:, aligned(p, kg)]).astype(dst.dtype)

    def own():
        products(r, lin)
        cols_t[...] = cols[...].T

    relay_sum(r, e, products, own, lin, *relay, 32)


def project_qkv(normed, wq, wk, wv):
    tok = normed.shape[0]
    rows = 4 * tok
    group = (wq.shape[1] + wk.shape[1] + wv.shape[1]) // 4
    return pl.pallas_call(
        functools.partial(qkv_kernel, tok),
        out_shape=(
            jax.ShapeDtypeStruct((rows, group), F32),
            jax.ShapeDtypeStruct((wq.shape[0], rows), BF16),
            jax.ShapeDtypeStruct((rows, wq.shape[0]), BF16),
        ),
        in_specs=[VMEM_SPEC] * 4,
        out_specs=(VMEM_SPEC,) * 3,
        scratch_shapes=[pltpu.SemaphoreType.DMA((3,))] * 2
        + relay_scratch(rows, group),
        compiler_params=params(1),
        name="qkv_exchange",
    )(normed, wq, wk, wv)


def out_kernel(attn, wo, total, *relay):
    r, e = lax.axis_index("dp"), lax.axis_index("expert")
    tok, width = total.shape
    step = width // 4
    greet([(r ^ m, e) for m in PEER_MASKS])

    def products(p, dst):
        def chunk(c, carry):
            n = aligned(c, step)
            dst[:, n] = dot_nn(attn[aligned(p, tok), :], wo[:, n]).astype(dst.dtype)
            return carry

        lax.fori_loop(0, width // step, chunk, 0)

    relay_sum(r, e, products, lambda: products(r, total), total, *relay, 16)


def project_out(attn, wo):
    tok = attn.shape[0] // 4
    return pl.pallas_call(
        out_kernel,
        out_shape=jax.ShapeDtypeStruct((tok, wo.shape[1]), F32),
        in_specs=[VMEM_SPEC] * 2,
        out_specs=VMEM_SPEC,
        scratch_shapes=relay_scratch(tok, wo.shape[1]),
        compiler_params=params(2),
        name="out_exchange",
    )(attn, wo)


def dgrad_kernel(
    mine, wq, wk, wv, cols_t, out_part, normal, grads, out_grad,
    blocks, dsum, dsend, drecv, ssem, rsem, bsend, brecv, *scratch,
):
    r, e = lax.axis_index("dp"), lax.axis_index("expert")
    rows = mine.shape[0]
    tok = rows // 4
    half = rows // 2
    qg = wq.shape[1] // 4
    kg = wk.shape[1] // 4
    width = wq.shape[0]
    peers = [r ^ m for m in PEER_MASKS]
    near, far, diag = r ^ 1, r ^ 2, r ^ 3
    pair_in, send, recv, *sems = scratch
    begin, middle, finish = owner_sum([out_part], [out_grad], [pair_in], [send], [recv], *sems)
    greet([(p, e) for p in peers] + [(r, e ^ 1)] + owner_peers())
    begin()
    low, high = pl.ds(0, half), pl.ds(half, half)
    first_near = remote(mine.at[low], blocks.at[0, low], ssem.at[0], rsem.at[0], (near, e))
    first_far = remote(mine.at[high], blocks.at[1, high], ssem.at[1], rsem.at[1], (far, e))
    second_near = remote(mine.at[high], blocks.at[0, high], ssem.at[2], rsem.at[2], (near, e))
    second_far = remote(mine.at[low], blocks.at[1, low], ssem.at[3], rsem.at[3], (far, e))
    pass_far = remote(blocks.at[0, low], blocks.at[2, low], ssem.at[4], rsem.at[4], (far, e))
    pass_near = remote(blocks.at[1, high], blocks.at[2, high], ssem.at[5], rsem.at[5], (near, e))
    for copy in (first_near, first_far, second_near, second_far):
        copy.start()

    def products(p, src, start):
        def chunk(c, carry):
            t = aligned(c, tok)
            x = src[t, :]
            value = (
                dot_nt(x[:, :qg], wq[:, aligned(p, qg)])
                + dot_nt(x[:, qg : qg + kg], wk[:, aligned(p, kg)])
                + dot_nt(x[:, qg + kg :], wv[:, aligned(p, kg)])
            )
            if start:
                dsum[t, :] = value
            else:
                dsum[t, :] = dsum[t, :] + value
            return carry

        lax.fori_loop(0, 4, chunk, 0)

        def outer(c, carry):
            n = aligned(c, 128)
            grads[aligned(p, width), n] = dot_nn(cols_t[...], src[:, n]).astype(BF16)
            return carry

        lax.fori_loop(0, (qg + 2 * kg) // 128, outer, 0)

    middle()
    products(r, mine, True)
    first_near.wait()
    pass_far.start()
    first_far.wait()
    pass_near.start()
    second_near.wait()
    products(near, blocks.at[0], False)
    second_far.wait()
    products(far, blocks.at[1], False)
    pass_far.wait()
    pass_near.wait()
    products(diag, blocks.at[2], False)
    back = []
    for i, p in enumerate(peers):
        dsend[i] = dsum[aligned(p, tok), :].astype(BF16)
        copy = remote(dsend.at[i], drecv.at[i], bsend.at[i], brecv.at[i], (p, e))
        copy.start()
        back.append(copy)
    normal[:, aligned(r, width)] = dsum[aligned(r, tok), :]
    for i, p in enumerate(peers):
        back[i].wait()
        normal[:, aligned(p, width)] = drecv[i].astype(F32)
    finish()


def grad_qkv(mine, wq, wk, wv, cols_t, out_part):
    rows, group = mine.shape
    tok = rows // 4
    width = wq.shape[0]
    return pl.pallas_call(
        dgrad_kernel,
        out_shape=(
            jax.ShapeDtypeStruct((tok, 4 * width), F32),
            jax.ShapeDtypeStruct((4 * width, group), BF16),
            jax.ShapeDtypeStruct(out_part.shape[1:], F32),
        ),
        in_specs=[VMEM_SPEC] * 6,
        out_specs=(VMEM_SPEC,) * 3,
        scratch_shapes=[
            pltpu.VMEM((3, rows, group), BF16),
            pltpu.VMEM((rows, width), F32),
            pltpu.VMEM((3, tok, width), BF16),
            pltpu.VMEM((3, tok, width), BF16),
            pltpu.SemaphoreType.DMA((6,)),
            pltpu.SemaphoreType.DMA((6,)),
            pltpu.SemaphoreType.DMA((3,)),
            pltpu.SemaphoreType.DMA((3,)),
        ]
        + owner_scratch([out_part]),
        compiler_params=params(4),
        name="dqkv_exchange",
    )(mine, wq, wk, wv, cols_t, out_part)


def branch_kernel(mine, wo, attn, d_attn, full, attn_t, ssem, rsem):
    r, e = lax.axis_index("dp"), lax.axis_index("expert")
    tok = mine.shape[0]
    half = tok // 2
    peers = [r ^ m for m in PEER_MASKS]
    near, far, diag = r ^ 1, r ^ 2, r ^ 3
    greet([(p, e) for p in peers])

    def part(q, which):
        return pl.ds(pl.multiple_of(q * tok + which * half, half), half)

    low, high = pl.ds(0, half), pl.ds(half, half)
    first_near = remote(mine.at[low], full.at[part(r, 0)], ssem.at[0], rsem.at[0], (near, e))
    first_far = remote(mine.at[high], full.at[part(r, 1)], ssem.at[1], rsem.at[1], (far, e))
    second_near = remote(mine.at[high], full.at[part(r, 1)], ssem.at[2], rsem.at[2], (near, e))
    second_far = remote(mine.at[low], full.at[part(r, 0)], ssem.at[3], rsem.at[3], (far, e))
    pass_far = remote(full.at[part(near, 0)], full.at[part(near, 0)], ssem.at[4], rsem.at[4], (far, e))
    pass_near = remote(full.at[part(far, 1)], full.at[part(far, 1)], ssem.at[5], rsem.at[5], (near, e))
    for copy in (first_near, first_far, second_near, second_far):
        copy.start()
    full[aligned(r, tok), :] = mine[...]
    attn_t[...] = attn[...].T
    heads = wo.shape[0]
    step = heads // 4

    def products(q):
        def chunk(c, carry):
            n = aligned(c, step)
            d_attn[aligned(q, tok), n] = dot_nt(full[aligned(q, tok), :], wo[n, :]).astype(BF16)
            return carry

        lax.fori_loop(0, 4, chunk, 0)

    products(r)
    first_near.wait()
    pass_far.start()
    first_far.wait()
    pass_near.start()
    second_near.wait()
    products(near)
    second_far.wait()
    products(far)
    pass_far.wait()
    pass_near.wait()
    products(diag)


def grad_branch(mine, wo, attn):
    tok, width = mine.shape
    return pl.pallas_call(
        branch_kernel,
        out_shape=(
            jax.ShapeDtypeStruct((4 * tok, wo.shape[0]), BF16),
            jax.ShapeDtypeStruct((4 * tok, width), BF16),
            jax.ShapeDtypeStruct((wo.shape[0], 4 * tok), BF16),
        ),
        in_specs=[VMEM_SPEC] * 3,
        out_specs=(VMEM_SPEC,) * 3,
        scratch_shapes=[
            pltpu.SemaphoreType.DMA((6,)),
            pltpu.SemaphoreType.DMA((6,)),
        ],
        compiler_params=params(3),
        name="branch_exchange",
    )(mine, wo, attn)


def owner_order(n_z):
    order = list(range(1, n_z)) + [0]
    return order[1:2] + order[:1] + order[2:] if n_z > 2 else order


def owner_sum(arrays, outs, pair_in, send, recv, psend, precv, zsend, zrecv):
    r, e = lax.axis_index("dp"), lax.axis_index("expert")
    n_z = arrays[0].shape[0] // 2
    z, core = e // 2, e % 2
    targets = [lax.rem(z + j, n_z) for j in range(n_z)]
    order = owner_order(n_z)
    n_arrays = len(arrays)
    pair, moves = {}, []

    def begin():
        for j in order:
            for a in range(n_arrays):
                copy = remote(
                    arrays[a].at[targets[j] * 2 + (1 - core)], pair_in[a].at[j],
                    psend.at[a, j], precv.at[a, j], (r, e ^ 1),
                )
                copy.start()
                pair[a, j] = copy

    def middle():
        for j in order:
            for a in range(n_arrays):
                pair[a, j].wait()
                own = arrays[a][targets[j] * 2 + core].astype(F32) + pair_in[a][j].astype(F32)
                if j == 0:
                    outs[a][...] = own
                else:
                    send[a][j - 1] = own.astype(BF16)
                    copy = remote(
                        send[a].at[j - 1], recv[a].at[j - 1],
                        zsend.at[a, j - 1], zrecv.at[a, j - 1], (r, targets[j] * 2 + core),
                    )
                    copy.start()
                    moves.append(copy)

    def finish():
        for copy in moves:
            copy.wait()
        for a in range(n_arrays):
            value = outs[a][...]
            for j in range(n_z - 1):
                value = value + recv[a][j].astype(F32)
            outs[a][...] = value

    return begin, middle, finish


def owner_scratch(arrays):
    n_z = arrays[0].shape[0] // 2
    n = len(arrays)
    shapes = [a.shape[1:] for a in arrays]
    return (
        [pltpu.VMEM((n_z, *s), BF16) for s in shapes]
        + [pltpu.VMEM((n_z - 1, *s), BF16) for s in shapes]
        + [pltpu.VMEM((n_z - 1, *s), BF16) for s in shapes]
        + [pltpu.SemaphoreType.DMA((n, n_z))] * 2
        + [pltpu.SemaphoreType.DMA((n, n_z - 1))] * 2
    )


def owner_peers():
    r, e = lax.axis_index("dp"), lax.axis_index("expert")
    n_z = lax.axis_size("expert") // 2
    return [(r, lax.rem(e // 2 + j, n_z) * 2 + e % 2) for j in range(1, n_z)]


def last_sums_kernel(grads, small, grads_out, small_out, *scratch):
    r, e = lax.axis_index("dp"), lax.axis_index("expert")
    z, core = e // 2, e % 2
    n_z = grads.shape[0] // 2
    pair_in, send, recv, psend, precv, zsend, zrecv = scratch[:7]
    first_in, piece, line_in, s1, r1, s2, r2, s3, r3 = scratch[7:]
    begin, middle, finish = owner_sum(
        [grads], [grads_out], [pair_in], [send], [recv], psend, precv, zsend, zrecv
    )
    others = [(m // 2, m % 2) for m in range(1, 8)]
    plane = [(r ^ a, e ^ c) for a, c in others]
    greet(plane + owner_peers())
    begin()
    firsts = []
    for i, (a, c) in enumerate(others):
        copy = remote(
            small.at[(r ^ a) * 2 + (core ^ c)], first_in.at[i], s1.at[i], r1.at[i], plane[i]
        )
        copy.start()
        firsts.append(copy)
    middle()
    for copy in firsts:
        copy.wait()
    mine = r * 2 + core
    value = small[mine]
    for i in range(7):
        value = value + first_in[i]
    piece[0] = value
    seconds = []
    for j in range(1, n_z):
        copy = remote(
            piece.at[0], line_in.at[j - 1], s2.at[j - 1], r2.at[j - 1], owner_peers()[j - 1]
        )
        copy.start()
        seconds.append(copy)
    for copy in seconds:
        copy.wait()
    value = piece[0]
    for j in range(n_z - 1):
        value = value + line_in[j]
    small_out[mine] = value
    thirds = []
    for i, (a, c) in enumerate(others):
        copy = remote(small_out.at[mine], small_out.at[mine], s3.at[i], r3.at[i], plane[i])
        copy.start()
        thirds.append(copy)
    finish()
    for copy in thirds:
        copy.wait()


def last_sums(grads, small):
    n_z = grads.shape[0] // 2
    piece = small.shape[1:]
    return pl.pallas_call(
        last_sums_kernel,
        out_shape=(
            jax.ShapeDtypeStruct(grads.shape[1:], F32),
            jax.ShapeDtypeStruct(small.shape, F32),
        ),
        in_specs=[VMEM_SPEC] * 2,
        out_specs=(VMEM_SPEC,) * 2,
        scratch_shapes=owner_scratch([grads])
        + [
            pltpu.VMEM((7, *piece), F32),
            pltpu.VMEM((1, *piece), F32),
            pltpu.VMEM((n_z - 1, *piece), F32),
            pltpu.SemaphoreType.DMA((7,)),
            pltpu.SemaphoreType.DMA((7,)),
            pltpu.SemaphoreType.DMA((n_z - 1,)),
            pltpu.SemaphoreType.DMA((n_z - 1,)),
            pltpu.SemaphoreType.DMA((7,)),
            pltpu.SemaphoreType.DMA((7,)),
        ],
        compiler_params=params(5),
        name="last_sums",
    )(grads, small)


def line_sum(block, out, pair_in, work, lines, ps, pr, zs, zr):
    r, e = lax.axis_index("dp"), lax.axis_index("expert")
    z, core = e // 2, e % 2
    order = plane_order(z)[::-1]
    right = jnp.minimum(z + 1, 3) * 2 + core
    left = jnp.maximum(z - 1, 0) * 2 + core
    pairs, moves = [], []

    def begin():
        for k in range(4):
            copy = remote(
                block(order[k] * 2 + (1 - core)), pair_in.at[k], ps.at[k], pr.at[k], (r, e ^ 1)
            )
            copy.start()
            pairs.append(copy)

    def move(k, side, cond, to, add):
        b = order[k]
        copy = remote(work.at[k], lines.at[side, b], zs.at[side, k], zr.at[side, b], (r, to))
        moves.append((cond, copy))

        @pl.when(cond)
        def _():
            if add:
                copy.wait_recv()
                value = work[k].astype(F32) + lines[side, b].astype(F32)
                work[k] = value.astype(BF16)
            copy.start()

    def first():
        for k in range(4):
            pairs[k].wait_recv()
            value = block(order[k] * 2 + core)[...].astype(F32) + pair_in[k].astype(F32)
            if k == 3:
                out[...] = value
            else:
                work[k] = value.astype(BF16)
        ends(0)

    def ends(k):
        move(k, 0, z == 0, right, False)
        move(k, 1, z == 3, left, False)

    def inner(k):
        inside = (z > 0) & (z < 3)
        move(k, 0, inside & (order[k] > z), right, True)
        move(k, 1, inside & (order[k] < z), left, True)
        if k < 2:
            ends(k + 1)

    def last():
        for side, cond in ((0, z > 0), (1, z < 3)):

            @pl.when(cond)
            def _():
                at = lines.at[side, z]
                remote(at, at, zs.at[side, 3], zr.at[side, z], (r, e ^ 1)).wait_recv()
                out[...] = out[...] + lines[side, z].astype(F32)

        for copy in pairs:
            copy.wait_send()
        for cond, copy in moves:

            @pl.when(cond)
            def _():
                copy.wait_send()

    return begin, first, inner, last


LINE_SEMS = [
    pltpu.SemaphoreType.DMA((4,)),
    pltpu.SemaphoreType.DMA((4,)),
    pltpu.SemaphoreType.DMA((2, 4)),
    pltpu.SemaphoreType.DMA((2, 4)),
]


def dgrad_line_kernel(
    mine, wq, wk, wv, cols_t, cols, out_part, small, gain,
    normal, q_out, k_out, v_out, out_sum, small_out, gain_out,
    qkv_sum, grads, blocks, dsum, dsend, drecv, opair, owork, olines, qpair, qwork, qlines,
    first_in, piece, line_in, gain_v, gain_in,
    ssem, rsem, bsend, brecv, s1, r1, s2, r2, s3, r3, s4, r4, s5, r5, *sems,
):
    r, e = lax.axis_index("dp"), lax.axis_index("expert")
    z, core = e // 2, e % 2
    rows = mine.shape[0]
    tok = rows // 4
    half = rows // 2
    qg = wq.shape[1] // 4
    kg = wk.shape[1] // 4
    width = wq.shape[0]
    share = width // 8
    peers = [r ^ m for m in PEER_MASKS]
    near, far, diag = r ^ 1, r ^ 2, r ^ 3
    order = (r, near, far, diag)
    out_begin, out_first, out_inner, out_last = line_sum(
        lambda o: out_part.at[o], out_sum, opair, owork, olines, *sems[:4]
    )
    units = [
        line_sum(
            lambda o, p=p: grads.at[o, p], qkv_sum.at[p], qpair.at[i], qwork.at[i], qlines.at[i],
            *(sem.at[i] for sem in sems[4:]),
        )
        for i, p in enumerate(order)
    ]
    line_peers = [(r, lax.rem(z + j, 4) * 2 + core) for j in (1, 2, 3)]
    others = [(m // 2, m % 2) for m in (6, 7, 2, 3, 4, 5, 1)]
    plane = [(r ^ a, e ^ c) for a, c in others]
    owners = [(r, e ^ m) for m in range(1, 8)]
    greet(plane + owners[1:])
    low, high = pl.ds(0, half), pl.ds(half, half)
    first_near = remote(mine.at[low], blocks.at[0, low], ssem.at[0], rsem.at[0], (near, e))
    first_far = remote(mine.at[high], blocks.at[1, high], ssem.at[1], rsem.at[1], (far, e))
    second_near = remote(mine.at[high], blocks.at[0, high], ssem.at[2], rsem.at[2], (near, e))
    second_far = remote(mine.at[low], blocks.at[1, low], ssem.at[3], rsem.at[3], (far, e))
    pass_far = remote(blocks.at[0, low], blocks.at[2, low], ssem.at[4], rsem.at[4], (far, e))
    pass_near = remote(blocks.at[1, high], blocks.at[2, high], ssem.at[5], rsem.at[5], (near, e))
    me = r * 2 + core
    firsts = []
    for i, (a, c) in enumerate(others):
        copy = remote(small.at[(r ^ a) * 2 + (core ^ c)], first_in.at[i], s1.at[i], r1.at[i], plane[i])
        copy.start()
        firsts.append(copy)
    for copy in (first_near, first_far, second_near, second_far):
        copy.start()
    out_begin()
    seconds, thirds = [], []

    def small_second():
        for copy in firsts:
            copy.wait()
        value = small[me]
        for i in range(7):
            value = value + first_in[i]
        piece[0] = value
        for j in range(3):
            copy = remote(piece.at[0], line_in.at[j], s2.at[j], r2.at[j], line_peers[j])
            copy.start()
            seconds.append(copy)

    def small_third():
        for copy in seconds:
            copy.wait()
        small_out[me] = piece[0] + line_in[0] + line_in[1] + line_in[2]
        for i in range(7):
            copy = remote(small_out.at[me], small_out.at[me], s3.at[i], r3.at[i], plane[i])
            copy.start()
            thirds.append(copy)

    def outer(p, src):
        def step(c, carry):
            n = aligned(c, 256)
            value = dot_nn(cols_t[...], src[:, n]).astype(BF16)
            for o in range(8):
                grads[o, p, :, n] = value[o * share : (o + 1) * share]
            return carry

        lax.fori_loop(0, (qg + 2 * kg) // 256, step, 0)

    def inner(p, src, start):
        def chunk(c, carry):
            n = aligned(c, 128)
            value = (
                dot_nt(src[:, :qg], wq[n, aligned(p, qg)])
                + dot_nt(src[:, qg : qg + kg], wk[n, aligned(p, kg)])
                + dot_nt(src[:, qg + kg :], wv[n, aligned(p, kg)])
            )
            if start:
                dsum[:, n] = value
            else:
                dsum[:, n] = dsum[:, n] + value
            return carry

        lax.fori_loop(0, width // 128, chunk, 0)

    def begin(i):
        units[i][0]()

    def first(i):
        units[i][1]()

    def onward(i, k):
        units[i][2](k)

    outer(r, mine)
    begin(0)
    out_first()
    small_second()
    inner(r, mine, True)
    first_near.wait()
    pass_far.start()
    first_far.wait()
    pass_near.start()
    out_inner(0)
    first(0)
    out_inner(1)
    small_third()
    onward(0, 0)
    second_near.wait()
    outer(near, blocks.at[0])
    begin(1)
    second_far.wait()
    outer(far, blocks.at[1])
    begin(2)
    out_inner(2)
    onward(0, 1)
    first(1)
    inner(near, blocks.at[0], False)
    onward(0, 2)
    onward(1, 0)
    first(2)
    inner(far, blocks.at[1], False)
    onward(1, 1)
    pass_far.wait()
    pass_near.wait()
    outer(diag, blocks.at[2])
    begin(3)
    inner(diag, blocks.at[2], False)
    back = []
    for i, p in enumerate(peers):
        dsend[i] = dsum[aligned(p, tok), :].astype(BF16)
        copy = remote(dsend.at[i], drecv.at[i], bsend.at[i], brecv.at[i], (p, e))
        copy.start()
        back.append(copy)
    scale = 1.0 / gain[:, aligned(r, width)]
    gain_v[...] = jnp.broadcast_to(
        jnp.sum(dsum[...] * cols[...].astype(F32), axis=0, keepdims=True) * scale, gain_v.shape
    )
    fourths = []
    for i in range(7):
        copy = remote(gain_v, gain_in.at[i], s4.at[i], r4.at[i], owners[i])
        copy.start()
        fourths.append(copy)
    onward(1, 2)
    onward(2, 0)
    first(3)
    onward(2, 1)
    for copy in fourths:
        copy.wait()
    value = gain_v[...]
    for i in range(7):
        value = value + gain_in[i]
    gain_out[r] = value
    fifths = []
    for i, p in enumerate(peers):
        copy = remote(gain_out.at[r], gain_out.at[r], s5.at[i], r5.at[i], (p, e))
        copy.start()
        fifths.append(copy)
    onward(3, 0)
    normal[:, aligned(r, width)] = dsum[aligned(r, tok), :]
    for i, p in enumerate(peers):
        back[i].wait()
        normal[:, aligned(p, width)] = drecv[i].astype(F32)
    onward(2, 2)
    onward(3, 1)
    out_last()

    def close(i):
        p = order[i]
        units[i][3]()
        q_out[:, aligned(p, qg)] = qkv_sum[p, :, :qg]
        k_out[:, aligned(p, kg)] = qkv_sum[p, :, qg : qg + kg]
        v_out[:, aligned(p, kg)] = qkv_sum[p, :, qg + kg :]

    close(0)
    close(1)
    onward(3, 2)
    close(2)
    close(3)
    for copy in fifths + thirds:
        copy.wait()


def grad_qkv_line(mine, wq, wk, wv, cols_t, cols, out_part, small, gain):
    rows, group = mine.shape
    tok = rows // 4
    width = wq.shape[0]
    piece = (width // 8, group)
    out_piece = out_part.shape[1:]
    small_piece = small.shape[1:]
    return pl.pallas_call(
        dgrad_line_kernel,
        out_shape=(
            jax.ShapeDtypeStruct((tok, 4 * width), F32),
            jax.ShapeDtypeStruct((width // 8, wq.shape[1]), F32),
            jax.ShapeDtypeStruct((width // 8, wk.shape[1]), F32),
            jax.ShapeDtypeStruct((width // 8, wv.shape[1]), F32),
            jax.ShapeDtypeStruct(out_piece, F32),
            jax.ShapeDtypeStruct(small.shape, F32),
            jax.ShapeDtypeStruct((4, 8, width), F32),
        ),
        in_specs=[VMEM_SPEC] * 9,
        out_specs=(VMEM_SPEC,) * 7,
        scratch_shapes=[
            pltpu.VMEM((4, *piece), F32),
            pltpu.VMEM((8, 4, *piece), BF16),
            pltpu.VMEM((3, rows, group), BF16),
            pltpu.VMEM((rows, width), F32),
            pltpu.VMEM((3, tok, width), BF16),
            pltpu.VMEM((3, tok, width), BF16),
            pltpu.VMEM((4, *out_piece), BF16),
            pltpu.VMEM((3, *out_piece), BF16),
            pltpu.VMEM((2, 4, *out_piece), BF16),
            pltpu.VMEM((4, 4, *piece), BF16),
            pltpu.VMEM((4, 3, *piece), BF16),
            pltpu.VMEM((4, 2, 4, *piece), BF16),
            pltpu.VMEM((7, *small_piece), F32),
            pltpu.VMEM((1, *small_piece), F32),
            pltpu.VMEM((3, *small_piece), F32),
            pltpu.VMEM((8, width), F32),
            pltpu.VMEM((7, 8, width), F32),
            pltpu.SemaphoreType.DMA((6,)),
            pltpu.SemaphoreType.DMA((6,)),
        ]
        + [pltpu.SemaphoreType.DMA((n,)) for n in (3, 3, 7, 7, 3, 3, 7, 7, 7, 7, 3, 3)]
        + LINE_SEMS
        + [
            pltpu.SemaphoreType.DMA((4, 4)),
            pltpu.SemaphoreType.DMA((4, 4)),
            pltpu.SemaphoreType.DMA((4, 2, 4)),
            pltpu.SemaphoreType.DMA((4, 2, 4)),
        ],
        compiler_params=params(10),
        name="dqkv_line_exchange",
    )(mine, wq, wk, wv, cols_t, cols, out_part, small, gain)


def masks_of(block, own_length, slots, prompt_block, prompt_len, column, keys):
    slot = lax.broadcasted_iota(jnp.int32, (slots, keys), 0)
    key = lax.broadcasted_iota(jnp.int32, (slots, keys), 1)
    is_prompt = slot < prompt_block
    position = (column * 4 + block) * prompt_block + slot
    sees_prompt = (key < prompt_len) & (jnp.logical_not(is_prompt) | (key <= position))
    cont = key - prompt_len
    sees_cont = (
        (key >= prompt_len)
        & jnp.logical_not(is_prompt)
        & (cont <= slot - prompt_block)
        & (cont < own_length)
    )
    return sees_prompt | sees_cont


def attention_fwd_kernel(prompt_len, lengths, lin, gain, cos, sin, keys, values, queries, attn):
    block = pl.program_id(0)
    slots = lin.shape[0]
    head = gain.shape[1]
    allowed = masks_of(
        block, lengths[block], slots, slots - CMAX, prompt_len, lengths[4], keys.shape[1]
    )
    scale = head ** (-0.5)
    k, v = keys[0], values[0]
    c, s, g = cos[0], sin[0], gain[...]
    for h in range(lin.shape[1] // head):
        part = slice(h * head, (h + 1) * head)
        x = lin[:, part]
        x = x * lax.rsqrt(jnp.mean(x * x, axis=-1, keepdims=True) + norm_eps) * g
        q = (x * c + pltpu.roll(x, head // 2, 1) * s).astype(BF16)
        queries[:, part] = q
        score = jnp.where(allowed, dot_nt(q, k) * scale, -jnp.inf)
        peak = jnp.max(score, axis=-1, keepdims=True)
        exponent = jnp.exp(score - peak)
        low = (exponent * (1.0 / jnp.sum(exponent, axis=-1, keepdims=True))).astype(BF16)
        attn[:, part] = dot_nn(low, v).astype(BF16)


def attention_fwd(lengths, lin, gain, cos, sin, keys, values, prompt_len):
    blocks, total_keys, head = keys.shape
    slots = lin.shape[0] // blocks
    width = lin.shape[1] - 2 * head
    row = pl.BlockSpec((slots, width), lambda i, *_: (i, 0))
    table = pl.BlockSpec((1, slots, head), lambda i, *_: (i, 0, 0))
    kv = pl.BlockSpec((1, total_keys, head), lambda i, *_: (i, 0, 0))
    one = pl.BlockSpec((1, head), lambda i, *_: (0, 0))
    return pl.pallas_call(
        functools.partial(attention_fwd_kernel, prompt_len),
        grid_spec=pltpu.PrefetchScalarGridSpec(
            num_scalar_prefetch=1,
            grid=(blocks,),
            in_specs=[row, one, table, table, kv, kv],
            out_specs=[row, row],
        ),
        out_shape=(
            jax.ShapeDtypeStruct((lin.shape[0], width), BF16),
            jax.ShapeDtypeStruct((lin.shape[0], width), BF16),
        ),
        compiler_params=params(),
        name="attention_fwd",
    )(lengths, lin, gain, cos, sin, keys, values)


def attention_bwd_kernel(
    prompt_len, lengths, lin, queries, d_attn, gain, cos, sin, keys, values, attn_t, d_branch,
    d_lin, d_keys, d_values, d_gain, out_part,
):
    block = pl.program_id(0)
    slots = lin.shape[0]
    head = gain.shape[1]
    allowed = masks_of(
        block, lengths[block], slots, slots - CMAX, prompt_len, lengths[4], keys.shape[1]
    )
    scale = head ** (-0.5)
    k, v = keys[0], values[0]
    c, s, g = cos[0], sin[0], gain[...]
    key_total = jnp.zeros(k.shape, F32)
    value_total = jnp.zeros(v.shape, F32)
    gain_total = jnp.zeros((8, head), F32)
    for h in range(lin.shape[1] // head):
        part = slice(h * head, (h + 1) * head)
        q = queries[:, part]
        score = jnp.where(allowed, dot_nt(q, k) * scale, -jnp.inf)
        peak = jnp.max(score, axis=-1, keepdims=True)
        exponent = jnp.exp(score - peak)
        probs = exponent * (1.0 / jnp.sum(exponent, axis=-1, keepdims=True))
        d_out = d_attn[:, part]
        d_probs = dot_nt(d_out, v)
        inner = jnp.sum(probs * d_probs, axis=-1, keepdims=True)
        d_score = (probs * (d_probs - inner)).astype(BF16)
        key_total = key_total + dot_tn(d_score, q)
        value_total = value_total + dot_tn(probs.astype(BF16), d_out)
        d_q = dot_nn(d_score, k) * scale
        turned = d_q * c + pltpu.roll(d_q * s, head // 2, 1)
        x = lin[:, part]
        inverse = lax.rsqrt(jnp.mean(x * x, axis=-1, keepdims=True) + norm_eps)
        unit = x * inverse
        pairs = turned * unit
        for j in range(slots // 8):
            gain_total = gain_total + pairs[j * 8 : (j + 1) * 8]
        weighted = turned * g
        d_lin[:, part] = (
            inverse * (weighted - unit * jnp.mean(weighted * unit, axis=-1, keepdims=True))
        ).astype(BF16)
        if h % 4 == 3:
            n = slice(h // 4 * 256, h // 4 * 256 + 256)
            out_part[:, n] = dot_nn(attn_t[...], d_branch[:, n]).astype(BF16)
    d_keys[0] = key_total * scale
    d_values[0] = value_total
    d_gain[0] = gain_total


def attention_bwd(
    lengths, lin, queries, d_attn, gain, cos, sin, keys, values, attn_t, d_branch, prompt_len
):
    blocks, total_keys, head = keys.shape
    slots = lin.shape[0] // blocks
    width = lin.shape[1] - 2 * head
    row = pl.BlockSpec((slots, width), lambda i, *_: (i, 0))
    table = pl.BlockSpec((1, slots, head), lambda i, *_: (i, 0, 0))
    kv = pl.BlockSpec((1, total_keys, head), lambda i, *_: (i, 0, 0))
    step = d_branch.shape[1] // blocks
    one = pl.BlockSpec((1, head), lambda i, *_: (0, 0))
    return pl.pallas_call(
        functools.partial(attention_bwd_kernel, prompt_len),
        grid_spec=pltpu.PrefetchScalarGridSpec(
            num_scalar_prefetch=1,
            grid=(blocks,),
            in_specs=[row, row, row, one, table, table, kv, kv]
            + [
                pl.BlockSpec(attn_t.shape, lambda i, *_: (0, 0)),
                pl.BlockSpec((d_branch.shape[0], step), lambda i, *_: (0, i)),
            ],
            out_specs=[
                row,
                kv,
                kv,
                pl.BlockSpec((1, 8, head), lambda i, *_: (i, 0, 0)),
                pl.BlockSpec((attn_t.shape[0], step), lambda i, *_: (0, i)),
            ],
        ),
        out_shape=(
            jax.ShapeDtypeStruct((lin.shape[0], width), BF16),
            jax.ShapeDtypeStruct(keys.shape, F32),
            jax.ShapeDtypeStruct(values.shape, F32),
            jax.ShapeDtypeStruct((blocks, 8, head), F32),
            jax.ShapeDtypeStruct((attn_t.shape[0], d_branch.shape[1]), BF16),
        ),
        compiler_params=params(),
        name="attention_bwd",
    )(lengths, lin, queries, d_attn, gain, cos, sin, keys, values, attn_t, d_branch)


def partner(shard, axis, bit):
    return lax.ppermute(shard, axis, [(i, i ^ 1 << bit) for i in range(lax.axis_size(axis))])


def root_mean_scale(value_rows, gain_vec):
    return (
        value_rows
        * lax.rsqrt(jnp.mean(value_rows * value_rows, axis=-1, keepdims=True) + norm_eps)
        * gain_vec
    )


def contract(left_side, right_side, left_dim, right_dim):
    return lax.dot_general(
        left_side,
        right_side,
        (((left_dim,), (right_dim,)), ((), ())),
        preferred_element_type=F32,
    )


def plane_order(z):
    upper, odd = z // 2, z % 2
    return [z, z + 1 - 2 * upper, 2 + upper - 2 * odd, 3 - 3 * upper]


def world(with_diag):
    r, e = lax.axis_index("dp"), lax.axis_index("expert")
    z, core = e // 2, e % 2
    near, far = r ^ 1, r ^ 2
    devices = [(near, e), (far, e), (r, e ^ 1)]
    devices += [(r, lax.rem(z + j, 4) * 2 + core) for j in (1, 2, 3)]
    return r, e, z, core, near, far, devices


def gather_world(mine, buf, zs, zr, ps, pr, ds, dr, before, group, done):
    r, e, z, core, near, far, greeted = world(True)
    half = mine.shape[0] // 2
    low, high = pl.ds(0, half), pl.ds(half, half)
    order = plane_order(z)
    greet(greeted)

    def slot(q, b, c):
        return q * 8 + b * 2 + c

    buf[slot(r, z, core)] = mine[...]
    diag = r ^ 3
    plane, pairs, lines = {}, {}, []

    def hand(k, i, q):
        at = slot(q, order[k], core)
        copy = remote(buf.at[at], buf.at[at], ds.at[k, i], dr.at[k, i], (r, e ^ 1))
        copy.start()
        pairs[k, i] = copy

    def issue(k):
        b = order[k]
        at = slot(r, b, core)
        for side, cond, to in (
            (0, (b <= z) & (z < 3), jnp.minimum(z + 1, 3)),
            (1, (b >= z) & (z > 0), jnp.maximum(z - 1, 0)),
        ):
            copy = remote(buf.at[at], buf.at[at], zs.at[k, side], zr.at[b], (r, to * 2 + core))
            lines.append((cond, copy))

            @pl.when(cond)
            def _():
                copy.start()

        mine_at, near_at, far_at = at, slot(near, b, core), slot(far, b, core)
        for i, (src, part, p) in enumerate(
            (
                (mine_at, low, near),
                (mine_at, high, far),
                (mine_at, high, near),
                (mine_at, low, far),
                (near_at, low, far),
                (far_at, high, near),
            )
        ):
            plane[k, i] = remote(
                buf.at[src, part], buf.at[src, part], ps.at[k, i], pr.at[k, i], (p, e)
            )
        for i in range(4):
            plane[k, i].start()
        hand(k, 0, r)

    def line_wait(k):
        b = order[k]
        at = slot(r, b, core)
        remote(buf.at[at], buf.at[at], zs.at[k, 0], zr.at[b], (r, e ^ 1)).wait_recv()
        issue(k)

    def passes(k):
        plane[k, 0].wait_recv()
        plane[k, 4].start()
        plane[k, 1].wait_recv()
        plane[k, 5].start()

    def finish(k):
        plane[k, 2].wait_recv()
        hand(k, 1, near)
        plane[k, 3].wait_recv()
        hand(k, 2, far)

    def corner(k):
        plane[k, 4].wait_recv()
        plane[k, 5].wait_recv()
        hand(k, 3, diag)

    who = (r, near, far, diag)

    def ready(k):
        before(k)
        for i in range(4):
            pairs[k, i].wait_recv()
        group(k, [(k * 4 + i, who[i] * 8 + order[k] * 2) for i in range(4)])

    issue(0)
    passes(0)
    line_wait(1)
    finish(0)
    passes(1)
    line_wait(2)
    corner(0)
    finish(1)
    ready(0)
    passes(2)
    line_wait(3)
    corner(1)
    finish(2)
    ready(1)
    passes(3)
    corner(2)
    finish(3)
    ready(2)
    corner(3)
    ready(3)
    done()
    for copy in plane.values():
        copy.wait_send()
    for copy in pairs.values():
        copy.wait_send()
    for cond, copy in lines:

        @pl.when(cond)
        def _():
            copy.wait_send()


def group_rows(k, room):
    return pl.ds(k * 4 * room, 4 * room)


GATHER_SEMS = [
    pltpu.SemaphoreType.DMA((4, 2)),
    pltpu.SemaphoreType.DMA((4,)),
    pltpu.SemaphoreType.DMA((4, 6)),
    pltpu.SemaphoreType.DMA((4, 6)),
    pltpu.SemaphoreType.DMA((4, 4)),
    pltpu.SemaphoreType.DMA((4, 4)),
]


def selector(row, room):
    ids = lax.broadcasted_iota(jnp.int32, (room, row.shape[1]), 0).astype(F32)
    return jnp.where(ids == row, 1.0, 0.0).astype(BF16)


def start_all(copies):
    for copy in copies:
        copy.start()
    return copies


def wait_all(copies):
    for copy in copies:
        copy.wait()
    copies.clear()


def experts_fwd_kernel(
    capacity, mine, wg, wu, wd, pos, x_out, y_out, g_out, u_out, o_out, hid_out, gate_out,
    buf, wg_v, wu_v, wd_v, x_v, y_v, g_v, u_v, o_v, hid_v, gate_v, local, *sems,
):
    model = wg.shape[0]
    rows_in = mine.shape[0]
    room = x_v.shape[0] // 4
    me = lax.axis_index("dp") * 8 + lax.axis_index("expert")
    loads = start_all(
        [
            pltpu.make_async_copy(a, b, local.at[0, i])
            for i, (a, b) in enumerate(((wg, wg_v), (wu, wu_v), (wd, wd_v)))
        ]
    )
    leaving = {g: [] for g in range(4)}

    def leave(g, pairs):
        kept = group_rows(g, room)
        leaving[g].extend(
            start_all(
                [
                    pltpu.make_async_copy(v, o.at[kept], local.at[g % 2, i])
                    for i, v, o in pairs
                ]
            )
        )

    def before(g):
        wait_all(loads)
        if g > 0:
            wait_all(leaving[g - 1])

    upto = jnp.where(
        lax.broadcasted_iota(jnp.int32, (rows_in, rows_in), 0)
        <= lax.broadcasted_iota(jnp.int32, (rows_in, rows_in), 1),
        1.0,
        0.0,
    ).astype(BF16)
    is_me = jnp.where(lax.broadcasted_iota(jnp.int32, (16, 128), 1) == me, 1.0, 0.0).astype(BF16)

    def pick(at, s, start):
        rows = pl.ds(start, room)
        sels = []
        for c in range(2):
            named = jnp.where(dot_nt(is_me, buf[s + c, :, model:]) > 0.0, 1.0, 0.0)
            place = (dot_nn(named.astype(BF16), upto) + (c * capacity)) * named - 1.0
            pos[at * 2 + c] = place[:1]
            sels.append(selector(place[:1], room))
        for c in range(4):
            n = slice(c * model // 4, (c + 1) * model // 4)
            x_v[rows, n] = (dot_nn(sels[0], buf[s, :, n]) + dot_nn(sels[1], buf[s + 1, :, n])).astype(BF16)
        extra = dot_nn(sels[0], buf[s, :, model:]) + dot_nn(sels[1], buf[s + 1, :, model:])
        lane = lax.broadcasted_iota(jnp.int32, extra.shape, 1)
        hit = (lane == me) | (lane == me + 64)
        gate = jnp.sum(jnp.where(hit, extra, 0.0), axis=-1, keepdims=True)
        gate_v[rows, :] = jnp.broadcast_to(gate, extra.shape)

    def group(g, blocks):
        for j, (at, s) in enumerate(blocks):
            pick(at, s, j * room)
        leave(g, ((0, x_v, x_out), (1, gate_v, gate_out)))

        def first(c, carry):
            n = aligned(c, 256)
            x = x_v[...]
            gates = dot_nn(x, wg_v[:, n])
            u = dot_nn(x, wu_v[:, n])
            g_v[:, n] = gates.astype(BF16)
            u_v[:, n] = u.astype(BF16)
            hid_v[:, n] = (gates / (1.0 + jnp.exp(-gates)) * u).astype(BF16)
            return carry

        lax.fori_loop(0, wg.shape[1] // 256, first, 0)
        leave(g, ((2, g_v, g_out), (3, u_v, u_out), (4, hid_v, hid_out)))

        def second(c, carry):
            n = aligned(c, 256)
            o = dot_nn(hid_v[...], wd_v[:, n]).astype(BF16)
            o_v[:, n] = o
            y_v[:, n] = (o.astype(F32) * gate_v[:, :1]).astype(BF16)
            return carry

        lax.fori_loop(0, model // 256, second, 0)
        leave(g, ((5, o_v, o_out), (6, y_v, y_out)))

    def done():
        for copies in leaving.values():
            wait_all(copies)

    gather_world(mine, buf, *sems, before, group, done)


def experts_fwd(mine, wg, wu, wd, capacity, room):
    rows, width = mine.shape
    model, ff = wg.shape
    group = 4 * room
    wide = jax.ShapeDtypeStruct((16 * room, model), BF16)
    thin = jax.ShapeDtypeStruct((16 * room, ff), BF16)
    pos, x, y, g, u, o, hidden, gates = pl.pallas_call(
        functools.partial(experts_fwd_kernel, capacity),
        out_shape=(
            jax.ShapeDtypeStruct((32, 1, rows), F32),
            wide,
            wide,
            thin,
            thin,
            wide,
            thin,
            jax.ShapeDtypeStruct((16 * room, 128), F32),
        ),
        in_specs=[VMEM_SPEC, ANY_SPEC, ANY_SPEC, ANY_SPEC],
        out_specs=(VMEM_SPEC,) + (ANY_SPEC,) * 7,
        scratch_shapes=[
            pltpu.VMEM((32, rows, width), BF16),
            pltpu.VMEM((model, ff), BF16),
            pltpu.VMEM((model, ff), BF16),
            pltpu.VMEM((ff, model), BF16),
            pltpu.VMEM((group, model), BF16),
            pltpu.VMEM((group, model), BF16),
            pltpu.VMEM((group, ff), BF16),
            pltpu.VMEM((group, ff), BF16),
            pltpu.VMEM((group, model), BF16),
            pltpu.VMEM((group, ff), BF16),
            pltpu.VMEM((group, 128), F32),
            pltpu.SemaphoreType.DMA((2, 7)),
        ]
        + GATHER_SEMS,
        compiler_params=params(6),
        name="experts_fwd",
    )(mine, wg, wu, wd)
    return pos, x, y, (g, u, o, hidden, gates)


def experts_bwd_kernel(
    mine, pos, g_in, u_in, o_in, gate_in, wg, wu, wd, y_out, d_copy_out, dg_out, du_out,
    buf, wg_v, wu_v, wd_v, g_v, u_v, o_v, gate_v, y_v, d_copy_v, dg_v, du_v,
    local, ins, *sems,
):
    model, ff = wg.shape
    room = d_copy_v.shape[0] // 4
    me = lax.axis_index("dp") * 8 + lax.axis_index("expert")
    loads = start_all(
        [
            pltpu.make_async_copy(a, b, local.at[0, i])
            for i, (a, b) in enumerate(((wg, wg_v), (wu, wu_v), (wd, wd_v)))
        ]
    )
    leaving, coming = {g: [] for g in range(4)}, {}

    def fetch(g):
        kept = group_rows(g, room)
        coming[g] = start_all(
            [
                pltpu.make_async_copy(a.at[kept], v.at[g % 2], ins.at[g % 2, i])
                for i, (a, v) in enumerate(
                    ((g_in, g_v), (u_in, u_v), (o_in, o_v), (gate_in, gate_v))
                )
            ]
        )

    fetch(0)

    def leave(g, pairs):
        kept = group_rows(g, room)
        leaving[g].extend(
            start_all(
                [
                    pltpu.make_async_copy(v, o.at[kept], local.at[g % 2, i])
                    for i, v, o in pairs
                ]
            )
        )

    def before(g):
        wait_all(loads)
        wait_all(coming[g])
        if g + 1 < 4:
            fetch(g + 1)
        if g > 0:
            wait_all(leaving[g - 1])

    def pick(slot, at, s, start):
        rows = pl.ds(start, room)
        sels = [selector(pos[at * 2 + c], room) for c in range(2)]
        gate = gate_v[slot, rows, :1]
        inner = jnp.zeros((room, 1), F32)
        for c in range(4):
            n = slice(c * model // 4, (c + 1) * model // 4)
            picked = dot_nn(sels[0], buf[s, :, n]) + dot_nn(sels[1], buf[s + 1, :, n])
            d_copy_v[rows, n] = (gate * picked).astype(BF16)
            inner = inner + jnp.sum(picked * o_v[slot, rows, n].astype(F32), axis=-1, keepdims=True)
        top = inner.astype(BF16).astype(F32)
        rest = inner - top
        lane = lax.broadcasted_iota(jnp.int32, (room, 128), 1)
        extra = jnp.where(lane == me, top, 0.0) + jnp.where(lane == me + 64, rest, 0.0)
        y_v[rows, model:] = extra.astype(BF16)

    def group(g, blocks):
        slot = g % 2
        for j, (at, s) in enumerate(blocks):
            pick(slot, at, s, j * room)
        leave(g, ((0, d_copy_v, d_copy_out),))

        def third(c, carry):
            n = aligned(c, 256)
            d_hidden = dot_nt(d_copy_v[...], wd_v[n, :])
            gates, u = g_v[slot, :, n].astype(F32), u_v[slot, :, n].astype(F32)
            s = 1.0 / (1.0 + jnp.exp(-gates))
            dg_v[:, n] = (d_hidden * u * s * (1.0 + gates * (1.0 - s))).astype(BF16)
            du_v[:, n] = (d_hidden * gates * s).astype(BF16)
            return carry

        lax.fori_loop(0, ff // 256, third, 0)
        leave(g, ((1, dg_v, dg_out), (2, du_v, du_out)))

        def fourth(c, carry):
            n = aligned(c, 256)
            y_v[:, n] = (
                dot_nt(dg_v[...], wg_v[n, :]) + dot_nt(du_v[...], wu_v[n, :])
            ).astype(BF16)
            return carry

        lax.fori_loop(0, model // 256, fourth, 0)
        leave(g, ((3, y_v, y_out),))

    def done():
        for copies in leaving.values():
            wait_all(copies)

    gather_world(mine, buf, *sems, before, group, done)


def experts_bwd(mine, pos, kept, wg, wu, wd, room):
    rows, width = mine.shape
    model, ff = wg.shape
    group = 4 * room
    return pl.pallas_call(
        experts_bwd_kernel,
        out_shape=(
            jax.ShapeDtypeStruct((16 * room, model + 128), BF16),
            jax.ShapeDtypeStruct((16 * room, model), BF16),
            jax.ShapeDtypeStruct((16 * room, ff), BF16),
            jax.ShapeDtypeStruct((16 * room, ff), BF16),
        ),
        in_specs=[VMEM_SPEC, VMEM_SPEC] + [ANY_SPEC] * 7,
        out_specs=(ANY_SPEC,) * 4,
        scratch_shapes=[
            pltpu.VMEM((32, rows, width), BF16),
            pltpu.VMEM((model, ff), BF16),
            pltpu.VMEM((model, ff), BF16),
            pltpu.VMEM((ff, model), BF16),
            pltpu.VMEM((2, group, ff), BF16),
            pltpu.VMEM((2, group, ff), BF16),
            pltpu.VMEM((2, group, model), BF16),
            pltpu.VMEM((2, group, 128), F32),
            pltpu.VMEM((group, model + 128), BF16),
            pltpu.VMEM((group, model), BF16),
            pltpu.VMEM((group, ff), BF16),
            pltpu.VMEM((group, ff), BF16),
            pltpu.SemaphoreType.DMA((2, 4)),
            pltpu.SemaphoreType.DMA((2, 4)),
        ]
        + GATHER_SEMS,
        compiler_params=params(7),
        name="experts_bwd",
    )(mine, pos, *kept, wg, wu, wd)


def sum_world_kernel(
    y, pos, out, psend, pair, half_near, half_far, full_near, full_far, lines,
    ds, dr, hs, hr, fs, fr, zs, zr,
):
    r, e, z, core, near, far, greeted = world(True)
    rows, width = out.shape
    room = y.shape[1]
    half = rows // 2
    low, high = pl.ds(0, half), pl.ds(half, half)
    order = plane_order(z)[::-1]
    body_width = width // 512 * 512
    greet(greeted)

    def for_columns(fn):
        def step(c, carry):
            fn(aligned(c, 512))
            return carry

        lax.fori_loop(0, body_width // 512, step, 0)
        if width > body_width:
            fn(pl.ds(body_width, width - body_width))

    def scattered(sel, k, i, n):
        return dot_tn(sel, y[(3 - k) * 4 + i, :, n])

    def select(k, i, c):
        return selector(pos[((3 - k) * 4 + i) * 2 + c], room)

    pairs, halves, fulls, moves = {}, {}, {}, []

    def stage_a(k):
        for i in (3, 1, 2, 0):
            at = k * 4 + i
            sel = select(k, i, 1 - core)

            def fill(n):
                psend[at, :, n] = scattered(sel, k, i, n).astype(BF16)

            for_columns(fill)
            copy = remote(psend.at[at], pair.at[at], ds.at[at], dr.at[at], (r, e ^ 1))
            copy.start()
            pairs[at] = copy
        for i in (3, 1, 2, 0):
            at = k * 4 + i
            sel = select(k, i, core)
            pairs[at].wait_recv()

            def add(n):
                value = scattered(sel, k, i, n) + pair[at, :, n].astype(F32)
                pair[at, :, n] = value.astype(BF16)

            for_columns(add)
            if i == 3:
                for side, (part, dst, p) in enumerate(
                    ((low, half_near, near), (high, half_far, far))
                ):
                    copy = remote(
                        pair.at[at, part], dst.at[k], hs.at[k, side], hr.at[k, side], (p, e)
                    )
                    copy.start()
                    halves[k, side] = copy

    def stage_b(k):
        for side, (i, part, src, dst, p) in enumerate(
            (
                (2, low, half_near, full_far, far),
                (1, high, half_far, full_near, near),
            )
        ):
            at = k * 4 + i
            halves[k, side].wait_recv()

            def add(n):
                value = pair[at, part, n].astype(F32) + src[k, :, n].astype(F32)
                pair[at, part, n] = value.astype(BF16)

            for_columns(add)
            copy = remote(pair.at[at], dst.at[k], fs.at[k, side], fr.at[k, side], (p, e))
            copy.start()
            fulls[k, side] = copy

    def stage_c(k):
        b = order[k]
        at = k * 4
        fulls[k, 0].wait_recv()
        fulls[k, 1].wait_recv()

        def add(n):
            out[:, n] = (
                pair[at, :, n].astype(F32)
                + full_near[k, :, n].astype(F32)
                + full_far[k, :, n].astype(F32)
            )

        for_columns(add)
        for side, cond in ((0, (b >= z) & (z > 0)), (1, (b <= z) & (z < 3))):

            @pl.when(cond)
            def _():
                remote(
                    lines.at[side, b], lines.at[side, b], zs.at[side, k], zr.at[side, b], (r, e ^ 1)
                ).wait_recv()

                def more(n):
                    out[:, n] = out[:, n] + lines[side, b, :, n].astype(F32)

                for_columns(more)

        if k < 3:

            def keep(n):
                pair[at, :, n] = out[:, n].astype(BF16)

            for_columns(keep)
            for side, cond, to in (
                (0, b > z, jnp.minimum(z + 1, 3)),
                (1, b < z, jnp.maximum(z - 1, 0)),
            ):
                copy = remote(
                    pair.at[at], lines.at[side, b], zs.at[side, k], zr.at[side, b], (r, to * 2 + core)
                )
                moves.append((cond, copy))

                @pl.when(cond)
                def _():
                    copy.start()

    stage_a(0)
    stage_a(1)
    stage_b(0)
    stage_a(2)
    stage_b(1)
    stage_c(0)
    stage_a(3)
    stage_b(2)
    stage_c(1)
    stage_b(3)
    stage_c(2)
    stage_c(3)
    for copies in (pairs, halves, fulls):
        for copy in copies.values():
            copy.wait_send()
    for cond, copy in moves:

        @pl.when(cond)
        def _():
            copy.wait_send()


def sum_world(y, pos, rows, collective_id):
    width = y.shape[-1]

    def blocks(n, size):
        return pltpu.VMEM((n, size, width), BF16)

    return pl.pallas_call(
        sum_world_kernel,
        out_shape=jax.ShapeDtypeStruct((rows, width), F32),
        in_specs=[VMEM_SPEC, VMEM_SPEC],
        out_specs=VMEM_SPEC,
        scratch_shapes=[
            blocks(16, rows),
            blocks(16, rows),
            blocks(4, rows // 2),
            blocks(4, rows // 2),
            blocks(4, rows),
            blocks(4, rows),
            pltpu.VMEM((2, 4, rows, width), BF16),
            pltpu.SemaphoreType.DMA((16,)),
            pltpu.SemaphoreType.DMA((16,)),
            pltpu.SemaphoreType.DMA((4, 2)),
            pltpu.SemaphoreType.DMA((4, 2)),
            pltpu.SemaphoreType.DMA((4, 2)),
            pltpu.SemaphoreType.DMA((4, 2)),
            pltpu.SemaphoreType.DMA((2, 4)),
            pltpu.SemaphoreType.DMA((2, 4)),
        ],
        compiler_params=params(collective_id),
        name="sum_world",
    )(y, pos)


def expert_grads_kernel(x, d_gate, d_up, hidden, d_copy, gate_grad, up_grad, down_grad, hidden_t):
    @pl.when(pl.program_id(0) == 0)
    def _():
        hidden_t[...] = hidden[...].T

    rows = x[...].T
    gate_grad[...] = dot_nn(rows, d_gate[...])
    up_grad[...] = dot_nn(rows, d_up[...])
    down_grad[...] = dot_nn(hidden_t[...], d_copy[...])


def expert_grads(x, d_gate, d_up, hidden, d_copy):
    slots, model = x.shape
    ff = hidden.shape[1]
    step = 256
    whole = pl.BlockSpec((slots, ff), lambda i: (0, 0))
    columns = pl.BlockSpec((slots, step), lambda i: (0, i))
    return pl.pallas_call(
        expert_grads_kernel,
        grid=(model // step,),
        in_specs=[columns, whole, whole, whole, columns],
        out_specs=[
            pl.BlockSpec((step, ff), lambda i: (i, 0)),
            pl.BlockSpec((step, ff), lambda i: (i, 0)),
            pl.BlockSpec((ff, step), lambda i: (0, i)),
        ],
        out_shape=(
            jax.ShapeDtypeStruct((model, ff), F32),
            jax.ShapeDtypeStruct((model, ff), F32),
            jax.ShapeDtypeStruct((ff, model), F32),
        ),
        scratch_shapes=[pltpu.VMEM((ff, slots), BF16)],
        compiler_params=params(),
        name="expert_grads",
    )(x, d_gate, d_up, hidden, d_copy)


def experts_by_all_to_all(
    mixed, state, teacher, routes, valid_slot, valid_count, router_weight, gate_weight, up_weight, down_weight,
    devices, capacity, slots_all,
):
    tok_dev, model_width = mixed.shape
    top_count = routes.shape[1]
    ffn_width = gate_weight.shape[2]
    logits = jnp.dot(mixed, router_weight, preferred_element_type=jnp.float32)
    gates = jax.nn.softmax(jnp.take_along_axis(logits, routes, axis=1), axis=-1)
    rows_total = tok_dev * top_count
    expert_ids = routes.reshape(rows_total)
    live_rows = jnp.repeat(valid_slot, top_count)
    expert_range = jnp.arange(devices, dtype=jnp.int32)
    hit_table = ((expert_ids[:, None] == expert_range[None, :]) & live_rows[:, None]).astype(
        jnp.int32
    )
    earlier = jnp.cumsum(hit_table, axis=0) - hit_table
    position_in = jnp.sum(earlier * hit_table, axis=1)
    slot_index = jnp.where(live_rows, expert_ids * capacity + position_in, devices * capacity)
    row_of_slot = (
        jnp.full((devices * capacity + 1,), rows_total, jnp.int32)
        .at[slot_index]
        .set(jnp.arange(rows_total, dtype=jnp.int32))[: devices * capacity]
    )
    token_of_slot = jnp.where(row_of_slot < rows_total, row_of_slot // top_count, tok_dev)
    mixed_pad = jnp.concatenate([mixed, jnp.zeros((1, model_width), jnp.bfloat16)], axis=0)
    send_rows = mixed_pad[token_of_slot].reshape(devices, capacity, model_width)
    arrived = lax.all_to_all(send_rows, ("dp", "expert"), split_axis=0, concat_axis=0, tiled=True)
    sources = arrived.shape[0]
    items = arrived.shape[1]
    flat_in = arrived.reshape(sources * items, model_width)
    gate_pre = jnp.dot(flat_in, gate_weight[0], preferred_element_type=jnp.float32)
    up_pre = jnp.dot(flat_in, up_weight[0], preferred_element_type=jnp.float32)
    hidden_units = (jax.nn.silu(gate_pre) * up_pre).astype(jnp.bfloat16)
    produced = jnp.dot(hidden_units, down_weight[0], preferred_element_type=jnp.float32).astype(
        jnp.bfloat16
    )
    produced, gate_pre, up_pre, hidden_units, arrived = (
        produced.reshape(sources, items, model_width),
        gate_pre.reshape(sources, items, ffn_width),
        up_pre.reshape(sources, items, ffn_width),
        hidden_units.reshape(sources, items, ffn_width),
        arrived,
    )
    returned = lax.all_to_all(produced, ("dp", "expert"), split_axis=0, concat_axis=0, tiled=True)
    returned_pad = jnp.concatenate(
        [
            returned.reshape(devices * capacity, model_width),
            jnp.zeros((1, model_width), jnp.bfloat16),
        ],
        axis=0,
    )
    copies = returned_pad[slot_index].reshape(tok_dev, top_count, model_width)
    layer_out = state + jnp.sum(gates[:, :, None] * copies, axis=1)
    live_tokens = valid_slot.astype(jnp.float32)[:, None]
    diff = (layer_out - teacher.astype(jnp.float32)) * live_tokens
    local_square = jnp.sum(diff * diff)
    d_out = 2.0 * slots_all * diff / valid_count
    d_gates = jnp.sum(d_out[:, None, :] * copies, axis=-1)
    d_chosen = gates * (d_gates - jnp.sum(gates * d_gates, axis=-1, keepdims=True))
    d_logits = jnp.sum(
        jnp.where(routes[:, :, None] == expert_range[None, None, :], d_chosen[:, :, None], 0.0),
        axis=1,
    ).astype(jnp.bfloat16)
    d_copies = (
        (gates[:, :, None] * d_out[:, None, :])
        .astype(jnp.bfloat16)
        .reshape(rows_total, model_width)
    )
    d_copies_pad = jnp.concatenate([d_copies, jnp.zeros((1, model_width), jnp.bfloat16)], axis=0)
    d_send = d_copies_pad[row_of_slot].reshape(devices, capacity, model_width)
    d_arrived = lax.all_to_all(d_send, ("dp", "expert"), split_axis=0, concat_axis=0, tiled=True)
    flat_d = d_arrived.reshape(-1, model_width)
    flat_in = arrived.reshape(-1, model_width)
    flat_gate = gate_pre.reshape(-1, ffn_width)
    flat_up = up_pre.reshape(-1, ffn_width)
    flat_hidden = hidden_units.reshape(-1, ffn_width)
    d_hidden = contract(flat_d, down_weight[0], 1, 1)
    sigmoid_gate = jax.nn.sigmoid(flat_gate)
    d_gate = (d_hidden * flat_up * sigmoid_gate * (1.0 + flat_gate * (1.0 - sigmoid_gate))).astype(
        jnp.bfloat16
    )
    d_up = (d_hidden * flat_gate * sigmoid_gate).astype(jnp.bfloat16)
    down_grad = contract(flat_hidden, flat_d, 0, 0)[None]
    gate_grad = contract(flat_in, d_gate, 0, 0)[None]
    up_grad = contract(flat_in, d_up, 0, 0)[None]
    d_in = (contract(d_gate, gate_weight[0], 1, 1) + contract(d_up, up_weight[0], 1, 1)).astype(
        jnp.bfloat16
    )
    d_returned = lax.all_to_all(
        d_in.reshape(devices, capacity, model_width),
        ("dp", "expert"),
        split_axis=0,
        concat_axis=0,
        tiled=True,
    )
    d_returned_pad = jnp.concatenate(
        [
            d_returned.reshape(devices * capacity, model_width),
            jnp.zeros((1, model_width), jnp.bfloat16),
        ],
        axis=0,
    )
    d_mixed = jnp.sum(
        d_returned_pad[slot_index].reshape(tok_dev, top_count, model_width),
        axis=1,
        dtype=jnp.float32,
    )
    d_mixed = d_mixed + contract(d_logits, router_weight, 1, 1)
    router_local = contract(d_logits, mixed, 0, 0)
    return layer_out, d_out, d_mixed, local_square, router_local, gate_grad, up_grad, down_grad


def experts_by_gather(
    mixed, state, teacher, routes, valid_slot, valid_count, router_weight,
    gate_weight, up_weight, down_weight, devices, capacity, slots_all,
):
    tok_dev, model_width = mixed.shape
    room = -(-2 * capacity // 16) * 16
    expert_range = jnp.arange(devices, dtype=jnp.int32)
    logits = jnp.dot(mixed, router_weight, preferred_element_type=F32)
    chosen = jnp.any(routes[:, :, None] == expert_range[None, None], axis=1)
    gates = jax.nn.softmax(jnp.where(chosen, logits, -jnp.inf), axis=-1)
    live_gates = jnp.where(valid_slot[:, None], gates, 0.0)
    gates_high = live_gates.astype(BF16)
    gates_low = (live_gates - gates_high.astype(F32)).astype(BF16)
    gap = jnp.zeros((tok_dev, 64 - devices), BF16)
    payload = jnp.concatenate([mixed, gates_high, gap, gates_low, gap], axis=1)
    pos, x_rows, y_rows, kept = experts_fwd(
        payload, gate_weight[0], up_weight[0], down_weight[0], capacity, room
    )
    layer_out = state + sum_world(y_rows.reshape(16, room, model_width), pos, tok_dev, 8)
    live_tokens = valid_slot.astype(F32)[:, None]
    diff = (layer_out - teacher.astype(F32)) * live_tokens
    local_square = jnp.sum(diff * diff)
    d_out = 2.0 * slots_all * diff / valid_count
    hidden = kept[3]
    d_rows, d_copy, d_gate, d_up = experts_bwd(
        d_out.astype(BF16), pos, kept[:3] + kept[4:], gate_weight[0], up_weight[0], down_weight[0], room
    )
    back = sum_world(d_rows.reshape(16, room, model_width + 128), pos, tok_dev, 9)

    gate_grad, up_grad, down_grad = (
        grad[None] for grad in expert_grads(x_rows, d_gate, d_up, hidden, d_copy)
    )
    d_gates = back[:, model_width : model_width + devices] + back[:, model_width + 64 : model_width + 64 + devices]
    d_logits = (gates * (d_gates - jnp.sum(gates * d_gates, axis=-1, keepdims=True))).astype(BF16)
    d_mixed = back[:, :model_width] + contract(d_logits, router_weight, 1, 1)
    router_local = contract(d_logits, mixed, 0, 0)
    return layer_out, d_out, d_mixed, local_square, router_local, gate_grad, up_grad, down_grad


def head_rope(linear, gain_vec, cos, sin):
    value = root_mean_scale(linear, gain_vec)
    half = value.shape[-1] // 2
    return value * cos + jnp.roll(value, half, axis=-1) * sin


def body(
    tokens,
    teacher,
    routes,
    cont_lengths,
    query_weight,
    key_projection,
    value_projection,
    output_weight,
    router_weight,
    gate_weight,
    up_weight,
    down_weight,
    input_gain,
    post_gain,
    query_gain,
    key_gain,
):
    n_dp = lax.axis_size("dp")
    n_owner = lax.axis_size("expert")
    devices = n_dp * n_owner
    rank_dp = lax.axis_index("dp")
    rank_owner = lax.axis_index("expert")
    flat_rank = rank_dp * n_owner + rank_owner
    column = rank_owner % 2
    first_column = column == 0
    tok_dev, model_width = tokens.shape
    top_count = routes.shape[1]
    head_dim = query_gain.shape[0]
    kv_width = key_projection.shape[1]
    query_width = query_weight.shape[1]
    query_group = query_width // n_dp
    assert n_dp == 4 and kv_width == n_dp * head_dim
    prompt_block = tok_dev - CMAX
    half_prompt = n_dp * prompt_block
    prompt_len = 2 * half_prompt
    capacity = max(2, tok_dev * top_count * 5 // (4 * devices))
    slots_all = devices * tok_dev
    slot_ids = jnp.arange(tok_dev, dtype=jnp.int32)
    own_length = cont_lengths[flat_rank]
    valid_slot = (slot_ids < prompt_block) | (slot_ids - prompt_block < own_length)
    valid_count = (devices * prompt_block + jnp.sum(cont_lengths)).astype(F32)
    tokens_float = tokens.astype(F32)
    normed_float, first_norm_back = jax.vjp(root_mean_scale, tokens_float, input_gain)
    normed = normed_float.astype(BF16)

    block_ids = jnp.arange(n_dp, dtype=jnp.int32)[:, None]
    positions = jnp.where(
        slot_ids[None] < prompt_block,
        (column * n_dp + block_ids) * prompt_block + slot_ids[None],
        prompt_len + slot_ids[None] - prompt_block,
    )
    half_head = head_dim // 2
    frequency = rope_base ** (-(jnp.arange(half_head, dtype=F32) * 2.0) / head_dim)
    angles = positions.astype(F32)[:, :, None] * frequency
    cos_half, sin_half = jnp.cos(angles), jnp.sin(angles)
    cos = jnp.concatenate([cos_half, cos_half], axis=-1)
    sin = jnp.concatenate([-sin_half, sin_half], axis=-1)
    lengths = jnp.concatenate(
        [lax.dynamic_index_in_dim(cont_lengths.reshape(n_dp, n_owner), rank_owner, 1, False), column[None]]
    ).astype(jnp.int32)

    lin, normed_cols_t, normed_cols = project_qkv(normed, query_weight, key_projection, value_projection)
    key_lin = lin[:, query_group : query_group + head_dim].reshape(n_dp, tok_dev, head_dim)
    keys_float, key_back = jax.vjp(lambda a, b: head_rope(a, b, cos, sin), key_lin, key_gain)
    keys_own = keys_float.astype(BF16)
    values_own = lin[:, query_group + head_dim :].reshape(n_dp, tok_dev, head_dim).astype(BF16)
    column_kv = jnp.stack([keys_own[:, :prompt_block], values_own[:, :prompt_block]]).reshape(
        2, half_prompt, head_dim
    )
    other_kv = partner(column_kv, "expert", 0)
    full_kv = jnp.where(
        first_column,
        jnp.concatenate([column_kv, other_kv], axis=1),
        jnp.concatenate([other_kv, column_kv], axis=1),
    )
    spread = jnp.broadcast_to(full_kv[:, None], (2, n_dp, prompt_len, head_dim))
    all_keys = jnp.concatenate([spread[0], keys_own[:, prompt_block:]], axis=1)
    all_values = jnp.concatenate([spread[1], values_own[:, prompt_block:]], axis=1)
    query_gain_row = query_gain[None]
    queries, attended = attention_fwd(
        lengths, lin, query_gain_row, cos, sin, all_keys, all_values, prompt_len
    )
    state = tokens_float + project_out(attended, output_weight)
    mixed_float, second_norm_back = jax.vjp(root_mean_scale, state, post_gain)
    mixed = mixed_float.astype(BF16)
    sizes = (devices, capacity, slots_all)
    weights = (router_weight, gate_weight, up_weight, down_weight)
    if n_dp == 4 and n_owner == 8:
        moe = experts_by_gather(
            mixed, state, teacher, routes, valid_slot, valid_count, *weights, *sizes
        )
    else:
        moe = experts_by_all_to_all(
            mixed, state, teacher, routes, valid_slot, valid_count, *weights, *sizes
        )
    layer_out, d_out, d_mixed, local_square, router_local, gate_grad, up_grad, down_grad = moe
    d_state_norm, d_post_gain = second_norm_back(d_mixed)
    d_state = d_out + d_state_norm
    d_branch = d_state.astype(BF16)
    d_attended, d_branch_all, attended_t = grad_branch(d_branch, output_weight, attended)
    d_query_lin, d_keys, d_values, gain_parts, out_part = attention_bwd(
        lengths, lin, queries, d_attended, query_gain_row, cos, sin, all_keys, all_values,
        attended_t, d_branch_all, prompt_len,
    )
    d_query_gain = jnp.sum(gain_parts, axis=(0, 1))
    prompt_grads = jnp.stack(
        [jnp.sum(d_keys[:, :prompt_len], axis=0), jnp.sum(d_values[:, :prompt_len], axis=0)]
    )
    mine_part = jnp.where(first_column, prompt_grads[:, :half_prompt], prompt_grads[:, half_prompt:])
    their_part = jnp.where(first_column, prompt_grads[:, half_prompt:], prompt_grads[:, :half_prompt])
    own_prompt = (mine_part + partner(their_part, "expert", 0)).reshape(
        2, n_dp, prompt_block, head_dim
    )
    d_key_post = jnp.concatenate([own_prompt[0], d_keys[:, prompt_len:]], axis=1)
    d_value_lin = jnp.concatenate([own_prompt[1], d_values[:, prompt_len:]], axis=1)
    d_key_float, d_key_gain = key_back(d_key_post)
    rows = n_dp * tok_dev
    d_lin = jnp.concatenate(
        [
            d_query_lin,
            d_key_float.astype(BF16).reshape(rows, head_dim),
            d_value_lin.astype(BF16).reshape(rows, head_dim),
        ],
        axis=1,
    )
    small_parts = [router_local, d_post_gain, d_query_gain, d_key_gain, local_square[None]]
    width = query_weight.shape[0]
    group = d_lin.shape[1]
    rows_here = width // n_owner
    by_line = n_dp == 4 and n_owner == 8

    def packed(parts):
        small = jnp.concatenate([a.reshape(-1) for a in parts])
        piece_rows = -(-small.shape[0] // (8 * 8 * 128)) * 8
        small = jnp.pad(small, (0, 8 * piece_rows * 128 - small.shape[0]))
        return small.reshape(8, piece_rows, 128)

    out_part = out_part.reshape(n_owner, -1, model_width)
    weights = (query_weight, key_projection, value_projection)
    if by_line:

        def line(parts):
            flat = jnp.concatenate(parts)
            return jnp.pad(flat, (0, model_width - flat.shape[0]))[None]

        small = jnp.concatenate(
            [router_local, d_post_gain[None], line([d_query_gain, d_key_gain]), line([local_square[None]])]
        )
        small_rows = -(-small.shape[0] // 8) * 8
        small = jnp.pad(small, ((0, small_rows - small.shape[0]), (0, 0)))
        small = small.reshape(small_rows, 8, -1).transpose(1, 0, 2)
        d_normed, query_grad, key_grad, value_grad, output_grad, small, input_gain_grad = grad_qkv_line(
            d_lin, *weights, normed_cols_t, normed_cols, out_part, small, input_gain[None]
        )
        input_gain_grad = input_gain_grad[:, 0].reshape(-1)
        sums = small.transpose(1, 0, 2).reshape(small_rows, model_width)
        at = router_local.shape[0]
        router_grad, post_gain_grad = sums[:at].T, sums[at]
        query_gain_grad, key_gain_grad = sums[at + 1, :head_dim], sums[at + 1, head_dim : 2 * head_dim]
        total_square = sums[at + 2, :1]
        d_tokens_norm = first_norm_back(d_normed)[0]
    else:
        d_normed, qkv_part, output_grad = grad_qkv(d_lin, *weights, normed_cols_t, out_part)
        d_tokens_norm, d_input_gain = first_norm_back(d_normed)
        small_parts.append(d_input_gain)
        by_owner = (
            qkv_part.reshape(n_dp, n_owner, rows_here, group)
            .transpose(1, 0, 2, 3)
            .reshape(n_owner, n_dp * rows_here, group)
        )
        qkv_rows, small = last_sums(by_owner, packed(small_parts))
        qkv_rows = qkv_rows.reshape(n_dp, rows_here, group)

        def columns(start, size):
            part = qkv_rows[:, :, start : start + size]
            return part.transpose(1, 0, 2).reshape(rows_here, n_dp * size)

        query_grad = columns(0, query_group)
        key_grad = columns(query_group, head_dim)
        value_grad = columns(query_group + head_dim, head_dim)
        small = small.reshape(-1)
        starts = [0]
        for a in small_parts:
            starts.append(starts[-1] + a.size)
        sums = [small[i:j].reshape(a.shape) for a, i, j in zip(small_parts, starts, starts[1:])]
        router_grad, post_gain_grad, query_gain_grad, key_gain_grad, total_square, input_gain_grad = sums
        router_grad = router_grad.T
    tokens_grad = d_state + d_tokens_norm
    loss = total_square[0] / (valid_count * model_width)
    return (
        layer_out,
        loss,
        tokens_grad,
        query_grad,
        key_grad,
        value_grad,
        output_grad,
        router_grad,
        gate_grad,
        up_grad,
        down_grad,
        input_gain_grad,
        post_gain_grad,
        query_gain_grad,
        key_gain_grad,
    )


def solution(mesh):
    in_specs = (
        P(("dp", "expert"), None),
        P(("dp", "expert"), None),
        P(("dp", "expert"), None),
        P(),
        P("dp", None),
        P("dp", None),
        P("dp", None),
        P("dp", None),
        P(),
        P(("dp", "expert"), None, None),
        P(("dp", "expert"), None, None),
        P(("dp", "expert"), None, None),
        P(),
        P(),
        P(),
        P(),
    )
    out_specs = (
        P(("dp", "expert"), None),
        P(),
        P(("dp", "expert"), None),
        P(("dp", "expert"), None),
        P(("dp", "expert"), None),
        P(("dp", "expert"), None),
        P(("dp", "expert"), None),
        P(),
        P(("dp", "expert"), None, None),
        P(("dp", "expert"), None, None),
        P(("dp", "expert"), None, None),
        P(),
        P(),
        P(),
        P(),
    )
    return jax.shard_map(body, mesh=mesh, in_specs=in_specs, out_specs=out_specs, check_vma=False)
```

```python
import functools

import jax
import jax.numpy as jnp
from jax import lax
from jax.experimental import pallas as pl
from jax.experimental.pallas import tpu as pltpu
from jax.sharding import PartitionSpec as P

CMAX = 128
norm_eps = 1e-06
rope_base = 1000000.0
MESH = pl.DeviceIdType.MESH
F32 = jnp.float32
BF16 = jnp.bfloat16
VMEM_SPEC = pl.BlockSpec(memory_space=pltpu.VMEM)
ANY_SPEC = pl.BlockSpec(memory_space=pl.ANY)
VMEM_LIMIT = 56 * 1024 * 1024


def params(collective_id=None):
    return pltpu.CompilerParams(
        collective_id=collective_id,
        has_side_effects=collective_id is not None,
        vmem_limit_bytes=VMEM_LIMIT,
    )


def greet(devices):
    barrier = pltpu.get_barrier_semaphore()
    for device in devices:
        pl.semaphore_signal(barrier, inc=1, device_id=device, device_id_type=MESH)
    pl.semaphore_wait(barrier, len(devices))


def remote(src, dst, send_sem, recv_sem, device):
    return pltpu.make_async_remote_copy(
        src_ref=src,
        dst_ref=dst,
        send_sem=send_sem,
        recv_sem=recv_sem,
        device_id=device,
        device_id_type=MESH,
    )


def start_all(copies):
    for copy in copies:
        copy.start()
    return copies


def wait_all(copies):
    for copy in copies:
        copy.wait()
    copies.clear()


def loading(pairs, sems):
    return [start_all([pltpu.make_async_copy(a, b, sems.at[i])]) for i, (a, b) in enumerate(pairs)]


def aligned(index, size):
    return pl.ds(pl.multiple_of(index * size, size), size)


def dot_nn(a, b):
    return lax.dot_general(a, b, (((1,), (0,)), ((), ())), preferred_element_type=F32)


def dot_nt(a, b):
    return lax.dot_general(a, b, (((1,), (1,)), ((), ())), preferred_element_type=F32)


def dot_tn(a, b):
    return lax.dot_general(a, b, (((0,), (0,)), ((), ())), preferred_element_type=F32)


PEER_MASKS = (3, 1, 2)


def relay_sum(r, e, products, own, mine, send, half_in, full_in, hs, hr, fs, fr, step):
    near, far, diag = r ^ 1, r ^ 2, r ^ 3
    rows = mine.shape[0]
    half = rows // 2
    low, high = pl.ds(0, half), pl.ds(half, half)
    products(diag, send.at[2])
    relays = [
        remote(send.at[2, low], half_in.at[0], hs.at[0], hr.at[0], (near, e)),
        remote(send.at[2, high], half_in.at[1], hs.at[1], hr.at[1], (far, e)),
    ]
    for copy in relays:
        copy.start()
    parts = ((0, low, near), (1, high, far), (0, high, near), (1, low, far))
    fulls = [
        remote(send.at[i, part], full_in.at[i, part], fs.at[n], fr.at[n], (p, e))
        for n, (i, part, p) in enumerate(parts)
    ]
    products(near, send.at[0])
    fulls[0].start()
    products(far, send.at[1])
    fulls[1].start()
    for i, start, slot, n in ((1, 0, 0, 3), (0, half, 1, 2)):
        relays[slot].wait_recv()

        def add(c, carry):
            t = pl.ds(pl.multiple_of(start + c * step, step), step)
            value = send[i, t, :].astype(F32) + half_in[slot, aligned(c, step), :].astype(F32)
            send[i, t, :] = value.astype(BF16)
            return carry

        lax.fori_loop(0, half // step, add, 0)
        fulls[n].start()
    own()
    for copy in fulls:
        copy.wait_recv()

    def total(c, carry):
        t = aligned(c, step)
        mine[t, :] = mine[t, :] + (full_in[0, t, :].astype(F32) + full_in[1, t, :].astype(F32))
        return carry

    lax.fori_loop(0, rows // step, total, 0)
    for copy in relays + fulls:
        copy.wait_send()


def relay_scratch(rows, width):
    return [
        pltpu.VMEM((3, rows, width), BF16),
        pltpu.VMEM((2, rows // 2, width), BF16),
        pltpu.VMEM((2, rows, width), BF16),
        pltpu.SemaphoreType.DMA((2,)),
        pltpu.SemaphoreType.DMA((2,)),
        pltpu.SemaphoreType.DMA((4,)),
        pltpu.SemaphoreType.DMA((4,)),
    ]


def qkv_kernel(
    tok, normed, wq_in, wk_in, wv_in, gain, cos, sin, lin, cols_t, cols, key_lin, keys, values,
    wq, wk, wv, own_kv, other_kv, local, asend, arecv, ksend, krecv, *relay,
):
    r, e = lax.axis_index("dp"), lax.axis_index("expert")
    peers = [r ^ m for m in PEER_MASKS]
    width = wq.shape[0]
    qg = wq.shape[1] // 4
    kg = wk.shape[1] // 4
    rows = cols.shape[0]
    loads = loading(((wq_in, wq), (wk_in, wk), (wv_in, wv)), local)
    greet([(p, e) for p in peers] + [(r, e ^ 1)])
    first = []
    for i, p in enumerate(peers):
        copy = remote(
            normed.at[:, aligned(p, width)], cols.at[aligned(r, tok), :],
            asend.at[i], arecv.at[i], (p, e),
        )
        copy.start()
        first.append(copy)
    cols[aligned(r, tok), :] = normed[:, aligned(r, width)]
    for copy in first:
        copy.wait()
    for copies in loads:
        wait_all(copies)

    def products(p, dst):
        def chunk(c, carry):
            columns = pl.ds(pl.multiple_of(p * qg + c * 256, 256), 256)
            dst[:, aligned(c, 256)] = dot_nn(cols[...], wq[:, columns]).astype(dst.dtype)
            return carry

        lax.fori_loop(0, qg // 256, chunk, 0)
        dst[:, qg : qg + kg] = dot_nn(cols[...], wk[:, aligned(p, kg)]).astype(dst.dtype)
        dst[:, qg + kg :] = dot_nn(cols[...], wv[:, aligned(p, kg)]).astype(dst.dtype)

    def own():
        products(r, lin)
        cols_t[...] = cols[...].T

    relay_sum(r, e, products, own, lin, *relay, 32)
    core = e % 2
    head = gain.shape[1]
    prompt = tok - CMAX
    column = 4 * prompt
    for i in range(4):
        rows_i = slice(i * tok, (i + 1) * tok)
        x = lin[rows_i, qg : qg + kg]
        key_lin[rows_i, :] = x
        x = x * lax.rsqrt(jnp.mean(x * x, axis=-1, keepdims=True) + norm_eps) * gain[...]
        k = (x * cos[i] + pltpu.roll(x, head // 2, 1) * sin[i]).astype(BF16)
        v = lin[rows_i, qg + kg :].astype(BF16)
        for n, (part, out) in enumerate(((k, keys), (v, values))):
            own_kv[n, i * prompt : (i + 1) * prompt] = part[:prompt]
            out[i, 2 * column :] = part[prompt:]
    copy = remote(own_kv, other_kv, ksend.at[0], krecv.at[0], (r, e ^ 1))
    copy.start()
    for n, out in enumerate((keys, values)):
        for i in range(4):
            out[i, aligned(core, column)] = own_kv[n]
    copy.wait()
    for n, out in enumerate((keys, values)):
        for i in range(4):
            out[i, aligned(1 - core, column)] = other_kv[n]


def project_qkv(normed, wq, wk, wv, gain, cos, sin):
    tok = normed.shape[0]
    rows = 4 * tok
    group = (wq.shape[1] + wk.shape[1] + wv.shape[1]) // 4
    head = gain.shape[1]
    total_keys = 8 * (tok - CMAX) + CMAX
    return pl.pallas_call(
        functools.partial(qkv_kernel, tok),
        out_shape=(
            jax.ShapeDtypeStruct((rows, group), F32),
            jax.ShapeDtypeStruct((wq.shape[0], rows), BF16),
            jax.ShapeDtypeStruct((rows, wq.shape[0]), BF16),
            jax.ShapeDtypeStruct((rows, head), F32),
            jax.ShapeDtypeStruct((4, total_keys, head), BF16),
            jax.ShapeDtypeStruct((4, total_keys, head), BF16),
        ),
        in_specs=[VMEM_SPEC] + [ANY_SPEC] * 3 + [VMEM_SPEC] * 3,
        out_specs=(VMEM_SPEC,) * 6,
        scratch_shapes=[pltpu.VMEM(w.shape, BF16) for w in (wq, wk, wv)]
        + [pltpu.VMEM((2, 4 * (tok - CMAX), head), BF16)] * 2
        + [pltpu.SemaphoreType.DMA((3,))] * 3
        + [pltpu.SemaphoreType.DMA((1,))] * 2
        + relay_scratch(rows, group),
        compiler_params=params(1),
        name="qkv_exchange",
    )(normed, wq, wk, wv, gain, cos, sin)


def out_kernel(attn_in, wo_in, total, attn, wo, local, *relay):
    r, e = lax.axis_index("dp"), lax.axis_index("expert")
    tok, width = total.shape
    step = width // 4
    loads = loading(((attn_in, attn), (wo_in, wo)), local)
    greet([(r ^ m, e) for m in PEER_MASKS])
    for copies in loads:
        wait_all(copies)

    def products(p, dst):
        def chunk(c, carry):
            n = aligned(c, step)
            dst[:, n] = dot_nn(attn[aligned(p, tok), :], wo[:, n]).astype(dst.dtype)
            return carry

        lax.fori_loop(0, width // step, chunk, 0)

    relay_sum(r, e, products, lambda: products(r, total), total, *relay, 16)


def project_out(attn, wo):
    tok = attn.shape[0] // 4
    return pl.pallas_call(
        out_kernel,
        out_shape=jax.ShapeDtypeStruct((tok, wo.shape[1]), F32),
        in_specs=[ANY_SPEC] * 2,
        out_specs=VMEM_SPEC,
        scratch_shapes=[
            pltpu.VMEM(attn.shape, BF16),
            pltpu.VMEM(wo.shape, BF16),
            pltpu.SemaphoreType.DMA((2,)),
        ]
        + relay_scratch(tok, wo.shape[1]),
        compiler_params=params(2),
        name="out_exchange",
    )(attn, wo)


def dgrad_kernel(
    mine, wq, wk, wv, cols_t, out_part, normal, grads, out_grad,
    blocks, dsum, dsend, drecv, ssem, rsem, bsend, brecv, *scratch,
):
    r, e = lax.axis_index("dp"), lax.axis_index("expert")
    rows = mine.shape[0]
    tok = rows // 4
    half = rows // 2
    qg = wq.shape[1] // 4
    kg = wk.shape[1] // 4
    width = wq.shape[0]
    peers = [r ^ m for m in PEER_MASKS]
    near, far, diag = r ^ 1, r ^ 2, r ^ 3
    pair_in, send, recv, *sems = scratch
    begin, middle, finish = owner_sum([out_part], [out_grad], [pair_in], [send], [recv], *sems)
    greet([(p, e) for p in peers] + [(r, e ^ 1)] + owner_peers())
    begin()
    low, high = pl.ds(0, half), pl.ds(half, half)
    first_near = remote(mine.at[low], blocks.at[0, low], ssem.at[0], rsem.at[0], (near, e))
    first_far = remote(mine.at[high], blocks.at[1, high], ssem.at[1], rsem.at[1], (far, e))
    second_near = remote(mine.at[high], blocks.at[0, high], ssem.at[2], rsem.at[2], (near, e))
    second_far = remote(mine.at[low], blocks.at[1, low], ssem.at[3], rsem.at[3], (far, e))
    pass_far = remote(blocks.at[0, low], blocks.at[2, low], ssem.at[4], rsem.at[4], (far, e))
    pass_near = remote(blocks.at[1, high], blocks.at[2, high], ssem.at[5], rsem.at[5], (near, e))
    for copy in (first_near, first_far, second_near, second_far):
        copy.start()

    def products(p, src, start):
        def chunk(c, carry):
            t = aligned(c, tok)
            x = src[t, :]
            value = (
                dot_nt(x[:, :qg], wq[:, aligned(p, qg)])
                + dot_nt(x[:, qg : qg + kg], wk[:, aligned(p, kg)])
                + dot_nt(x[:, qg + kg :], wv[:, aligned(p, kg)])
            )
            if start:
                dsum[t, :] = value
            else:
                dsum[t, :] = dsum[t, :] + value
            return carry

        lax.fori_loop(0, 4, chunk, 0)

        def outer(c, carry):
            n = aligned(c, 128)
            grads[aligned(p, width), n] = dot_nn(cols_t[...], src[:, n]).astype(BF16)
            return carry

        lax.fori_loop(0, (qg + 2 * kg) // 128, outer, 0)

    middle()
    products(r, mine, True)
    first_near.wait()
    pass_far.start()
    first_far.wait()
    pass_near.start()
    second_near.wait()
    products(near, blocks.at[0], False)
    second_far.wait()
    products(far, blocks.at[1], False)
    pass_far.wait()
    pass_near.wait()
    products(diag, blocks.at[2], False)
    back = []
    for i, p in enumerate(peers):
        dsend[i] = dsum[aligned(p, tok), :].astype(BF16)
        copy = remote(dsend.at[i], drecv.at[i], bsend.at[i], brecv.at[i], (p, e))
        copy.start()
        back.append(copy)
    normal[:, aligned(r, width)] = dsum[aligned(r, tok), :]
    for i, p in enumerate(peers):
        back[i].wait()
        normal[:, aligned(p, width)] = drecv[i].astype(F32)
    finish()


def grad_qkv(mine, wq, wk, wv, cols_t, out_part):
    rows, group = mine.shape
    tok = rows // 4
    width = wq.shape[0]
    return pl.pallas_call(
        dgrad_kernel,
        out_shape=(
            jax.ShapeDtypeStruct((tok, 4 * width), F32),
            jax.ShapeDtypeStruct((4 * width, group), BF16),
            jax.ShapeDtypeStruct(out_part.shape[1:], F32),
        ),
        in_specs=[VMEM_SPEC] * 6,
        out_specs=(VMEM_SPEC,) * 3,
        scratch_shapes=[
            pltpu.VMEM((3, rows, group), BF16),
            pltpu.VMEM((rows, width), F32),
            pltpu.VMEM((3, tok, width), BF16),
            pltpu.VMEM((3, tok, width), BF16),
            pltpu.SemaphoreType.DMA((6,)),
            pltpu.SemaphoreType.DMA((6,)),
            pltpu.SemaphoreType.DMA((3,)),
            pltpu.SemaphoreType.DMA((3,)),
        ]
        + owner_scratch([out_part]),
        compiler_params=params(4),
        name="dqkv_exchange",
    )(mine, wq, wk, wv, cols_t, out_part)


def branch_kernel(
    mine, wo_in, attn_in, d_attn, full_out, attn_t_out, wo, attn, full, attn_t, local, ssem, rsem
):
    r, e = lax.axis_index("dp"), lax.axis_index("expert")
    tok = mine.shape[0]
    half = tok // 2
    peers = [r ^ m for m in PEER_MASKS]
    near, far, diag = r ^ 1, r ^ 2, r ^ 3
    loads = loading(((attn_in, attn), (wo_in, wo)), local)
    greet([(p, e) for p in peers])

    def part(q, which):
        return pl.ds(pl.multiple_of(q * tok + which * half, half), half)

    low, high = pl.ds(0, half), pl.ds(half, half)
    first_near = remote(mine.at[low], full.at[part(r, 0)], ssem.at[0], rsem.at[0], (near, e))
    first_far = remote(mine.at[high], full.at[part(r, 1)], ssem.at[1], rsem.at[1], (far, e))
    second_near = remote(mine.at[high], full.at[part(r, 1)], ssem.at[2], rsem.at[2], (near, e))
    second_far = remote(mine.at[low], full.at[part(r, 0)], ssem.at[3], rsem.at[3], (far, e))
    pass_far = remote(full.at[part(near, 0)], full.at[part(near, 0)], ssem.at[4], rsem.at[4], (far, e))
    pass_near = remote(full.at[part(far, 1)], full.at[part(far, 1)], ssem.at[5], rsem.at[5], (near, e))
    for copy in (first_near, first_far, second_near, second_far):
        copy.start()
    full[aligned(r, tok), :] = mine[...]
    wait_all(loads[0])
    attn_t[...] = attn[...].T
    leaving = start_all([pltpu.make_async_copy(attn_t, attn_t_out, local.at[0])])
    wait_all(loads[1])
    heads = wo.shape[0]
    step = heads // 4

    def products(q):
        def chunk(c, carry):
            n = aligned(c, step)
            d_attn[aligned(q, tok), n] = dot_nt(full[aligned(q, tok), :], wo[n, :]).astype(BF16)
            return carry

        lax.fori_loop(0, 4, chunk, 0)

    products(r)
    first_near.wait()
    pass_far.start()
    first_far.wait()
    pass_near.start()
    second_near.wait()
    products(near)
    second_far.wait()
    products(far)
    pass_far.wait()
    pass_near.wait()
    leaving += start_all([pltpu.make_async_copy(full, full_out, local.at[1])])
    products(diag)
    wait_all(leaving)


def grad_branch(mine, wo, attn):
    tok, width = mine.shape
    return pl.pallas_call(
        branch_kernel,
        out_shape=(
            jax.ShapeDtypeStruct((4 * tok, wo.shape[0]), BF16),
            jax.ShapeDtypeStruct((4 * tok, width), BF16),
            jax.ShapeDtypeStruct((wo.shape[0], 4 * tok), BF16),
        ),
        in_specs=[VMEM_SPEC, ANY_SPEC, ANY_SPEC],
        out_specs=(VMEM_SPEC, ANY_SPEC, ANY_SPEC),
        scratch_shapes=[
            pltpu.VMEM(wo.shape, BF16),
            pltpu.VMEM(attn.shape, BF16),
            pltpu.VMEM((4 * tok, width), BF16),
            pltpu.VMEM((wo.shape[0], 4 * tok), BF16),
            pltpu.SemaphoreType.DMA((2,)),
            pltpu.SemaphoreType.DMA((6,)),
            pltpu.SemaphoreType.DMA((6,)),
        ],
        compiler_params=params(3),
        name="branch_exchange",
    )(mine, wo, attn)


def owner_order(n_z):
    order = list(range(1, n_z)) + [0]
    return order[1:2] + order[:1] + order[2:] if n_z > 2 else order


def owner_sum(arrays, outs, pair_in, send, recv, psend, precv, zsend, zrecv):
    r, e = lax.axis_index("dp"), lax.axis_index("expert")
    n_z = arrays[0].shape[0] // 2
    z, core = e // 2, e % 2
    targets = [lax.rem(z + j, n_z) for j in range(n_z)]
    order = owner_order(n_z)
    n_arrays = len(arrays)
    pair, moves = {}, []

    def begin():
        for j in order:
            for a in range(n_arrays):
                copy = remote(
                    arrays[a].at[targets[j] * 2 + (1 - core)], pair_in[a].at[j],
                    psend.at[a, j], precv.at[a, j], (r, e ^ 1),
                )
                copy.start()
                pair[a, j] = copy

    def middle():
        for j in order:
            for a in range(n_arrays):
                pair[a, j].wait()
                own = arrays[a][targets[j] * 2 + core].astype(F32) + pair_in[a][j].astype(F32)
                if j == 0:
                    outs[a][...] = own
                else:
                    send[a][j - 1] = own.astype(BF16)
                    copy = remote(
                        send[a].at[j - 1], recv[a].at[j - 1],
                        zsend.at[a, j - 1], zrecv.at[a, j - 1], (r, targets[j] * 2 + core),
                    )
                    copy.start()
                    moves.append(copy)

    def finish():
        for copy in moves:
            copy.wait()
        for a in range(n_arrays):
            value = outs[a][...]
            for j in range(n_z - 1):
                value = value + recv[a][j].astype(F32)
            outs[a][...] = value

    return begin, middle, finish


def owner_scratch(arrays):
    n_z = arrays[0].shape[0] // 2
    n = len(arrays)
    shapes = [a.shape[1:] for a in arrays]
    return (
        [pltpu.VMEM((n_z, *s), BF16) for s in shapes]
        + [pltpu.VMEM((n_z - 1, *s), BF16) for s in shapes]
        + [pltpu.VMEM((n_z - 1, *s), BF16) for s in shapes]
        + [pltpu.SemaphoreType.DMA((n, n_z))] * 2
        + [pltpu.SemaphoreType.DMA((n, n_z - 1))] * 2
    )


def owner_peers():
    r, e = lax.axis_index("dp"), lax.axis_index("expert")
    n_z = lax.axis_size("expert") // 2
    return [(r, lax.rem(e // 2 + j, n_z) * 2 + e % 2) for j in range(1, n_z)]


def last_sums_kernel(grads, small, grads_out, small_out, *scratch):
    r, e = lax.axis_index("dp"), lax.axis_index("expert")
    z, core = e // 2, e % 2
    n_z = grads.shape[0] // 2
    pair_in, send, recv, psend, precv, zsend, zrecv = scratch[:7]
    first_in, piece, line_in, s1, r1, s2, r2, s3, r3 = scratch[7:]
    begin, middle, finish = owner_sum(
        [grads], [grads_out], [pair_in], [send], [recv], psend, precv, zsend, zrecv
    )
    others = [(m // 2, m % 2) for m in range(1, 8)]
    plane = [(r ^ a, e ^ c) for a, c in others]
    greet(plane + owner_peers())
    begin()
    firsts = []
    for i, (a, c) in enumerate(others):
        copy = remote(
            small.at[(r ^ a) * 2 + (core ^ c)], first_in.at[i], s1.at[i], r1.at[i], plane[i]
        )
        copy.start()
        firsts.append(copy)
    middle()
    for copy in firsts:
        copy.wait()
    mine = r * 2 + core
    value = small[mine]
    for i in range(7):
        value = value + first_in[i]
    piece[0] = value
    seconds = []
    for j in range(1, n_z):
        copy = remote(
            piece.at[0], line_in.at[j - 1], s2.at[j - 1], r2.at[j - 1], owner_peers()[j - 1]
        )
        copy.start()
        seconds.append(copy)
    for copy in seconds:
        copy.wait()
    value = piece[0]
    for j in range(n_z - 1):
        value = value + line_in[j]
    small_out[mine] = value
    thirds = []
    for i, (a, c) in enumerate(others):
        copy = remote(small_out.at[mine], small_out.at[mine], s3.at[i], r3.at[i], plane[i])
        copy.start()
        thirds.append(copy)
    finish()
    for copy in thirds:
        copy.wait()


def last_sums(grads, small):
    n_z = grads.shape[0] // 2
    piece = small.shape[1:]
    return pl.pallas_call(
        last_sums_kernel,
        out_shape=(
            jax.ShapeDtypeStruct(grads.shape[1:], F32),
            jax.ShapeDtypeStruct(small.shape, F32),
        ),
        in_specs=[VMEM_SPEC] * 2,
        out_specs=(VMEM_SPEC,) * 2,
        scratch_shapes=owner_scratch([grads])
        + [
            pltpu.VMEM((7, *piece), F32),
            pltpu.VMEM((1, *piece), F32),
            pltpu.VMEM((n_z - 1, *piece), F32),
            pltpu.SemaphoreType.DMA((7,)),
            pltpu.SemaphoreType.DMA((7,)),
            pltpu.SemaphoreType.DMA((n_z - 1,)),
            pltpu.SemaphoreType.DMA((n_z - 1,)),
            pltpu.SemaphoreType.DMA((7,)),
            pltpu.SemaphoreType.DMA((7,)),
        ],
        compiler_params=params(5),
        name="last_sums",
    )(grads, small)


def line_sum(block, out, pair_in, work, lines, ps, pr, zs, zr):
    r, e = lax.axis_index("dp"), lax.axis_index("expert")
    z, core = e // 2, e % 2
    order = plane_order(z)[::-1]
    right = jnp.minimum(z + 1, 3) * 2 + core
    left = jnp.maximum(z - 1, 0) * 2 + core
    pairs, moves = [], []

    def begin():
        for k in range(4):
            copy = remote(
                block(order[k] * 2 + (1 - core)), pair_in.at[k], ps.at[k], pr.at[k], (r, e ^ 1)
            )
            copy.start()
            pairs.append(copy)

    def move(k, side, cond, to, add):
        b = order[k]
        copy = remote(work.at[k], lines.at[side, b], zs.at[side, k], zr.at[side, b], (r, to))
        moves.append((cond, copy))

        @pl.when(cond)
        def _():
            if add:
                copy.wait_recv()
                value = work[k].astype(F32) + lines[side, b].astype(F32)
                work[k] = value.astype(BF16)
            copy.start()

    def first():
        for k in range(4):
            pairs[k].wait_recv()
            value = block(order[k] * 2 + core)[...].astype(F32) + pair_in[k].astype(F32)
            if k == 3:
                out[...] = value
            else:
                work[k] = value.astype(BF16)
        ends(0)

    def ends(k):
        move(k, 0, z == 0, right, False)
        move(k, 1, z == 3, left, False)

    def inner(k):
        inside = (z > 0) & (z < 3)
        move(k, 0, inside & (order[k] > z), right, True)
        move(k, 1, inside & (order[k] < z), left, True)
        if k < 2:
            ends(k + 1)

    def last():
        for side, cond in ((0, z > 0), (1, z < 3)):

            @pl.when(cond)
            def _():
                at = lines.at[side, z]
                remote(at, at, zs.at[side, 3], zr.at[side, z], (r, e ^ 1)).wait_recv()
                out[...] = out[...] + lines[side, z].astype(F32)

        for copy in pairs:
            copy.wait_send()
        for cond, copy in moves:

            @pl.when(cond)
            def _():
                copy.wait_send()

    return begin, first, inner, last


LINE_SEMS = [
    pltpu.SemaphoreType.DMA((4,)),
    pltpu.SemaphoreType.DMA((4,)),
    pltpu.SemaphoreType.DMA((2, 4)),
    pltpu.SemaphoreType.DMA((2, 4)),
]


def dgrad_line_kernel(
    d_q, d_keys, d_values, key_lin, cos, sin, key_gain,
    wq_in, wk_in, wv_in, cols_t_in, cols_in, out_part_in, small, gain,
    normal, q_out, k_out, v_out, out_sum, small_out, gain_out,
    mine, prompt_sum, prompt_in, ksend, krecv, wq, wk, wv, cols_t, cols, out_part, local, qkv_sum, grads, blocks, dsum, dsend, drecv, opair, owork, olines, qpair, qwork, qlines,
    first_in, piece, line_in, gain_v, gain_in,
    ssem, rsem, bsend, brecv, s1, r1, s2, r2, s3, r3, s4, r4, s5, r5, *sems,
):
    r, e = lax.axis_index("dp"), lax.axis_index("expert")
    z, core = e // 2, e % 2
    rows = mine.shape[0]
    tok = rows // 4
    half = rows // 2
    qg = wq.shape[1] // 4
    kg = wk.shape[1] // 4
    width = wq.shape[0]
    share = width // 8
    peers = [r ^ m for m in PEER_MASKS]
    near, far, diag = r ^ 1, r ^ 2, r ^ 3
    order = (r, near, far, diag)
    out_begin, out_first, out_inner, out_last = line_sum(
        lambda o: out_part.at[o], out_sum, opair, owork, olines, *sems[:4]
    )
    units = [
        line_sum(
            lambda o, p=p: grads.at[o, p], qkv_sum.at[p], qpair.at[i], qwork.at[i], qlines.at[i],
            *(sem.at[i] for sem in sems[4:]),
        )
        for i, p in enumerate(order)
    ]
    line_peers = [(r, lax.rem(z + j, 4) * 2 + core) for j in (1, 2, 3)]
    others = [(m // 2, m % 2) for m in (6, 7, 2, 3, 4, 5, 1)]
    plane = [(r ^ a, e ^ c) for a, c in others]
    owners = [(r, e ^ m) for m in range(1, 8)]
    loads = loading(
        (
            (out_part_in, out_part), (cols_t_in, cols_t), (wq_in, wq), (wk_in, wk), (wv_in, wv),
            (cols_in, cols),
        ),
        local,
    )
    mine[:, :qg] = d_q[...]
    prompt = tok - CMAX
    column = 4 * prompt
    for n, d in enumerate((d_keys, d_values)):
        for c in range(2):
            part = slice(c * column, (c + 1) * column)
            prompt_sum[c, n] = d[0, part] + d[1, part] + d[2, part] + d[3, part]
    greet(plane + owners[1:])
    swap = remote(prompt_sum.at[1 - core], prompt_in, ksend.at[0], krecv.at[0], (r, e ^ 1))
    swap.start()
    swap.wait()
    prompt_in[...] = prompt_in[...] + prompt_sum[core]
    head = key_gain.shape[1]
    key_gain_sum = jnp.zeros((1, head), F32)
    for i in range(4):
        for at, size, dk, dv in (
            (0, prompt, prompt_in[0, i * prompt : (i + 1) * prompt], prompt_in[1, i * prompt : (i + 1) * prompt]),
            (prompt, CMAX, d_keys[i, 2 * column :], d_values[i, 2 * column :]),
        ):
            t = slice(at, at + size)
            rows_i = slice(i * tok + at, i * tok + at + size)
            turned = dk * cos[i, t] + pltpu.roll(dk * sin[i, t], head // 2, 1)
            x = key_lin[rows_i, :]
            inverse = lax.rsqrt(jnp.mean(x * x, axis=-1, keepdims=True) + norm_eps)
            unit = x * inverse
            key_gain_sum = key_gain_sum + jnp.sum(turned * unit, axis=0, keepdims=True)
            weighted = turned * key_gain[...]
            mine[rows_i, qg : qg + kg] = (
                inverse * (weighted - unit * jnp.mean(weighted * unit, axis=-1, keepdims=True))
            ).astype(BF16)
            mine[rows_i, qg + kg :] = dv.astype(BF16)
    low, high = pl.ds(0, half), pl.ds(half, half)
    first_near = remote(mine.at[low], blocks.at[0, low], ssem.at[0], rsem.at[0], (near, e))
    first_far = remote(mine.at[high], blocks.at[1, high], ssem.at[1], rsem.at[1], (far, e))
    second_near = remote(mine.at[high], blocks.at[0, high], ssem.at[2], rsem.at[2], (near, e))
    second_far = remote(mine.at[low], blocks.at[1, low], ssem.at[3], rsem.at[3], (far, e))
    pass_far = remote(blocks.at[0, low], blocks.at[2, low], ssem.at[4], rsem.at[4], (far, e))
    pass_near = remote(blocks.at[1, high], blocks.at[2, high], ssem.at[5], rsem.at[5], (near, e))
    me = r * 2 + core
    firsts = []
    for i, (a, c) in enumerate(others):
        copy = remote(small.at[(r ^ a) * 2 + (core ^ c)], first_in.at[i], s1.at[i], r1.at[i], plane[i])
        copy.start()
        firsts.append(copy)
    for copy in (first_near, first_far, second_near, second_far):
        copy.start()
    wait_all(loads[0])
    out_begin()
    seconds, thirds = [], []

    def small_second():
        for copy in firsts:
            copy.wait()
        value = small[me]
        for i in range(7):
            value = value + first_in[i]
        piece[0] = value
        for j in range(3):
            copy = remote(piece.at[0], line_in.at[j], s2.at[j], r2.at[j], line_peers[j])
            copy.start()
            seconds.append(copy)

    def small_third():
        for copy in seconds:
            copy.wait()
        small_out[me] = piece[0] + line_in[0] + line_in[1] + line_in[2]
        for i in range(7):
            copy = remote(small_out.at[me], small_out.at[me], s3.at[i], r3.at[i], plane[i])
            copy.start()
            thirds.append(copy)

    def outer(p, src):
        def step(c, carry):
            n = aligned(c, 256)
            value = dot_nn(cols_t[...], src[:, n]).astype(BF16)
            for o in range(8):
                grads[o, p, :, n] = value[o * share : (o + 1) * share]
            return carry

        lax.fori_loop(0, (qg + 2 * kg) // 256, step, 0)

    def inner(p, src, start):
        def chunk(c, carry):
            n = aligned(c, 128)
            value = (
                dot_nt(src[:, :qg], wq[n, aligned(p, qg)])
                + dot_nt(src[:, qg : qg + kg], wk[n, aligned(p, kg)])
                + dot_nt(src[:, qg + kg :], wv[n, aligned(p, kg)])
            )
            if start:
                dsum[:, n] = value
            else:
                dsum[:, n] = dsum[:, n] + value
            return carry

        lax.fori_loop(0, width // 128, chunk, 0)

    def begin(i):
        units[i][0]()

    def first(i):
        units[i][1]()

    def onward(i, k):
        units[i][2](k)

    wait_all(loads[1])
    outer(r, mine)
    begin(0)
    out_first()
    small_second()
    for copies in loads[2:5]:
        wait_all(copies)
    inner(r, mine, True)
    first_near.wait()
    pass_far.start()
    first_far.wait()
    pass_near.start()
    out_inner(0)
    first(0)
    out_inner(1)
    small_third()
    onward(0, 0)
    second_near.wait()
    outer(near, blocks.at[0])
    begin(1)
    second_far.wait()
    outer(far, blocks.at[1])
    begin(2)
    out_inner(2)
    onward(0, 1)
    first(1)
    inner(near, blocks.at[0], False)
    onward(0, 2)
    onward(1, 0)
    first(2)
    inner(far, blocks.at[1], False)
    onward(1, 1)
    pass_far.wait()
    pass_near.wait()
    outer(diag, blocks.at[2])
    begin(3)
    inner(diag, blocks.at[2], False)
    back = []
    for i, p in enumerate(peers):
        dsend[i] = dsum[aligned(p, tok), :].astype(BF16)
        copy = remote(dsend.at[i], drecv.at[i], bsend.at[i], brecv.at[i], (p, e))
        copy.start()
        back.append(copy)
    wait_all(loads[5])
    scale = 1.0 / gain[:, aligned(r, width)]
    gain_v[...] = jnp.broadcast_to(
        jnp.sum(dsum[...] * cols[...].astype(F32), axis=0, keepdims=True) * scale, gain_v.shape
    )
    gain_v[1:2, :head] = key_gain_sum
    fourths = []
    for i in range(7):
        copy = remote(gain_v, gain_in.at[i], s4.at[i], r4.at[i], owners[i])
        copy.start()
        fourths.append(copy)
    onward(1, 2)
    onward(2, 0)
    first(3)
    onward(2, 1)
    for copy in fourths:
        copy.wait()
    value = gain_v[...]
    for i in range(7):
        value = value + gain_in[i]
    gain_out[r] = value
    fifths = []
    for i, p in enumerate(peers):
        copy = remote(gain_out.at[r], gain_out.at[r], s5.at[i], r5.at[i], (p, e))
        copy.start()
        fifths.append(copy)
    onward(3, 0)
    normal[:, aligned(r, width)] = dsum[aligned(r, tok), :]
    for i, p in enumerate(peers):
        back[i].wait()
        normal[:, aligned(p, width)] = drecv[i].astype(F32)
    onward(2, 2)
    onward(3, 1)
    out_last()

    def close(i):
        p = order[i]
        units[i][3]()
        q_out[:, aligned(p, qg)] = qkv_sum[p, :, :qg]
        k_out[:, aligned(p, kg)] = qkv_sum[p, :, qg : qg + kg]
        v_out[:, aligned(p, kg)] = qkv_sum[p, :, qg + kg :]

    close(0)
    close(1)
    onward(3, 2)
    close(2)
    close(3)
    for copy in fifths + thirds:
        copy.wait()


def grad_qkv_line(
    d_q, d_keys, d_values, key_lin, cos, sin, key_gain, wq, wk, wv, cols_t, cols, out_part, small, gain
):
    rows, head = key_lin.shape
    group = d_q.shape[1] + 2 * head
    tok = rows // 4
    width = wq.shape[0]
    piece = (width // 8, group)
    out_piece = out_part.shape[1:]
    small_piece = small.shape[1:]
    return pl.pallas_call(
        dgrad_line_kernel,
        out_shape=(
            jax.ShapeDtypeStruct((tok, 4 * width), F32),
            jax.ShapeDtypeStruct((width // 8, wq.shape[1]), F32),
            jax.ShapeDtypeStruct((width // 8, wk.shape[1]), F32),
            jax.ShapeDtypeStruct((width // 8, wv.shape[1]), F32),
            jax.ShapeDtypeStruct(out_piece, F32),
            jax.ShapeDtypeStruct(small.shape, F32),
            jax.ShapeDtypeStruct((4, 8, width), F32),
        ),
        in_specs=[VMEM_SPEC] * 7 + [ANY_SPEC] * 6 + [VMEM_SPEC] * 2,
        out_specs=(VMEM_SPEC,) * 7,
        scratch_shapes=[
            pltpu.VMEM((rows, group), BF16),
            pltpu.VMEM((2, 2, 4 * (tok - CMAX), head), F32),
            pltpu.VMEM((2, 4 * (tok - CMAX), head), F32),
            pltpu.SemaphoreType.DMA((1,)),
            pltpu.SemaphoreType.DMA((1,)),
        ]
        + [pltpu.VMEM(a.shape, BF16) for a in (wq, wk, wv, cols_t, cols, out_part)]
        + [
            pltpu.SemaphoreType.DMA((6,)),
            pltpu.VMEM((4, *piece), F32),
            pltpu.VMEM((8, 4, *piece), BF16),
            pltpu.VMEM((3, rows, group), BF16),
            pltpu.VMEM((rows, width), F32),
            pltpu.VMEM((3, tok, width), BF16),
            pltpu.VMEM((3, tok, width), BF16),
            pltpu.VMEM((4, *out_piece), BF16),
            pltpu.VMEM((3, *out_piece), BF16),
            pltpu.VMEM((2, 4, *out_piece), BF16),
            pltpu.VMEM((4, 4, *piece), BF16),
            pltpu.VMEM((4, 3, *piece), BF16),
            pltpu.VMEM((4, 2, 4, *piece), BF16),
            pltpu.VMEM((7, *small_piece), F32),
            pltpu.VMEM((1, *small_piece), F32),
            pltpu.VMEM((3, *small_piece), F32),
            pltpu.VMEM((8, width), F32),
            pltpu.VMEM((7, 8, width), F32),
            pltpu.SemaphoreType.DMA((6,)),
            pltpu.SemaphoreType.DMA((6,)),
        ]
        + [pltpu.SemaphoreType.DMA((n,)) for n in (3, 3, 7, 7, 3, 3, 7, 7, 7, 7, 3, 3)]
        + LINE_SEMS
        + [
            pltpu.SemaphoreType.DMA((4, 4)),
            pltpu.SemaphoreType.DMA((4, 4)),
            pltpu.SemaphoreType.DMA((4, 2, 4)),
            pltpu.SemaphoreType.DMA((4, 2, 4)),
        ],
        compiler_params=params(10),
        name="dqkv_line_exchange",
    )(
        d_q, d_keys, d_values, key_lin, cos, sin, key_gain, wq, wk, wv, cols_t, cols, out_part, small, gain
    )


def masks_of(block, own_length, slots, prompt_block, prompt_len, column, keys):
    slot = lax.broadcasted_iota(jnp.int32, (slots, keys), 0)
    key = lax.broadcasted_iota(jnp.int32, (slots, keys), 1)
    is_prompt = slot < prompt_block
    position = (column * 4 + block) * prompt_block + slot
    sees_prompt = (key < prompt_len) & (jnp.logical_not(is_prompt) | (key <= position))
    cont = key - prompt_len
    sees_cont = (
        (key >= prompt_len)
        & jnp.logical_not(is_prompt)
        & (cont <= slot - prompt_block)
        & (cont < own_length)
    )
    return sees_prompt | sees_cont


def attention_fwd_kernel(prompt_len, lengths, lin, gain, cos, sin, keys, values, queries, attn):
    block = pl.program_id(0)
    slots = lin.shape[0]
    head = gain.shape[1]
    allowed = masks_of(
        block, lengths[block], slots, slots - CMAX, prompt_len, lengths[4], keys.shape[1]
    )
    scale = head ** (-0.5)
    k, v = keys[0], values[0]
    c, s, g = cos[0], sin[0], gain[...]
    for h in range(lin.shape[1] // head):
        part = slice(h * head, (h + 1) * head)
        x = lin[:, part]
        x = x * lax.rsqrt(jnp.mean(x * x, axis=-1, keepdims=True) + norm_eps) * g
        q = (x * c + pltpu.roll(x, head // 2, 1) * s).astype(BF16)
        queries[:, part] = q
        score = jnp.where(allowed, dot_nt(q, k) * scale, -jnp.inf)
        peak = jnp.max(score, axis=-1, keepdims=True)
        exponent = jnp.exp(score - peak)
        low = (exponent * (1.0 / jnp.sum(exponent, axis=-1, keepdims=True))).astype(BF16)
        attn[:, part] = dot_nn(low, v).astype(BF16)


def attention_fwd(lengths, lin, gain, cos, sin, keys, values, prompt_len):
    blocks, total_keys, head = keys.shape
    slots = lin.shape[0] // blocks
    width = lin.shape[1] - 2 * head
    row = pl.BlockSpec((slots, width), lambda i, *_: (i, 0))
    table = pl.BlockSpec((1, slots, head), lambda i, *_: (i, 0, 0))
    kv = pl.BlockSpec((1, total_keys, head), lambda i, *_: (i, 0, 0))
    one = pl.BlockSpec((1, head), lambda i, *_: (0, 0))
    return pl.pallas_call(
        functools.partial(attention_fwd_kernel, prompt_len),
        grid_spec=pltpu.PrefetchScalarGridSpec(
            num_scalar_prefetch=1,
            grid=(blocks,),
            in_specs=[row, one, table, table, kv, kv],
            out_specs=[row, row],
        ),
        out_shape=(
            jax.ShapeDtypeStruct((lin.shape[0], width), BF16),
            jax.ShapeDtypeStruct((lin.shape[0], width), BF16),
        ),
        compiler_params=params(),
        name="attention_fwd",
    )(lengths, lin, gain, cos, sin, keys, values)


def attention_bwd_kernel(
    prompt_len, lengths, lin, queries, d_attn, gain, cos, sin, keys, values, attn_t, d_branch,
    d_lin, d_keys, d_values, d_gain, out_part,
):
    block = pl.program_id(0)
    slots = lin.shape[0]
    head = gain.shape[1]
    allowed = masks_of(
        block, lengths[block], slots, slots - CMAX, prompt_len, lengths[4], keys.shape[1]
    )
    scale = head ** (-0.5)
    k, v = keys[0], values[0]
    c, s, g = cos[0], sin[0], gain[...]
    key_total = jnp.zeros(k.shape, F32)
    value_total = jnp.zeros(v.shape, F32)
    gain_total = jnp.zeros((8, head), F32)
    for h in range(lin.shape[1] // head):
        part = slice(h * head, (h + 1) * head)
        q = queries[:, part]
        score = jnp.where(allowed, dot_nt(q, k) * scale, -jnp.inf)
        peak = jnp.max(score, axis=-1, keepdims=True)
        exponent = jnp.exp(score - peak)
        probs = exponent * (1.0 / jnp.sum(exponent, axis=-1, keepdims=True))
        d_out = d_attn[:, part]
        d_probs = dot_nt(d_out, v)
        inner = jnp.sum(probs * d_probs, axis=-1, keepdims=True)
        d_score = (probs * (d_probs - inner)).astype(BF16)
        key_total = key_total + dot_tn(d_score, q)
        value_total = value_total + dot_tn(probs.astype(BF16), d_out)
        d_q = dot_nn(d_score, k) * scale
        turned = d_q * c + pltpu.roll(d_q * s, head // 2, 1)
        x = lin[:, part]
        inverse = lax.rsqrt(jnp.mean(x * x, axis=-1, keepdims=True) + norm_eps)
        unit = x * inverse
        pairs = turned * unit
        for j in range(slots // 8):
            gain_total = gain_total + pairs[j * 8 : (j + 1) * 8]
        weighted = turned * g
        d_lin[:, part] = (
            inverse * (weighted - unit * jnp.mean(weighted * unit, axis=-1, keepdims=True))
        ).astype(BF16)
        if h % 4 == 3:
            n = slice(h // 4 * 256, h // 4 * 256 + 256)
            out_part[:, n] = dot_nn(attn_t[...], d_branch[:, n]).astype(BF16)
    d_keys[0] = key_total * scale
    d_values[0] = value_total
    d_gain[0] = gain_total


def attention_bwd(
    lengths, lin, queries, d_attn, gain, cos, sin, keys, values, attn_t, d_branch, prompt_len
):
    blocks, total_keys, head = keys.shape
    slots = lin.shape[0] // blocks
    width = lin.shape[1] - 2 * head
    row = pl.BlockSpec((slots, width), lambda i, *_: (i, 0))
    table = pl.BlockSpec((1, slots, head), lambda i, *_: (i, 0, 0))
    kv = pl.BlockSpec((1, total_keys, head), lambda i, *_: (i, 0, 0))
    step = d_branch.shape[1] // blocks
    one = pl.BlockSpec((1, head), lambda i, *_: (0, 0))
    return pl.pallas_call(
        functools.partial(attention_bwd_kernel, prompt_len),
        grid_spec=pltpu.PrefetchScalarGridSpec(
            num_scalar_prefetch=1,
            grid=(blocks,),
            in_specs=[row, row, row, one, table, table, kv, kv]
            + [
                pl.BlockSpec(attn_t.shape, lambda i, *_: (0, 0)),
                pl.BlockSpec((d_branch.shape[0], step), lambda i, *_: (0, i)),
            ],
            out_specs=[
                row,
                kv,
                kv,
                pl.BlockSpec((1, 8, head), lambda i, *_: (i, 0, 0)),
                pl.BlockSpec((attn_t.shape[0], step), lambda i, *_: (0, i)),
            ],
        ),
        out_shape=(
            jax.ShapeDtypeStruct((lin.shape[0], width), BF16),
            jax.ShapeDtypeStruct(keys.shape, F32),
            jax.ShapeDtypeStruct(values.shape, F32),
            jax.ShapeDtypeStruct((blocks, 8, head), F32),
            jax.ShapeDtypeStruct((attn_t.shape[0], d_branch.shape[1]), BF16),
        ),
        compiler_params=params(),
        name="attention_bwd",
    )(lengths, lin, queries, d_attn, gain, cos, sin, keys, values, attn_t, d_branch)


def partner(shard, axis, bit):
    return lax.ppermute(shard, axis, [(i, i ^ 1 << bit) for i in range(lax.axis_size(axis))])


def root_mean_scale(value_rows, gain_vec):
    return (
        value_rows
        * lax.rsqrt(jnp.mean(value_rows * value_rows, axis=-1, keepdims=True) + norm_eps)
        * gain_vec
    )


def contract(left_side, right_side, left_dim, right_dim):
    return lax.dot_general(
        left_side,
        right_side,
        (((left_dim,), (right_dim,)), ((), ())),
        preferred_element_type=F32,
    )


def plane_order(z):
    upper, odd = z // 2, z % 2
    return [z, z + 1 - 2 * upper, 2 + upper - 2 * odd, 3 - 3 * upper]


def world(with_diag):
    r, e = lax.axis_index("dp"), lax.axis_index("expert")
    z, core = e // 2, e % 2
    near, far = r ^ 1, r ^ 2
    devices = [(near, e), (far, e), (r, e ^ 1)]
    devices += [(r, lax.rem(z + j, 4) * 2 + core) for j in (1, 2, 3)]
    return r, e, z, core, near, far, devices


def gather_world(mine, buf, zs, zr, ps, pr, ds, dr, before, group, done):
    r, e, z, core, near, far, greeted = world(True)
    half = mine.shape[0] // 2
    low, high = pl.ds(0, half), pl.ds(half, half)
    order = plane_order(z)
    greet(greeted)

    def slot(q, b, c):
        return q * 8 + b * 2 + c

    buf[slot(r, z, core)] = mine[...]
    diag = r ^ 3
    plane, pairs, lines = {}, {}, []

    def hand(k, i, q):
        at = slot(q, order[k], core)
        copy = remote(buf.at[at], buf.at[at], ds.at[k, i], dr.at[k, i], (r, e ^ 1))
        copy.start()
        pairs[k, i] = copy

    def issue(k):
        b = order[k]
        at = slot(r, b, core)
        for side, cond, to in (
            (0, (b <= z) & (z < 3), jnp.minimum(z + 1, 3)),
            (1, (b >= z) & (z > 0), jnp.maximum(z - 1, 0)),
        ):
            copy = remote(buf.at[at], buf.at[at], zs.at[k, side], zr.at[b], (r, to * 2 + core))
            lines.append((cond, copy))

            @pl.when(cond)
            def _():
                copy.start()

        mine_at, near_at, far_at = at, slot(near, b, core), slot(far, b, core)
        for i, (src, part, p) in enumerate(
            (
                (mine_at, low, near),
                (mine_at, high, far),
                (mine_at, high, near),
                (mine_at, low, far),
                (near_at, low, far),
                (far_at, high, near),
            )
        ):
            plane[k, i] = remote(
                buf.at[src, part], buf.at[src, part], ps.at[k, i], pr.at[k, i], (p, e)
            )
        for i in range(4):
            plane[k, i].start()
        hand(k, 0, r)

    def line_wait(k):
        b = order[k]
        at = slot(r, b, core)
        remote(buf.at[at], buf.at[at], zs.at[k, 0], zr.at[b], (r, e ^ 1)).wait_recv()
        issue(k)

    def passes(k):
        plane[k, 0].wait_recv()
        plane[k, 4].start()
        plane[k, 1].wait_recv()
        plane[k, 5].start()

    def finish(k):
        plane[k, 2].wait_recv()
        hand(k, 1, near)
        plane[k, 3].wait_recv()
        hand(k, 2, far)

    def corner(k):
        plane[k, 4].wait_recv()
        plane[k, 5].wait_recv()
        hand(k, 3, diag)

    who = (r, near, far, diag)

    def ready(k):
        before(k)
        for i in range(4):
            pairs[k, i].wait_recv()
        group(k, [(k * 4 + i, who[i] * 8 + order[k] * 2) for i in range(4)])

    issue(0)
    passes(0)
    line_wait(1)
    finish(0)
    passes(1)
    line_wait(2)
    corner(0)
    finish(1)
    ready(0)
    passes(2)
    line_wait(3)
    corner(1)
    finish(2)
    ready(1)
    passes(3)
    corner(2)
    finish(3)
    ready(2)
    corner(3)
    ready(3)
    done()
    for copy in plane.values():
        copy.wait_send()
    for copy in pairs.values():
        copy.wait_send()
    for cond, copy in lines:

        @pl.when(cond)
        def _():
            copy.wait_send()


def group_rows(k, room):
    return pl.ds(k * 4 * room, 4 * room)


GATHER_SEMS = [
    pltpu.SemaphoreType.DMA((4, 2)),
    pltpu.SemaphoreType.DMA((4,)),
    pltpu.SemaphoreType.DMA((4, 6)),
    pltpu.SemaphoreType.DMA((4, 6)),
    pltpu.SemaphoreType.DMA((4, 4)),
    pltpu.SemaphoreType.DMA((4, 4)),
]


def selector(row, room):
    ids = lax.broadcasted_iota(jnp.int32, (room, row.shape[1]), 0).astype(F32)
    return jnp.where(ids == row, 1.0, 0.0).astype(BF16)


def experts_fwd_kernel(
    capacity, mine, wg, wu, wd, pos, x_out, y_out, g_out, u_out, o_out, hid_out, gate_out,
    buf, wg_v, wu_v, wd_v, x_v, y_v, g_v, u_v, o_v, hid_v, gate_v, local, *sems,
):
    model = wg.shape[0]
    rows_in = mine.shape[0]
    room = x_v.shape[0] // 4
    me = lax.axis_index("dp") * 8 + lax.axis_index("expert")
    loads = start_all(
        [
            pltpu.make_async_copy(a, b, local.at[0, i])
            for i, (a, b) in enumerate(((wg, wg_v), (wu, wu_v), (wd, wd_v)))
        ]
    )
    leaving = {g: [] for g in range(4)}

    def leave(g, pairs):
        kept = group_rows(g, room)
        leaving[g].extend(
            start_all(
                [
                    pltpu.make_async_copy(v, o.at[kept], local.at[g % 2, i])
                    for i, v, o in pairs
                ]
            )
        )

    def before(g):
        wait_all(loads)
        if g > 0:
            wait_all(leaving[g - 1])

    upto = jnp.where(
        lax.broadcasted_iota(jnp.int32, (rows_in, rows_in), 0)
        <= lax.broadcasted_iota(jnp.int32, (rows_in, rows_in), 1),
        1.0,
        0.0,
    ).astype(BF16)
    is_me = jnp.where(lax.broadcasted_iota(jnp.int32, (16, 128), 1) == me, 1.0, 0.0).astype(BF16)

    def pick(at, s, start):
        rows = pl.ds(start, room)
        sels = []
        for c in range(2):
            named = jnp.where(dot_nt(is_me, buf[s + c, :, model:]) > 0.0, 1.0, 0.0)
            place = (dot_nn(named.astype(BF16), upto) + (c * capacity)) * named - 1.0
            pos[at * 2 + c] = place[:1]
            sels.append(selector(place[:1], room))
        for c in range(4):
            n = slice(c * model // 4, (c + 1) * model // 4)
            x_v[rows, n] = (dot_nn(sels[0], buf[s, :, n]) + dot_nn(sels[1], buf[s + 1, :, n])).astype(BF16)
        extra = dot_nn(sels[0], buf[s, :, model:]) + dot_nn(sels[1], buf[s + 1, :, model:])
        lane = lax.broadcasted_iota(jnp.int32, extra.shape, 1)
        hit = (lane == me) | (lane == me + 64)
        gate = jnp.sum(jnp.where(hit, extra, 0.0), axis=-1, keepdims=True)
        gate_v[rows, :] = jnp.broadcast_to(gate, extra.shape)

    def group(g, blocks):
        for j, (at, s) in enumerate(blocks):
            pick(at, s, j * room)
        leave(g, ((0, x_v, x_out), (1, gate_v, gate_out)))

        def first(c, carry):
            n = aligned(c, 256)
            x = x_v[...]
            gates = dot_nn(x, wg_v[:, n])
            u = dot_nn(x, wu_v[:, n])
            g_v[:, n] = gates.astype(BF16)
            u_v[:, n] = u.astype(BF16)
            hid_v[:, n] = (gates / (1.0 + jnp.exp(-gates)) * u).astype(BF16)
            return carry

        lax.fori_loop(0, wg.shape[1] // 256, first, 0)
        leave(g, ((2, g_v, g_out), (3, u_v, u_out), (4, hid_v, hid_out)))

        def second(c, carry):
            n = aligned(c, 256)
            o = dot_nn(hid_v[...], wd_v[:, n]).astype(BF16)
            o_v[:, n] = o
            y_v[:, n] = (o.astype(F32) * gate_v[:, :1]).astype(BF16)
            return carry

        lax.fori_loop(0, model // 256, second, 0)
        leave(g, ((5, o_v, o_out), (6, y_v, y_out)))

    def done():
        for copies in leaving.values():
            wait_all(copies)

    gather_world(mine, buf, *sems, before, group, done)


def experts_fwd(mine, wg, wu, wd, capacity, room):
    rows, width = mine.shape
    model, ff = wg.shape
    group = 4 * room
    wide = jax.ShapeDtypeStruct((16 * room, model), BF16)
    thin = jax.ShapeDtypeStruct((16 * room, ff), BF16)
    pos, x, y, g, u, o, hidden, gates = pl.pallas_call(
        functools.partial(experts_fwd_kernel, capacity),
        out_shape=(
            jax.ShapeDtypeStruct((32, 1, rows), F32),
            wide,
            wide,
            thin,
            thin,
            wide,
            thin,
            jax.ShapeDtypeStruct((16 * room, 128), F32),
        ),
        in_specs=[VMEM_SPEC, ANY_SPEC, ANY_SPEC, ANY_SPEC],
        out_specs=(VMEM_SPEC,) + (ANY_SPEC,) * 7,
        scratch_shapes=[
            pltpu.VMEM((32, rows, width), BF16),
            pltpu.VMEM((model, ff), BF16),
            pltpu.VMEM((model, ff), BF16),
            pltpu.VMEM((ff, model), BF16),
            pltpu.VMEM((group, model), BF16),
            pltpu.VMEM((group, model), BF16),
            pltpu.VMEM((group, ff), BF16),
            pltpu.VMEM((group, ff), BF16),
            pltpu.VMEM((group, model), BF16),
            pltpu.VMEM((group, ff), BF16),
            pltpu.VMEM((group, 128), F32),
            pltpu.SemaphoreType.DMA((2, 7)),
        ]
        + GATHER_SEMS,
        compiler_params=params(6),
        name="experts_fwd",
    )(mine, wg, wu, wd)
    return pos, x, y, (g, u, o, hidden, gates)


def experts_bwd_kernel(
    mine, pos, g_in, u_in, o_in, gate_in, wg, wu, wd, y_out, d_copy_out, dg_out, du_out,
    buf, wg_v, wu_v, wd_v, g_v, u_v, o_v, gate_v, y_v, d_copy_v, dg_v, du_v,
    local, ins, *sems,
):
    model, ff = wg.shape
    room = d_copy_v.shape[0] // 4
    me = lax.axis_index("dp") * 8 + lax.axis_index("expert")
    loads = start_all(
        [
            pltpu.make_async_copy(a, b, local.at[0, i])
            for i, (a, b) in enumerate(((wg, wg_v), (wu, wu_v), (wd, wd_v)))
        ]
    )
    leaving, coming = {g: [] for g in range(4)}, {}

    def fetch(g):
        kept = group_rows(g, room)
        coming[g] = start_all(
            [
                pltpu.make_async_copy(a.at[kept], v.at[g % 2], ins.at[g % 2, i])
                for i, (a, v) in enumerate(
                    ((g_in, g_v), (u_in, u_v), (o_in, o_v), (gate_in, gate_v))
                )
            ]
        )

    fetch(0)

    def leave(g, pairs):
        kept = group_rows(g, room)
        leaving[g].extend(
            start_all(
                [
                    pltpu.make_async_copy(v, o.at[kept], local.at[g % 2, i])
                    for i, v, o in pairs
                ]
            )
        )

    def before(g):
        wait_all(loads)
        wait_all(coming[g])
        if g + 1 < 4:
            fetch(g + 1)
        if g > 0:
            wait_all(leaving[g - 1])

    def pick(slot, at, s, start):
        rows = pl.ds(start, room)
        sels = [selector(pos[at * 2 + c], room) for c in range(2)]
        gate = gate_v[slot, rows, :1]
        inner = jnp.zeros((room, 1), F32)
        for c in range(4):
            n = slice(c * model // 4, (c + 1) * model // 4)
            picked = dot_nn(sels[0], buf[s, :, n]) + dot_nn(sels[1], buf[s + 1, :, n])
            d_copy_v[rows, n] = (gate * picked).astype(BF16)
            inner = inner + jnp.sum(picked * o_v[slot, rows, n].astype(F32), axis=-1, keepdims=True)
        top = inner.astype(BF16).astype(F32)
        rest = inner - top
        lane = lax.broadcasted_iota(jnp.int32, (room, 128), 1)
        extra = jnp.where(lane == me, top, 0.0) + jnp.where(lane == me + 64, rest, 0.0)
        y_v[rows, model:] = extra.astype(BF16)

    def group(g, blocks):
        slot = g % 2
        for j, (at, s) in enumerate(blocks):
            pick(slot, at, s, j * room)
        leave(g, ((0, d_copy_v, d_copy_out),))

        def third(c, carry):
            n = aligned(c, 256)
            d_hidden = dot_nt(d_copy_v[...], wd_v[n, :])
            gates, u = g_v[slot, :, n].astype(F32), u_v[slot, :, n].astype(F32)
            s = 1.0 / (1.0 + jnp.exp(-gates))
            dg_v[:, n] = (d_hidden * u * s * (1.0 + gates * (1.0 - s))).astype(BF16)
            du_v[:, n] = (d_hidden * gates * s).astype(BF16)
            return carry

        lax.fori_loop(0, ff // 256, third, 0)
        leave(g, ((1, dg_v, dg_out), (2, du_v, du_out)))

        def fourth(c, carry):
            n = aligned(c, 256)
            y_v[:, n] = (
                dot_nt(dg_v[...], wg_v[n, :]) + dot_nt(du_v[...], wu_v[n, :])
            ).astype(BF16)
            return carry

        lax.fori_loop(0, model // 256, fourth, 0)
        leave(g, ((3, y_v, y_out),))

    def done():
        for copies in leaving.values():
            wait_all(copies)

    gather_world(mine, buf, *sems, before, group, done)


def experts_bwd(mine, pos, kept, wg, wu, wd, room):
    rows, width = mine.shape
    model, ff = wg.shape
    group = 4 * room
    return pl.pallas_call(
        experts_bwd_kernel,
        out_shape=(
            jax.ShapeDtypeStruct((16 * room, model + 128), BF16),
            jax.ShapeDtypeStruct((16 * room, model), BF16),
            jax.ShapeDtypeStruct((16 * room, ff), BF16),
            jax.ShapeDtypeStruct((16 * room, ff), BF16),
        ),
        in_specs=[VMEM_SPEC, VMEM_SPEC] + [ANY_SPEC] * 7,
        out_specs=(ANY_SPEC,) * 4,
        scratch_shapes=[
            pltpu.VMEM((32, rows, width), BF16),
            pltpu.VMEM((model, ff), BF16),
            pltpu.VMEM((model, ff), BF16),
            pltpu.VMEM((ff, model), BF16),
            pltpu.VMEM((2, group, ff), BF16),
            pltpu.VMEM((2, group, ff), BF16),
            pltpu.VMEM((2, group, model), BF16),
            pltpu.VMEM((2, group, 128), F32),
            pltpu.VMEM((group, model + 128), BF16),
            pltpu.VMEM((group, model), BF16),
            pltpu.VMEM((group, ff), BF16),
            pltpu.VMEM((group, ff), BF16),
            pltpu.SemaphoreType.DMA((2, 4)),
            pltpu.SemaphoreType.DMA((2, 4)),
        ]
        + GATHER_SEMS,
        compiler_params=params(7),
        name="experts_bwd",
    )(mine, pos, *kept, wg, wu, wd)


def sum_world_kernel(
    y_in, pos, out, y, local, psend, pair, half_near, half_far, full_near, full_far, lines,
    ds, dr, hs, hr, fs, fr, zs, zr,
):
    r, e, z, core, near, far, greeted = world(True)
    rows, width = out.shape
    room = y.shape[1]
    half = rows // 2
    low, high = pl.ds(0, half), pl.ds(half, half)
    order = plane_order(z)[::-1]
    body_width = width // 512 * 512
    loads = loading(
        [(y_in.at[pl.ds(12 - 4 * k, 4)], y.at[pl.ds(12 - 4 * k, 4)]) for k in range(4)], local
    )
    greet(greeted)

    def for_columns(fn):
        def step(c, carry):
            fn(aligned(c, 512))
            return carry

        lax.fori_loop(0, body_width // 512, step, 0)
        if width > body_width:
            fn(pl.ds(body_width, width - body_width))

    def scattered(sel, k, i, n):
        return dot_tn(sel, y[(3 - k) * 4 + i, :, n])

    def select(k, i, c):
        return selector(pos[((3 - k) * 4 + i) * 2 + c], room)

    pairs, halves, fulls, moves = {}, {}, {}, []

    def stage_a(k):
        wait_all(loads[k])
        for i in (3, 1, 2, 0):
            at = k * 4 + i
            sel = select(k, i, 1 - core)

            def fill(n):
                psend[at, :, n] = scattered(sel, k, i, n).astype(BF16)

            for_columns(fill)
            copy = remote(psend.at[at], pair.at[at], ds.at[at], dr.at[at], (r, e ^ 1))
            copy.start()
            pairs[at] = copy
        for i in (3, 1, 2, 0):
            at = k * 4 + i
            sel = select(k, i, core)
            pairs[at].wait_recv()

            def add(n):
                value = scattered(sel, k, i, n) + pair[at, :, n].astype(F32)
                pair[at, :, n] = value.astype(BF16)

            for_columns(add)
            if i == 3:
                for side, (part, dst, p) in enumerate(
                    ((low, half_near, near), (high, half_far, far))
                ):
                    copy = remote(
                        pair.at[at, part], dst.at[k], hs.at[k, side], hr.at[k, side], (p, e)
                    )
                    copy.start()
                    halves[k, side] = copy

    def stage_b(k):
        for side, (i, part, src, dst, p) in enumerate(
            (
                (2, low, half_near, full_far, far),
                (1, high, half_far, full_near, near),
            )
        ):
            at = k * 4 + i
            halves[k, side].wait_recv()

            def add(n):
                value = pair[at, part, n].astype(F32) + src[k, :, n].astype(F32)
                pair[at, part, n] = value.astype(BF16)

            for_columns(add)
            copy = remote(pair.at[at], dst.at[k], fs.at[k, side], fr.at[k, side], (p, e))
            copy.start()
            fulls[k, side] = copy

    def stage_c(k):
        b = order[k]
        at = k * 4
        fulls[k, 0].wait_recv()
        fulls[k, 1].wait_recv()

        def add(n):
            out[:, n] = (
                pair[at, :, n].astype(F32)
                + full_near[k, :, n].astype(F32)
                + full_far[k, :, n].astype(F32)
            )

        for_columns(add)
        for side, cond in ((0, (b >= z) & (z > 0)), (1, (b <= z) & (z < 3))):

            @pl.when(cond)
            def _():
                remote(
                    lines.at[side, b], lines.at[side, b], zs.at[side, k], zr.at[side, b], (r, e ^ 1)
                ).wait_recv()

                def more(n):
                    out[:, n] = out[:, n] + lines[side, b, :, n].astype(F32)

                for_columns(more)

        if k < 3:

            def keep(n):
                pair[at, :, n] = out[:, n].astype(BF16)

            for_columns(keep)
            for side, cond, to in (
                (0, b > z, jnp.minimum(z + 1, 3)),
                (1, b < z, jnp.maximum(z - 1, 0)),
            ):
                copy = remote(
                    pair.at[at], lines.at[side, b], zs.at[side, k], zr.at[side, b], (r, to * 2 + core)
                )
                moves.append((cond, copy))

                @pl.when(cond)
                def _():
                    copy.start()

    stage_a(0)
    stage_a(1)
    stage_b(0)
    stage_a(2)
    stage_b(1)
    stage_c(0)
    stage_a(3)
    stage_b(2)
    stage_c(1)
    stage_b(3)
    stage_c(2)
    stage_c(3)
    for copies in (pairs, halves, fulls):
        for copy in copies.values():
            copy.wait_send()
    for cond, copy in moves:

        @pl.when(cond)
        def _():
            copy.wait_send()


def sum_world(y, pos, rows, collective_id):
    width = y.shape[-1]

    def blocks(n, size):
        return pltpu.VMEM((n, size, width), BF16)

    return pl.pallas_call(
        sum_world_kernel,
        out_shape=jax.ShapeDtypeStruct((rows, width), F32),
        in_specs=[ANY_SPEC, VMEM_SPEC],
        out_specs=VMEM_SPEC,
        scratch_shapes=[
            pltpu.VMEM(y.shape, BF16),
            pltpu.SemaphoreType.DMA((4,)),
            blocks(16, rows),
            blocks(16, rows),
            blocks(4, rows // 2),
            blocks(4, rows // 2),
            blocks(4, rows),
            blocks(4, rows),
            pltpu.VMEM((2, 4, rows, width), BF16),
            pltpu.SemaphoreType.DMA((16,)),
            pltpu.SemaphoreType.DMA((16,)),
            pltpu.SemaphoreType.DMA((4, 2)),
            pltpu.SemaphoreType.DMA((4, 2)),
            pltpu.SemaphoreType.DMA((4, 2)),
            pltpu.SemaphoreType.DMA((4, 2)),
            pltpu.SemaphoreType.DMA((2, 4)),
            pltpu.SemaphoreType.DMA((2, 4)),
        ],
        compiler_params=params(collective_id),
        name="sum_world",
    )(y, pos)


def expert_grads_kernel(x, d_gate, d_up, hidden, d_copy, gate_grad, up_grad, down_grad, hidden_t):
    @pl.when(pl.program_id(0) == 0)
    def _():
        hidden_t[...] = hidden[...].T

    rows = x[...].T
    gate_grad[...] = dot_nn(rows, d_gate[...])
    up_grad[...] = dot_nn(rows, d_up[...])
    down_grad[...] = dot_nn(hidden_t[...], d_copy[...])


def expert_grads(x, d_gate, d_up, hidden, d_copy):
    slots, model = x.shape
    ff = hidden.shape[1]
    step = 256
    whole = pl.BlockSpec((slots, ff), lambda i: (0, 0))
    columns = pl.BlockSpec((slots, step), lambda i: (0, i))
    return pl.pallas_call(
        expert_grads_kernel,
        grid=(model // step,),
        in_specs=[columns, whole, whole, whole, columns],
        out_specs=[
            pl.BlockSpec((step, ff), lambda i: (i, 0)),
            pl.BlockSpec((step, ff), lambda i: (i, 0)),
            pl.BlockSpec((ff, step), lambda i: (0, i)),
        ],
        out_shape=(
            jax.ShapeDtypeStruct((model, ff), F32),
            jax.ShapeDtypeStruct((model, ff), F32),
            jax.ShapeDtypeStruct((ff, model), F32),
        ),
        scratch_shapes=[pltpu.VMEM((ff, slots), BF16)],
        compiler_params=params(),
        name="expert_grads",
    )(x, d_gate, d_up, hidden, d_copy)


def experts_by_all_to_all(
    mixed, state, teacher, routes, valid_slot, valid_count, router_weight, gate_weight, up_weight, down_weight,
    devices, capacity, slots_all,
):
    tok_dev, model_width = mixed.shape
    top_count = routes.shape[1]
    ffn_width = gate_weight.shape[2]
    logits = jnp.dot(mixed, router_weight, preferred_element_type=jnp.float32)
    gates = jax.nn.softmax(jnp.take_along_axis(logits, routes, axis=1), axis=-1)
    rows_total = tok_dev * top_count
    expert_ids = routes.reshape(rows_total)
    live_rows = jnp.repeat(valid_slot, top_count)
    expert_range = jnp.arange(devices, dtype=jnp.int32)
    hit_table = ((expert_ids[:, None] == expert_range[None, :]) & live_rows[:, None]).astype(
        jnp.int32
    )
    earlier = jnp.cumsum(hit_table, axis=0) - hit_table
    position_in = jnp.sum(earlier * hit_table, axis=1)
    slot_index = jnp.where(live_rows, expert_ids * capacity + position_in, devices * capacity)
    row_of_slot = (
        jnp.full((devices * capacity + 1,), rows_total, jnp.int32)
        .at[slot_index]
        .set(jnp.arange(rows_total, dtype=jnp.int32))[: devices * capacity]
    )
    token_of_slot = jnp.where(row_of_slot < rows_total, row_of_slot // top_count, tok_dev)
    mixed_pad = jnp.concatenate([mixed, jnp.zeros((1, model_width), jnp.bfloat16)], axis=0)
    send_rows = mixed_pad[token_of_slot].reshape(devices, capacity, model_width)
    arrived = lax.all_to_all(send_rows, ("dp", "expert"), split_axis=0, concat_axis=0, tiled=True)
    sources = arrived.shape[0]
    items = arrived.shape[1]
    flat_in = arrived.reshape(sources * items, model_width)
    gate_pre = jnp.dot(flat_in, gate_weight[0], preferred_element_type=jnp.float32)
    up_pre = jnp.dot(flat_in, up_weight[0], preferred_element_type=jnp.float32)
    hidden_units = (jax.nn.silu(gate_pre) * up_pre).astype(jnp.bfloat16)
    produced = jnp.dot(hidden_units, down_weight[0], preferred_element_type=jnp.float32).astype(
        jnp.bfloat16
    )
    produced, gate_pre, up_pre, hidden_units, arrived = (
        produced.reshape(sources, items, model_width),
        gate_pre.reshape(sources, items, ffn_width),
        up_pre.reshape(sources, items, ffn_width),
        hidden_units.reshape(sources, items, ffn_width),
        arrived,
    )
    returned = lax.all_to_all(produced, ("dp", "expert"), split_axis=0, concat_axis=0, tiled=True)
    returned_pad = jnp.concatenate(
        [
            returned.reshape(devices * capacity, model_width),
            jnp.zeros((1, model_width), jnp.bfloat16),
        ],
        axis=0,
    )
    copies = returned_pad[slot_index].reshape(tok_dev, top_count, model_width)
    layer_out = state + jnp.sum(gates[:, :, None] * copies, axis=1)
    live_tokens = valid_slot.astype(jnp.float32)[:, None]
    diff = (layer_out - teacher.astype(jnp.float32)) * live_tokens
    local_square = jnp.sum(diff * diff)
    d_out = 2.0 * slots_all * diff / valid_count
    d_gates = jnp.sum(d_out[:, None, :] * copies, axis=-1)
    d_chosen = gates * (d_gates - jnp.sum(gates * d_gates, axis=-1, keepdims=True))
    d_logits = jnp.sum(
        jnp.where(routes[:, :, None] == expert_range[None, None, :], d_chosen[:, :, None], 0.0),
        axis=1,
    ).astype(jnp.bfloat16)
    d_copies = (
        (gates[:, :, None] * d_out[:, None, :])
        .astype(jnp.bfloat16)
        .reshape(rows_total, model_width)
    )
    d_copies_pad = jnp.concatenate([d_copies, jnp.zeros((1, model_width), jnp.bfloat16)], axis=0)
    d_send = d_copies_pad[row_of_slot].reshape(devices, capacity, model_width)
    d_arrived = lax.all_to_all(d_send, ("dp", "expert"), split_axis=0, concat_axis=0, tiled=True)
    flat_d = d_arrived.reshape(-1, model_width)
    flat_in = arrived.reshape(-1, model_width)
    flat_gate = gate_pre.reshape(-1, ffn_width)
    flat_up = up_pre.reshape(-1, ffn_width)
    flat_hidden = hidden_units.reshape(-1, ffn_width)
    d_hidden = contract(flat_d, down_weight[0], 1, 1)
    sigmoid_gate = jax.nn.sigmoid(flat_gate)
    d_gate = (d_hidden * flat_up * sigmoid_gate * (1.0 + flat_gate * (1.0 - sigmoid_gate))).astype(
        jnp.bfloat16
    )
    d_up = (d_hidden * flat_gate * sigmoid_gate).astype(jnp.bfloat16)
    down_grad = contract(flat_hidden, flat_d, 0, 0)[None]
    gate_grad = contract(flat_in, d_gate, 0, 0)[None]
    up_grad = contract(flat_in, d_up, 0, 0)[None]
    d_in = (contract(d_gate, gate_weight[0], 1, 1) + contract(d_up, up_weight[0], 1, 1)).astype(
        jnp.bfloat16
    )
    d_returned = lax.all_to_all(
        d_in.reshape(devices, capacity, model_width),
        ("dp", "expert"),
        split_axis=0,
        concat_axis=0,
        tiled=True,
    )
    d_returned_pad = jnp.concatenate(
        [
            d_returned.reshape(devices * capacity, model_width),
            jnp.zeros((1, model_width), jnp.bfloat16),
        ],
        axis=0,
    )
    d_mixed = jnp.sum(
        d_returned_pad[slot_index].reshape(tok_dev, top_count, model_width),
        axis=1,
        dtype=jnp.float32,
    )
    d_mixed = d_mixed + contract(d_logits, router_weight, 1, 1)
    router_local = contract(d_logits, mixed, 0, 0)
    return layer_out, d_out, d_mixed, local_square, router_local, gate_grad, up_grad, down_grad


def experts_by_gather(
    mixed, state, teacher, routes, valid_slot, valid_count, router_weight,
    gate_weight, up_weight, down_weight, devices, capacity, slots_all,
):
    tok_dev, model_width = mixed.shape
    room = -(-2 * capacity // 16) * 16
    expert_range = jnp.arange(devices, dtype=jnp.int32)
    logits = jnp.dot(mixed, router_weight, preferred_element_type=F32)
    chosen = jnp.any(routes[:, :, None] == expert_range[None, None], axis=1)
    gates = jax.nn.softmax(jnp.where(chosen, logits, -jnp.inf), axis=-1)
    live_gates = jnp.where(valid_slot[:, None], gates, 0.0)
    gates_high = live_gates.astype(BF16)
    gates_low = (live_gates - gates_high.astype(F32)).astype(BF16)
    gap = jnp.zeros((tok_dev, 64 - devices), BF16)
    payload = jnp.concatenate([mixed, gates_high, gap, gates_low, gap], axis=1)
    pos, x_rows, y_rows, kept = experts_fwd(
        payload, gate_weight[0], up_weight[0], down_weight[0], capacity, room
    )
    layer_out = state + sum_world(y_rows.reshape(16, room, model_width), pos, tok_dev, 8)
    live_tokens = valid_slot.astype(F32)[:, None]
    diff = (layer_out - teacher.astype(F32)) * live_tokens
    local_square = jnp.sum(diff * diff)
    d_out = 2.0 * slots_all * diff / valid_count
    hidden = kept[3]
    d_rows, d_copy, d_gate, d_up = experts_bwd(
        d_out.astype(BF16), pos, kept[:3] + kept[4:], gate_weight[0], up_weight[0], down_weight[0], room
    )
    back = sum_world(d_rows.reshape(16, room, model_width + 128), pos, tok_dev, 9)

    gate_grad, up_grad, down_grad = (
        grad[None] for grad in expert_grads(x_rows, d_gate, d_up, hidden, d_copy)
    )
    d_gates = back[:, model_width : model_width + devices] + back[:, model_width + 64 : model_width + 64 + devices]
    d_logits = (gates * (d_gates - jnp.sum(gates * d_gates, axis=-1, keepdims=True))).astype(BF16)
    d_mixed = back[:, :model_width] + contract(d_logits, router_weight, 1, 1)
    router_local = contract(d_logits, mixed, 0, 0)
    return layer_out, d_out, d_mixed, local_square, router_local, gate_grad, up_grad, down_grad


def head_rope(linear, gain_vec, cos, sin):
    value = root_mean_scale(linear, gain_vec)
    half = value.shape[-1] // 2
    return value * cos + jnp.roll(value, half, axis=-1) * sin


def body(
    tokens,
    teacher,
    routes,
    cont_lengths,
    query_weight,
    key_projection,
    value_projection,
    output_weight,
    router_weight,
    gate_weight,
    up_weight,
    down_weight,
    input_gain,
    post_gain,
    query_gain,
    key_gain,
):
    n_dp = lax.axis_size("dp")
    n_owner = lax.axis_size("expert")
    devices = n_dp * n_owner
    rank_dp = lax.axis_index("dp")
    rank_owner = lax.axis_index("expert")
    flat_rank = rank_dp * n_owner + rank_owner
    column = rank_owner % 2
    first_column = column == 0
    tok_dev, model_width = tokens.shape
    top_count = routes.shape[1]
    head_dim = query_gain.shape[0]
    kv_width = key_projection.shape[1]
    query_width = query_weight.shape[1]
    query_group = query_width // n_dp
    assert n_dp == 4 and kv_width == n_dp * head_dim
    prompt_block = tok_dev - CMAX
    half_prompt = n_dp * prompt_block
    prompt_len = 2 * half_prompt
    capacity = max(2, tok_dev * top_count * 5 // (4 * devices))
    slots_all = devices * tok_dev
    slot_ids = jnp.arange(tok_dev, dtype=jnp.int32)
    own_length = cont_lengths[flat_rank]
    valid_slot = (slot_ids < prompt_block) | (slot_ids - prompt_block < own_length)
    valid_count = (devices * prompt_block + jnp.sum(cont_lengths)).astype(F32)
    tokens_float = tokens.astype(F32)
    normed_float, first_norm_back = jax.vjp(root_mean_scale, tokens_float, input_gain)
    normed = normed_float.astype(BF16)

    block_ids = jnp.arange(n_dp, dtype=jnp.int32)[:, None]
    positions = jnp.where(
        slot_ids[None] < prompt_block,
        (column * n_dp + block_ids) * prompt_block + slot_ids[None],
        prompt_len + slot_ids[None] - prompt_block,
    )
    half_head = head_dim // 2
    frequency = rope_base ** (-(jnp.arange(half_head, dtype=F32) * 2.0) / head_dim)
    angles = positions.astype(F32)[:, :, None] * frequency
    cos_half, sin_half = jnp.cos(angles), jnp.sin(angles)
    cos = jnp.concatenate([cos_half, cos_half], axis=-1)
    sin = jnp.concatenate([-sin_half, sin_half], axis=-1)
    lengths = jnp.concatenate(
        [lax.dynamic_index_in_dim(cont_lengths.reshape(n_dp, n_owner), rank_owner, 1, False), column[None]]
    ).astype(jnp.int32)

    lin, normed_cols_t, normed_cols, key_lin, all_keys, all_values = project_qkv(
        normed, query_weight, key_projection, value_projection, key_gain[None], cos, sin
    )
    query_gain_row = query_gain[None]
    queries, attended = attention_fwd(
        lengths, lin, query_gain_row, cos, sin, all_keys, all_values, prompt_len
    )
    state = tokens_float + project_out(attended, output_weight)
    mixed_float, second_norm_back = jax.vjp(root_mean_scale, state, post_gain)
    mixed = mixed_float.astype(BF16)
    sizes = (devices, capacity, slots_all)
    weights = (router_weight, gate_weight, up_weight, down_weight)
    if n_dp == 4 and n_owner == 8:
        moe = experts_by_gather(
            mixed, state, teacher, routes, valid_slot, valid_count, *weights, *sizes
        )
    else:
        moe = experts_by_all_to_all(
            mixed, state, teacher, routes, valid_slot, valid_count, *weights, *sizes
        )
    layer_out, d_out, d_mixed, local_square, router_local, gate_grad, up_grad, down_grad = moe
    d_state_norm, d_post_gain = second_norm_back(d_mixed)
    d_state = d_out + d_state_norm
    d_branch = d_state.astype(BF16)
    d_attended, d_branch_all, attended_t = grad_branch(d_branch, output_weight, attended)
    d_query_lin, d_keys, d_values, gain_parts, out_part = attention_bwd(
        lengths, lin, queries, d_attended, query_gain_row, cos, sin, all_keys, all_values,
        attended_t, d_branch_all, prompt_len,
    )
    d_query_gain = jnp.sum(gain_parts, axis=(0, 1))
    width = query_weight.shape[0]
    group = query_group + 2 * head_dim
    rows_here = width // n_owner
    by_line = n_dp == 4 and n_owner == 8

    def packed(parts):
        small = jnp.concatenate([a.reshape(-1) for a in parts])
        piece_rows = -(-small.shape[0] // (8 * 8 * 128)) * 8
        small = jnp.pad(small, (0, 8 * piece_rows * 128 - small.shape[0]))
        return small.reshape(8, piece_rows, 128)

    out_part = out_part.reshape(n_owner, -1, model_width)
    weights = (query_weight, key_projection, value_projection)
    if by_line:

        def line(parts):
            flat = jnp.concatenate(parts)
            return jnp.pad(flat, (0, model_width - flat.shape[0]))[None]

        small = jnp.concatenate(
            [router_local, d_post_gain[None], line([d_query_gain]), line([local_square[None]])]
        )
        small_rows = -(-small.shape[0] // 8) * 8
        small = jnp.pad(small, ((0, small_rows - small.shape[0]), (0, 0)))
        small = small.reshape(small_rows, 8, -1).transpose(1, 0, 2)
        d_normed, query_grad, key_grad, value_grad, output_grad, small, input_gain_grad = grad_qkv_line(
            d_query_lin, d_keys, d_values, key_lin, cos, sin, key_gain[None],
            *weights, normed_cols_t, normed_cols, out_part, small, input_gain[None],
        )
        key_gain_grad = jnp.sum(input_gain_grad[:, 1, :head_dim], axis=0)
        input_gain_grad = input_gain_grad[:, 0].reshape(-1)
        sums = small.transpose(1, 0, 2).reshape(small_rows, model_width)
        at = router_local.shape[0]
        router_grad, post_gain_grad = sums[:at].T, sums[at]
        query_gain_grad = sums[at + 1, :head_dim]
        total_square = sums[at + 2, :1]
        d_tokens_norm = first_norm_back(d_normed)[0]
    else:
        _, key_back = jax.vjp(
            lambda a, b: head_rope(a, b, cos, sin), key_lin.reshape(n_dp, tok_dev, head_dim), key_gain
        )
        prompt_grads = jnp.stack(
            [jnp.sum(d_keys[:, :prompt_len], axis=0), jnp.sum(d_values[:, :prompt_len], axis=0)]
        )
        mine_part = jnp.where(first_column, prompt_grads[:, :half_prompt], prompt_grads[:, half_prompt:])
        their_part = jnp.where(first_column, prompt_grads[:, half_prompt:], prompt_grads[:, :half_prompt])
        own_prompt = (mine_part + partner(their_part, "expert", 0)).reshape(
            2, n_dp, prompt_block, head_dim
        )
        d_key_post = jnp.concatenate([own_prompt[0], d_keys[:, prompt_len:]], axis=1)
        d_value_lin = jnp.concatenate([own_prompt[1], d_values[:, prompt_len:]], axis=1)
        d_key_float, d_key_gain = key_back(d_key_post)
        rows = n_dp * tok_dev
        d_lin = jnp.concatenate(
            [
                d_query_lin,
                d_key_float.astype(BF16).reshape(rows, head_dim),
                d_value_lin.astype(BF16).reshape(rows, head_dim),
            ],
            axis=1,
        )
        small_parts = [router_local, d_post_gain, d_query_gain, d_key_gain, local_square[None]]
        d_normed, qkv_part, output_grad = grad_qkv(d_lin, *weights, normed_cols_t, out_part)
        d_tokens_norm, d_input_gain = first_norm_back(d_normed)
        small_parts.append(d_input_gain)
        by_owner = (
            qkv_part.reshape(n_dp, n_owner, rows_here, group)
            .transpose(1, 0, 2, 3)
            .reshape(n_owner, n_dp * rows_here, group)
        )
        qkv_rows, small = last_sums(by_owner, packed(small_parts))
        qkv_rows = qkv_rows.reshape(n_dp, rows_here, group)

        def columns(start, size):
            part = qkv_rows[:, :, start : start + size]
            return part.transpose(1, 0, 2).reshape(rows_here, n_dp * size)

        query_grad = columns(0, query_group)
        key_grad = columns(query_group, head_dim)
        value_grad = columns(query_group + head_dim, head_dim)
        small = small.reshape(-1)
        starts = [0]
        for a in small_parts:
            starts.append(starts[-1] + a.size)
        sums = [small[i:j].reshape(a.shape) for a, i, j in zip(small_parts, starts, starts[1:])]
        router_grad, post_gain_grad, query_gain_grad, key_gain_grad, total_square, input_gain_grad = sums
        router_grad = router_grad.T
    tokens_grad = d_state + d_tokens_norm
    loss = total_square[0] / (valid_count * model_width)
    return (
        layer_out,
        loss,
        tokens_grad,
        query_grad,
        key_grad,
        value_grad,
        output_grad,
        router_grad,
        gate_grad,
        up_grad,
        down_grad,
        input_gain_grad,
        post_gain_grad,
        query_gain_grad,
        key_gain_grad,
    )


def solution(mesh):
    in_specs = (
        P(("dp", "expert"), None),
        P(("dp", "expert"), None),
        P(("dp", "expert"), None),
        P(),
        P("dp", None),
        P("dp", None),
        P("dp", None),
        P("dp", None),
        P(),
        P(("dp", "expert"), None, None),
        P(("dp", "expert"), None, None),
        P(("dp", "expert"), None, None),
        P(),
        P(),
        P(),
        P(),
    )
    out_specs = (
        P(("dp", "expert"), None),
        P(),
        P(("dp", "expert"), None),
        P(("dp", "expert"), None),
        P(("dp", "expert"), None),
        P(("dp", "expert"), None),
        P(("dp", "expert"), None),
        P(),
        P(("dp", "expert"), None, None),
        P(("dp", "expert"), None, None),
        P(("dp", "expert"), None, None),
        P(),
        P(),
        P(),
        P(),
    )
    return jax.shard_map(body, mesh=mesh, in_specs=in_specs, out_specs=out_specs, check_vma=False)
```

```python
import functools

import jax
import jax.numpy as jnp
from jax import lax
from jax.experimental import pallas as pl
from jax.experimental.pallas import tpu as pltpu
from jax.sharding import PartitionSpec as P

CMAX = 128
norm_eps = 1e-06
rope_base = 1000000.0
MESH = pl.DeviceIdType.MESH
F32 = jnp.float32
BF16 = jnp.bfloat16
VMEM_SPEC = pl.BlockSpec(memory_space=pltpu.VMEM)
ANY_SPEC = pl.BlockSpec(memory_space=pl.ANY)
VMEM_LIMIT = 56 * 1024 * 1024


def params(collective_id=None):
    return pltpu.CompilerParams(
        collective_id=collective_id,
        has_side_effects=collective_id is not None,
        vmem_limit_bytes=VMEM_LIMIT,
    )


def greet(devices):
    barrier = pltpu.get_barrier_semaphore()
    for device in devices:
        pl.semaphore_signal(barrier, inc=1, device_id=device, device_id_type=MESH)
    pl.semaphore_wait(barrier, len(devices))


def remote(src, dst, send_sem, recv_sem, device):
    return pltpu.make_async_remote_copy(
        src_ref=src,
        dst_ref=dst,
        send_sem=send_sem,
        recv_sem=recv_sem,
        device_id=device,
        device_id_type=MESH,
    )


def start_all(copies):
    for copy in copies:
        copy.start()
    return copies


def wait_all(copies):
    for copy in copies:
        copy.wait()
    copies.clear()


def loading(pairs, sems):
    return [start_all([pltpu.make_async_copy(a, b, sems.at[i])]) for i, (a, b) in enumerate(pairs)]


def aligned(index, size):
    return pl.ds(pl.multiple_of(index * size, size), size)


def dot_nn(a, b):
    return lax.dot_general(a, b, (((1,), (0,)), ((), ())), preferred_element_type=F32)


def dot_nt(a, b):
    return lax.dot_general(a, b, (((1,), (1,)), ((), ())), preferred_element_type=F32)


def dot_tn(a, b):
    return lax.dot_general(a, b, (((0,), (0,)), ((), ())), preferred_element_type=F32)


PEER_MASKS = (3, 1, 2)


def relay_sum(r, e, products, own, mine, send, half_in, full_in, hs, hr, fs, fr, step):
    near, far, diag = r ^ 1, r ^ 2, r ^ 3
    rows = mine.shape[0]
    half = rows // 2
    low, high = pl.ds(0, half), pl.ds(half, half)
    products(diag, send.at[2])
    relays = [
        remote(send.at[2, low], half_in.at[0], hs.at[0], hr.at[0], (near, e)),
        remote(send.at[2, high], half_in.at[1], hs.at[1], hr.at[1], (far, e)),
    ]
    for copy in relays:
        copy.start()
    parts = ((0, low, near), (1, high, far), (0, high, near), (1, low, far))
    fulls = [
        remote(send.at[i, part], full_in.at[i, part], fs.at[n], fr.at[n], (p, e))
        for n, (i, part, p) in enumerate(parts)
    ]
    products(near, send.at[0])
    fulls[0].start()
    products(far, send.at[1])
    fulls[1].start()
    for i, start, slot, n in ((1, 0, 0, 3), (0, half, 1, 2)):
        relays[slot].wait_recv()

        def add(c, carry):
            t = pl.ds(pl.multiple_of(start + c * step, step), step)
            value = send[i, t, :].astype(F32) + half_in[slot, aligned(c, step), :].astype(F32)
            send[i, t, :] = value.astype(BF16)
            return carry

        lax.fori_loop(0, half // step, add, 0)
        fulls[n].start()
    own()
    for copy in fulls:
        copy.wait_recv()

    def total(c, carry):
        t = aligned(c, step)
        mine[t, :] = mine[t, :] + (full_in[0, t, :].astype(F32) + full_in[1, t, :].astype(F32))
        return carry

    lax.fori_loop(0, rows // step, total, 0)
    for copy in relays + fulls:
        copy.wait_send()


def relay_scratch(rows, width):
    return [
        pltpu.VMEM((3, rows, width), BF16),
        pltpu.VMEM((2, rows // 2, width), BF16),
        pltpu.VMEM((2, rows, width), BF16),
        pltpu.SemaphoreType.DMA((2,)),
        pltpu.SemaphoreType.DMA((2,)),
        pltpu.SemaphoreType.DMA((4,)),
        pltpu.SemaphoreType.DMA((4,)),
    ]


def qkv_kernel(
    tok, normed, wq_in, wk_in, wv_in, gain, cos, sin, lin, cols_t, cols, key_lin, keys, values,
    wq, wk, wv, own_kv, other_kv, local, asend, arecv, ksend, krecv, *relay,
):
    r, e = lax.axis_index("dp"), lax.axis_index("expert")
    peers = [r ^ m for m in PEER_MASKS]
    width = wq.shape[0]
    qg = wq.shape[1] // 4
    kg = wk.shape[1] // 4
    rows = cols.shape[0]
    loads = loading(((wq_in, wq), (wk_in, wk), (wv_in, wv)), local)
    greet([(p, e) for p in peers] + [(r, e ^ 1)])
    first = []
    for i, p in enumerate(peers):
        copy = remote(
            normed.at[:, aligned(p, width)], cols.at[aligned(r, tok), :],
            asend.at[i], arecv.at[i], (p, e),
        )
        copy.start()
        first.append(copy)
    cols[aligned(r, tok), :] = normed[:, aligned(r, width)]
    for copy in first:
        copy.wait()
    for copies in loads:
        wait_all(copies)

    def products(p, dst):
        def chunk(c, carry):
            columns = pl.ds(pl.multiple_of(p * qg + c * 256, 256), 256)
            dst[:, aligned(c, 256)] = dot_nn(cols[...], wq[:, columns]).astype(dst.dtype)
            return carry

        lax.fori_loop(0, qg // 256, chunk, 0)
        dst[:, qg : qg + kg] = dot_nn(cols[...], wk[:, aligned(p, kg)]).astype(dst.dtype)
        dst[:, qg + kg :] = dot_nn(cols[...], wv[:, aligned(p, kg)]).astype(dst.dtype)

    def own():
        products(r, lin)
        cols_t[...] = cols[...].T

    relay_sum(r, e, products, own, lin, *relay, 32)
    core = e % 2
    head = gain.shape[1]
    prompt = tok - CMAX
    column = 4 * prompt
    for i in range(4):
        rows_i = slice(i * tok, (i + 1) * tok)
        x = lin[rows_i, qg : qg + kg]
        key_lin[rows_i, :] = x
        x = x * lax.rsqrt(jnp.mean(x * x, axis=-1, keepdims=True) + norm_eps) * gain[...]
        k = (x * cos[i] + pltpu.roll(x, head // 2, 1) * sin[i]).astype(BF16)
        v = lin[rows_i, qg + kg :].astype(BF16)
        for n, (part, out) in enumerate(((k, keys), (v, values))):
            own_kv[n, i * prompt : (i + 1) * prompt] = part[:prompt]
            out[i, 2 * column :] = part[prompt:]
    copy = remote(own_kv, other_kv, ksend.at[0], krecv.at[0], (r, e ^ 1))
    copy.start()
    for n, out in enumerate((keys, values)):
        for i in range(4):
            out[i, aligned(core, column)] = own_kv[n]
    copy.wait()
    for n, out in enumerate((keys, values)):
        for i in range(4):
            out[i, aligned(1 - core, column)] = other_kv[n]


def project_qkv(normed, wq, wk, wv, gain, cos, sin):
    tok = normed.shape[0]
    rows = 4 * tok
    group = (wq.shape[1] + wk.shape[1] + wv.shape[1]) // 4
    head = gain.shape[1]
    total_keys = 8 * (tok - CMAX) + CMAX
    return pl.pallas_call(
        functools.partial(qkv_kernel, tok),
        out_shape=(
            jax.ShapeDtypeStruct((rows, group), F32),
            jax.ShapeDtypeStruct((wq.shape[0], rows), BF16),
            jax.ShapeDtypeStruct((rows, wq.shape[0]), BF16),
            jax.ShapeDtypeStruct((rows, head), F32),
            jax.ShapeDtypeStruct((4, total_keys, head), BF16),
            jax.ShapeDtypeStruct((4, total_keys, head), BF16),
        ),
        in_specs=[VMEM_SPEC] + [ANY_SPEC] * 3 + [VMEM_SPEC] * 3,
        out_specs=(VMEM_SPEC,) * 6,
        scratch_shapes=[pltpu.VMEM(w.shape, BF16) for w in (wq, wk, wv)]
        + [pltpu.VMEM((2, 4 * (tok - CMAX), head), BF16)] * 2
        + [pltpu.SemaphoreType.DMA((3,))] * 3
        + [pltpu.SemaphoreType.DMA((1,))] * 2
        + relay_scratch(rows, group),
        compiler_params=params(1),
        name="qkv_exchange",
    )(normed, wq, wk, wv, gain, cos, sin)


def out_kernel(attn_in, wo_in, total, attn, wo, local, *relay):
    r, e = lax.axis_index("dp"), lax.axis_index("expert")
    tok, width = total.shape
    step = width // 4
    loads = loading(((attn_in, attn), (wo_in, wo)), local)
    greet([(r ^ m, e) for m in PEER_MASKS])
    for copies in loads:
        wait_all(copies)

    def products(p, dst):
        def chunk(c, carry):
            n = aligned(c, step)
            dst[:, n] = dot_nn(attn[aligned(p, tok), :], wo[:, n]).astype(dst.dtype)
            return carry

        lax.fori_loop(0, width // step, chunk, 0)

    relay_sum(r, e, products, lambda: products(r, total), total, *relay, 16)


def project_out(attn, wo):
    tok = attn.shape[0] // 4
    return pl.pallas_call(
        out_kernel,
        out_shape=jax.ShapeDtypeStruct((tok, wo.shape[1]), F32),
        in_specs=[ANY_SPEC] * 2,
        out_specs=VMEM_SPEC,
        scratch_shapes=[
            pltpu.VMEM(attn.shape, BF16),
            pltpu.VMEM(wo.shape, BF16),
            pltpu.SemaphoreType.DMA((2,)),
        ]
        + relay_scratch(tok, wo.shape[1]),
        compiler_params=params(2),
        name="out_exchange",
    )(attn, wo)


def dgrad_kernel(
    mine, wq, wk, wv, cols_t, out_part, normal, grads, out_grad,
    blocks, dsum, dsend, drecv, ssem, rsem, bsend, brecv, *scratch,
):
    r, e = lax.axis_index("dp"), lax.axis_index("expert")
    rows = mine.shape[0]
    tok = rows // 4
    half = rows // 2
    qg = wq.shape[1] // 4
    kg = wk.shape[1] // 4
    width = wq.shape[0]
    peers = [r ^ m for m in PEER_MASKS]
    near, far, diag = r ^ 1, r ^ 2, r ^ 3
    pair_in, send, recv, *sems = scratch
    begin, middle, finish = owner_sum([out_part], [out_grad], [pair_in], [send], [recv], *sems)
    greet([(p, e) for p in peers] + [(r, e ^ 1)] + owner_peers())
    begin()
    low, high = pl.ds(0, half), pl.ds(half, half)
    first_near = remote(mine.at[low], blocks.at[0, low], ssem.at[0], rsem.at[0], (near, e))
    first_far = remote(mine.at[high], blocks.at[1, high], ssem.at[1], rsem.at[1], (far, e))
    second_near = remote(mine.at[high], blocks.at[0, high], ssem.at[2], rsem.at[2], (near, e))
    second_far = remote(mine.at[low], blocks.at[1, low], ssem.at[3], rsem.at[3], (far, e))
    pass_far = remote(blocks.at[0, low], blocks.at[2, low], ssem.at[4], rsem.at[4], (far, e))
    pass_near = remote(blocks.at[1, high], blocks.at[2, high], ssem.at[5], rsem.at[5], (near, e))
    for copy in (first_near, first_far, second_near, second_far):
        copy.start()

    def products(p, src, start):
        def chunk(c, carry):
            t = aligned(c, tok)
            x = src[t, :]
            value = (
                dot_nt(x[:, :qg], wq[:, aligned(p, qg)])
                + dot_nt(x[:, qg : qg + kg], wk[:, aligned(p, kg)])
                + dot_nt(x[:, qg + kg :], wv[:, aligned(p, kg)])
            )
            if start:
                dsum[t, :] = value
            else:
                dsum[t, :] = dsum[t, :] + value
            return carry

        lax.fori_loop(0, 4, chunk, 0)

        def outer(c, carry):
            n = aligned(c, 128)
            grads[aligned(p, width), n] = dot_nn(cols_t[...], src[:, n]).astype(BF16)
            return carry

        lax.fori_loop(0, (qg + 2 * kg) // 128, outer, 0)

    middle()
    products(r, mine, True)
    first_near.wait()
    pass_far.start()
    first_far.wait()
    pass_near.start()
    second_near.wait()
    products(near, blocks.at[0], False)
    second_far.wait()
    products(far, blocks.at[1], False)
    pass_far.wait()
    pass_near.wait()
    products(diag, blocks.at[2], False)
    back = []
    for i, p in enumerate(peers):
        dsend[i] = dsum[aligned(p, tok), :].astype(BF16)
        copy = remote(dsend.at[i], drecv.at[i], bsend.at[i], brecv.at[i], (p, e))
        copy.start()
        back.append(copy)
    normal[:, aligned(r, width)] = dsum[aligned(r, tok), :]
    for i, p in enumerate(peers):
        back[i].wait()
        normal[:, aligned(p, width)] = drecv[i].astype(F32)
    finish()


def grad_qkv(mine, wq, wk, wv, cols_t, out_part):
    rows, group = mine.shape
    tok = rows // 4
    width = wq.shape[0]
    return pl.pallas_call(
        dgrad_kernel,
        out_shape=(
            jax.ShapeDtypeStruct((tok, 4 * width), F32),
            jax.ShapeDtypeStruct((4 * width, group), BF16),
            jax.ShapeDtypeStruct(out_part.shape[1:], F32),
        ),
        in_specs=[VMEM_SPEC] * 6,
        out_specs=(VMEM_SPEC,) * 3,
        scratch_shapes=[
            pltpu.VMEM((3, rows, group), BF16),
            pltpu.VMEM((rows, width), F32),
            pltpu.VMEM((3, tok, width), BF16),
            pltpu.VMEM((3, tok, width), BF16),
            pltpu.SemaphoreType.DMA((6,)),
            pltpu.SemaphoreType.DMA((6,)),
            pltpu.SemaphoreType.DMA((3,)),
            pltpu.SemaphoreType.DMA((3,)),
        ]
        + owner_scratch([out_part]),
        compiler_params=params(4),
        name="dqkv_exchange",
    )(mine, wq, wk, wv, cols_t, out_part)


def branch_kernel(
    mine, wo_in, attn_in, d_attn, full_out, attn_t_out, wo, attn, full, attn_t, local, ssem, rsem
):
    r, e = lax.axis_index("dp"), lax.axis_index("expert")
    tok = mine.shape[0]
    half = tok // 2
    peers = [r ^ m for m in PEER_MASKS]
    near, far, diag = r ^ 1, r ^ 2, r ^ 3
    loads = loading(((attn_in, attn), (wo_in, wo)), local)
    greet([(p, e) for p in peers])

    def part(q, which):
        return pl.ds(pl.multiple_of(q * tok + which * half, half), half)

    low, high = pl.ds(0, half), pl.ds(half, half)
    first_near = remote(mine.at[low], full.at[part(r, 0)], ssem.at[0], rsem.at[0], (near, e))
    first_far = remote(mine.at[high], full.at[part(r, 1)], ssem.at[1], rsem.at[1], (far, e))
    second_near = remote(mine.at[high], full.at[part(r, 1)], ssem.at[2], rsem.at[2], (near, e))
    second_far = remote(mine.at[low], full.at[part(r, 0)], ssem.at[3], rsem.at[3], (far, e))
    pass_far = remote(full.at[part(near, 0)], full.at[part(near, 0)], ssem.at[4], rsem.at[4], (far, e))
    pass_near = remote(full.at[part(far, 1)], full.at[part(far, 1)], ssem.at[5], rsem.at[5], (near, e))
    for copy in (first_near, first_far, second_near, second_far):
        copy.start()
    full[aligned(r, tok), :] = mine[...]
    wait_all(loads[0])
    attn_t[...] = attn[...].T
    leaving = start_all([pltpu.make_async_copy(attn_t, attn_t_out, local.at[0])])
    wait_all(loads[1])
    heads = wo.shape[0]
    step = heads // 4

    def products(q):
        def chunk(c, carry):
            n = aligned(c, step)
            d_attn[aligned(q, tok), n] = dot_nt(full[aligned(q, tok), :], wo[n, :]).astype(BF16)
            return carry

        lax.fori_loop(0, 4, chunk, 0)

    products(r)
    first_near.wait()
    pass_far.start()
    first_far.wait()
    pass_near.start()
    second_near.wait()
    products(near)
    second_far.wait()
    products(far)
    pass_far.wait()
    pass_near.wait()
    leaving += start_all([pltpu.make_async_copy(full, full_out, local.at[1])])
    products(diag)
    wait_all(leaving)


def grad_branch(mine, wo, attn):
    tok, width = mine.shape
    return pl.pallas_call(
        branch_kernel,
        out_shape=(
            jax.ShapeDtypeStruct((4 * tok, wo.shape[0]), BF16),
            jax.ShapeDtypeStruct((4 * tok, width), BF16),
            jax.ShapeDtypeStruct((wo.shape[0], 4 * tok), BF16),
        ),
        in_specs=[VMEM_SPEC, ANY_SPEC, ANY_SPEC],
        out_specs=(VMEM_SPEC, ANY_SPEC, ANY_SPEC),
        scratch_shapes=[
            pltpu.VMEM(wo.shape, BF16),
            pltpu.VMEM(attn.shape, BF16),
            pltpu.VMEM((4 * tok, width), BF16),
            pltpu.VMEM((wo.shape[0], 4 * tok), BF16),
            pltpu.SemaphoreType.DMA((2,)),
            pltpu.SemaphoreType.DMA((6,)),
            pltpu.SemaphoreType.DMA((6,)),
        ],
        compiler_params=params(3),
        name="branch_exchange",
    )(mine, wo, attn)


def owner_order(n_z):
    order = list(range(1, n_z)) + [0]
    return order[1:2] + order[:1] + order[2:] if n_z > 2 else order


def owner_sum(arrays, outs, pair_in, send, recv, psend, precv, zsend, zrecv):
    r, e = lax.axis_index("dp"), lax.axis_index("expert")
    n_z = arrays[0].shape[0] // 2
    z, core = e // 2, e % 2
    targets = [lax.rem(z + j, n_z) for j in range(n_z)]
    order = owner_order(n_z)
    n_arrays = len(arrays)
    pair, moves = {}, []

    def begin():
        for j in order:
            for a in range(n_arrays):
                copy = remote(
                    arrays[a].at[targets[j] * 2 + (1 - core)], pair_in[a].at[j],
                    psend.at[a, j], precv.at[a, j], (r, e ^ 1),
                )
                copy.start()
                pair[a, j] = copy

    def middle():
        for j in order:
            for a in range(n_arrays):
                pair[a, j].wait()
                own = arrays[a][targets[j] * 2 + core].astype(F32) + pair_in[a][j].astype(F32)
                if j == 0:
                    outs[a][...] = own
                else:
                    send[a][j - 1] = own.astype(BF16)
                    copy = remote(
                        send[a].at[j - 1], recv[a].at[j - 1],
                        zsend.at[a, j - 1], zrecv.at[a, j - 1], (r, targets[j] * 2 + core),
                    )
                    copy.start()
                    moves.append(copy)

    def finish():
        for copy in moves:
            copy.wait()
        for a in range(n_arrays):
            value = outs[a][...]
            for j in range(n_z - 1):
                value = value + recv[a][j].astype(F32)
            outs[a][...] = value

    return begin, middle, finish


def owner_scratch(arrays):
    n_z = arrays[0].shape[0] // 2
    n = len(arrays)
    shapes = [a.shape[1:] for a in arrays]
    return (
        [pltpu.VMEM((n_z, *s), BF16) for s in shapes]
        + [pltpu.VMEM((n_z - 1, *s), BF16) for s in shapes]
        + [pltpu.VMEM((n_z - 1, *s), BF16) for s in shapes]
        + [pltpu.SemaphoreType.DMA((n, n_z))] * 2
        + [pltpu.SemaphoreType.DMA((n, n_z - 1))] * 2
    )


def owner_peers():
    r, e = lax.axis_index("dp"), lax.axis_index("expert")
    n_z = lax.axis_size("expert") // 2
    return [(r, lax.rem(e // 2 + j, n_z) * 2 + e % 2) for j in range(1, n_z)]


def last_sums_kernel(grads, small, grads_out, small_out, *scratch):
    r, e = lax.axis_index("dp"), lax.axis_index("expert")
    z, core = e // 2, e % 2
    n_z = grads.shape[0] // 2
    pair_in, send, recv, psend, precv, zsend, zrecv = scratch[:7]
    first_in, piece, line_in, s1, r1, s2, r2, s3, r3 = scratch[7:]
    begin, middle, finish = owner_sum(
        [grads], [grads_out], [pair_in], [send], [recv], psend, precv, zsend, zrecv
    )
    others = [(m // 2, m % 2) for m in range(1, 8)]
    plane = [(r ^ a, e ^ c) for a, c in others]
    greet(plane + owner_peers())
    begin()
    firsts = []
    for i, (a, c) in enumerate(others):
        copy = remote(
            small.at[(r ^ a) * 2 + (core ^ c)], first_in.at[i], s1.at[i], r1.at[i], plane[i]
        )
        copy.start()
        firsts.append(copy)
    middle()
    for copy in firsts:
        copy.wait()
    mine = r * 2 + core
    value = small[mine]
    for i in range(7):
        value = value + first_in[i]
    piece[0] = value
    seconds = []
    for j in range(1, n_z):
        copy = remote(
            piece.at[0], line_in.at[j - 1], s2.at[j - 1], r2.at[j - 1], owner_peers()[j - 1]
        )
        copy.start()
        seconds.append(copy)
    for copy in seconds:
        copy.wait()
    value = piece[0]
    for j in range(n_z - 1):
        value = value + line_in[j]
    small_out[mine] = value
    thirds = []
    for i, (a, c) in enumerate(others):
        copy = remote(small_out.at[mine], small_out.at[mine], s3.at[i], r3.at[i], plane[i])
        copy.start()
        thirds.append(copy)
    finish()
    for copy in thirds:
        copy.wait()


def last_sums(grads, small):
    n_z = grads.shape[0] // 2
    piece = small.shape[1:]
    return pl.pallas_call(
        last_sums_kernel,
        out_shape=(
            jax.ShapeDtypeStruct(grads.shape[1:], F32),
            jax.ShapeDtypeStruct(small.shape, F32),
        ),
        in_specs=[VMEM_SPEC] * 2,
        out_specs=(VMEM_SPEC,) * 2,
        scratch_shapes=owner_scratch([grads])
        + [
            pltpu.VMEM((7, *piece), F32),
            pltpu.VMEM((1, *piece), F32),
            pltpu.VMEM((n_z - 1, *piece), F32),
            pltpu.SemaphoreType.DMA((7,)),
            pltpu.SemaphoreType.DMA((7,)),
            pltpu.SemaphoreType.DMA((n_z - 1,)),
            pltpu.SemaphoreType.DMA((n_z - 1,)),
            pltpu.SemaphoreType.DMA((7,)),
            pltpu.SemaphoreType.DMA((7,)),
        ],
        compiler_params=params(5),
        name="last_sums",
    )(grads, small)


def line_sum(block, out, pair_in, work, lines, ps, pr, zs, zr):
    r, e = lax.axis_index("dp"), lax.axis_index("expert")
    z, core = e // 2, e % 2
    order = plane_order(z)[::-1]
    right = jnp.minimum(z + 1, 3) * 2 + core
    left = jnp.maximum(z - 1, 0) * 2 + core
    pairs, moves = [], []

    def begin():
        for k in range(4):
            copy = remote(
                block(order[k] * 2 + (1 - core)), pair_in.at[k], ps.at[k], pr.at[k], (r, e ^ 1)
            )
            copy.start()
            pairs.append(copy)

    def move(k, side, cond, to, add):
        b = order[k]
        copy = remote(work.at[k], lines.at[side, b], zs.at[side, k], zr.at[side, b], (r, to))
        moves.append((cond, copy))

        @pl.when(cond)
        def _():
            if add:
                copy.wait_recv()
                value = work[k].astype(F32) + lines[side, b].astype(F32)
                work[k] = value.astype(BF16)
            copy.start()

    def first():
        for k in range(4):
            pairs[k].wait_recv()
            value = block(order[k] * 2 + core)[...].astype(F32) + pair_in[k].astype(F32)
            if k == 3:
                out[...] = value
            else:
                work[k] = value.astype(BF16)
        ends(0)

    def ends(k):
        move(k, 0, z == 0, right, False)
        move(k, 1, z == 3, left, False)

    def inner(k):
        inside = (z > 0) & (z < 3)
        move(k, 0, inside & (order[k] > z), right, True)
        move(k, 1, inside & (order[k] < z), left, True)
        if k < 2:
            ends(k + 1)

    def last():
        for side, cond in ((0, z > 0), (1, z < 3)):

            @pl.when(cond)
            def _():
                at = lines.at[side, z]
                remote(at, at, zs.at[side, 3], zr.at[side, z], (r, e ^ 1)).wait_recv()
                out[...] = out[...] + lines[side, z].astype(F32)

        for copy in pairs:
            copy.wait_send()
        for cond, copy in moves:

            @pl.when(cond)
            def _():
                copy.wait_send()

    return begin, first, inner, last


LINE_SEMS = [
    pltpu.SemaphoreType.DMA((4,)),
    pltpu.SemaphoreType.DMA((4,)),
    pltpu.SemaphoreType.DMA((2, 4)),
    pltpu.SemaphoreType.DMA((2, 4)),
]


def dgrad_line_kernel(
    d_q, d_keys, d_values, key_lin, cos, sin, key_gain,
    wq_in, wk_in, wv_in, cols_t_in, cols_in, out_part_in, small, gain,
    normal, q_out, k_out, v_out, out_sum, small_out, gain_out,
    mine, prompt_sum, prompt_in, ksend, krecv, wq, wk, wv, cols_t, cols, out_part, local, qkv_sum, grads, blocks, dsum, dsend, drecv, opair, owork, olines, qpair, qwork, qlines,
    first_in, piece, line_in, gain_v, gain_in,
    ssem, rsem, bsend, brecv, s1, r1, s2, r2, s3, r3, s4, r4, s5, r5, *sems,
):
    r, e = lax.axis_index("dp"), lax.axis_index("expert")
    z, core = e // 2, e % 2
    rows = mine.shape[0]
    tok = rows // 4
    half = rows // 2
    qg = wq.shape[1] // 4
    kg = wk.shape[1] // 4
    width = wq.shape[0]
    share = width // 8
    peers = [r ^ m for m in PEER_MASKS]
    near, far, diag = r ^ 1, r ^ 2, r ^ 3
    order = (r, near, far, diag)
    out_begin, out_first, out_inner, out_last = line_sum(
        lambda o: out_part.at[o], out_sum, opair, owork, olines, *sems[:4]
    )
    units = [
        line_sum(
            lambda o, p=p: grads.at[o, p], qkv_sum.at[p], qpair.at[i], qwork.at[i], qlines.at[i],
            *(sem.at[i] for sem in sems[4:]),
        )
        for i, p in enumerate(order)
    ]
    line_peers = [(r, lax.rem(z + j, 4) * 2 + core) for j in (1, 2, 3)]
    others = [(m // 2, m % 2) for m in (6, 7, 2, 3, 4, 5, 1)]
    plane = [(r ^ a, e ^ c) for a, c in others]
    owners = [(r, e ^ m) for m in range(1, 8)]
    loads = loading(
        (
            (out_part_in, out_part), (cols_t_in, cols_t), (wq_in, wq), (wk_in, wk), (wv_in, wv),
            (cols_in, cols),
        ),
        local,
    )
    mine[:, :qg] = d_q[...]
    prompt = tok - CMAX
    column = 4 * prompt
    for n, d in enumerate((d_keys, d_values)):
        for c in range(2):
            part = slice(c * column, (c + 1) * column)
            prompt_sum[c, n] = d[0, part] + d[1, part] + d[2, part] + d[3, part]
    greet(plane + owners[1:])
    swap = remote(prompt_sum.at[1 - core], prompt_in, ksend.at[0], krecv.at[0], (r, e ^ 1))
    swap.start()
    swap.wait()
    prompt_in[...] = prompt_in[...] + prompt_sum[core]
    head = key_gain.shape[1]
    key_gain_sum = jnp.zeros((1, head), F32)
    for i in range(4):
        for at, size, dk, dv in (
            (0, prompt, prompt_in[0, i * prompt : (i + 1) * prompt], prompt_in[1, i * prompt : (i + 1) * prompt]),
            (prompt, CMAX, d_keys[i, 2 * column :], d_values[i, 2 * column :]),
        ):
            t = slice(at, at + size)
            rows_i = slice(i * tok + at, i * tok + at + size)
            turned = dk * cos[i, t] + pltpu.roll(dk * sin[i, t], head // 2, 1)
            x = key_lin[rows_i, :]
            inverse = lax.rsqrt(jnp.mean(x * x, axis=-1, keepdims=True) + norm_eps)
            unit = x * inverse
            key_gain_sum = key_gain_sum + jnp.sum(turned * unit, axis=0, keepdims=True)
            weighted = turned * key_gain[...]
            mine[rows_i, qg : qg + kg] = (
                inverse * (weighted - unit * jnp.mean(weighted * unit, axis=-1, keepdims=True))
            ).astype(BF16)
            mine[rows_i, qg + kg :] = dv.astype(BF16)
    low, high = pl.ds(0, half), pl.ds(half, half)
    first_near = remote(mine.at[low], blocks.at[0, low], ssem.at[0], rsem.at[0], (near, e))
    first_far = remote(mine.at[high], blocks.at[1, high], ssem.at[1], rsem.at[1], (far, e))
    second_near = remote(mine.at[high], blocks.at[0, high], ssem.at[2], rsem.at[2], (near, e))
    second_far = remote(mine.at[low], blocks.at[1, low], ssem.at[3], rsem.at[3], (far, e))
    pass_far = remote(blocks.at[0, low], blocks.at[2, low], ssem.at[4], rsem.at[4], (far, e))
    pass_near = remote(blocks.at[1, high], blocks.at[2, high], ssem.at[5], rsem.at[5], (near, e))
    me = r * 2 + core
    firsts = []
    for i, (a, c) in enumerate(others):
        copy = remote(small.at[(r ^ a) * 2 + (core ^ c)], first_in.at[i], s1.at[i], r1.at[i], plane[i])
        copy.start()
        firsts.append(copy)
    for copy in (first_near, first_far, second_near, second_far):
        copy.start()
    wait_all(loads[0])
    out_begin()
    seconds, thirds = [], []

    def small_second():
        for copy in firsts:
            copy.wait()
        value = small[me]
        for i in range(7):
            value = value + first_in[i]
        piece[0] = value
        for j in range(3):
            copy = remote(piece.at[0], line_in.at[j], s2.at[j], r2.at[j], line_peers[j])
            copy.start()
            seconds.append(copy)

    def small_third():
        for copy in seconds:
            copy.wait()
        small_out[me] = piece[0] + line_in[0] + line_in[1] + line_in[2]
        for i in range(7):
            copy = remote(small_out.at[me], small_out.at[me], s3.at[i], r3.at[i], plane[i])
            copy.start()
            thirds.append(copy)

    def outer(p, src):
        def step(c, carry):
            n = aligned(c, 256)
            value = dot_nn(cols_t[...], src[:, n]).astype(BF16)
            for o in range(8):
                grads[o, p, :, n] = value[o * share : (o + 1) * share]
            return carry

        lax.fori_loop(0, (qg + 2 * kg) // 256, step, 0)

    def inner(p, src, start):
        def chunk(c, carry):
            n = aligned(c, 128)
            value = (
                dot_nt(src[:, :qg], wq[n, aligned(p, qg)])
                + dot_nt(src[:, qg : qg + kg], wk[n, aligned(p, kg)])
                + dot_nt(src[:, qg + kg :], wv[n, aligned(p, kg)])
            )
            if start:
                dsum[:, n] = value
            else:
                dsum[:, n] = dsum[:, n] + value
            return carry

        lax.fori_loop(0, width // 128, chunk, 0)

    def begin(i):
        units[i][0]()

    def first(i):
        units[i][1]()

    def onward(i, k):
        units[i][2](k)

    wait_all(loads[1])
    outer(r, mine)
    begin(0)
    out_first()
    small_second()
    for copies in loads[2:5]:
        wait_all(copies)
    inner(r, mine, True)
    first_near.wait()
    pass_far.start()
    first_far.wait()
    pass_near.start()
    out_inner(0)
    first(0)
    out_inner(1)
    small_third()
    onward(0, 0)
    second_near.wait()
    outer(near, blocks.at[0])
    begin(1)
    second_far.wait()
    outer(far, blocks.at[1])
    begin(2)
    out_inner(2)
    onward(0, 1)
    first(1)
    inner(near, blocks.at[0], False)
    onward(0, 2)
    onward(1, 0)
    first(2)
    inner(far, blocks.at[1], False)
    onward(1, 1)
    pass_far.wait()
    pass_near.wait()
    outer(diag, blocks.at[2])
    begin(3)
    inner(diag, blocks.at[2], False)
    back = []
    for i, p in enumerate(peers):
        dsend[i] = dsum[aligned(p, tok), :].astype(BF16)
        copy = remote(dsend.at[i], drecv.at[i], bsend.at[i], brecv.at[i], (p, e))
        copy.start()
        back.append(copy)
    wait_all(loads[5])
    scale = 1.0 / gain[:, aligned(r, width)]
    gain_v[...] = jnp.broadcast_to(
        jnp.sum(dsum[...] * cols[...].astype(F32), axis=0, keepdims=True) * scale, gain_v.shape
    )
    gain_v[1:2, :head] = key_gain_sum
    fourths = []
    for i in range(7):
        copy = remote(gain_v, gain_in.at[i], s4.at[i], r4.at[i], owners[i])
        copy.start()
        fourths.append(copy)
    onward(1, 2)
    onward(2, 0)
    first(3)
    onward(2, 1)
    for copy in fourths:
        copy.wait()
    value = gain_v[...]
    for i in range(7):
        value = value + gain_in[i]
    gain_out[r] = value
    fifths = []
    for i, p in enumerate(peers):
        copy = remote(gain_out.at[r], gain_out.at[r], s5.at[i], r5.at[i], (p, e))
        copy.start()
        fifths.append(copy)
    onward(3, 0)
    normal[:, aligned(r, width)] = dsum[aligned(r, tok), :]
    for i, p in enumerate(peers):
        back[i].wait()
        normal[:, aligned(p, width)] = drecv[i].astype(F32)
    onward(2, 2)
    onward(3, 1)
    out_last()

    def close(i):
        p = order[i]
        units[i][3]()
        q_out[:, aligned(p, qg)] = qkv_sum[p, :, :qg]
        k_out[:, aligned(p, kg)] = qkv_sum[p, :, qg : qg + kg]
        v_out[:, aligned(p, kg)] = qkv_sum[p, :, qg + kg :]

    close(0)
    close(1)
    onward(3, 2)
    close(2)
    close(3)
    for copy in fifths + thirds:
        copy.wait()


def grad_qkv_line(
    d_q, d_keys, d_values, key_lin, cos, sin, key_gain, wq, wk, wv, cols_t, cols, out_part, small, gain
):
    rows, head = key_lin.shape
    group = d_q.shape[1] + 2 * head
    tok = rows // 4
    width = wq.shape[0]
    piece = (width // 8, group)
    out_piece = out_part.shape[1:]
    small_piece = small.shape[1:]
    return pl.pallas_call(
        dgrad_line_kernel,
        out_shape=(
            jax.ShapeDtypeStruct((tok, 4 * width), F32),
            jax.ShapeDtypeStruct((width // 8, wq.shape[1]), F32),
            jax.ShapeDtypeStruct((width // 8, wk.shape[1]), F32),
            jax.ShapeDtypeStruct((width // 8, wv.shape[1]), F32),
            jax.ShapeDtypeStruct(out_piece, F32),
            jax.ShapeDtypeStruct(small.shape, F32),
            jax.ShapeDtypeStruct((4, 8, width), F32),
        ),
        in_specs=[VMEM_SPEC] * 7 + [ANY_SPEC] * 6 + [VMEM_SPEC] * 2,
        out_specs=(VMEM_SPEC,) * 7,
        scratch_shapes=[
            pltpu.VMEM((rows, group), BF16),
            pltpu.VMEM((2, 2, 4 * (tok - CMAX), head), F32),
            pltpu.VMEM((2, 4 * (tok - CMAX), head), F32),
            pltpu.SemaphoreType.DMA((1,)),
            pltpu.SemaphoreType.DMA((1,)),
        ]
        + [pltpu.VMEM(a.shape, BF16) for a in (wq, wk, wv, cols_t, cols, out_part)]
        + [
            pltpu.SemaphoreType.DMA((6,)),
            pltpu.VMEM((4, *piece), F32),
            pltpu.VMEM((8, 4, *piece), BF16),
            pltpu.VMEM((3, rows, group), BF16),
            pltpu.VMEM((rows, width), F32),
            pltpu.VMEM((3, tok, width), BF16),
            pltpu.VMEM((3, tok, width), BF16),
            pltpu.VMEM((4, *out_piece), BF16),
            pltpu.VMEM((3, *out_piece), BF16),
            pltpu.VMEM((2, 4, *out_piece), BF16),
            pltpu.VMEM((4, 4, *piece), BF16),
            pltpu.VMEM((4, 3, *piece), BF16),
            pltpu.VMEM((4, 2, 4, *piece), BF16),
            pltpu.VMEM((7, *small_piece), F32),
            pltpu.VMEM((1, *small_piece), F32),
            pltpu.VMEM((3, *small_piece), F32),
            pltpu.VMEM((8, width), F32),
            pltpu.VMEM((7, 8, width), F32),
            pltpu.SemaphoreType.DMA((6,)),
            pltpu.SemaphoreType.DMA((6,)),
        ]
        + [pltpu.SemaphoreType.DMA((n,)) for n in (3, 3, 7, 7, 3, 3, 7, 7, 7, 7, 3, 3)]
        + LINE_SEMS
        + [
            pltpu.SemaphoreType.DMA((4, 4)),
            pltpu.SemaphoreType.DMA((4, 4)),
            pltpu.SemaphoreType.DMA((4, 2, 4)),
            pltpu.SemaphoreType.DMA((4, 2, 4)),
        ],
        compiler_params=params(10),
        name="dqkv_line_exchange",
    )(
        d_q, d_keys, d_values, key_lin, cos, sin, key_gain, wq, wk, wv, cols_t, cols, out_part, small, gain
    )


def masks_of(block, own_length, slots, prompt_block, prompt_len, column, keys):
    slot = lax.broadcasted_iota(jnp.int32, (slots, keys), 0)
    key = lax.broadcasted_iota(jnp.int32, (slots, keys), 1)
    is_prompt = slot < prompt_block
    position = (column * 4 + block) * prompt_block + slot
    sees_prompt = (key < prompt_len) & (jnp.logical_not(is_prompt) | (key <= position))
    cont = key - prompt_len
    sees_cont = (
        (key >= prompt_len)
        & jnp.logical_not(is_prompt)
        & (cont <= slot - prompt_block)
        & (cont < own_length)
    )
    return sees_prompt | sees_cont


def attention_fwd_kernel(prompt_len, lengths, lin, gain, cos, sin, keys, values, queries, attn):
    block = pl.program_id(0)
    slots = lin.shape[0]
    head = gain.shape[1]
    e = lax.axis_index("expert")
    own_length = lengths[block * lax.axis_size("expert") + e]
    allowed = masks_of(block, own_length, slots, slots - CMAX, prompt_len, e % 2, keys.shape[1])
    scale = head ** (-0.5)
    k, v = keys[0], values[0]
    c, s, g = cos[0], sin[0], gain[...]
    for h in range(lin.shape[1] // head):
        part = slice(h * head, (h + 1) * head)
        x = lin[:, part]
        x = x * lax.rsqrt(jnp.mean(x * x, axis=-1, keepdims=True) + norm_eps) * g
        q = (x * c + pltpu.roll(x, head // 2, 1) * s).astype(BF16)
        queries[:, part] = q
        score = jnp.where(allowed, dot_nt(q, k) * scale, -jnp.inf)
        peak = jnp.max(score, axis=-1, keepdims=True)
        exponent = jnp.exp(score - peak)
        low = (exponent * (1.0 / jnp.sum(exponent, axis=-1, keepdims=True))).astype(BF16)
        attn[:, part] = dot_nn(low, v).astype(BF16)


def attention_fwd(lengths, lin, gain, cos, sin, keys, values, prompt_len):
    blocks, total_keys, head = keys.shape
    slots = lin.shape[0] // blocks
    width = lin.shape[1] - 2 * head
    row = pl.BlockSpec((slots, width), lambda i, *_: (i, 0))
    table = pl.BlockSpec((1, slots, head), lambda i, *_: (i, 0, 0))
    kv = pl.BlockSpec((1, total_keys, head), lambda i, *_: (i, 0, 0))
    one = pl.BlockSpec((1, head), lambda i, *_: (0, 0))
    return pl.pallas_call(
        functools.partial(attention_fwd_kernel, prompt_len),
        grid_spec=pltpu.PrefetchScalarGridSpec(
            num_scalar_prefetch=1,
            grid=(blocks,),
            in_specs=[row, one, table, table, kv, kv],
            out_specs=[row, row],
        ),
        out_shape=(
            jax.ShapeDtypeStruct((lin.shape[0], width), BF16),
            jax.ShapeDtypeStruct((lin.shape[0], width), BF16),
        ),
        compiler_params=params(),
        name="attention_fwd",
    )(lengths, lin, gain, cos, sin, keys, values)


def attention_bwd_kernel(
    prompt_len, lengths, lin, queries, d_attn, gain, cos, sin, keys, values, attn_t, d_branch,
    d_lin, d_keys, d_values, d_gain, out_part,
):
    block = pl.program_id(0)
    slots = lin.shape[0]
    head = gain.shape[1]
    e = lax.axis_index("expert")
    own_length = lengths[block * lax.axis_size("expert") + e]
    allowed = masks_of(block, own_length, slots, slots - CMAX, prompt_len, e % 2, keys.shape[1])
    scale = head ** (-0.5)
    k, v = keys[0], values[0]
    c, s, g = cos[0], sin[0], gain[...]
    key_total = jnp.zeros(k.shape, F32)
    value_total = jnp.zeros(v.shape, F32)
    gain_total = jnp.zeros((8, head), F32)
    for h in range(lin.shape[1] // head):
        part = slice(h * head, (h + 1) * head)
        q = queries[:, part]
        score = jnp.where(allowed, dot_nt(q, k) * scale, -jnp.inf)
        peak = jnp.max(score, axis=-1, keepdims=True)
        exponent = jnp.exp(score - peak)
        probs = exponent * (1.0 / jnp.sum(exponent, axis=-1, keepdims=True))
        d_out = d_attn[:, part]
        d_probs = dot_nt(d_out, v)
        inner = jnp.sum(probs * d_probs, axis=-1, keepdims=True)
        d_score = (probs * (d_probs - inner)).astype(BF16)
        key_total = key_total + dot_tn(d_score, q)
        value_total = value_total + dot_tn(probs.astype(BF16), d_out)
        d_q = dot_nn(d_score, k) * scale
        turned = d_q * c + pltpu.roll(d_q * s, head // 2, 1)
        x = lin[:, part]
        inverse = lax.rsqrt(jnp.mean(x * x, axis=-1, keepdims=True) + norm_eps)
        unit = x * inverse
        pairs = turned * unit
        for j in range(slots // 8):
            gain_total = gain_total + pairs[j * 8 : (j + 1) * 8]
        weighted = turned * g
        d_lin[:, part] = (
            inverse * (weighted - unit * jnp.mean(weighted * unit, axis=-1, keepdims=True))
        ).astype(BF16)
        if h % 4 == 3:
            n = slice(h // 4 * 256, h // 4 * 256 + 256)
            out_part[:, n] = dot_nn(attn_t[...], d_branch[:, n]).astype(BF16)
    d_keys[0] = key_total * scale
    d_values[0] = value_total
    d_gain[0] = gain_total


def attention_bwd(
    lengths, lin, queries, d_attn, gain, cos, sin, keys, values, attn_t, d_branch, prompt_len
):
    blocks, total_keys, head = keys.shape
    slots = lin.shape[0] // blocks
    width = lin.shape[1] - 2 * head
    row = pl.BlockSpec((slots, width), lambda i, *_: (i, 0))
    table = pl.BlockSpec((1, slots, head), lambda i, *_: (i, 0, 0))
    kv = pl.BlockSpec((1, total_keys, head), lambda i, *_: (i, 0, 0))
    step = d_branch.shape[1] // blocks
    one = pl.BlockSpec((1, head), lambda i, *_: (0, 0))
    return pl.pallas_call(
        functools.partial(attention_bwd_kernel, prompt_len),
        grid_spec=pltpu.PrefetchScalarGridSpec(
            num_scalar_prefetch=1,
            grid=(blocks,),
            in_specs=[row, row, row, one, table, table, kv, kv]
            + [
                pl.BlockSpec(attn_t.shape, lambda i, *_: (0, 0)),
                pl.BlockSpec((d_branch.shape[0], step), lambda i, *_: (0, i)),
            ],
            out_specs=[
                row,
                kv,
                kv,
                pl.BlockSpec((1, 8, head), lambda i, *_: (i, 0, 0)),
                pl.BlockSpec((attn_t.shape[0], step), lambda i, *_: (0, i)),
            ],
        ),
        out_shape=(
            jax.ShapeDtypeStruct((lin.shape[0], width), BF16),
            jax.ShapeDtypeStruct(keys.shape, F32),
            jax.ShapeDtypeStruct(values.shape, F32),
            jax.ShapeDtypeStruct((blocks, 8, head), F32),
            jax.ShapeDtypeStruct((attn_t.shape[0], d_branch.shape[1]), BF16),
        ),
        compiler_params=params(),
        name="attention_bwd",
    )(lengths, lin, queries, d_attn, gain, cos, sin, keys, values, attn_t, d_branch)


def partner(shard, axis, bit):
    return lax.ppermute(shard, axis, [(i, i ^ 1 << bit) for i in range(lax.axis_size(axis))])


def root_mean_scale(value_rows, gain_vec):
    return (
        value_rows
        * lax.rsqrt(jnp.mean(value_rows * value_rows, axis=-1, keepdims=True) + norm_eps)
        * gain_vec
    )


def contract(left_side, right_side, left_dim, right_dim):
    return lax.dot_general(
        left_side,
        right_side,
        (((left_dim,), (right_dim,)), ((), ())),
        preferred_element_type=F32,
    )


def plane_order(z):
    upper, odd = z // 2, z % 2
    return [z, z + 1 - 2 * upper, 2 + upper - 2 * odd, 3 - 3 * upper]


def world(with_diag):
    r, e = lax.axis_index("dp"), lax.axis_index("expert")
    z, core = e // 2, e % 2
    near, far = r ^ 1, r ^ 2
    devices = [(near, e), (far, e), (r, e ^ 1)]
    devices += [(r, lax.rem(z + j, 4) * 2 + core) for j in (1, 2, 3)]
    return r, e, z, core, near, far, devices


def everyone():
    me = lax.axis_index("dp") * 8 + lax.axis_index("expert")
    return me, [lax.rem(me + j, 32) for j in range(1, 32)]


def scatter_rows(rows, rows_in, ss, rs):
    me, others = everyone()
    copies = start_all(
        [
            remote(rows.at[d], rows_in.at[me], ss.at[j], rs.at[j], (d // 8, lax.rem(d, 8)))
            for j, d in enumerate(others)
        ]
    )
    rows_in[me] = rows[me]
    return copies


def greet_everyone():
    greet([(d // 8, lax.rem(d, 8)) for d in everyone()[1]])


ROW_SEMS = [pltpu.SemaphoreType.DMA((31,)), pltpu.SemaphoreType.DMA((31,))]


def gather_world(mine, buf, zs, zr, ps, pr, ds, dr, before, group, done, greeting=None):
    r, e, z, core, near, far, greeted = world(True)
    half = mine.shape[0] // 2
    low, high = pl.ds(0, half), pl.ds(half, half)
    order = plane_order(z)
    if greeting is None:
        greet(greeted)
    else:
        greeting()

    def slot(q, b, c):
        return q * 8 + b * 2 + c

    buf[slot(r, z, core)] = mine[...]
    diag = r ^ 3
    plane, pairs, lines = {}, {}, []

    def hand(k, i, q):
        at = slot(q, order[k], core)
        copy = remote(buf.at[at], buf.at[at], ds.at[k, i], dr.at[k, i], (r, e ^ 1))
        copy.start()
        pairs[k, i] = copy

    def issue(k):
        b = order[k]
        at = slot(r, b, core)
        for side, cond, to in (
            (0, (b <= z) & (z < 3), jnp.minimum(z + 1, 3)),
            (1, (b >= z) & (z > 0), jnp.maximum(z - 1, 0)),
        ):
            copy = remote(buf.at[at], buf.at[at], zs.at[k, side], zr.at[b], (r, to * 2 + core))
            lines.append((cond, copy))

            @pl.when(cond)
            def _():
                copy.start()

        mine_at, near_at, far_at = at, slot(near, b, core), slot(far, b, core)
        for i, (src, part, p) in enumerate(
            (
                (mine_at, low, near),
                (mine_at, high, far),
                (mine_at, high, near),
                (mine_at, low, far),
                (near_at, low, far),
                (far_at, high, near),
            )
        ):
            plane[k, i] = remote(
                buf.at[src, part], buf.at[src, part], ps.at[k, i], pr.at[k, i], (p, e)
            )
        for i in range(4):
            plane[k, i].start()
        hand(k, 0, r)

    def line_wait(k):
        b = order[k]
        at = slot(r, b, core)
        remote(buf.at[at], buf.at[at], zs.at[k, 0], zr.at[b], (r, e ^ 1)).wait_recv()
        issue(k)

    def passes(k):
        plane[k, 0].wait_recv()
        plane[k, 4].start()
        plane[k, 1].wait_recv()
        plane[k, 5].start()

    def finish(k):
        plane[k, 2].wait_recv()
        hand(k, 1, near)
        plane[k, 3].wait_recv()
        hand(k, 2, far)

    def corner(k):
        plane[k, 4].wait_recv()
        plane[k, 5].wait_recv()
        hand(k, 3, diag)

    who = (r, near, far, diag)

    def ready(k):
        before(k)
        for i in range(4):
            pairs[k, i].wait_recv()
        group(k, [(k * 4 + i, who[i] * 8 + order[k] * 2) for i in range(4)])

    issue(0)
    passes(0)
    line_wait(1)
    finish(0)
    passes(1)
    line_wait(2)
    corner(0)
    finish(1)
    ready(0)
    passes(2)
    line_wait(3)
    corner(1)
    finish(2)
    ready(1)
    passes(3)
    corner(2)
    finish(3)
    ready(2)
    corner(3)
    ready(3)
    done()
    for copy in plane.values():
        copy.wait_send()
    for copy in pairs.values():
        copy.wait_send()
    for cond, copy in lines:

        @pl.when(cond)
        def _():
            copy.wait_send()


def group_rows(k, room):
    return pl.ds(k * 4 * room, 4 * room)


GATHER_SEMS = [
    pltpu.SemaphoreType.DMA((4, 2)),
    pltpu.SemaphoreType.DMA((4,)),
    pltpu.SemaphoreType.DMA((4, 6)),
    pltpu.SemaphoreType.DMA((4, 6)),
    pltpu.SemaphoreType.DMA((4, 4)),
    pltpu.SemaphoreType.DMA((4, 4)),
]


def selector(row, room):
    ids = lax.broadcasted_iota(jnp.int32, (room, row.shape[1]), 0).astype(F32)
    return jnp.where(ids == row, 1.0, 0.0).astype(BF16)


def experts_fwd_kernel(
    capacity, mine, gate_rows, wg, wu, wd, pos, x_out, y_out, g_out, u_out, o_out, hid_out, gate_out,
    buf, wg_v, wu_v, wd_v, x_v, y_v, g_v, u_v, o_v, hid_v, gate_v, gate_in, local, rs, rr, *sems,
):
    model = wg.shape[0]
    rows_in = mine.shape[0]
    room = x_v.shape[0] // 4
    loads = start_all(
        [
            pltpu.make_async_copy(a, b, local.at[0, i])
            for i, (a, b) in enumerate(((wg, wg_v), (wu, wu_v), (wd, wd_v)))
        ]
    )
    leaving = {g: [] for g in range(4)}
    scattered = []

    def greeting():
        greet_everyone()
        scattered.extend(scatter_rows(gate_rows, gate_in, rs, rr))

    def leave(g, pairs):
        kept = group_rows(g, room)
        leaving[g].extend(
            start_all(
                [
                    pltpu.make_async_copy(v, o.at[kept], local.at[g % 2, i])
                    for i, v, o in pairs
                ]
            )
        )

    def before(g):
        wait_all(loads)
        wait_all(scattered)
        if g > 0:
            wait_all(leaving[g - 1])

    upto = jnp.where(
        lax.broadcasted_iota(jnp.int32, (rows_in, rows_in), 0)
        <= lax.broadcasted_iota(jnp.int32, (rows_in, rows_in), 1),
        1.0,
        0.0,
    ).astype(BF16)
    line = lax.broadcasted_iota(jnp.int32, (16, rows_in), 0)

    def pick(at, s, start):
        rows = pl.ds(start, room)
        sels = []
        gate = jnp.zeros((room, 1), F32)
        for c in range(2):
            row = jnp.broadcast_to(gate_in[s + c], (16, rows_in))
            named = jnp.where(row > 0.0, 1.0, 0.0)
            place = (dot_nn(named.astype(BF16), upto) + (c * capacity)) * named - 1.0
            pos[at * 2 + c] = place[:1]
            sels.append(selector(place[:1], room))
            top = row.astype(BF16).astype(F32)
            parts = jnp.where(line == 0, top, jnp.where(line == 1, row - top, 0.0)).astype(BF16)
            gate = gate + jnp.sum(dot_nt(sels[c], parts), axis=-1, keepdims=True)
        for c in range(4):
            n = slice(c * model // 4, (c + 1) * model // 4)
            x_v[rows, n] = (dot_nn(sels[0], buf[s, :, n]) + dot_nn(sels[1], buf[s + 1, :, n])).astype(BF16)
        gate_v[rows, :] = jnp.broadcast_to(gate, (room, 128))

    def group(g, blocks):
        for j, (at, s) in enumerate(blocks):
            pick(at, s, j * room)
        leave(g, ((0, x_v, x_out), (1, gate_v, gate_out)))

        def first(c, carry):
            n = aligned(c, 256)
            x = x_v[...]
            gates = dot_nn(x, wg_v[:, n])
            u = dot_nn(x, wu_v[:, n])
            g_v[:, n] = gates.astype(BF16)
            u_v[:, n] = u.astype(BF16)
            hid_v[:, n] = (gates / (1.0 + jnp.exp(-gates)) * u).astype(BF16)
            return carry

        lax.fori_loop(0, wg.shape[1] // 256, first, 0)
        leave(g, ((2, g_v, g_out), (3, u_v, u_out), (4, hid_v, hid_out)))

        def second(c, carry):
            n = aligned(c, 256)
            o = dot_nn(hid_v[...], wd_v[:, n]).astype(BF16)
            o_v[:, n] = o
            y_v[:, n] = (o.astype(F32) * gate_v[:, :1]).astype(BF16)
            return carry

        lax.fori_loop(0, model // 256, second, 0)
        leave(g, ((5, o_v, o_out), (6, y_v, y_out)))

    def done():
        for copies in leaving.values():
            wait_all(copies)

    gather_world(mine, buf, *sems, before, group, done, greeting)


def experts_fwd(mine, gate_rows, wg, wu, wd, capacity, room):
    rows, width = mine.shape
    model, ff = wg.shape
    group = 4 * room
    wide = jax.ShapeDtypeStruct((16 * room, model), BF16)
    thin = jax.ShapeDtypeStruct((16 * room, ff), BF16)
    pos, x, y, g, u, o, hidden, gates = pl.pallas_call(
        functools.partial(experts_fwd_kernel, capacity),
        out_shape=(
            jax.ShapeDtypeStruct((32, 1, rows), F32),
            wide,
            wide,
            thin,
            thin,
            wide,
            thin,
            jax.ShapeDtypeStruct((16 * room, 128), F32),
        ),
        in_specs=[VMEM_SPEC, VMEM_SPEC, ANY_SPEC, ANY_SPEC, ANY_SPEC],
        out_specs=(VMEM_SPEC,) + (ANY_SPEC,) * 7,
        scratch_shapes=[
            pltpu.VMEM((32, rows, width), BF16),
            pltpu.VMEM((model, ff), BF16),
            pltpu.VMEM((model, ff), BF16),
            pltpu.VMEM((ff, model), BF16),
            pltpu.VMEM((group, model), BF16),
            pltpu.VMEM((group, model), BF16),
            pltpu.VMEM((group, ff), BF16),
            pltpu.VMEM((group, ff), BF16),
            pltpu.VMEM((group, model), BF16),
            pltpu.VMEM((group, ff), BF16),
            pltpu.VMEM((group, 128), F32),
            pltpu.VMEM((32, 1, rows), F32),
            pltpu.SemaphoreType.DMA((2, 7)),
        ]
        + ROW_SEMS
        + GATHER_SEMS,
        compiler_params=params(6),
        name="experts_fwd",
    )(mine, gate_rows, wg, wu, wd)
    return pos, x, y, (g, u, o, hidden, gates)


def experts_bwd_kernel(
    mine, pos, g_in, u_in, o_in, gate_in, wg, wu, wd, d_gates, y_out, d_copy_out, dg_out, du_out,
    buf, wg_v, wu_v, wd_v, g_v, u_v, o_v, gate_v, y_v, d_copy_v, dg_v, du_v,
    local, ins, *sems,
):
    model, ff = wg.shape
    room = d_copy_v.shape[0] // 4
    loads = start_all(
        [
            pltpu.make_async_copy(a, b, local.at[0, i])
            for i, (a, b) in enumerate(((wg, wg_v), (wu, wu_v), (wd, wd_v)))
        ]
    )
    leaving, coming = {g: [] for g in range(4)}, {}

    def fetch(g):
        kept = group_rows(g, room)
        coming[g] = start_all(
            [
                pltpu.make_async_copy(a.at[kept], v.at[g % 2], ins.at[g % 2, i])
                for i, (a, v) in enumerate(
                    ((g_in, g_v), (u_in, u_v), (o_in, o_v), (gate_in, gate_v))
                )
            ]
        )

    fetch(0)

    def leave(g, pairs):
        kept = group_rows(g, room)
        leaving[g].extend(
            start_all(
                [
                    pltpu.make_async_copy(v, o.at[kept], local.at[g % 2, i])
                    for i, v, o in pairs
                ]
            )
        )

    def before(g):
        wait_all(loads)
        wait_all(coming[g])
        if g + 1 < 4:
            fetch(g + 1)
        if g > 0:
            wait_all(leaving[g - 1])

    def pick(slot, at, s, start):
        rows = pl.ds(start, room)
        sels = [selector(pos[at * 2 + c], room) for c in range(2)]
        gate = gate_v[slot, rows, :1]
        inner = jnp.zeros((room, 1), F32)
        for c in range(4):
            n = slice(c * model // 4, (c + 1) * model // 4)
            picked = dot_nn(sels[0], buf[s, :, n]) + dot_nn(sels[1], buf[s + 1, :, n])
            d_copy_v[rows, n] = (gate * picked).astype(BF16)
            inner = inner + jnp.sum(picked * o_v[slot, rows, n].astype(F32), axis=-1, keepdims=True)
        top = inner.astype(BF16).astype(F32)
        rest = inner - top
        lane = lax.broadcasted_iota(jnp.int32, (room, 128), 1)
        parts = jnp.where(lane == 0, top, jnp.where(lane == 1, rest, 0.0)).astype(BF16)
        for c in range(2):
            both = dot_tn(parts, sels[c])
            d_gates[s + c] = both[:1] + both[1:2]

    def group(g, blocks):
        slot = g % 2
        for j, (at, s) in enumerate(blocks):
            pick(slot, at, s, j * room)
        leave(g, ((0, d_copy_v, d_copy_out),))

        def third(c, carry):
            n = aligned(c, 256)
            d_hidden = dot_nt(d_copy_v[...], wd_v[n, :])
            gates, u = g_v[slot, :, n].astype(F32), u_v[slot, :, n].astype(F32)
            s = 1.0 / (1.0 + jnp.exp(-gates))
            dg_v[:, n] = (d_hidden * u * s * (1.0 + gates * (1.0 - s))).astype(BF16)
            du_v[:, n] = (d_hidden * gates * s).astype(BF16)
            return carry

        lax.fori_loop(0, ff // 256, third, 0)
        leave(g, ((1, dg_v, dg_out), (2, du_v, du_out)))

        def fourth(c, carry):
            n = aligned(c, 256)
            y_v[:, n] = (
                dot_nt(dg_v[...], wg_v[n, :]) + dot_nt(du_v[...], wu_v[n, :])
            ).astype(BF16)
            return carry

        lax.fori_loop(0, model // 256, fourth, 0)
        leave(g, ((3, y_v, y_out),))

    def done():
        for copies in leaving.values():
            wait_all(copies)

    gather_world(mine, buf, *sems, before, group, done)


def experts_bwd(mine, pos, kept, wg, wu, wd, room):
    rows, width = mine.shape
    model, ff = wg.shape
    group = 4 * room
    return pl.pallas_call(
        experts_bwd_kernel,
        out_shape=(
            jax.ShapeDtypeStruct((32, 1, rows), F32),
            jax.ShapeDtypeStruct((16 * room, model), BF16),
            jax.ShapeDtypeStruct((16 * room, model), BF16),
            jax.ShapeDtypeStruct((16 * room, ff), BF16),
            jax.ShapeDtypeStruct((16 * room, ff), BF16),
        ),
        in_specs=[VMEM_SPEC, VMEM_SPEC] + [ANY_SPEC] * 7,
        out_specs=(VMEM_SPEC,) + (ANY_SPEC,) * 4,
        scratch_shapes=[
            pltpu.VMEM((32, rows, width), BF16),
            pltpu.VMEM((model, ff), BF16),
            pltpu.VMEM((model, ff), BF16),
            pltpu.VMEM((ff, model), BF16),
            pltpu.VMEM((2, group, ff), BF16),
            pltpu.VMEM((2, group, ff), BF16),
            pltpu.VMEM((2, group, model), BF16),
            pltpu.VMEM((2, group, 128), F32),
            pltpu.VMEM((group, model), BF16),
            pltpu.VMEM((group, model), BF16),
            pltpu.VMEM((group, ff), BF16),
            pltpu.VMEM((group, ff), BF16),
            pltpu.SemaphoreType.DMA((2, 4)),
            pltpu.SemaphoreType.DMA((2, 4)),
        ]
        + GATHER_SEMS,
        compiler_params=params(7),
        name="experts_bwd",
    )(mine, pos, *kept, wg, wu, wd)


def sum_world_kernel(with_rows, *refs):
    if with_rows:
        y_in, pos, rows_given, out, rows_out, *refs, rs, rr = refs
    else:
        y_in, pos, out, *refs = refs
    (
        y, local, psend, pair, half_near, half_far, full_near, full_far, lines,
        ds, dr, hs, hr, fs, fr, zs, zr,
    ) = refs
    r, e, z, core, near, far, greeted = world(True)
    rows, width = out.shape
    room = y.shape[1]
    half = rows // 2
    low, high = pl.ds(0, half), pl.ds(half, half)
    order = plane_order(z)[::-1]
    body_width = width // 512 * 512
    loads = loading(
        [(y_in.at[pl.ds(12 - 4 * k, 4)], y.at[pl.ds(12 - 4 * k, 4)]) for k in range(4)], local
    )
    if with_rows:
        greet_everyone()
        scattering = scatter_rows(rows_given, rows_out, rs, rr)
    else:
        greet(greeted)

    def for_columns(fn):
        def step(c, carry):
            fn(aligned(c, 512))
            return carry

        lax.fori_loop(0, body_width // 512, step, 0)
        if width > body_width:
            fn(pl.ds(body_width, width - body_width))

    def scattered(sel, k, i, n):
        return dot_tn(sel, y[(3 - k) * 4 + i, :, n])

    def select(k, i, c):
        return selector(pos[((3 - k) * 4 + i) * 2 + c], room)

    pairs, halves, fulls, moves = {}, {}, {}, []

    def stage_a(k):
        wait_all(loads[k])
        for i in (3, 1, 2, 0):
            at = k * 4 + i
            sel = select(k, i, 1 - core)

            def fill(n):
                psend[at, :, n] = scattered(sel, k, i, n).astype(BF16)

            for_columns(fill)
            copy = remote(psend.at[at], pair.at[at], ds.at[at], dr.at[at], (r, e ^ 1))
            copy.start()
            pairs[at] = copy
        for i in (3, 1, 2, 0):
            at = k * 4 + i
            sel = select(k, i, core)
            pairs[at].wait_recv()

            def add(n):
                value = scattered(sel, k, i, n) + pair[at, :, n].astype(F32)
                pair[at, :, n] = value.astype(BF16)

            for_columns(add)
            if i == 3:
                for side, (part, dst, p) in enumerate(
                    ((low, half_near, near), (high, half_far, far))
                ):
                    copy = remote(
                        pair.at[at, part], dst.at[k], hs.at[k, side], hr.at[k, side], (p, e)
                    )
                    copy.start()
                    halves[k, side] = copy

    def stage_b(k):
        for side, (i, part, src, dst, p) in enumerate(
            (
                (2, low, half_near, full_far, far),
                (1, high, half_far, full_near, near),
            )
        ):
            at = k * 4 + i
            halves[k, side].wait_recv()

            def add(n):
                value = pair[at, part, n].astype(F32) + src[k, :, n].astype(F32)
                pair[at, part, n] = value.astype(BF16)

            for_columns(add)
            copy = remote(pair.at[at], dst.at[k], fs.at[k, side], fr.at[k, side], (p, e))
            copy.start()
            fulls[k, side] = copy

    def stage_c(k):
        b = order[k]
        at = k * 4
        fulls[k, 0].wait_recv()
        fulls[k, 1].wait_recv()

        def add(n):
            out[:, n] = (
                pair[at, :, n].astype(F32)
                + full_near[k, :, n].astype(F32)
                + full_far[k, :, n].astype(F32)
            )

        for_columns(add)
        for side, cond in ((0, (b >= z) & (z > 0)), (1, (b <= z) & (z < 3))):

            @pl.when(cond)
            def _():
                remote(
                    lines.at[side, b], lines.at[side, b], zs.at[side, k], zr.at[side, b], (r, e ^ 1)
                ).wait_recv()

                def more(n):
                    out[:, n] = out[:, n] + lines[side, b, :, n].astype(F32)

                for_columns(more)

        if k < 3:

            def keep(n):
                pair[at, :, n] = out[:, n].astype(BF16)

            for_columns(keep)
            for side, cond, to in (
                (0, b > z, jnp.minimum(z + 1, 3)),
                (1, b < z, jnp.maximum(z - 1, 0)),
            ):
                copy = remote(
                    pair.at[at], lines.at[side, b], zs.at[side, k], zr.at[side, b], (r, to * 2 + core)
                )
                moves.append((cond, copy))

                @pl.when(cond)
                def _():
                    copy.start()

    stage_a(0)
    stage_a(1)
    stage_b(0)
    stage_a(2)
    stage_b(1)
    stage_c(0)
    stage_a(3)
    stage_b(2)
    stage_c(1)
    stage_b(3)
    stage_c(2)
    stage_c(3)
    for copies in (pairs, halves, fulls):
        for copy in copies.values():
            copy.wait_send()
    for cond, copy in moves:

        @pl.when(cond)
        def _():
            copy.wait_send()

    if with_rows:
        wait_all(scattering)


def sum_world(y, pos, rows, collective_id, given=None):
    width = y.shape[-1]

    def blocks(n, size):
        return pltpu.VMEM((n, size, width), BF16)

    extra = () if given is None else (given,)
    return pl.pallas_call(
        functools.partial(sum_world_kernel, len(extra) > 0),
        out_shape=(jax.ShapeDtypeStruct((rows, width), F32),)
        + tuple(jax.ShapeDtypeStruct(a.shape, F32) for a in extra),
        in_specs=[ANY_SPEC, VMEM_SPEC] + [VMEM_SPEC] * len(extra),
        out_specs=(VMEM_SPEC,) * (1 + len(extra)),
        scratch_shapes=[
            pltpu.VMEM(y.shape, BF16),
            pltpu.SemaphoreType.DMA((4,)),
            blocks(16, rows),
            blocks(16, rows),
            blocks(4, rows // 2),
            blocks(4, rows // 2),
            blocks(4, rows),
            blocks(4, rows),
            pltpu.VMEM((2, 4, rows, width), BF16),
            pltpu.SemaphoreType.DMA((16,)),
            pltpu.SemaphoreType.DMA((16,)),
            pltpu.SemaphoreType.DMA((4, 2)),
            pltpu.SemaphoreType.DMA((4, 2)),
            pltpu.SemaphoreType.DMA((4, 2)),
            pltpu.SemaphoreType.DMA((4, 2)),
            pltpu.SemaphoreType.DMA((2, 4)),
            pltpu.SemaphoreType.DMA((2, 4)),
        ]
        + (ROW_SEMS if extra else []),
        compiler_params=params(collective_id),
        name="sum_world",
    )(y, pos, *extra)


def expert_grads_kernel(x, d_gate, d_up, hidden, d_copy, gate_grad, up_grad, down_grad, hidden_t):
    @pl.when(pl.program_id(0) == 0)
    def _():
        hidden_t[...] = hidden[...].T

    rows = x[...].T
    gate_grad[...] = dot_nn(rows, d_gate[...])
    up_grad[...] = dot_nn(rows, d_up[...])
    down_grad[...] = dot_nn(hidden_t[...], d_copy[...])


def expert_grads(x, d_gate, d_up, hidden, d_copy):
    slots, model = x.shape
    ff = hidden.shape[1]
    step = 256
    whole = pl.BlockSpec((slots, ff), lambda i: (0, 0))
    columns = pl.BlockSpec((slots, step), lambda i: (0, i))
    return pl.pallas_call(
        expert_grads_kernel,
        grid=(model // step,),
        in_specs=[columns, whole, whole, whole, columns],
        out_specs=[
            pl.BlockSpec((step, ff), lambda i: (i, 0)),
            pl.BlockSpec((step, ff), lambda i: (i, 0)),
            pl.BlockSpec((ff, step), lambda i: (0, i)),
        ],
        out_shape=(
            jax.ShapeDtypeStruct((model, ff), F32),
            jax.ShapeDtypeStruct((model, ff), F32),
            jax.ShapeDtypeStruct((ff, model), F32),
        ),
        scratch_shapes=[pltpu.VMEM((ff, slots), BF16)],
        compiler_params=params(),
        name="expert_grads",
    )(x, d_gate, d_up, hidden, d_copy)


def experts_by_all_to_all(
    mixed, state, teacher, routes, valid_slot, valid_count, router_weight, gate_weight, up_weight, down_weight,
    devices, capacity, slots_all,
):
    tok_dev, model_width = mixed.shape
    top_count = routes.shape[1]
    ffn_width = gate_weight.shape[2]
    logits = jnp.dot(mixed, router_weight, preferred_element_type=jnp.float32)
    gates = jax.nn.softmax(jnp.take_along_axis(logits, routes, axis=1), axis=-1)
    rows_total = tok_dev * top_count
    expert_ids = routes.reshape(rows_total)
    live_rows = jnp.repeat(valid_slot, top_count)
    expert_range = jnp.arange(devices, dtype=jnp.int32)
    hit_table = ((expert_ids[:, None] == expert_range[None, :]) & live_rows[:, None]).astype(
        jnp.int32
    )
    earlier = jnp.cumsum(hit_table, axis=0) - hit_table
    position_in = jnp.sum(earlier * hit_table, axis=1)
    slot_index = jnp.where(live_rows, expert_ids * capacity + position_in, devices * capacity)
    row_of_slot = (
        jnp.full((devices * capacity + 1,), rows_total, jnp.int32)
        .at[slot_index]
        .set(jnp.arange(rows_total, dtype=jnp.int32))[: devices * capacity]
    )
    token_of_slot = jnp.where(row_of_slot < rows_total, row_of_slot // top_count, tok_dev)
    mixed_pad = jnp.concatenate([mixed, jnp.zeros((1, model_width), jnp.bfloat16)], axis=0)
    send_rows = mixed_pad[token_of_slot].reshape(devices, capacity, model_width)
    arrived = lax.all_to_all(send_rows, ("dp", "expert"), split_axis=0, concat_axis=0, tiled=True)
    sources = arrived.shape[0]
    items = arrived.shape[1]
    flat_in = arrived.reshape(sources * items, model_width)
    gate_pre = jnp.dot(flat_in, gate_weight[0], preferred_element_type=jnp.float32)
    up_pre = jnp.dot(flat_in, up_weight[0], preferred_element_type=jnp.float32)
    hidden_units = (jax.nn.silu(gate_pre) * up_pre).astype(jnp.bfloat16)
    produced = jnp.dot(hidden_units, down_weight[0], preferred_element_type=jnp.float32).astype(
        jnp.bfloat16
    )
    produced, gate_pre, up_pre, hidden_units, arrived = (
        produced.reshape(sources, items, model_width),
        gate_pre.reshape(sources, items, ffn_width),
        up_pre.reshape(sources, items, ffn_width),
        hidden_units.reshape(sources, items, ffn_width),
        arrived,
    )
    returned = lax.all_to_all(produced, ("dp", "expert"), split_axis=0, concat_axis=0, tiled=True)
    returned_pad = jnp.concatenate(
        [
            returned.reshape(devices * capacity, model_width),
            jnp.zeros((1, model_width), jnp.bfloat16),
        ],
        axis=0,
    )
    copies = returned_pad[slot_index].reshape(tok_dev, top_count, model_width)
    layer_out = state + jnp.sum(gates[:, :, None] * copies, axis=1)
    live_tokens = valid_slot.astype(jnp.float32)[:, None]
    diff = (layer_out - teacher.astype(jnp.float32)) * live_tokens
    local_square = jnp.sum(diff * diff)
    d_out = 2.0 * slots_all * diff / valid_count
    d_gates = jnp.sum(d_out[:, None, :] * copies, axis=-1)
    d_chosen = gates * (d_gates - jnp.sum(gates * d_gates, axis=-1, keepdims=True))
    d_logits = jnp.sum(
        jnp.where(routes[:, :, None] == expert_range[None, None, :], d_chosen[:, :, None], 0.0),
        axis=1,
    ).astype(jnp.bfloat16)
    d_copies = (
        (gates[:, :, None] * d_out[:, None, :])
        .astype(jnp.bfloat16)
        .reshape(rows_total, model_width)
    )
    d_copies_pad = jnp.concatenate([d_copies, jnp.zeros((1, model_width), jnp.bfloat16)], axis=0)
    d_send = d_copies_pad[row_of_slot].reshape(devices, capacity, model_width)
    d_arrived = lax.all_to_all(d_send, ("dp", "expert"), split_axis=0, concat_axis=0, tiled=True)
    flat_d = d_arrived.reshape(-1, model_width)
    flat_in = arrived.reshape(-1, model_width)
    flat_gate = gate_pre.reshape(-1, ffn_width)
    flat_up = up_pre.reshape(-1, ffn_width)
    flat_hidden = hidden_units.reshape(-1, ffn_width)
    d_hidden = contract(flat_d, down_weight[0], 1, 1)
    sigmoid_gate = jax.nn.sigmoid(flat_gate)
    d_gate = (d_hidden * flat_up * sigmoid_gate * (1.0 + flat_gate * (1.0 - sigmoid_gate))).astype(
        jnp.bfloat16
    )
    d_up = (d_hidden * flat_gate * sigmoid_gate).astype(jnp.bfloat16)
    down_grad = contract(flat_hidden, flat_d, 0, 0)[None]
    gate_grad = contract(flat_in, d_gate, 0, 0)[None]
    up_grad = contract(flat_in, d_up, 0, 0)[None]
    d_in = (contract(d_gate, gate_weight[0], 1, 1) + contract(d_up, up_weight[0], 1, 1)).astype(
        jnp.bfloat16
    )
    d_returned = lax.all_to_all(
        d_in.reshape(devices, capacity, model_width),
        ("dp", "expert"),
        split_axis=0,
        concat_axis=0,
        tiled=True,
    )
    d_returned_pad = jnp.concatenate(
        [
            d_returned.reshape(devices * capacity, model_width),
            jnp.zeros((1, model_width), jnp.bfloat16),
        ],
        axis=0,
    )
    d_mixed = jnp.sum(
        d_returned_pad[slot_index].reshape(tok_dev, top_count, model_width),
        axis=1,
        dtype=jnp.float32,
    )
    d_mixed = d_mixed + contract(d_logits, router_weight, 1, 1)
    router_local = contract(d_logits, mixed, 0, 0)
    return layer_out, d_out, d_mixed, local_square, router_local, gate_grad, up_grad, down_grad


def experts_by_gather(
    mixed, state, teacher, routes, valid_slot, valid_count, router_weight,
    gate_weight, up_weight, down_weight, devices, capacity, slots_all,
):
    tok_dev, model_width = mixed.shape
    room = -(-2 * capacity // 16) * 16
    expert_range = jnp.arange(devices, dtype=jnp.int32)
    logits = jnp.dot(mixed, router_weight, preferred_element_type=F32)
    chosen = jnp.any(routes[:, :, None] == expert_range[None, None], axis=1)
    gates = jax.nn.softmax(jnp.where(chosen, logits, -jnp.inf), axis=-1)
    live_gates = jnp.where(valid_slot[:, None], gates, 0.0)
    gate_rows = live_gates.T[:, None]
    pos, x_rows, y_rows, kept = experts_fwd(
        mixed, gate_rows, gate_weight[0], up_weight[0], down_weight[0], capacity, room
    )
    layer_out = state + sum_world(y_rows.reshape(16, room, model_width), pos, tok_dev, 8)[0]
    live_tokens = valid_slot.astype(F32)[:, None]
    diff = (layer_out - teacher.astype(F32)) * live_tokens
    local_square = jnp.sum(diff * diff)
    d_out = 2.0 * slots_all * diff / valid_count
    hidden = kept[3]
    d_gates, d_rows, d_copy, d_gate, d_up = experts_bwd(
        d_out.astype(BF16), pos, kept[:3] + kept[4:], gate_weight[0], up_weight[0], down_weight[0], room
    )
    back, d_gates = sum_world(d_rows.reshape(16, room, model_width), pos, tok_dev, 9, d_gates)
    d_gates = d_gates[:, 0].T

    gate_grad, up_grad, down_grad = (
        grad[None] for grad in expert_grads(x_rows, d_gate, d_up, hidden, d_copy)
    )
    d_logits = (gates * (d_gates - jnp.sum(gates * d_gates, axis=-1, keepdims=True))).astype(BF16)
    d_mixed = back + contract(d_logits, router_weight, 1, 1)
    router_local = contract(d_logits, mixed, 0, 0)
    return layer_out, d_out, d_mixed, local_square, router_local, gate_grad, up_grad, down_grad


def head_rope(linear, gain_vec, cos, sin):
    value = root_mean_scale(linear, gain_vec)
    half = value.shape[-1] // 2
    return value * cos + jnp.roll(value, half, axis=-1) * sin


def body(
    tokens,
    teacher,
    routes,
    cont_lengths,
    query_weight,
    key_projection,
    value_projection,
    output_weight,
    router_weight,
    gate_weight,
    up_weight,
    down_weight,
    input_gain,
    post_gain,
    query_gain,
    key_gain,
):
    n_dp = lax.axis_size("dp")
    n_owner = lax.axis_size("expert")
    devices = n_dp * n_owner
    rank_dp = lax.axis_index("dp")
    rank_owner = lax.axis_index("expert")
    flat_rank = rank_dp * n_owner + rank_owner
    column = rank_owner % 2
    first_column = column == 0
    tok_dev, model_width = tokens.shape
    top_count = routes.shape[1]
    head_dim = query_gain.shape[0]
    kv_width = key_projection.shape[1]
    query_width = query_weight.shape[1]
    query_group = query_width // n_dp
    assert n_dp == 4 and kv_width == n_dp * head_dim
    prompt_block = tok_dev - CMAX
    half_prompt = n_dp * prompt_block
    prompt_len = 2 * half_prompt
    capacity = max(2, tok_dev * top_count * 5 // (4 * devices))
    slots_all = devices * tok_dev
    slot_ids = jnp.arange(tok_dev, dtype=jnp.int32)
    own_length = cont_lengths[flat_rank]
    valid_slot = (slot_ids < prompt_block) | (slot_ids - prompt_block < own_length)
    valid_count = (devices * prompt_block + jnp.sum(cont_lengths)).astype(F32)
    tokens_float = tokens.astype(F32)
    normed_float, first_norm_back = jax.vjp(root_mean_scale, tokens_float, input_gain)
    normed = normed_float.astype(BF16)

    block_ids = jnp.arange(n_dp, dtype=jnp.int32)[:, None]
    positions = jnp.where(
        slot_ids[None] < prompt_block,
        (column * n_dp + block_ids) * prompt_block + slot_ids[None],
        prompt_len + slot_ids[None] - prompt_block,
    )
    half_head = head_dim // 2
    frequency = rope_base ** (-(jnp.arange(half_head, dtype=F32) * 2.0) / head_dim)
    angles = positions.astype(F32)[:, :, None] * frequency
    cos_half, sin_half = jnp.cos(angles), jnp.sin(angles)
    cos = jnp.concatenate([cos_half, cos_half], axis=-1)
    sin = jnp.concatenate([-sin_half, sin_half], axis=-1)
    lin, normed_cols_t, normed_cols, key_lin, all_keys, all_values = project_qkv(
        normed, query_weight, key_projection, value_projection, key_gain[None], cos, sin
    )
    query_gain_row = query_gain[None]
    queries, attended = attention_fwd(
        cont_lengths, lin, query_gain_row, cos, sin, all_keys, all_values, prompt_len
    )
    state = tokens_float + project_out(attended, output_weight)
    mixed_float, second_norm_back = jax.vjp(root_mean_scale, state, post_gain)
    mixed = mixed_float.astype(BF16)
    sizes = (devices, capacity, slots_all)
    weights = (router_weight, gate_weight, up_weight, down_weight)
    if n_dp == 4 and n_owner == 8:
        moe = experts_by_gather(
            mixed, state, teacher, routes, valid_slot, valid_count, *weights, *sizes
        )
    else:
        moe = experts_by_all_to_all(
            mixed, state, teacher, routes, valid_slot, valid_count, *weights, *sizes
        )
    layer_out, d_out, d_mixed, local_square, router_local, gate_grad, up_grad, down_grad = moe
    d_state_norm, d_post_gain = second_norm_back(d_mixed)
    d_state = d_out + d_state_norm
    d_branch = d_state.astype(BF16)
    d_attended, d_branch_all, attended_t = grad_branch(d_branch, output_weight, attended)
    d_query_lin, d_keys, d_values, gain_parts, out_part = attention_bwd(
        cont_lengths, lin, queries, d_attended, query_gain_row, cos, sin, all_keys, all_values,
        attended_t, d_branch_all, prompt_len,
    )
    d_query_gain = jnp.sum(gain_parts, axis=(0, 1))
    width = query_weight.shape[0]
    group = query_group + 2 * head_dim
    rows_here = width // n_owner
    by_line = n_dp == 4 and n_owner == 8

    def packed(parts):
        small = jnp.concatenate([a.reshape(-1) for a in parts])
        piece_rows = -(-small.shape[0] // (8 * 8 * 128)) * 8
        small = jnp.pad(small, (0, 8 * piece_rows * 128 - small.shape[0]))
        return small.reshape(8, piece_rows, 128)

    out_part = out_part.reshape(n_owner, -1, model_width)
    weights = (query_weight, key_projection, value_projection)
    if by_line:

        def line(parts):
            flat = jnp.concatenate(parts)
            return jnp.pad(flat, (0, model_width - flat.shape[0]))[None]

        small = jnp.concatenate(
            [router_local, d_post_gain[None], line([d_query_gain]), line([local_square[None]])]
        )
        small_rows = -(-small.shape[0] // 8) * 8
        small = jnp.pad(small, ((0, small_rows - small.shape[0]), (0, 0)))
        small = small.reshape(small_rows, 8, -1).transpose(1, 0, 2)
        d_normed, query_grad, key_grad, value_grad, output_grad, small, input_gain_grad = grad_qkv_line(
            d_query_lin, d_keys, d_values, key_lin, cos, sin, key_gain[None],
            *weights, normed_cols_t, normed_cols, out_part, small, input_gain[None],
        )
        key_gain_grad = jnp.sum(input_gain_grad[:, 1, :head_dim], axis=0)
        input_gain_grad = input_gain_grad[:, 0].reshape(-1)
        sums = small.transpose(1, 0, 2).reshape(small_rows, model_width)
        at = router_local.shape[0]
        router_grad, post_gain_grad = sums[:at].T, sums[at]
        query_gain_grad = sums[at + 1, :head_dim]
        total_square = sums[at + 2, :1]
        d_tokens_norm = first_norm_back(d_normed)[0]
    else:
        _, key_back = jax.vjp(
            lambda a, b: head_rope(a, b, cos, sin), key_lin.reshape(n_dp, tok_dev, head_dim), key_gain
        )
        prompt_grads = jnp.stack(
            [jnp.sum(d_keys[:, :prompt_len], axis=0), jnp.sum(d_values[:, :prompt_len], axis=0)]
        )
        mine_part = jnp.where(first_column, prompt_grads[:, :half_prompt], prompt_grads[:, half_prompt:])
        their_part = jnp.where(first_column, prompt_grads[:, half_prompt:], prompt_grads[:, :half_prompt])
        own_prompt = (mine_part + partner(their_part, "expert", 0)).reshape(
            2, n_dp, prompt_block, head_dim
        )
        d_key_post = jnp.concatenate([own_prompt[0], d_keys[:, prompt_len:]], axis=1)
        d_value_lin = jnp.concatenate([own_prompt[1], d_values[:, prompt_len:]], axis=1)
        d_key_float, d_key_gain = key_back(d_key_post)
        rows = n_dp * tok_dev
        d_lin = jnp.concatenate(
            [
                d_query_lin,
                d_key_float.astype(BF16).reshape(rows, head_dim),
                d_value_lin.astype(BF16).reshape(rows, head_dim),
            ],
            axis=1,
        )
        small_parts = [router_local, d_post_gain, d_query_gain, d_key_gain, local_square[None]]
        d_normed, qkv_part, output_grad = grad_qkv(d_lin, *weights, normed_cols_t, out_part)
        d_tokens_norm, d_input_gain = first_norm_back(d_normed)
        small_parts.append(d_input_gain)
        by_owner = (
            qkv_part.reshape(n_dp, n_owner, rows_here, group)
            .transpose(1, 0, 2, 3)
            .reshape(n_owner, n_dp * rows_here, group)
        )
        qkv_rows, small = last_sums(by_owner, packed(small_parts))
        qkv_rows = qkv_rows.reshape(n_dp, rows_here, group)

        def columns(start, size):
            part = qkv_rows[:, :, start : start + size]
            return part.transpose(1, 0, 2).reshape(rows_here, n_dp * size)

        query_grad = columns(0, query_group)
        key_grad = columns(query_group, head_dim)
        value_grad = columns(query_group + head_dim, head_dim)
        small = small.reshape(-1)
        starts = [0]
        for a in small_parts:
            starts.append(starts[-1] + a.size)
        sums = [small[i:j].reshape(a.shape) for a, i, j in zip(small_parts, starts, starts[1:])]
        router_grad, post_gain_grad, query_gain_grad, key_gain_grad, total_square, input_gain_grad = sums
        router_grad = router_grad.T
    tokens_grad = d_state + d_tokens_norm
    loss = total_square[0] / (valid_count * model_width)
    return (
        layer_out,
        loss,
        tokens_grad,
        query_grad,
        key_grad,
        value_grad,
        output_grad,
        router_grad,
        gate_grad,
        up_grad,
        down_grad,
        input_gain_grad,
        post_gain_grad,
        query_gain_grad,
        key_gain_grad,
    )


def solution(mesh):
    in_specs = (
        P(("dp", "expert"), None),
        P(("dp", "expert"), None),
        P(("dp", "expert"), None),
        P(),
        P("dp", None),
        P("dp", None),
        P("dp", None),
        P("dp", None),
        P(),
        P(("dp", "expert"), None, None),
        P(("dp", "expert"), None, None),
        P(("dp", "expert"), None, None),
        P(),
        P(),
        P(),
        P(),
    )
    out_specs = (
        P(("dp", "expert"), None),
        P(),
        P(("dp", "expert"), None),
        P(("dp", "expert"), None),
        P(("dp", "expert"), None),
        P(("dp", "expert"), None),
        P(("dp", "expert"), None),
        P(),
        P(("dp", "expert"), None, None),
        P(("dp", "expert"), None, None),
        P(("dp", "expert"), None, None),
        P(),
        P(),
        P(),
        P(),
    )
    return jax.shard_map(body, mesh=mesh, in_specs=in_specs, out_specs=out_specs, check_vma=False)
```

```python
import functools

import jax
import jax.numpy as jnp
from jax import lax
from jax.experimental import pallas as pl
from jax.experimental.pallas import tpu as pltpu
from jax.sharding import PartitionSpec as P

CMAX = 128
norm_eps = 1e-06
rope_base = 1000000.0
MESH = pl.DeviceIdType.MESH
F32 = jnp.float32
BF16 = jnp.bfloat16
VMEM_SPEC = pl.BlockSpec(memory_space=pltpu.VMEM)
ANY_SPEC = pl.BlockSpec(memory_space=pl.ANY)
VMEM_LIMIT = 56 * 1024 * 1024


def params(collective_id=None):
    return pltpu.CompilerParams(
        collective_id=collective_id,
        has_side_effects=collective_id is not None,
        vmem_limit_bytes=VMEM_LIMIT,
    )


def greet(devices):
    barrier = pltpu.get_barrier_semaphore()
    for device in devices:
        pl.semaphore_signal(barrier, inc=1, device_id=device, device_id_type=MESH)
    pl.semaphore_wait(barrier, len(devices))


def remote(src, dst, send_sem, recv_sem, device):
    return pltpu.make_async_remote_copy(
        src_ref=src,
        dst_ref=dst,
        send_sem=send_sem,
        recv_sem=recv_sem,
        device_id=device,
        device_id_type=MESH,
    )


def start_all(copies):
    for copy in copies:
        copy.start()
    return copies


def wait_all(copies):
    for copy in copies:
        copy.wait()
    copies.clear()


def loading(pairs, sems):
    return [start_all([pltpu.make_async_copy(a, b, sems.at[i])]) for i, (a, b) in enumerate(pairs)]


def aligned(index, size):
    return pl.ds(pl.multiple_of(index * size, size), size)


def dot_nn(a, b):
    return lax.dot_general(a, b, (((1,), (0,)), ((), ())), preferred_element_type=F32)


def dot_nt(a, b):
    return lax.dot_general(a, b, (((1,), (1,)), ((), ())), preferred_element_type=F32)


def dot_tn(a, b):
    return lax.dot_general(a, b, (((0,), (0,)), ((), ())), preferred_element_type=F32)


PEER_MASKS = (3, 1, 2)


def relay_sum(r, e, products, own, mine, send, half_in, full_in, hs, hr, fs, fr, step):
    near, far, diag = r ^ 1, r ^ 2, r ^ 3
    rows = mine.shape[0]
    half = rows // 2
    low, high = pl.ds(0, half), pl.ds(half, half)
    products(diag, send.at[2])
    relays = [
        remote(send.at[2, low], half_in.at[0], hs.at[0], hr.at[0], (near, e)),
        remote(send.at[2, high], half_in.at[1], hs.at[1], hr.at[1], (far, e)),
    ]
    for copy in relays:
        copy.start()
    parts = ((0, low, near), (1, high, far), (0, high, near), (1, low, far))
    fulls = [
        remote(send.at[i, part], full_in.at[i, part], fs.at[n], fr.at[n], (p, e))
        for n, (i, part, p) in enumerate(parts)
    ]
    products(near, send.at[0])
    fulls[0].start()
    products(far, send.at[1])
    fulls[1].start()
    for i, start, slot, n in ((1, 0, 0, 3), (0, half, 1, 2)):
        relays[slot].wait_recv()

        def add(c, carry):
            t = pl.ds(pl.multiple_of(start + c * step, step), step)
            value = send[i, t, :].astype(F32) + half_in[slot, aligned(c, step), :].astype(F32)
            send[i, t, :] = value.astype(BF16)
            return carry

        lax.fori_loop(0, half // step, add, 0)
        fulls[n].start()
    own()
    for copy in fulls:
        copy.wait_recv()

    def total(c, carry):
        t = aligned(c, step)
        mine[t, :] = mine[t, :] + (full_in[0, t, :].astype(F32) + full_in[1, t, :].astype(F32))
        return carry

    lax.fori_loop(0, rows // step, total, 0)
    for copy in relays + fulls:
        copy.wait_send()


def relay_scratch(rows, width):
    return [
        pltpu.VMEM((3, rows, width), BF16),
        pltpu.VMEM((2, rows // 2, width), BF16),
        pltpu.VMEM((2, rows, width), BF16),
        pltpu.SemaphoreType.DMA((2,)),
        pltpu.SemaphoreType.DMA((2,)),
        pltpu.SemaphoreType.DMA((4,)),
        pltpu.SemaphoreType.DMA((4,)),
    ]


def qkv_kernel(
    tok, normed, wq_in, wk_in, wv_in, gain, cos, sin, lin, cols_t, cols, key_lin, keys, values,
    wq, wk, wv, own_kv, other_kv, local, asend, arecv, ksend, krecv, *relay,
):
    r, e = lax.axis_index("dp"), lax.axis_index("expert")
    peers = [r ^ m for m in PEER_MASKS]
    width = wq.shape[0]
    qg = wq.shape[1] // 4
    kg = wk.shape[1] // 4
    rows = cols.shape[0]
    loads = loading(((wq_in, wq), (wk_in, wk), (wv_in, wv)), local)
    greet([(p, e) for p in peers] + [(r, e ^ 1)])
    first = []
    for i, p in enumerate(peers):
        copy = remote(
            normed.at[:, aligned(p, width)], cols.at[aligned(r, tok), :],
            asend.at[i], arecv.at[i], (p, e),
        )
        copy.start()
        first.append(copy)
    cols[aligned(r, tok), :] = normed[:, aligned(r, width)]
    for copy in first:
        copy.wait()
    for copies in loads:
        wait_all(copies)

    def products(p, dst):
        def chunk(c, carry):
            columns = pl.ds(pl.multiple_of(p * qg + c * 256, 256), 256)
            dst[:, aligned(c, 256)] = dot_nn(cols[...], wq[:, columns]).astype(dst.dtype)
            return carry

        lax.fori_loop(0, qg // 256, chunk, 0)
        dst[:, qg : qg + kg] = dot_nn(cols[...], wk[:, aligned(p, kg)]).astype(dst.dtype)
        dst[:, qg + kg :] = dot_nn(cols[...], wv[:, aligned(p, kg)]).astype(dst.dtype)

    def own():
        products(r, lin)
        cols_t[...] = cols[...].T

    relay_sum(r, e, products, own, lin, *relay, 32)
    core = e % 2
    head = gain.shape[1]
    prompt = tok - CMAX
    column = 4 * prompt
    for i in range(4):
        rows_i = slice(i * tok, (i + 1) * tok)
        x = lin[rows_i, qg : qg + kg]
        key_lin[rows_i, :] = x
        x = x * lax.rsqrt(jnp.mean(x * x, axis=-1, keepdims=True) + norm_eps) * gain[...]
        k = (x * cos[i] + pltpu.roll(x, head // 2, 1) * sin[i]).astype(BF16)
        v = lin[rows_i, qg + kg :].astype(BF16)
        for n, (part, out) in enumerate(((k, keys), (v, values))):
            own_kv[n, i * prompt : (i + 1) * prompt] = part[:prompt]
            out[i, 2 * column :] = part[prompt:]
    copy = remote(own_kv, other_kv, ksend.at[0], krecv.at[0], (r, e ^ 1))
    copy.start()
    for n, out in enumerate((keys, values)):
        for i in range(4):
            out[i, aligned(core, column)] = own_kv[n]
    copy.wait()
    for n, out in enumerate((keys, values)):
        for i in range(4):
            out[i, aligned(1 - core, column)] = other_kv[n]


def project_qkv(normed, wq, wk, wv, gain, cos, sin):
    tok = normed.shape[0]
    rows = 4 * tok
    group = (wq.shape[1] + wk.shape[1] + wv.shape[1]) // 4
    head = gain.shape[1]
    total_keys = 8 * (tok - CMAX) + CMAX
    return pl.pallas_call(
        functools.partial(qkv_kernel, tok),
        out_shape=(
            jax.ShapeDtypeStruct((rows, group), F32),
            jax.ShapeDtypeStruct((wq.shape[0], rows), BF16),
            jax.ShapeDtypeStruct((rows, wq.shape[0]), BF16),
            jax.ShapeDtypeStruct((rows, head), F32),
            jax.ShapeDtypeStruct((4, total_keys, head), BF16),
            jax.ShapeDtypeStruct((4, total_keys, head), BF16),
        ),
        in_specs=[VMEM_SPEC] + [ANY_SPEC] * 3 + [VMEM_SPEC] * 3,
        out_specs=(VMEM_SPEC,) * 6,
        scratch_shapes=[pltpu.VMEM(w.shape, BF16) for w in (wq, wk, wv)]
        + [pltpu.VMEM((2, 4 * (tok - CMAX), head), BF16)] * 2
        + [pltpu.SemaphoreType.DMA((3,))] * 3
        + [pltpu.SemaphoreType.DMA((1,))] * 2
        + relay_scratch(rows, group),
        compiler_params=params(1),
        name="qkv_exchange",
    )(normed, wq, wk, wv, gain, cos, sin)


def out_kernel(attn_in, wo_in, total, attn, wo, local, *relay):
    r, e = lax.axis_index("dp"), lax.axis_index("expert")
    tok, width = total.shape
    step = width // 4
    loads = loading(((attn_in, attn), (wo_in, wo)), local)
    greet([(r ^ m, e) for m in PEER_MASKS])
    for copies in loads:
        wait_all(copies)

    def products(p, dst):
        def chunk(c, carry):
            n = aligned(c, step)
            dst[:, n] = dot_nn(attn[aligned(p, tok), :], wo[:, n]).astype(dst.dtype)
            return carry

        lax.fori_loop(0, width // step, chunk, 0)

    relay_sum(r, e, products, lambda: products(r, total), total, *relay, 16)


def project_out(attn, wo):
    tok = attn.shape[0] // 4
    return pl.pallas_call(
        out_kernel,
        out_shape=jax.ShapeDtypeStruct((tok, wo.shape[1]), F32),
        in_specs=[ANY_SPEC] * 2,
        out_specs=VMEM_SPEC,
        scratch_shapes=[
            pltpu.VMEM(attn.shape, BF16),
            pltpu.VMEM(wo.shape, BF16),
            pltpu.SemaphoreType.DMA((2,)),
        ]
        + relay_scratch(tok, wo.shape[1]),
        compiler_params=params(2),
        name="out_exchange",
    )(attn, wo)


def dgrad_kernel(
    mine, wq, wk, wv, cols_t, out_part, normal, grads, out_grad,
    blocks, dsum, dsend, drecv, ssem, rsem, bsend, brecv, *scratch,
):
    r, e = lax.axis_index("dp"), lax.axis_index("expert")
    rows = mine.shape[0]
    tok = rows // 4
    half = rows // 2
    qg = wq.shape[1] // 4
    kg = wk.shape[1] // 4
    width = wq.shape[0]
    peers = [r ^ m for m in PEER_MASKS]
    near, far, diag = r ^ 1, r ^ 2, r ^ 3
    pair_in, send, recv, *sems = scratch
    begin, middle, finish = owner_sum([out_part], [out_grad], [pair_in], [send], [recv], *sems)
    greet([(p, e) for p in peers] + [(r, e ^ 1)] + owner_peers())
    begin()
    low, high = pl.ds(0, half), pl.ds(half, half)
    first_near = remote(mine.at[low], blocks.at[0, low], ssem.at[0], rsem.at[0], (near, e))
    first_far = remote(mine.at[high], blocks.at[1, high], ssem.at[1], rsem.at[1], (far, e))
    second_near = remote(mine.at[high], blocks.at[0, high], ssem.at[2], rsem.at[2], (near, e))
    second_far = remote(mine.at[low], blocks.at[1, low], ssem.at[3], rsem.at[3], (far, e))
    pass_far = remote(blocks.at[0, low], blocks.at[2, low], ssem.at[4], rsem.at[4], (far, e))
    pass_near = remote(blocks.at[1, high], blocks.at[2, high], ssem.at[5], rsem.at[5], (near, e))
    for copy in (first_near, first_far, second_near, second_far):
        copy.start()

    def products(p, src, start):
        def chunk(c, carry):
            t = aligned(c, tok)
            x = src[t, :]
            value = (
                dot_nt(x[:, :qg], wq[:, aligned(p, qg)])
                + dot_nt(x[:, qg : qg + kg], wk[:, aligned(p, kg)])
                + dot_nt(x[:, qg + kg :], wv[:, aligned(p, kg)])
            )
            if start:
                dsum[t, :] = value
            else:
                dsum[t, :] = dsum[t, :] + value
            return carry

        lax.fori_loop(0, 4, chunk, 0)

        def outer(c, carry):
            n = aligned(c, 128)
            grads[aligned(p, width), n] = dot_nn(cols_t[...], src[:, n]).astype(BF16)
            return carry

        lax.fori_loop(0, (qg + 2 * kg) // 128, outer, 0)

    middle()
    products(r, mine, True)
    first_near.wait()
    pass_far.start()
    first_far.wait()
    pass_near.start()
    second_near.wait()
    products(near, blocks.at[0], False)
    second_far.wait()
    products(far, blocks.at[1], False)
    pass_far.wait()
    pass_near.wait()
    products(diag, blocks.at[2], False)
    back = []
    for i, p in enumerate(peers):
        dsend[i] = dsum[aligned(p, tok), :].astype(BF16)
        copy = remote(dsend.at[i], drecv.at[i], bsend.at[i], brecv.at[i], (p, e))
        copy.start()
        back.append(copy)
    normal[:, aligned(r, width)] = dsum[aligned(r, tok), :]
    for i, p in enumerate(peers):
        back[i].wait()
        normal[:, aligned(p, width)] = drecv[i].astype(F32)
    finish()


def grad_qkv(mine, wq, wk, wv, cols_t, out_part):
    rows, group = mine.shape
    tok = rows // 4
    width = wq.shape[0]
    return pl.pallas_call(
        dgrad_kernel,
        out_shape=(
            jax.ShapeDtypeStruct((tok, 4 * width), F32),
            jax.ShapeDtypeStruct((4 * width, group), BF16),
            jax.ShapeDtypeStruct(out_part.shape[1:], F32),
        ),
        in_specs=[VMEM_SPEC] * 6,
        out_specs=(VMEM_SPEC,) * 3,
        scratch_shapes=[
            pltpu.VMEM((3, rows, group), BF16),
            pltpu.VMEM((rows, width), F32),
            pltpu.VMEM((3, tok, width), BF16),
            pltpu.VMEM((3, tok, width), BF16),
            pltpu.SemaphoreType.DMA((6,)),
            pltpu.SemaphoreType.DMA((6,)),
            pltpu.SemaphoreType.DMA((3,)),
            pltpu.SemaphoreType.DMA((3,)),
        ]
        + owner_scratch([out_part]),
        compiler_params=params(4),
        name="dqkv_exchange",
    )(mine, wq, wk, wv, cols_t, out_part)


def branch_kernel(
    mine, wo_in, attn_in, d_attn, full_out, attn_t_out, wo, attn, full, attn_t, local, ssem, rsem
):
    r, e = lax.axis_index("dp"), lax.axis_index("expert")
    tok = mine.shape[0]
    half = tok // 2
    peers = [r ^ m for m in PEER_MASKS]
    near, far, diag = r ^ 1, r ^ 2, r ^ 3
    loads = loading(((attn_in, attn), (wo_in, wo)), local)
    greet([(p, e) for p in peers])

    def part(q, which):
        return pl.ds(pl.multiple_of(q * tok + which * half, half), half)

    low, high = pl.ds(0, half), pl.ds(half, half)
    first_near = remote(mine.at[low], full.at[part(r, 0)], ssem.at[0], rsem.at[0], (near, e))
    first_far = remote(mine.at[high], full.at[part(r, 1)], ssem.at[1], rsem.at[1], (far, e))
    second_near = remote(mine.at[high], full.at[part(r, 1)], ssem.at[2], rsem.at[2], (near, e))
    second_far = remote(mine.at[low], full.at[part(r, 0)], ssem.at[3], rsem.at[3], (far, e))
    pass_far = remote(full.at[part(near, 0)], full.at[part(near, 0)], ssem.at[4], rsem.at[4], (far, e))
    pass_near = remote(full.at[part(far, 1)], full.at[part(far, 1)], ssem.at[5], rsem.at[5], (near, e))
    for copy in (first_near, first_far, second_near, second_far):
        copy.start()
    full[aligned(r, tok), :] = mine[...]
    wait_all(loads[0])
    attn_t[...] = attn[...].T
    leaving = start_all([pltpu.make_async_copy(attn_t, attn_t_out, local.at[0])])
    wait_all(loads[1])
    heads = wo.shape[0]
    step = heads // 4

    def products(q):
        def chunk(c, carry):
            n = aligned(c, step)
            d_attn[aligned(q, tok), n] = dot_nt(full[aligned(q, tok), :], wo[n, :]).astype(BF16)
            return carry

        lax.fori_loop(0, 4, chunk, 0)

    products(r)
    first_near.wait()
    pass_far.start()
    first_far.wait()
    pass_near.start()
    second_near.wait()
    products(near)
    second_far.wait()
    products(far)
    pass_far.wait()
    pass_near.wait()
    leaving += start_all([pltpu.make_async_copy(full, full_out, local.at[1])])
    products(diag)
    wait_all(leaving)


def grad_branch(mine, wo, attn):
    tok, width = mine.shape
    return pl.pallas_call(
        branch_kernel,
        out_shape=(
            jax.ShapeDtypeStruct((4 * tok, wo.shape[0]), BF16),
            jax.ShapeDtypeStruct((4 * tok, width), BF16),
            jax.ShapeDtypeStruct((wo.shape[0], 4 * tok), BF16),
        ),
        in_specs=[VMEM_SPEC, ANY_SPEC, ANY_SPEC],
        out_specs=(VMEM_SPEC, ANY_SPEC, ANY_SPEC),
        scratch_shapes=[
            pltpu.VMEM(wo.shape, BF16),
            pltpu.VMEM(attn.shape, BF16),
            pltpu.VMEM((4 * tok, width), BF16),
            pltpu.VMEM((wo.shape[0], 4 * tok), BF16),
            pltpu.SemaphoreType.DMA((2,)),
            pltpu.SemaphoreType.DMA((6,)),
            pltpu.SemaphoreType.DMA((6,)),
        ],
        compiler_params=params(3),
        name="branch_exchange",
    )(mine, wo, attn)


def owner_order(n_z):
    order = list(range(1, n_z)) + [0]
    return order[1:2] + order[:1] + order[2:] if n_z > 2 else order


def owner_sum(arrays, outs, pair_in, send, recv, psend, precv, zsend, zrecv):
    r, e = lax.axis_index("dp"), lax.axis_index("expert")
    n_z = arrays[0].shape[0] // 2
    z, core = e // 2, e % 2
    targets = [lax.rem(z + j, n_z) for j in range(n_z)]
    order = owner_order(n_z)
    n_arrays = len(arrays)
    pair, moves = {}, []

    def begin():
        for j in order:
            for a in range(n_arrays):
                copy = remote(
                    arrays[a].at[targets[j] * 2 + (1 - core)], pair_in[a].at[j],
                    psend.at[a, j], precv.at[a, j], (r, e ^ 1),
                )
                copy.start()
                pair[a, j] = copy

    def middle():
        for j in order:
            for a in range(n_arrays):
                pair[a, j].wait()
                own = arrays[a][targets[j] * 2 + core].astype(F32) + pair_in[a][j].astype(F32)
                if j == 0:
                    outs[a][...] = own
                else:
                    send[a][j - 1] = own.astype(BF16)
                    copy = remote(
                        send[a].at[j - 1], recv[a].at[j - 1],
                        zsend.at[a, j - 1], zrecv.at[a, j - 1], (r, targets[j] * 2 + core),
                    )
                    copy.start()
                    moves.append(copy)

    def finish():
        for copy in moves:
            copy.wait()
        for a in range(n_arrays):
            value = outs[a][...]
            for j in range(n_z - 1):
                value = value + recv[a][j].astype(F32)
            outs[a][...] = value

    return begin, middle, finish


def owner_scratch(arrays):
    n_z = arrays[0].shape[0] // 2
    n = len(arrays)
    shapes = [a.shape[1:] for a in arrays]
    return (
        [pltpu.VMEM((n_z, *s), BF16) for s in shapes]
        + [pltpu.VMEM((n_z - 1, *s), BF16) for s in shapes]
        + [pltpu.VMEM((n_z - 1, *s), BF16) for s in shapes]
        + [pltpu.SemaphoreType.DMA((n, n_z))] * 2
        + [pltpu.SemaphoreType.DMA((n, n_z - 1))] * 2
    )


def owner_peers():
    r, e = lax.axis_index("dp"), lax.axis_index("expert")
    n_z = lax.axis_size("expert") // 2
    return [(r, lax.rem(e // 2 + j, n_z) * 2 + e % 2) for j in range(1, n_z)]


def last_sums_kernel(grads, small, grads_out, small_out, *scratch):
    r, e = lax.axis_index("dp"), lax.axis_index("expert")
    z, core = e // 2, e % 2
    n_z = grads.shape[0] // 2
    pair_in, send, recv, psend, precv, zsend, zrecv = scratch[:7]
    first_in, piece, line_in, s1, r1, s2, r2, s3, r3 = scratch[7:]
    begin, middle, finish = owner_sum(
        [grads], [grads_out], [pair_in], [send], [recv], psend, precv, zsend, zrecv
    )
    others = [(m // 2, m % 2) for m in range(1, 8)]
    plane = [(r ^ a, e ^ c) for a, c in others]
    greet(plane + owner_peers())
    begin()
    firsts = []
    for i, (a, c) in enumerate(others):
        copy = remote(
            small.at[(r ^ a) * 2 + (core ^ c)], first_in.at[i], s1.at[i], r1.at[i], plane[i]
        )
        copy.start()
        firsts.append(copy)
    middle()
    for copy in firsts:
        copy.wait()
    mine = r * 2 + core
    value = small[mine]
    for i in range(7):
        value = value + first_in[i]
    piece[0] = value
    seconds = []
    for j in range(1, n_z):
        copy = remote(
            piece.at[0], line_in.at[j - 1], s2.at[j - 1], r2.at[j - 1], owner_peers()[j - 1]
        )
        copy.start()
        seconds.append(copy)
    for copy in seconds:
        copy.wait()
    value = piece[0]
    for j in range(n_z - 1):
        value = value + line_in[j]
    small_out[mine] = value
    thirds = []
    for i, (a, c) in enumerate(others):
        copy = remote(small_out.at[mine], small_out.at[mine], s3.at[i], r3.at[i], plane[i])
        copy.start()
        thirds.append(copy)
    finish()
    for copy in thirds:
        copy.wait()


def last_sums(grads, small):
    n_z = grads.shape[0] // 2
    piece = small.shape[1:]
    return pl.pallas_call(
        last_sums_kernel,
        out_shape=(
            jax.ShapeDtypeStruct(grads.shape[1:], F32),
            jax.ShapeDtypeStruct(small.shape, F32),
        ),
        in_specs=[VMEM_SPEC] * 2,
        out_specs=(VMEM_SPEC,) * 2,
        scratch_shapes=owner_scratch([grads])
        + [
            pltpu.VMEM((7, *piece), F32),
            pltpu.VMEM((1, *piece), F32),
            pltpu.VMEM((n_z - 1, *piece), F32),
            pltpu.SemaphoreType.DMA((7,)),
            pltpu.SemaphoreType.DMA((7,)),
            pltpu.SemaphoreType.DMA((n_z - 1,)),
            pltpu.SemaphoreType.DMA((n_z - 1,)),
            pltpu.SemaphoreType.DMA((7,)),
            pltpu.SemaphoreType.DMA((7,)),
        ],
        compiler_params=params(5),
        name="last_sums",
    )(grads, small)


def line_sum(block, out, pair_in, work, lines, ps, pr, zs, zr):
    r, e = lax.axis_index("dp"), lax.axis_index("expert")
    z, core = e // 2, e % 2
    order = plane_order(z)[::-1]
    right = jnp.minimum(z + 1, 3) * 2 + core
    left = jnp.maximum(z - 1, 0) * 2 + core
    pairs, moves = [], []

    def begin():
        for k in range(4):
            copy = remote(
                block(order[k] * 2 + (1 - core)), pair_in.at[k], ps.at[k], pr.at[k], (r, e ^ 1)
            )
            copy.start()
            pairs.append(copy)

    def move(k, side, cond, to, add):
        b = order[k]
        copy = remote(work.at[k], lines.at[side, b], zs.at[side, k], zr.at[side, b], (r, to))
        moves.append((cond, copy))

        @pl.when(cond)
        def _():
            if add:
                copy.wait_recv()
                value = work[k].astype(F32) + lines[side, b].astype(F32)
                work[k] = value.astype(BF16)
            copy.start()

    def first():
        for k in range(4):
            pairs[k].wait_recv()
            value = block(order[k] * 2 + core)[...].astype(F32) + pair_in[k].astype(F32)
            if k == 3:
                out[...] = value
            else:
                work[k] = value.astype(BF16)
        ends(0)

    def ends(k):
        move(k, 0, z == 0, right, False)
        move(k, 1, z == 3, left, False)

    def inner(k):
        inside = (z > 0) & (z < 3)
        move(k, 0, inside & (order[k] > z), right, True)
        move(k, 1, inside & (order[k] < z), left, True)
        if k < 2:
            ends(k + 1)

    def last():
        for side, cond in ((0, z > 0), (1, z < 3)):

            @pl.when(cond)
            def _():
                at = lines.at[side, z]
                remote(at, at, zs.at[side, 3], zr.at[side, z], (r, e ^ 1)).wait_recv()
                out[...] = out[...] + lines[side, z].astype(F32)

        for copy in pairs:
            copy.wait_send()
        for cond, copy in moves:

            @pl.when(cond)
            def _():
                copy.wait_send()

    return begin, first, inner, last


LINE_SEMS = [
    pltpu.SemaphoreType.DMA((4,)),
    pltpu.SemaphoreType.DMA((4,)),
    pltpu.SemaphoreType.DMA((2, 4)),
    pltpu.SemaphoreType.DMA((2, 4)),
]


def dgrad_line_kernel(
    d_q, d_keys, d_values, key_lin, cos, sin, key_gain,
    wq_in, wk_in, wv_in, cols_t_in, cols_in, out_part_in, small, gain,
    normal, q_out, k_out, v_out, out_sum, small_out, gain_out,
    mine, prompt_sum, prompt_in, ksend, krecv, wq, wk, wv, cols_t, cols, out_part, local, qkv_sum, grads, blocks, dsum, dsend, drecv, opair, owork, olines, qpair, qwork, qlines,
    first_in, piece, line_in, gain_v, gain_in,
    ssem, rsem, bsend, brecv, s1, r1, s2, r2, s3, r3, s4, r4, s5, r5, *sems,
):
    r, e = lax.axis_index("dp"), lax.axis_index("expert")
    z, core = e // 2, e % 2
    rows = mine.shape[0]
    tok = rows // 4
    half = rows // 2
    qg = wq.shape[1] // 4
    kg = wk.shape[1] // 4
    width = wq.shape[0]
    share = width // 8
    peers = [r ^ m for m in PEER_MASKS]
    near, far, diag = r ^ 1, r ^ 2, r ^ 3
    order = (r, near, far, diag)
    out_begin, out_first, out_inner, out_last = line_sum(
        lambda o: out_part.at[o], out_sum, opair, owork, olines, *sems[:4]
    )
    units = [
        line_sum(
            lambda o, p=p: grads.at[o, p], qkv_sum.at[p], qpair.at[i], qwork.at[i], qlines.at[i],
            *(sem.at[i] for sem in sems[4:]),
        )
        for i, p in enumerate(order)
    ]
    line_peers = [(r, lax.rem(z + j, 4) * 2 + core) for j in (1, 2, 3)]
    others = [(m // 2, m % 2) for m in (6, 7, 2, 3, 4, 5, 1)]
    plane = [(r ^ a, e ^ c) for a, c in others]
    owners = [(r, e ^ m) for m in range(1, 8)]
    loads = loading(
        (
            (out_part_in, out_part), (cols_t_in, cols_t), (wq_in, wq), (wk_in, wk), (wv_in, wv),
            (cols_in, cols),
        ),
        local,
    )
    mine[:, :qg] = d_q[...]
    prompt = tok - CMAX
    column = 4 * prompt
    for n, d in enumerate((d_keys, d_values)):
        for c in range(2):
            part = slice(c * column, (c + 1) * column)
            prompt_sum[c, n] = d[0, part] + d[1, part] + d[2, part] + d[3, part]
    greet(plane + owners[1:])
    swap = remote(prompt_sum.at[1 - core], prompt_in, ksend.at[0], krecv.at[0], (r, e ^ 1))
    swap.start()
    swap.wait()
    prompt_in[...] = prompt_in[...] + prompt_sum[core]
    head = key_gain.shape[1]
    key_gain_sum = jnp.zeros((1, head), F32)
    for i in range(4):
        for at, size, dk, dv in (
            (0, prompt, prompt_in[0, i * prompt : (i + 1) * prompt], prompt_in[1, i * prompt : (i + 1) * prompt]),
            (prompt, CMAX, d_keys[i, 2 * column :], d_values[i, 2 * column :]),
        ):
            t = slice(at, at + size)
            rows_i = slice(i * tok + at, i * tok + at + size)
            turned = dk * cos[i, t] + pltpu.roll(dk * sin[i, t], head // 2, 1)
            x = key_lin[rows_i, :]
            inverse = lax.rsqrt(jnp.mean(x * x, axis=-1, keepdims=True) + norm_eps)
            unit = x * inverse
            key_gain_sum = key_gain_sum + jnp.sum(turned * unit, axis=0, keepdims=True)
            weighted = turned * key_gain[...]
            mine[rows_i, qg : qg + kg] = (
                inverse * (weighted - unit * jnp.mean(weighted * unit, axis=-1, keepdims=True))
            ).astype(BF16)
            mine[rows_i, qg + kg :] = dv.astype(BF16)
    low, high = pl.ds(0, half), pl.ds(half, half)
    first_near = remote(mine.at[low], blocks.at[0, low], ssem.at[0], rsem.at[0], (near, e))
    first_far = remote(mine.at[high], blocks.at[1, high], ssem.at[1], rsem.at[1], (far, e))
    second_near = remote(mine.at[high], blocks.at[0, high], ssem.at[2], rsem.at[2], (near, e))
    second_far = remote(mine.at[low], blocks.at[1, low], ssem.at[3], rsem.at[3], (far, e))
    pass_far = remote(blocks.at[0, low], blocks.at[2, low], ssem.at[4], rsem.at[4], (far, e))
    pass_near = remote(blocks.at[1, high], blocks.at[2, high], ssem.at[5], rsem.at[5], (near, e))
    me = r * 2 + core
    firsts = []
    for i, (a, c) in enumerate(others):
        copy = remote(small.at[(r ^ a) * 2 + (core ^ c)], first_in.at[i], s1.at[i], r1.at[i], plane[i])
        copy.start()
        firsts.append(copy)
    for copy in (first_near, first_far, second_near, second_far):
        copy.start()
    wait_all(loads[0])
    out_begin()
    seconds, thirds = [], []

    def small_second():
        for copy in firsts:
            copy.wait()
        value = small[me]
        for i in range(7):
            value = value + first_in[i]
        piece[0] = value
        for j in range(3):
            copy = remote(piece.at[0], line_in.at[j], s2.at[j], r2.at[j], line_peers[j])
            copy.start()
            seconds.append(copy)

    def small_third():
        for copy in seconds:
            copy.wait()
        small_out[me] = piece[0] + line_in[0] + line_in[1] + line_in[2]
        for i in range(7):
            copy = remote(small_out.at[me], small_out.at[me], s3.at[i], r3.at[i], plane[i])
            copy.start()
            thirds.append(copy)

    def outer(p, src):
        def step(c, carry):
            n = aligned(c, 256)
            value = dot_nn(cols_t[...], src[:, n]).astype(BF16)
            for o in range(8):
                grads[o, p, :, n] = value[o * share : (o + 1) * share]
            return carry

        lax.fori_loop(0, (qg + 2 * kg) // 256, step, 0)

    def inner(p, src, start):
        def chunk(c, carry):
            n = aligned(c, 128)
            value = (
                dot_nt(src[:, :qg], wq[n, aligned(p, qg)])
                + dot_nt(src[:, qg : qg + kg], wk[n, aligned(p, kg)])
                + dot_nt(src[:, qg + kg :], wv[n, aligned(p, kg)])
            )
            if start:
                dsum[:, n] = value
            else:
                dsum[:, n] = dsum[:, n] + value
            return carry

        lax.fori_loop(0, width // 128, chunk, 0)

    def begin(i):
        units[i][0]()

    def first(i):
        units[i][1]()

    def onward(i, k):
        units[i][2](k)

    wait_all(loads[1])
    outer(r, mine)
    begin(0)
    out_first()
    small_second()
    for copies in loads[2:5]:
        wait_all(copies)
    inner(r, mine, True)
    first_near.wait()
    pass_far.start()
    first_far.wait()
    pass_near.start()
    out_inner(0)
    first(0)
    out_inner(1)
    small_third()
    onward(0, 0)
    second_near.wait()
    outer(near, blocks.at[0])
    begin(1)
    second_far.wait()
    outer(far, blocks.at[1])
    begin(2)
    out_inner(2)
    onward(0, 1)
    first(1)
    inner(near, blocks.at[0], False)
    onward(0, 2)
    onward(1, 0)
    first(2)
    inner(far, blocks.at[1], False)
    onward(1, 1)
    pass_far.wait()
    pass_near.wait()
    outer(diag, blocks.at[2])
    begin(3)
    inner(diag, blocks.at[2], False)
    back = []
    for i, p in enumerate(peers):
        dsend[i] = dsum[aligned(p, tok), :].astype(BF16)
        copy = remote(dsend.at[i], drecv.at[i], bsend.at[i], brecv.at[i], (p, e))
        copy.start()
        back.append(copy)
    wait_all(loads[5])
    scale = 1.0 / gain[:, aligned(r, width)]
    gain_v[...] = jnp.broadcast_to(
        jnp.sum(dsum[...] * cols[...].astype(F32), axis=0, keepdims=True) * scale, gain_v.shape
    )
    gain_v[1:2, :head] = key_gain_sum
    fourths = []
    for i in range(7):
        copy = remote(gain_v, gain_in.at[i], s4.at[i], r4.at[i], owners[i])
        copy.start()
        fourths.append(copy)
    onward(1, 2)
    onward(2, 0)
    first(3)
    onward(2, 1)
    for copy in fourths:
        copy.wait()
    value = gain_v[...]
    for i in range(7):
        value = value + gain_in[i]
    gain_out[r] = value
    fifths = []
    for i, p in enumerate(peers):
        copy = remote(gain_out.at[r], gain_out.at[r], s5.at[i], r5.at[i], (p, e))
        copy.start()
        fifths.append(copy)
    onward(3, 0)
    normal[:, aligned(r, width)] = dsum[aligned(r, tok), :]
    for i, p in enumerate(peers):
        back[i].wait()
        normal[:, aligned(p, width)] = drecv[i].astype(F32)
    onward(2, 2)
    onward(3, 1)
    out_last()

    def close(i):
        p = order[i]
        units[i][3]()
        q_out[:, aligned(p, qg)] = qkv_sum[p, :, :qg]
        k_out[:, aligned(p, kg)] = qkv_sum[p, :, qg : qg + kg]
        v_out[:, aligned(p, kg)] = qkv_sum[p, :, qg + kg :]

    close(0)
    close(1)
    onward(3, 2)
    close(2)
    close(3)
    for copy in fifths + thirds:
        copy.wait()


def grad_qkv_line(
    d_q, d_keys, d_values, key_lin, cos, sin, key_gain, wq, wk, wv, cols_t, cols, out_part, small, gain
):
    rows, head = key_lin.shape
    group = d_q.shape[1] + 2 * head
    tok = rows // 4
    width = wq.shape[0]
    piece = (width // 8, group)
    out_piece = out_part.shape[1:]
    small_piece = small.shape[1:]
    return pl.pallas_call(
        dgrad_line_kernel,
        out_shape=(
            jax.ShapeDtypeStruct((tok, 4 * width), F32),
            jax.ShapeDtypeStruct((width // 8, wq.shape[1]), F32),
            jax.ShapeDtypeStruct((width // 8, wk.shape[1]), F32),
            jax.ShapeDtypeStruct((width // 8, wv.shape[1]), F32),
            jax.ShapeDtypeStruct(out_piece, F32),
            jax.ShapeDtypeStruct(small.shape, F32),
            jax.ShapeDtypeStruct((4, 8, width), F32),
        ),
        in_specs=[VMEM_SPEC] * 7 + [ANY_SPEC] * 6 + [VMEM_SPEC] * 2,
        out_specs=(VMEM_SPEC,) * 7,
        scratch_shapes=[
            pltpu.VMEM((rows, group), BF16),
            pltpu.VMEM((2, 2, 4 * (tok - CMAX), head), F32),
            pltpu.VMEM((2, 4 * (tok - CMAX), head), F32),
            pltpu.SemaphoreType.DMA((1,)),
            pltpu.SemaphoreType.DMA((1,)),
        ]
        + [pltpu.VMEM(a.shape, BF16) for a in (wq, wk, wv, cols_t, cols, out_part)]
        + [
            pltpu.SemaphoreType.DMA((6,)),
            pltpu.VMEM((4, *piece), F32),
            pltpu.VMEM((8, 4, *piece), BF16),
            pltpu.VMEM((3, rows, group), BF16),
            pltpu.VMEM((rows, width), F32),
            pltpu.VMEM((3, tok, width), BF16),
            pltpu.VMEM((3, tok, width), BF16),
            pltpu.VMEM((4, *out_piece), BF16),
            pltpu.VMEM((3, *out_piece), BF16),
            pltpu.VMEM((2, 4, *out_piece), BF16),
            pltpu.VMEM((4, 4, *piece), BF16),
            pltpu.VMEM((4, 3, *piece), BF16),
            pltpu.VMEM((4, 2, 4, *piece), BF16),
            pltpu.VMEM((7, *small_piece), F32),
            pltpu.VMEM((1, *small_piece), F32),
            pltpu.VMEM((3, *small_piece), F32),
            pltpu.VMEM((8, width), F32),
            pltpu.VMEM((7, 8, width), F32),
            pltpu.SemaphoreType.DMA((6,)),
            pltpu.SemaphoreType.DMA((6,)),
        ]
        + [pltpu.SemaphoreType.DMA((n,)) for n in (3, 3, 7, 7, 3, 3, 7, 7, 7, 7, 3, 3)]
        + LINE_SEMS
        + [
            pltpu.SemaphoreType.DMA((4, 4)),
            pltpu.SemaphoreType.DMA((4, 4)),
            pltpu.SemaphoreType.DMA((4, 2, 4)),
            pltpu.SemaphoreType.DMA((4, 2, 4)),
        ],
        compiler_params=params(10),
        name="dqkv_line_exchange",
    )(
        d_q, d_keys, d_values, key_lin, cos, sin, key_gain, wq, wk, wv, cols_t, cols, out_part, small, gain
    )


def masks_of(block, own_length, slots, prompt_block, prompt_len, column, keys):
    slot = lax.broadcasted_iota(jnp.int32, (slots, keys), 0)
    key = lax.broadcasted_iota(jnp.int32, (slots, keys), 1)
    is_prompt = slot < prompt_block
    position = (column * 4 + block) * prompt_block + slot
    sees_prompt = (key < prompt_len) & (jnp.logical_not(is_prompt) | (key <= position))
    cont = key - prompt_len
    sees_cont = (
        (key >= prompt_len)
        & jnp.logical_not(is_prompt)
        & (cont <= slot - prompt_block)
        & (cont < own_length)
    )
    return sees_prompt | sees_cont


def attention_fwd_kernel(
    prompt_len, lengths, lin, gain, cos, sin, keys, values, queries, attn, q_all, score_all, low_all
):
    block = pl.program_id(0)
    slots = lin.shape[0]
    head = gain.shape[1]
    e = lax.axis_index("expert")
    own_length = lengths[block * lax.axis_size("expert") + e]
    allowed = masks_of(block, own_length, slots, slots - CMAX, prompt_len, e % 2, keys.shape[1])
    scale = head ** (-0.5)
    k, v = keys[0], values[0]
    c, s, g = cos[0], sin[0], gain[...]
    heads = lin.shape[1] // head
    parts = [slice(h * head, (h + 1) * head) for h in range(heads)]
    rows = [slice(h * slots, (h + 1) * slots) for h in range(heads)]
    for h in range(heads):
        x = lin[:, parts[h]]
        x = x * lax.rsqrt(jnp.mean(x * x, axis=-1, keepdims=True) + norm_eps) * g
        q = (x * c + pltpu.roll(x, head // 2, 1) * s).astype(BF16)
        queries[:, parts[h]] = q
        q_all[rows[h]] = q
    score_all[...] = dot_nt(q_all[...], k)
    for h in range(heads):
        score = jnp.where(allowed, score_all[rows[h]] * scale, -jnp.inf)
        peak = jnp.max(score, axis=-1, keepdims=True)
        exponent = jnp.exp(score - peak)
        low_all[rows[h]] = (exponent * (1.0 / jnp.sum(exponent, axis=-1, keepdims=True))).astype(BF16)
    out = dot_nn(low_all[...], v)
    for h in range(heads):
        attn[:, parts[h]] = out[rows[h]].astype(BF16)


def attention_fwd(lengths, lin, gain, cos, sin, keys, values, prompt_len):
    blocks, total_keys, head = keys.shape
    slots = lin.shape[0] // blocks
    width = lin.shape[1] - 2 * head
    row = pl.BlockSpec((slots, width), lambda i, *_: (i, 0))
    table = pl.BlockSpec((1, slots, head), lambda i, *_: (i, 0, 0))
    kv = pl.BlockSpec((1, total_keys, head), lambda i, *_: (i, 0, 0))
    one = pl.BlockSpec((1, head), lambda i, *_: (0, 0))
    return pl.pallas_call(
        functools.partial(attention_fwd_kernel, prompt_len),
        grid_spec=pltpu.PrefetchScalarGridSpec(
            num_scalar_prefetch=1,
            grid=(blocks,),
            in_specs=[row, one, table, table, kv, kv],
            out_specs=[row, row],
            scratch_shapes=[
                pltpu.VMEM((slots * width // head, head), BF16),
                pltpu.VMEM((slots * width // head, total_keys), F32),
                pltpu.VMEM((slots * width // head, total_keys), BF16),
            ],
        ),
        out_shape=(
            jax.ShapeDtypeStruct((lin.shape[0], width), BF16),
            jax.ShapeDtypeStruct((lin.shape[0], width), BF16),
        ),
        compiler_params=params(),
        name="attention_fwd",
    )(lengths, lin, gain, cos, sin, keys, values)


def attention_bwd_kernel(
    prompt_len, lengths, lin, queries, d_attn, gain, cos, sin, keys, values, attn_t, d_branch,
    d_lin, d_keys, d_values, d_gain, out_part,
    q_all, d_all, score_all, d_probs_all, low_all, d_score_all, d_q_all,
):
    block = pl.program_id(0)
    slots = lin.shape[0]
    head = gain.shape[1]
    e = lax.axis_index("expert")
    own_length = lengths[block * lax.axis_size("expert") + e]
    allowed = masks_of(block, own_length, slots, slots - CMAX, prompt_len, e % 2, keys.shape[1])
    scale = head ** (-0.5)
    k, v = keys[0], values[0]
    c, s, g = cos[0], sin[0], gain[...]
    heads = lin.shape[1] // head
    parts = [slice(h * head, (h + 1) * head) for h in range(heads)]
    rows = [slice(h * slots, (h + 1) * slots) for h in range(heads)]
    for h in range(heads):
        q_all[rows[h]] = queries[:, parts[h]]
        d_all[rows[h]] = d_attn[:, parts[h]]
    score_all[...] = dot_nt(q_all[...], k)
    d_probs_all[...] = dot_nt(d_all[...], v)
    for h in range(heads):
        score = jnp.where(allowed, score_all[rows[h]] * scale, -jnp.inf)
        peak = jnp.max(score, axis=-1, keepdims=True)
        exponent = jnp.exp(score - peak)
        probs = exponent * (1.0 / jnp.sum(exponent, axis=-1, keepdims=True))
        d_probs = d_probs_all[rows[h]]
        inner = jnp.sum(probs * d_probs, axis=-1, keepdims=True)
        low_all[rows[h]] = probs.astype(BF16)
        d_score_all[rows[h]] = (probs * (d_probs - inner)).astype(BF16)
    d_q_all[...] = dot_nn(d_score_all[...], k)
    d_keys[0] = dot_tn(d_score_all[...], q_all[...]) * scale
    d_values[0] = dot_tn(low_all[...], d_all[...])
    for n in range(2):
        half = slice(n * out_part.shape[1] // 2, (n + 1) * out_part.shape[1] // 2)
        out_part[:, half] = dot_nn(attn_t[...], d_branch[:, half]).astype(BF16)
    gain_total = jnp.zeros((8, head), F32)
    for h in range(heads):
        d_q = d_q_all[rows[h]] * scale
        turned = d_q * c + pltpu.roll(d_q * s, head // 2, 1)
        x = lin[:, parts[h]]
        inverse = lax.rsqrt(jnp.mean(x * x, axis=-1, keepdims=True) + norm_eps)
        unit = x * inverse
        pairs = turned * unit
        for j in range(slots // 8):
            gain_total = gain_total + pairs[j * 8 : (j + 1) * 8]
        weighted = turned * g
        d_lin[:, parts[h]] = (
            inverse * (weighted - unit * jnp.mean(weighted * unit, axis=-1, keepdims=True))
        ).astype(BF16)
    d_gain[0] = gain_total


def attention_bwd(
    lengths, lin, queries, d_attn, gain, cos, sin, keys, values, attn_t, d_branch, prompt_len
):
    blocks, total_keys, head = keys.shape
    slots = lin.shape[0] // blocks
    width = lin.shape[1] - 2 * head
    row = pl.BlockSpec((slots, width), lambda i, *_: (i, 0))
    table = pl.BlockSpec((1, slots, head), lambda i, *_: (i, 0, 0))
    kv = pl.BlockSpec((1, total_keys, head), lambda i, *_: (i, 0, 0))
    step = d_branch.shape[1] // blocks
    one = pl.BlockSpec((1, head), lambda i, *_: (0, 0))
    return pl.pallas_call(
        functools.partial(attention_bwd_kernel, prompt_len),
        grid_spec=pltpu.PrefetchScalarGridSpec(
            num_scalar_prefetch=1,
            grid=(blocks,),
            in_specs=[row, row, row, one, table, table, kv, kv]
            + [
                pl.BlockSpec(attn_t.shape, lambda i, *_: (0, 0)),
                pl.BlockSpec((d_branch.shape[0], step), lambda i, *_: (0, i)),
            ],
            out_specs=[
                row,
                kv,
                kv,
                pl.BlockSpec((1, 8, head), lambda i, *_: (i, 0, 0)),
                pl.BlockSpec((attn_t.shape[0], step), lambda i, *_: (0, i)),
            ],
            scratch_shapes=[
                pltpu.VMEM((slots * width // head, head), BF16),
                pltpu.VMEM((slots * width // head, head), BF16),
                pltpu.VMEM((slots * width // head, total_keys), F32),
                pltpu.VMEM((slots * width // head, total_keys), F32),
                pltpu.VMEM((slots * width // head, total_keys), BF16),
                pltpu.VMEM((slots * width // head, total_keys), BF16),
                pltpu.VMEM((slots * width // head, head), F32),
            ],
        ),
        out_shape=(
            jax.ShapeDtypeStruct((lin.shape[0], width), BF16),
            jax.ShapeDtypeStruct(keys.shape, F32),
            jax.ShapeDtypeStruct(values.shape, F32),
            jax.ShapeDtypeStruct((blocks, 8, head), F32),
            jax.ShapeDtypeStruct((attn_t.shape[0], d_branch.shape[1]), BF16),
        ),
        compiler_params=params(),
        name="attention_bwd",
    )(lengths, lin, queries, d_attn, gain, cos, sin, keys, values, attn_t, d_branch)


def partner(shard, axis, bit):
    return lax.ppermute(shard, axis, [(i, i ^ 1 << bit) for i in range(lax.axis_size(axis))])


def root_mean_scale(value_rows, gain_vec):
    return (
        value_rows
        * lax.rsqrt(jnp.mean(value_rows * value_rows, axis=-1, keepdims=True) + norm_eps)
        * gain_vec
    )


def contract(left_side, right_side, left_dim, right_dim):
    return lax.dot_general(
        left_side,
        right_side,
        (((left_dim,), (right_dim,)), ((), ())),
        preferred_element_type=F32,
    )


def plane_order(z):
    upper, odd = z // 2, z % 2
    return [z, z + 1 - 2 * upper, 2 + upper - 2 * odd, 3 - 3 * upper]


def world(with_diag):
    r, e = lax.axis_index("dp"), lax.axis_index("expert")
    z, core = e // 2, e % 2
    near, far = r ^ 1, r ^ 2
    devices = [(near, e), (far, e), (r, e ^ 1)]
    devices += [(r, lax.rem(z + j, 4) * 2 + core) for j in (1, 2, 3)]
    return r, e, z, core, near, far, devices


def everyone():
    me = lax.axis_index("dp") * 8 + lax.axis_index("expert")
    return me, [lax.rem(me + j, 32) for j in range(1, 32)]


def scatter_rows(rows, rows_in, ss, rs):
    me, others = everyone()
    copies = start_all(
        [
            remote(rows.at[d], rows_in.at[me], ss.at[j], rs.at[j], (d // 8, lax.rem(d, 8)))
            for j, d in enumerate(others)
        ]
    )
    rows_in[me] = rows[me]
    return copies


def greet_everyone():
    greet([(d // 8, lax.rem(d, 8)) for d in everyone()[1]])


ROW_SEMS = [pltpu.SemaphoreType.DMA((31,)), pltpu.SemaphoreType.DMA((31,))]


def gather_world(mine, buf, zs, zr, ps, pr, ds, dr, before, group, done, greeting=None):
    r, e, z, core, near, far, greeted = world(True)
    half = mine.shape[0] // 2
    low, high = pl.ds(0, half), pl.ds(half, half)
    order = plane_order(z)
    if greeting is None:
        greet(greeted)
    else:
        greeting()

    def slot(q, b, c):
        return q * 8 + b * 2 + c

    buf[slot(r, z, core)] = mine[...]
    diag = r ^ 3
    plane, pairs, lines = {}, {}, []

    def hand(k, i, q):
        at = slot(q, order[k], core)
        copy = remote(buf.at[at], buf.at[at], ds.at[k, i], dr.at[k, i], (r, e ^ 1))
        copy.start()
        pairs[k, i] = copy

    def issue(k):
        b = order[k]
        at = slot(r, b, core)
        for side, cond, to in (
            (0, (b <= z) & (z < 3), jnp.minimum(z + 1, 3)),
            (1, (b >= z) & (z > 0), jnp.maximum(z - 1, 0)),
        ):
            copy = remote(buf.at[at], buf.at[at], zs.at[k, side], zr.at[b], (r, to * 2 + core))
            lines.append((cond, copy))

            @pl.when(cond)
            def _():
                copy.start()

        mine_at, near_at, far_at = at, slot(near, b, core), slot(far, b, core)
        for i, (src, part, p) in enumerate(
            (
                (mine_at, low, near),
                (mine_at, high, far),
                (mine_at, high, near),
                (mine_at, low, far),
                (near_at, low, far),
                (far_at, high, near),
            )
        ):
            plane[k, i] = remote(
                buf.at[src, part], buf.at[src, part], ps.at[k, i], pr.at[k, i], (p, e)
            )
        for i in range(4):
            plane[k, i].start()
        hand(k, 0, r)

    def line_wait(k):
        b = order[k]
        at = slot(r, b, core)
        remote(buf.at[at], buf.at[at], zs.at[k, 0], zr.at[b], (r, e ^ 1)).wait_recv()
        issue(k)

    def passes(k):
        plane[k, 0].wait_recv()
        plane[k, 4].start()
        plane[k, 1].wait_recv()
        plane[k, 5].start()

    def finish(k):
        plane[k, 2].wait_recv()
        hand(k, 1, near)
        plane[k, 3].wait_recv()
        hand(k, 2, far)

    def corner(k):
        plane[k, 4].wait_recv()
        plane[k, 5].wait_recv()
        hand(k, 3, diag)

    who = (r, near, far, diag)

    def ready(k):
        before(k)
        for i in range(4):
            pairs[k, i].wait_recv()
        group(k, [(k * 4 + i, who[i] * 8 + order[k] * 2) for i in range(4)])

    issue(0)
    passes(0)
    line_wait(1)
    finish(0)
    passes(1)
    line_wait(2)
    corner(0)
    finish(1)
    ready(0)
    passes(2)
    line_wait(3)
    corner(1)
    finish(2)
    ready(1)
    passes(3)
    corner(2)
    finish(3)
    ready(2)
    corner(3)
    ready(3)
    done()
    for copy in plane.values():
        copy.wait_send()
    for copy in pairs.values():
        copy.wait_send()
    for cond, copy in lines:

        @pl.when(cond)
        def _():
            copy.wait_send()


def group_rows(k, room):
    return pl.ds(k * 4 * room, 4 * room)


GATHER_SEMS = [
    pltpu.SemaphoreType.DMA((4, 2)),
    pltpu.SemaphoreType.DMA((4,)),
    pltpu.SemaphoreType.DMA((4, 6)),
    pltpu.SemaphoreType.DMA((4, 6)),
    pltpu.SemaphoreType.DMA((4, 4)),
    pltpu.SemaphoreType.DMA((4, 4)),
]


def selector(row, room):
    ids = lax.broadcasted_iota(jnp.int32, (room, row.shape[1]), 0).astype(F32)
    return jnp.where(ids == row, 1.0, 0.0).astype(BF16)


def experts_fwd_kernel(
    capacity, mine, gate_rows, wg, wu, wd, pos, x_out, y_out, g_out, u_out, o_out, hid_out, gate_out,
    buf, wg_v, wu_v, wd_v, x_v, y_v, g_v, u_v, o_v, hid_v, gate_v, gate_in, local, rs, rr, *sems,
):
    model = wg.shape[0]
    rows_in = mine.shape[0]
    room = x_v.shape[0] // 4
    loads = start_all(
        [
            pltpu.make_async_copy(a, b, local.at[0, i])
            for i, (a, b) in enumerate(((wg, wg_v), (wu, wu_v), (wd, wd_v)))
        ]
    )
    leaving = {g: [] for g in range(4)}
    scattered = []

    def greeting():
        greet_everyone()
        scattered.extend(scatter_rows(gate_rows, gate_in, rs, rr))

    def leave(g, pairs):
        kept = group_rows(g, room)
        leaving[g].extend(
            start_all(
                [
                    pltpu.make_async_copy(v, o.at[kept], local.at[g % 2, i])
                    for i, v, o in pairs
                ]
            )
        )

    def before(g):
        wait_all(loads)
        wait_all(scattered)
        if g > 0:
            wait_all(leaving[g - 1])

    upto = jnp.where(
        lax.broadcasted_iota(jnp.int32, (rows_in, rows_in), 0)
        <= lax.broadcasted_iota(jnp.int32, (rows_in, rows_in), 1),
        1.0,
        0.0,
    ).astype(BF16)
    line = lax.broadcasted_iota(jnp.int32, (16, rows_in), 0)

    def pick(at, s, start):
        rows = pl.ds(start, room)
        sels = []
        gate = jnp.zeros((room, 1), F32)
        for c in range(2):
            row = jnp.broadcast_to(gate_in[s + c], (16, rows_in))
            named = jnp.where(row > 0.0, 1.0, 0.0)
            place = (dot_nn(named.astype(BF16), upto) + (c * capacity)) * named - 1.0
            pos[at * 2 + c] = place[:1]
            sels.append(selector(place[:1], room))
            top = row.astype(BF16).astype(F32)
            parts = jnp.where(line == 0, top, jnp.where(line == 1, row - top, 0.0)).astype(BF16)
            gate = gate + jnp.sum(dot_nt(sels[c], parts), axis=-1, keepdims=True)
        for c in range(4):
            n = slice(c * model // 4, (c + 1) * model // 4)
            x_v[rows, n] = (dot_nn(sels[0], buf[s, :, n]) + dot_nn(sels[1], buf[s + 1, :, n])).astype(BF16)
        gate_v[rows, :] = jnp.broadcast_to(gate, (room, 128))

    def group(g, blocks):
        for j, (at, s) in enumerate(blocks):
            pick(at, s, j * room)
        leave(g, ((0, x_v, x_out), (1, gate_v, gate_out)))

        def first(c, carry):
            n = aligned(c, 256)
            x = x_v[...]
            gates = dot_nn(x, wg_v[:, n])
            u = dot_nn(x, wu_v[:, n])
            g_v[:, n] = gates.astype(BF16)
            u_v[:, n] = u.astype(BF16)
            hid_v[:, n] = (gates / (1.0 + jnp.exp(-gates)) * u).astype(BF16)
            return carry

        lax.fori_loop(0, wg.shape[1] // 256, first, 0)
        leave(g, ((2, g_v, g_out), (3, u_v, u_out), (4, hid_v, hid_out)))

        def second(c, carry):
            n = aligned(c, 256)
            o = dot_nn(hid_v[...], wd_v[:, n]).astype(BF16)
            o_v[:, n] = o
            y_v[:, n] = (o.astype(F32) * gate_v[:, :1]).astype(BF16)
            return carry

        lax.fori_loop(0, model // 256, second, 0)
        leave(g, ((5, o_v, o_out), (6, y_v, y_out)))

    def done():
        for copies in leaving.values():
            wait_all(copies)

    gather_world(mine, buf, *sems, before, group, done, greeting)


def experts_fwd(mine, gate_rows, wg, wu, wd, capacity, room):
    rows, width = mine.shape
    model, ff = wg.shape
    group = 4 * room
    wide = jax.ShapeDtypeStruct((16 * room, model), BF16)
    thin = jax.ShapeDtypeStruct((16 * room, ff), BF16)
    pos, x, y, g, u, o, hidden, gates = pl.pallas_call(
        functools.partial(experts_fwd_kernel, capacity),
        out_shape=(
            jax.ShapeDtypeStruct((32, 1, rows), F32),
            wide,
            wide,
            thin,
            thin,
            wide,
            thin,
            jax.ShapeDtypeStruct((16 * room, 128), F32),
        ),
        in_specs=[VMEM_SPEC, VMEM_SPEC, ANY_SPEC, ANY_SPEC, ANY_SPEC],
        out_specs=(VMEM_SPEC,) + (ANY_SPEC,) * 7,
        scratch_shapes=[
            pltpu.VMEM((32, rows, width), BF16),
            pltpu.VMEM((model, ff), BF16),
            pltpu.VMEM((model, ff), BF16),
            pltpu.VMEM((ff, model), BF16),
            pltpu.VMEM((group, model), BF16),
            pltpu.VMEM((group, model), BF16),
            pltpu.VMEM((group, ff), BF16),
            pltpu.VMEM((group, ff), BF16),
            pltpu.VMEM((group, model), BF16),
            pltpu.VMEM((group, ff), BF16),
            pltpu.VMEM((group, 128), F32),
            pltpu.VMEM((32, 1, rows), F32),
            pltpu.SemaphoreType.DMA((2, 7)),
        ]
        + ROW_SEMS
        + GATHER_SEMS,
        compiler_params=params(6),
        name="experts_fwd",
    )(mine, gate_rows, wg, wu, wd)
    return pos, x, y, (g, u, o, hidden, gates)


def experts_bwd_kernel(
    mine, pos, g_in, u_in, o_in, gate_in, wg, wu, wd, d_gates, y_out, d_copy_out, dg_out, du_out,
    buf, wg_v, wu_v, wd_v, g_v, u_v, o_v, gate_v, y_v, d_copy_v, dg_v, du_v,
    local, ins, *sems,
):
    model, ff = wg.shape
    room = d_copy_v.shape[0] // 4
    loads = start_all(
        [
            pltpu.make_async_copy(a, b, local.at[0, i])
            for i, (a, b) in enumerate(((wg, wg_v), (wu, wu_v), (wd, wd_v)))
        ]
    )
    leaving, coming = {g: [] for g in range(4)}, {}

    def fetch(g):
        kept = group_rows(g, room)
        coming[g] = start_all(
            [
                pltpu.make_async_copy(a.at[kept], v.at[g % 2], ins.at[g % 2, i])
                for i, (a, v) in enumerate(
                    ((g_in, g_v), (u_in, u_v), (o_in, o_v), (gate_in, gate_v))
                )
            ]
        )

    fetch(0)

    def leave(g, pairs):
        kept = group_rows(g, room)
        leaving[g].extend(
            start_all(
                [
                    pltpu.make_async_copy(v, o.at[kept], local.at[g % 2, i])
                    for i, v, o in pairs
                ]
            )
        )

    def before(g):
        wait_all(loads)
        wait_all(coming[g])
        if g + 1 < 4:
            fetch(g + 1)
        if g > 0:
            wait_all(leaving[g - 1])

    def pick(slot, at, s, start):
        rows = pl.ds(start, room)
        sels = [selector(pos[at * 2 + c], room) for c in range(2)]
        gate = gate_v[slot, rows, :1]
        inner = jnp.zeros((room, 1), F32)
        for c in range(4):
            n = slice(c * model // 4, (c + 1) * model // 4)
            picked = dot_nn(sels[0], buf[s, :, n]) + dot_nn(sels[1], buf[s + 1, :, n])
            d_copy_v[rows, n] = (gate * picked).astype(BF16)
            inner = inner + jnp.sum(picked * o_v[slot, rows, n].astype(F32), axis=-1, keepdims=True)
        top = inner.astype(BF16).astype(F32)
        rest = inner - top
        lane = lax.broadcasted_iota(jnp.int32, (room, 128), 1)
        parts = jnp.where(lane == 0, top, jnp.where(lane == 1, rest, 0.0)).astype(BF16)
        for c in range(2):
            both = dot_tn(parts, sels[c])
            d_gates[s + c] = both[:1] + both[1:2]

    def group(g, blocks):
        slot = g % 2
        for j, (at, s) in enumerate(blocks):
            pick(slot, at, s, j * room)
        leave(g, ((0, d_copy_v, d_copy_out),))

        def third(c, carry):
            n = aligned(c, 256)
            d_hidden = dot_nt(d_copy_v[...], wd_v[n, :])
            gates, u = g_v[slot, :, n].astype(F32), u_v[slot, :, n].astype(F32)
            s = 1.0 / (1.0 + jnp.exp(-gates))
            dg_v[:, n] = (d_hidden * u * s * (1.0 + gates * (1.0 - s))).astype(BF16)
            du_v[:, n] = (d_hidden * gates * s).astype(BF16)
            return carry

        lax.fori_loop(0, ff // 256, third, 0)
        leave(g, ((1, dg_v, dg_out), (2, du_v, du_out)))

        def fourth(c, carry):
            n = aligned(c, 256)
            y_v[:, n] = (
                dot_nt(dg_v[...], wg_v[n, :]) + dot_nt(du_v[...], wu_v[n, :])
            ).astype(BF16)
            return carry

        lax.fori_loop(0, model // 256, fourth, 0)
        leave(g, ((3, y_v, y_out),))

    def done():
        for copies in leaving.values():
            wait_all(copies)

    gather_world(mine, buf, *sems, before, group, done)


def experts_bwd(mine, pos, kept, wg, wu, wd, room):
    rows, width = mine.shape
    model, ff = wg.shape
    group = 4 * room
    return pl.pallas_call(
        experts_bwd_kernel,
        out_shape=(
            jax.ShapeDtypeStruct((32, 1, rows), F32),
            jax.ShapeDtypeStruct((16 * room, model), BF16),
            jax.ShapeDtypeStruct((16 * room, model), BF16),
            jax.ShapeDtypeStruct((16 * room, ff), BF16),
            jax.ShapeDtypeStruct((16 * room, ff), BF16),
        ),
        in_specs=[VMEM_SPEC, VMEM_SPEC] + [ANY_SPEC] * 7,
        out_specs=(VMEM_SPEC,) + (ANY_SPEC,) * 4,
        scratch_shapes=[
            pltpu.VMEM((32, rows, width), BF16),
            pltpu.VMEM((model, ff), BF16),
            pltpu.VMEM((model, ff), BF16),
            pltpu.VMEM((ff, model), BF16),
            pltpu.VMEM((2, group, ff), BF16),
            pltpu.VMEM((2, group, ff), BF16),
            pltpu.VMEM((2, group, model), BF16),
            pltpu.VMEM((2, group, 128), F32),
            pltpu.VMEM((group, model), BF16),
            pltpu.VMEM((group, model), BF16),
            pltpu.VMEM((group, ff), BF16),
            pltpu.VMEM((group, ff), BF16),
            pltpu.SemaphoreType.DMA((2, 4)),
            pltpu.SemaphoreType.DMA((2, 4)),
        ]
        + GATHER_SEMS,
        compiler_params=params(7),
        name="experts_bwd",
    )(mine, pos, *kept, wg, wu, wd)


def sum_world_kernel(with_rows, *refs):
    if with_rows:
        y_in, pos, rows_given, out, rows_out, *refs, rs, rr = refs
    else:
        y_in, pos, out, *refs = refs
    (
        y, local, psend, pair, half_near, half_far, full_near, full_far, lines,
        ds, dr, hs, hr, fs, fr, zs, zr,
    ) = refs
    r, e, z, core, near, far, greeted = world(True)
    rows, width = out.shape
    room = y.shape[1]
    half = rows // 2
    low, high = pl.ds(0, half), pl.ds(half, half)
    order = plane_order(z)[::-1]
    body_width = width // 512 * 512
    loads = loading(
        [(y_in.at[pl.ds(12 - 4 * k, 4)], y.at[pl.ds(12 - 4 * k, 4)]) for k in range(4)], local
    )
    if with_rows:
        greet_everyone()
        scattering = scatter_rows(rows_given, rows_out, rs, rr)
    else:
        greet(greeted)

    def for_columns(fn):
        def step(c, carry):
            fn(aligned(c, 512))
            return carry

        lax.fori_loop(0, body_width // 512, step, 0)
        if width > body_width:
            fn(pl.ds(body_width, width - body_width))

    def scattered(sel, k, i, n):
        return dot_tn(sel, y[(3 - k) * 4 + i, :, n])

    def select(k, i, c):
        return selector(pos[((3 - k) * 4 + i) * 2 + c], room)

    pairs, halves, fulls, moves = {}, {}, {}, []

    def stage_a(k):
        wait_all(loads[k])
        for i in (3, 1, 2, 0):
            at = k * 4 + i
            sel = select(k, i, 1 - core)

            def fill(n):
                psend[at, :, n] = scattered(sel, k, i, n).astype(BF16)

            for_columns(fill)
            copy = remote(psend.at[at], pair.at[at], ds.at[at], dr.at[at], (r, e ^ 1))
            copy.start()
            pairs[at] = copy
        for i in (3, 1, 2, 0):
            at = k * 4 + i
            sel = select(k, i, core)
            pairs[at].wait_recv()

            def add(n):
                value = scattered(sel, k, i, n) + pair[at, :, n].astype(F32)
                pair[at, :, n] = value.astype(BF16)

            for_columns(add)
            if i == 3:
                for side, (part, dst, p) in enumerate(
                    ((low, half_near, near), (high, half_far, far))
                ):
                    copy = remote(
                        pair.at[at, part], dst.at[k], hs.at[k, side], hr.at[k, side], (p, e)
                    )
                    copy.start()
                    halves[k, side] = copy

    def stage_b(k):
        for side, (i, part, src, dst, p) in enumerate(
            (
                (2, low, half_near, full_far, far),
                (1, high, half_far, full_near, near),
            )
        ):
            at = k * 4 + i
            halves[k, side].wait_recv()

            def add(n):
                value = pair[at, part, n].astype(F32) + src[k, :, n].astype(F32)
                pair[at, part, n] = value.astype(BF16)

            for_columns(add)
            copy = remote(pair.at[at], dst.at[k], fs.at[k, side], fr.at[k, side], (p, e))
            copy.start()
            fulls[k, side] = copy

    def stage_c(k):
        b = order[k]
        at = k * 4
        fulls[k, 0].wait_recv()
        fulls[k, 1].wait_recv()

        def add(n):
            out[:, n] = (
                pair[at, :, n].astype(F32)
                + full_near[k, :, n].astype(F32)
                + full_far[k, :, n].astype(F32)
            )

        for_columns(add)
        for side, cond in ((0, (b >= z) & (z > 0)), (1, (b <= z) & (z < 3))):

            @pl.when(cond)
            def _():
                remote(
                    lines.at[side, b], lines.at[side, b], zs.at[side, k], zr.at[side, b], (r, e ^ 1)
                ).wait_recv()

                def more(n):
                    out[:, n] = out[:, n] + lines[side, b, :, n].astype(F32)

                for_columns(more)

        if k < 3:

            def keep(n):
                pair[at, :, n] = out[:, n].astype(BF16)

            for_columns(keep)
            for side, cond, to in (
                (0, b > z, jnp.minimum(z + 1, 3)),
                (1, b < z, jnp.maximum(z - 1, 0)),
            ):
                copy = remote(
                    pair.at[at], lines.at[side, b], zs.at[side, k], zr.at[side, b], (r, to * 2 + core)
                )
                moves.append((cond, copy))

                @pl.when(cond)
                def _():
                    copy.start()

    stage_a(0)
    stage_a(1)
    stage_b(0)
    stage_a(2)
    stage_b(1)
    stage_c(0)
    stage_a(3)
    stage_b(2)
    stage_c(1)
    stage_b(3)
    stage_c(2)
    stage_c(3)
    for copies in (pairs, halves, fulls):
        for copy in copies.values():
            copy.wait_send()
    for cond, copy in moves:

        @pl.when(cond)
        def _():
            copy.wait_send()

    if with_rows:
        wait_all(scattering)


def sum_world(y, pos, rows, collective_id, given=None):
    width = y.shape[-1]

    def blocks(n, size):
        return pltpu.VMEM((n, size, width), BF16)

    extra = () if given is None else (given,)
    return pl.pallas_call(
        functools.partial(sum_world_kernel, len(extra) > 0),
        out_shape=(jax.ShapeDtypeStruct((rows, width), F32),)
        + tuple(jax.ShapeDtypeStruct(a.shape, F32) for a in extra),
        in_specs=[ANY_SPEC, VMEM_SPEC] + [VMEM_SPEC] * len(extra),
        out_specs=(VMEM_SPEC,) * (1 + len(extra)),
        scratch_shapes=[
            pltpu.VMEM(y.shape, BF16),
            pltpu.SemaphoreType.DMA((4,)),
            blocks(16, rows),
            blocks(16, rows),
            blocks(4, rows // 2),
            blocks(4, rows // 2),
            blocks(4, rows),
            blocks(4, rows),
            pltpu.VMEM((2, 4, rows, width), BF16),
            pltpu.SemaphoreType.DMA((16,)),
            pltpu.SemaphoreType.DMA((16,)),
            pltpu.SemaphoreType.DMA((4, 2)),
            pltpu.SemaphoreType.DMA((4, 2)),
            pltpu.SemaphoreType.DMA((4, 2)),
            pltpu.SemaphoreType.DMA((4, 2)),
            pltpu.SemaphoreType.DMA((2, 4)),
            pltpu.SemaphoreType.DMA((2, 4)),
        ]
        + (ROW_SEMS if extra else []),
        compiler_params=params(collective_id),
        name="sum_world",
    )(y, pos, *extra)


def expert_grads_kernel(x, d_gate, d_up, hidden, d_copy, gate_grad, up_grad, down_grad, hidden_t):
    @pl.when(pl.program_id(0) == 0)
    def _():
        hidden_t[...] = hidden[...].T

    rows = x[...].T
    gate_grad[...] = dot_nn(rows, d_gate[...])
    up_grad[...] = dot_nn(rows, d_up[...])
    down_grad[...] = dot_nn(hidden_t[...], d_copy[...])


def expert_grads(x, d_gate, d_up, hidden, d_copy):
    slots, model = x.shape
    ff = hidden.shape[1]
    step = 256
    whole = pl.BlockSpec((slots, ff), lambda i: (0, 0))
    columns = pl.BlockSpec((slots, step), lambda i: (0, i))
    return pl.pallas_call(
        expert_grads_kernel,
        grid=(model // step,),
        in_specs=[columns, whole, whole, whole, columns],
        out_specs=[
            pl.BlockSpec((step, ff), lambda i: (i, 0)),
            pl.BlockSpec((step, ff), lambda i: (i, 0)),
            pl.BlockSpec((ff, step), lambda i: (0, i)),
        ],
        out_shape=(
            jax.ShapeDtypeStruct((model, ff), F32),
            jax.ShapeDtypeStruct((model, ff), F32),
            jax.ShapeDtypeStruct((ff, model), F32),
        ),
        scratch_shapes=[pltpu.VMEM((ff, slots), BF16)],
        compiler_params=params(),
        name="expert_grads",
    )(x, d_gate, d_up, hidden, d_copy)


def experts_by_all_to_all(
    mixed, state, teacher, routes, valid_slot, valid_count, router_weight, gate_weight, up_weight, down_weight,
    devices, capacity, slots_all,
):
    tok_dev, model_width = mixed.shape
    top_count = routes.shape[1]
    ffn_width = gate_weight.shape[2]
    logits = jnp.dot(mixed, router_weight, preferred_element_type=jnp.float32)
    gates = jax.nn.softmax(jnp.take_along_axis(logits, routes, axis=1), axis=-1)
    rows_total = tok_dev * top_count
    expert_ids = routes.reshape(rows_total)
    live_rows = jnp.repeat(valid_slot, top_count)
    expert_range = jnp.arange(devices, dtype=jnp.int32)
    hit_table = ((expert_ids[:, None] == expert_range[None, :]) & live_rows[:, None]).astype(
        jnp.int32
    )
    earlier = jnp.cumsum(hit_table, axis=0) - hit_table
    position_in = jnp.sum(earlier * hit_table, axis=1)
    slot_index = jnp.where(live_rows, expert_ids * capacity + position_in, devices * capacity)
    row_of_slot = (
        jnp.full((devices * capacity + 1,), rows_total, jnp.int32)
        .at[slot_index]
        .set(jnp.arange(rows_total, dtype=jnp.int32))[: devices * capacity]
    )
    token_of_slot = jnp.where(row_of_slot < rows_total, row_of_slot // top_count, tok_dev)
    mixed_pad = jnp.concatenate([mixed, jnp.zeros((1, model_width), jnp.bfloat16)], axis=0)
    send_rows = mixed_pad[token_of_slot].reshape(devices, capacity, model_width)
    arrived = lax.all_to_all(send_rows, ("dp", "expert"), split_axis=0, concat_axis=0, tiled=True)
    sources = arrived.shape[0]
    items = arrived.shape[1]
    flat_in = arrived.reshape(sources * items, model_width)
    gate_pre = jnp.dot(flat_in, gate_weight[0], preferred_element_type=jnp.float32)
    up_pre = jnp.dot(flat_in, up_weight[0], preferred_element_type=jnp.float32)
    hidden_units = (jax.nn.silu(gate_pre) * up_pre).astype(jnp.bfloat16)
    produced = jnp.dot(hidden_units, down_weight[0], preferred_element_type=jnp.float32).astype(
        jnp.bfloat16
    )
    produced, gate_pre, up_pre, hidden_units, arrived = (
        produced.reshape(sources, items, model_width),
        gate_pre.reshape(sources, items, ffn_width),
        up_pre.reshape(sources, items, ffn_width),
        hidden_units.reshape(sources, items, ffn_width),
        arrived,
    )
    returned = lax.all_to_all(produced, ("dp", "expert"), split_axis=0, concat_axis=0, tiled=True)
    returned_pad = jnp.concatenate(
        [
            returned.reshape(devices * capacity, model_width),
            jnp.zeros((1, model_width), jnp.bfloat16),
        ],
        axis=0,
    )
    copies = returned_pad[slot_index].reshape(tok_dev, top_count, model_width)
    layer_out = state + jnp.sum(gates[:, :, None] * copies, axis=1)
    live_tokens = valid_slot.astype(jnp.float32)[:, None]
    diff = (layer_out - teacher.astype(jnp.float32)) * live_tokens
    local_square = jnp.sum(diff * diff)
    d_out = 2.0 * slots_all * diff / valid_count
    d_gates = jnp.sum(d_out[:, None, :] * copies, axis=-1)
    d_chosen = gates * (d_gates - jnp.sum(gates * d_gates, axis=-1, keepdims=True))
    d_logits = jnp.sum(
        jnp.where(routes[:, :, None] == expert_range[None, None, :], d_chosen[:, :, None], 0.0),
        axis=1,
    ).astype(jnp.bfloat16)
    d_copies = (
        (gates[:, :, None] * d_out[:, None, :])
        .astype(jnp.bfloat16)
        .reshape(rows_total, model_width)
    )
    d_copies_pad = jnp.concatenate([d_copies, jnp.zeros((1, model_width), jnp.bfloat16)], axis=0)
    d_send = d_copies_pad[row_of_slot].reshape(devices, capacity, model_width)
    d_arrived = lax.all_to_all(d_send, ("dp", "expert"), split_axis=0, concat_axis=0, tiled=True)
    flat_d = d_arrived.reshape(-1, model_width)
    flat_in = arrived.reshape(-1, model_width)
    flat_gate = gate_pre.reshape(-1, ffn_width)
    flat_up = up_pre.reshape(-1, ffn_width)
    flat_hidden = hidden_units.reshape(-1, ffn_width)
    d_hidden = contract(flat_d, down_weight[0], 1, 1)
    sigmoid_gate = jax.nn.sigmoid(flat_gate)
    d_gate = (d_hidden * flat_up * sigmoid_gate * (1.0 + flat_gate * (1.0 - sigmoid_gate))).astype(
        jnp.bfloat16
    )
    d_up = (d_hidden * flat_gate * sigmoid_gate).astype(jnp.bfloat16)
    down_grad = contract(flat_hidden, flat_d, 0, 0)[None]
    gate_grad = contract(flat_in, d_gate, 0, 0)[None]
    up_grad = contract(flat_in, d_up, 0, 0)[None]
    d_in = (contract(d_gate, gate_weight[0], 1, 1) + contract(d_up, up_weight[0], 1, 1)).astype(
        jnp.bfloat16
    )
    d_returned = lax.all_to_all(
        d_in.reshape(devices, capacity, model_width),
        ("dp", "expert"),
        split_axis=0,
        concat_axis=0,
        tiled=True,
    )
    d_returned_pad = jnp.concatenate(
        [
            d_returned.reshape(devices * capacity, model_width),
            jnp.zeros((1, model_width), jnp.bfloat16),
        ],
        axis=0,
    )
    d_mixed = jnp.sum(
        d_returned_pad[slot_index].reshape(tok_dev, top_count, model_width),
        axis=1,
        dtype=jnp.float32,
    )
    d_mixed = d_mixed + contract(d_logits, router_weight, 1, 1)
    router_local = contract(d_logits, mixed, 0, 0)
    return layer_out, d_out, d_mixed, local_square, router_local, gate_grad, up_grad, down_grad


def experts_by_gather(
    mixed, state, teacher, routes, valid_slot, valid_count, router_weight,
    gate_weight, up_weight, down_weight, devices, capacity, slots_all,
):
    tok_dev, model_width = mixed.shape
    room = -(-2 * capacity // 16) * 16
    expert_range = jnp.arange(devices, dtype=jnp.int32)
    logits = jnp.dot(mixed, router_weight, preferred_element_type=F32)
    chosen = jnp.any(routes[:, :, None] == expert_range[None, None], axis=1)
    gates = jax.nn.softmax(jnp.where(chosen, logits, -jnp.inf), axis=-1)
    live_gates = jnp.where(valid_slot[:, None], gates, 0.0)
    gate_rows = live_gates.T[:, None]
    pos, x_rows, y_rows, kept = experts_fwd(
        mixed, gate_rows, gate_weight[0], up_weight[0], down_weight[0], capacity, room
    )
    layer_out = state + sum_world(y_rows.reshape(16, room, model_width), pos, tok_dev, 8)[0]
    live_tokens = valid_slot.astype(F32)[:, None]
    diff = (layer_out - teacher.astype(F32)) * live_tokens
    local_square = jnp.sum(diff * diff)
    d_out = 2.0 * slots_all * diff / valid_count
    hidden = kept[3]
    d_gates, d_rows, d_copy, d_gate, d_up = experts_bwd(
        d_out.astype(BF16), pos, kept[:3] + kept[4:], gate_weight[0], up_weight[0], down_weight[0], room
    )
    back, d_gates = sum_world(d_rows.reshape(16, room, model_width), pos, tok_dev, 9, d_gates)
    d_gates = d_gates[:, 0].T

    gate_grad, up_grad, down_grad = (
        grad[None] for grad in expert_grads(x_rows, d_gate, d_up, hidden, d_copy)
    )
    d_logits = (gates * (d_gates - jnp.sum(gates * d_gates, axis=-1, keepdims=True))).astype(BF16)
    d_mixed = back + contract(d_logits, router_weight, 1, 1)
    router_local = contract(d_logits, mixed, 0, 0)
    return layer_out, d_out, d_mixed, local_square, router_local, gate_grad, up_grad, down_grad


def head_rope(linear, gain_vec, cos, sin):
    value = root_mean_scale(linear, gain_vec)
    half = value.shape[-1] // 2
    return value * cos + jnp.roll(value, half, axis=-1) * sin


def body(
    tokens,
    teacher,
    routes,
    cont_lengths,
    query_weight,
    key_projection,
    value_projection,
    output_weight,
    router_weight,
    gate_weight,
    up_weight,
    down_weight,
    input_gain,
    post_gain,
    query_gain,
    key_gain,
):
    n_dp = lax.axis_size("dp")
    n_owner = lax.axis_size("expert")
    devices = n_dp * n_owner
    rank_dp = lax.axis_index("dp")
    rank_owner = lax.axis_index("expert")
    flat_rank = rank_dp * n_owner + rank_owner
    column = rank_owner % 2
    first_column = column == 0
    tok_dev, model_width = tokens.shape
    top_count = routes.shape[1]
    head_dim = query_gain.shape[0]
    kv_width = key_projection.shape[1]
    query_width = query_weight.shape[1]
    query_group = query_width // n_dp
    assert n_dp == 4 and kv_width == n_dp * head_dim
    prompt_block = tok_dev - CMAX
    half_prompt = n_dp * prompt_block
    prompt_len = 2 * half_prompt
    capacity = max(2, tok_dev * top_count * 5 // (4 * devices))
    slots_all = devices * tok_dev
    slot_ids = jnp.arange(tok_dev, dtype=jnp.int32)
    own_length = cont_lengths[flat_rank]
    valid_slot = (slot_ids < prompt_block) | (slot_ids - prompt_block < own_length)
    valid_count = (devices * prompt_block + jnp.sum(cont_lengths)).astype(F32)
    tokens_float = tokens.astype(F32)
    normed_float, first_norm_back = jax.vjp(root_mean_scale, tokens_float, input_gain)
    normed = normed_float.astype(BF16)

    block_ids = jnp.arange(n_dp, dtype=jnp.int32)[:, None]
    positions = jnp.where(
        slot_ids[None] < prompt_block,
        (column * n_dp + block_ids) * prompt_block + slot_ids[None],
        prompt_len + slot_ids[None] - prompt_block,
    )
    half_head = head_dim // 2
    frequency = rope_base ** (-(jnp.arange(half_head, dtype=F32) * 2.0) / head_dim)
    angles = positions.astype(F32)[:, :, None] * frequency
    cos_half, sin_half = jnp.cos(angles), jnp.sin(angles)
    cos = jnp.concatenate([cos_half, cos_half], axis=-1)
    sin = jnp.concatenate([-sin_half, sin_half], axis=-1)
    lin, normed_cols_t, normed_cols, key_lin, all_keys, all_values = project_qkv(
        normed, query_weight, key_projection, value_projection, key_gain[None], cos, sin
    )
    query_gain_row = query_gain[None]
    queries, attended = attention_fwd(
        cont_lengths, lin, query_gain_row, cos, sin, all_keys, all_values, prompt_len
    )
    state = tokens_float + project_out(attended, output_weight)
    mixed_float, second_norm_back = jax.vjp(root_mean_scale, state, post_gain)
    mixed = mixed_float.astype(BF16)
    sizes = (devices, capacity, slots_all)
    weights = (router_weight, gate_weight, up_weight, down_weight)
    if n_dp == 4 and n_owner == 8:
        moe = experts_by_gather(
            mixed, state, teacher, routes, valid_slot, valid_count, *weights, *sizes
        )
    else:
        moe = experts_by_all_to_all(
            mixed, state, teacher, routes, valid_slot, valid_count, *weights, *sizes
        )
    layer_out, d_out, d_mixed, local_square, router_local, gate_grad, up_grad, down_grad = moe
    d_state_norm, d_post_gain = second_norm_back(d_mixed)
    d_state = d_out + d_state_norm
    d_branch = d_state.astype(BF16)
    d_attended, d_branch_all, attended_t = grad_branch(d_branch, output_weight, attended)
    d_query_lin, d_keys, d_values, gain_parts, out_part = attention_bwd(
        cont_lengths, lin, queries, d_attended, query_gain_row, cos, sin, all_keys, all_values,
        attended_t, d_branch_all, prompt_len,
    )
    d_query_gain = jnp.sum(gain_parts, axis=(0, 1))
    width = query_weight.shape[0]
    group = query_group + 2 * head_dim
    rows_here = width // n_owner
    by_line = n_dp == 4 and n_owner == 8

    def packed(parts):
        small = jnp.concatenate([a.reshape(-1) for a in parts])
        piece_rows = -(-small.shape[0] // (8 * 8 * 128)) * 8
        small = jnp.pad(small, (0, 8 * piece_rows * 128 - small.shape[0]))
        return small.reshape(8, piece_rows, 128)

    out_part = out_part.reshape(n_owner, -1, model_width)
    weights = (query_weight, key_projection, value_projection)
    if by_line:

        def line(parts):
            flat = jnp.concatenate(parts)
            return jnp.pad(flat, (0, model_width - flat.shape[0]))[None]

        small = jnp.concatenate(
            [router_local, d_post_gain[None], line([d_query_gain]), line([local_square[None]])]
        )
        small_rows = -(-small.shape[0] // 8) * 8
        small = jnp.pad(small, ((0, small_rows - small.shape[0]), (0, 0)))
        small = small.reshape(small_rows, 8, -1).transpose(1, 0, 2)
        d_normed, query_grad, key_grad, value_grad, output_grad, small, input_gain_grad = grad_qkv_line(
            d_query_lin, d_keys, d_values, key_lin, cos, sin, key_gain[None],
            *weights, normed_cols_t, normed_cols, out_part, small, input_gain[None],
        )
        key_gain_grad = jnp.sum(input_gain_grad[:, 1, :head_dim], axis=0)
        input_gain_grad = input_gain_grad[:, 0].reshape(-1)
        sums = small.transpose(1, 0, 2).reshape(small_rows, model_width)
        at = router_local.shape[0]
        router_grad, post_gain_grad = sums[:at].T, sums[at]
        query_gain_grad = sums[at + 1, :head_dim]
        total_square = sums[at + 2, :1]
        d_tokens_norm = first_norm_back(d_normed)[0]
    else:
        _, key_back = jax.vjp(
            lambda a, b: head_rope(a, b, cos, sin), key_lin.reshape(n_dp, tok_dev, head_dim), key_gain
        )
        prompt_grads = jnp.stack(
            [jnp.sum(d_keys[:, :prompt_len], axis=0), jnp.sum(d_values[:, :prompt_len], axis=0)]
        )
        mine_part = jnp.where(first_column, prompt_grads[:, :half_prompt], prompt_grads[:, half_prompt:])
        their_part = jnp.where(first_column, prompt_grads[:, half_prompt:], prompt_grads[:, :half_prompt])
        own_prompt = (mine_part + partner(their_part, "expert", 0)).reshape(
            2, n_dp, prompt_block, head_dim
        )
        d_key_post = jnp.concatenate([own_prompt[0], d_keys[:, prompt_len:]], axis=1)
        d_value_lin = jnp.concatenate([own_prompt[1], d_values[:, prompt_len:]], axis=1)
        d_key_float, d_key_gain = key_back(d_key_post)
        rows = n_dp * tok_dev
        d_lin = jnp.concatenate(
            [
                d_query_lin,
                d_key_float.astype(BF16).reshape(rows, head_dim),
                d_value_lin.astype(BF16).reshape(rows, head_dim),
            ],
            axis=1,
        )
        small_parts = [router_local, d_post_gain, d_query_gain, d_key_gain, local_square[None]]
        d_normed, qkv_part, output_grad = grad_qkv(d_lin, *weights, normed_cols_t, out_part)
        d_tokens_norm, d_input_gain = first_norm_back(d_normed)
        small_parts.append(d_input_gain)
        by_owner = (
            qkv_part.reshape(n_dp, n_owner, rows_here, group)
            .transpose(1, 0, 2, 3)
            .reshape(n_owner, n_dp * rows_here, group)
        )
        qkv_rows, small = last_sums(by_owner, packed(small_parts))
        qkv_rows = qkv_rows.reshape(n_dp, rows_here, group)

        def columns(start, size):
            part = qkv_rows[:, :, start : start + size]
            return part.transpose(1, 0, 2).reshape(rows_here, n_dp * size)

        query_grad = columns(0, query_group)
        key_grad = columns(query_group, head_dim)
        value_grad = columns(query_group + head_dim, head_dim)
        small = small.reshape(-1)
        starts = [0]
        for a in small_parts:
            starts.append(starts[-1] + a.size)
        sums = [small[i:j].reshape(a.shape) for a, i, j in zip(small_parts, starts, starts[1:])]
        router_grad, post_gain_grad, query_gain_grad, key_gain_grad, total_square, input_gain_grad = sums
        router_grad = router_grad.T
    tokens_grad = d_state + d_tokens_norm
    loss = total_square[0] / (valid_count * model_width)
    return (
        layer_out,
        loss,
        tokens_grad,
        query_grad,
        key_grad,
        value_grad,
        output_grad,
        router_grad,
        gate_grad,
        up_grad,
        down_grad,
        input_gain_grad,
        post_gain_grad,
        query_gain_grad,
        key_gain_grad,
    )


def solution(mesh):
    in_specs = (
        P(("dp", "expert"), None),
        P(("dp", "expert"), None),
        P(("dp", "expert"), None),
        P(),
        P("dp", None),
        P("dp", None),
        P("dp", None),
        P("dp", None),
        P(),
        P(("dp", "expert"), None, None),
        P(("dp", "expert"), None, None),
        P(("dp", "expert"), None, None),
        P(),
        P(),
        P(),
        P(),
    )
    out_specs = (
        P(("dp", "expert"), None),
        P(),
        P(("dp", "expert"), None),
        P(("dp", "expert"), None),
        P(("dp", "expert"), None),
        P(("dp", "expert"), None),
        P(("dp", "expert"), None),
        P(),
        P(("dp", "expert"), None, None),
        P(("dp", "expert"), None, None),
        P(("dp", "expert"), None, None),
        P(),
        P(),
        P(),
        P(),
    )
    return jax.shard_map(body, mesh=mesh, in_specs=in_specs, out_specs=out_specs, check_vma=False)
```

```python
import functools

import jax
import jax.numpy as jnp
from jax import lax
from jax.experimental import pallas as pl
from jax.experimental.pallas import tpu as pltpu
from jax.sharding import PartitionSpec as P

CMAX = 128
norm_eps = 1e-06
rope_base = 1000000.0
MESH = pl.DeviceIdType.MESH
F32 = jnp.float32
BF16 = jnp.bfloat16
VMEM_SPEC = pl.BlockSpec(memory_space=pltpu.VMEM)
ANY_SPEC = pl.BlockSpec(memory_space=pl.ANY)
VMEM_LIMIT = 56 * 1024 * 1024


def params(collective_id=None):
    return pltpu.CompilerParams(
        collective_id=collective_id,
        has_side_effects=collective_id is not None,
        vmem_limit_bytes=VMEM_LIMIT,
    )


def greet(devices):
    barrier = pltpu.get_barrier_semaphore()
    for device in devices:
        pl.semaphore_signal(barrier, inc=1, device_id=device, device_id_type=MESH)
    pl.semaphore_wait(barrier, len(devices))


def remote(src, dst, send_sem, recv_sem, device):
    return pltpu.make_async_remote_copy(
        src_ref=src,
        dst_ref=dst,
        send_sem=send_sem,
        recv_sem=recv_sem,
        device_id=device,
        device_id_type=MESH,
    )


def start_all(copies):
    for copy in copies:
        copy.start()
    return copies


def wait_all(copies):
    for copy in copies:
        copy.wait()
    copies.clear()


def loading(pairs, sems):
    return [start_all([pltpu.make_async_copy(a, b, sems.at[i])]) for i, (a, b) in enumerate(pairs)]


def aligned(index, size):
    return pl.ds(pl.multiple_of(index * size, size), size)


def dot_nn(a, b):
    return lax.dot_general(a, b, (((1,), (0,)), ((), ())), preferred_element_type=F32)


def dot_nt(a, b):
    return lax.dot_general(a, b, (((1,), (1,)), ((), ())), preferred_element_type=F32)


def dot_tn(a, b):
    return lax.dot_general(a, b, (((0,), (0,)), ((), ())), preferred_element_type=F32)


PEER_MASKS = (3, 1, 2)


def relay_sum(r, e, products, own, mine, send, half_in, full_in, hs, hr, fs, fr, step):
    near, far, diag = r ^ 1, r ^ 2, r ^ 3
    rows = mine.shape[0]
    half = rows // 2
    low, high = pl.ds(0, half), pl.ds(half, half)
    products(diag, send.at[2])
    relays = [
        remote(send.at[2, low], half_in.at[0], hs.at[0], hr.at[0], (near, e)),
        remote(send.at[2, high], half_in.at[1], hs.at[1], hr.at[1], (far, e)),
    ]
    for copy in relays:
        copy.start()
    parts = ((0, low, near), (1, high, far), (0, high, near), (1, low, far))
    fulls = [
        remote(send.at[i, part], full_in.at[i, part], fs.at[n], fr.at[n], (p, e))
        for n, (i, part, p) in enumerate(parts)
    ]
    products(near, send.at[0])
    fulls[0].start()
    products(far, send.at[1])
    fulls[1].start()
    for i, start, slot, n in ((1, 0, 0, 3), (0, half, 1, 2)):
        relays[slot].wait_recv()

        def add(c, carry):
            t = pl.ds(pl.multiple_of(start + c * step, step), step)
            value = send[i, t, :].astype(F32) + half_in[slot, aligned(c, step), :].astype(F32)
            send[i, t, :] = value.astype(BF16)
            return carry

        lax.fori_loop(0, half // step, add, 0)
        fulls[n].start()
    own()
    for copy in fulls:
        copy.wait_recv()

    def total(c, carry):
        t = aligned(c, step)
        mine[t, :] = mine[t, :] + (full_in[0, t, :].astype(F32) + full_in[1, t, :].astype(F32))
        return carry

    lax.fori_loop(0, rows // step, total, 0)
    for copy in relays + fulls:
        copy.wait_send()


def relay_scratch(rows, width):
    return [
        pltpu.VMEM((3, rows, width), BF16),
        pltpu.VMEM((2, rows // 2, width), BF16),
        pltpu.VMEM((2, rows, width), BF16),
        pltpu.SemaphoreType.DMA((2,)),
        pltpu.SemaphoreType.DMA((2,)),
        pltpu.SemaphoreType.DMA((4,)),
        pltpu.SemaphoreType.DMA((4,)),
    ]


def qkv_kernel(
    tok, tokens, in_gain, wq_in, wk_in, wv_in, gain, cos, sin,
    lin, cols_t, cols, key_lin, keys, values, inverse_out,
    normed, wq, wk, wv, own_kv, other_kv, local, asend, arecv, ksend, krecv, *relay,
):
    r, e = lax.axis_index("dp"), lax.axis_index("expert")
    peers = [r ^ m for m in PEER_MASKS]
    width = wq.shape[0]
    qg = wq.shape[1] // 4
    kg = wk.shape[1] // 4
    rows = cols.shape[0]
    loads = loading(((wq_in, wq), (wk_in, wk), (wv_in, wv)), local)
    value = tokens[...].astype(F32)
    inverse = lax.rsqrt(jnp.mean(value * value, axis=-1, keepdims=True) + norm_eps)
    normed[...] = (value * inverse * in_gain[...]).astype(BF16)
    inverse_out[...] = jnp.broadcast_to(inverse, inverse_out.shape)
    greet([(p, e) for p in peers] + [(r, e ^ 1)])
    first = []
    for i, p in enumerate(peers):
        copy = remote(
            normed.at[:, aligned(p, width)], cols.at[aligned(r, tok), :],
            asend.at[i], arecv.at[i], (p, e),
        )
        copy.start()
        first.append(copy)
    cols[aligned(r, tok), :] = normed[:, aligned(r, width)]
    for copy in first:
        copy.wait()
    for copies in loads:
        wait_all(copies)

    def products(p, dst):
        def chunk(c, carry):
            columns = pl.ds(pl.multiple_of(p * qg + c * 256, 256), 256)
            dst[:, aligned(c, 256)] = dot_nn(cols[...], wq[:, columns]).astype(dst.dtype)
            return carry

        lax.fori_loop(0, qg // 256, chunk, 0)
        dst[:, qg : qg + kg] = dot_nn(cols[...], wk[:, aligned(p, kg)]).astype(dst.dtype)
        dst[:, qg + kg :] = dot_nn(cols[...], wv[:, aligned(p, kg)]).astype(dst.dtype)

    def own():
        products(r, lin)
        cols_t[...] = cols[...].T

    relay_sum(r, e, products, own, lin, *relay, 32)
    core = e % 2
    head = gain.shape[1]
    prompt = tok - CMAX
    column = 4 * prompt
    for i in range(4):
        rows_i = slice(i * tok, (i + 1) * tok)
        x = lin[rows_i, qg : qg + kg]
        key_lin[rows_i, :] = x
        x = x * lax.rsqrt(jnp.mean(x * x, axis=-1, keepdims=True) + norm_eps) * gain[...]
        k = (x * cos[i] + pltpu.roll(x, head // 2, 1) * sin[i]).astype(BF16)
        v = lin[rows_i, qg + kg :].astype(BF16)
        for n, (part, out) in enumerate(((k, keys), (v, values))):
            own_kv[n, i * prompt : (i + 1) * prompt] = part[:prompt]
            out[i, 2 * column :] = part[prompt:]
    copy = remote(own_kv, other_kv, ksend.at[0], krecv.at[0], (r, e ^ 1))
    copy.start()
    for n, out in enumerate((keys, values)):
        for i in range(4):
            out[i, aligned(core, column)] = own_kv[n]
    copy.wait()
    for n, out in enumerate((keys, values)):
        for i in range(4):
            out[i, aligned(1 - core, column)] = other_kv[n]


def project_qkv(tokens, in_gain, wq, wk, wv, gain, cos, sin):
    tok = tokens.shape[0]
    rows = 4 * tok
    group = (wq.shape[1] + wk.shape[1] + wv.shape[1]) // 4
    head = gain.shape[1]
    total_keys = 8 * (tok - CMAX) + CMAX
    return pl.pallas_call(
        functools.partial(qkv_kernel, tok),
        out_shape=(
            jax.ShapeDtypeStruct((rows, group), F32),
            jax.ShapeDtypeStruct((wq.shape[0], rows), BF16),
            jax.ShapeDtypeStruct((rows, wq.shape[0]), BF16),
            jax.ShapeDtypeStruct((rows, head), F32),
            jax.ShapeDtypeStruct((4, total_keys, head), BF16),
            jax.ShapeDtypeStruct((4, total_keys, head), BF16),
            jax.ShapeDtypeStruct((tok, 128), F32),
        ),
        in_specs=[VMEM_SPEC] * 2 + [ANY_SPEC] * 3 + [VMEM_SPEC] * 3,
        out_specs=(VMEM_SPEC,) * 7,
        scratch_shapes=[pltpu.VMEM(w.shape, BF16) for w in (tokens, wq, wk, wv)]
        + [pltpu.VMEM((2, 4 * (tok - CMAX), head), BF16)] * 2
        + [pltpu.SemaphoreType.DMA((3,))] * 3
        + [pltpu.SemaphoreType.DMA((1,))] * 2
        + relay_scratch(rows, group),
        compiler_params=params(1),
        name="qkv_exchange",
    )(tokens, in_gain, wq, wk, wv, gain, cos, sin)


def out_kernel(attn_in, wo_in, total, attn, wo, local, *relay):
    r, e = lax.axis_index("dp"), lax.axis_index("expert")
    tok, width = total.shape
    step = width // 4
    loads = loading(((attn_in, attn), (wo_in, wo)), local)
    greet([(r ^ m, e) for m in PEER_MASKS])
    for copies in loads:
        wait_all(copies)

    def products(p, dst):
        def chunk(c, carry):
            n = aligned(c, step)
            dst[:, n] = dot_nn(attn[aligned(p, tok), :], wo[:, n]).astype(dst.dtype)
            return carry

        lax.fori_loop(0, width // step, chunk, 0)

    relay_sum(r, e, products, lambda: products(r, total), total, *relay, 16)


def project_out(attn, wo):
    tok = attn.shape[0] // 4
    return pl.pallas_call(
        out_kernel,
        out_shape=jax.ShapeDtypeStruct((tok, wo.shape[1]), F32),
        in_specs=[ANY_SPEC] * 2,
        out_specs=VMEM_SPEC,
        scratch_shapes=[
            pltpu.VMEM(attn.shape, BF16),
            pltpu.VMEM(wo.shape, BF16),
            pltpu.SemaphoreType.DMA((2,)),
        ]
        + relay_scratch(tok, wo.shape[1]),
        compiler_params=params(2),
        name="out_exchange",
    )(attn, wo)


def dgrad_kernel(
    mine, wq, wk, wv, cols_t, out_part, normal, grads, out_grad,
    blocks, dsum, dsend, drecv, ssem, rsem, bsend, brecv, *scratch,
):
    r, e = lax.axis_index("dp"), lax.axis_index("expert")
    rows = mine.shape[0]
    tok = rows // 4
    half = rows // 2
    qg = wq.shape[1] // 4
    kg = wk.shape[1] // 4
    width = wq.shape[0]
    peers = [r ^ m for m in PEER_MASKS]
    near, far, diag = r ^ 1, r ^ 2, r ^ 3
    pair_in, send, recv, *sems = scratch
    begin, middle, finish = owner_sum([out_part], [out_grad], [pair_in], [send], [recv], *sems)
    greet([(p, e) for p in peers] + [(r, e ^ 1)] + owner_peers())
    begin()
    low, high = pl.ds(0, half), pl.ds(half, half)
    first_near = remote(mine.at[low], blocks.at[0, low], ssem.at[0], rsem.at[0], (near, e))
    first_far = remote(mine.at[high], blocks.at[1, high], ssem.at[1], rsem.at[1], (far, e))
    second_near = remote(mine.at[high], blocks.at[0, high], ssem.at[2], rsem.at[2], (near, e))
    second_far = remote(mine.at[low], blocks.at[1, low], ssem.at[3], rsem.at[3], (far, e))
    pass_far = remote(blocks.at[0, low], blocks.at[2, low], ssem.at[4], rsem.at[4], (far, e))
    pass_near = remote(blocks.at[1, high], blocks.at[2, high], ssem.at[5], rsem.at[5], (near, e))
    for copy in (first_near, first_far, second_near, second_far):
        copy.start()

    def products(p, src, start):
        def chunk(c, carry):
            t = aligned(c, tok)
            x = src[t, :]
            value = (
                dot_nt(x[:, :qg], wq[:, aligned(p, qg)])
                + dot_nt(x[:, qg : qg + kg], wk[:, aligned(p, kg)])
                + dot_nt(x[:, qg + kg :], wv[:, aligned(p, kg)])
            )
            if start:
                dsum[t, :] = value
            else:
                dsum[t, :] = dsum[t, :] + value
            return carry

        lax.fori_loop(0, 4, chunk, 0)

        def outer(c, carry):
            n = aligned(c, 128)
            grads[aligned(p, width), n] = dot_nn(cols_t[...], src[:, n]).astype(BF16)
            return carry

        lax.fori_loop(0, (qg + 2 * kg) // 128, outer, 0)

    middle()
    products(r, mine, True)
    first_near.wait()
    pass_far.start()
    first_far.wait()
    pass_near.start()
    second_near.wait()
    products(near, blocks.at[0], False)
    second_far.wait()
    products(far, blocks.at[1], False)
    pass_far.wait()
    pass_near.wait()
    products(diag, blocks.at[2], False)
    back = []
    for i, p in enumerate(peers):
        dsend[i] = dsum[aligned(p, tok), :].astype(BF16)
        copy = remote(dsend.at[i], drecv.at[i], bsend.at[i], brecv.at[i], (p, e))
        copy.start()
        back.append(copy)
    normal[:, aligned(r, width)] = dsum[aligned(r, tok), :]
    for i, p in enumerate(peers):
        back[i].wait()
        normal[:, aligned(p, width)] = drecv[i].astype(F32)
    finish()


def grad_qkv(mine, wq, wk, wv, cols_t, out_part):
    rows, group = mine.shape
    tok = rows // 4
    width = wq.shape[0]
    return pl.pallas_call(
        dgrad_kernel,
        out_shape=(
            jax.ShapeDtypeStruct((tok, 4 * width), F32),
            jax.ShapeDtypeStruct((4 * width, group), BF16),
            jax.ShapeDtypeStruct(out_part.shape[1:], F32),
        ),
        in_specs=[VMEM_SPEC] * 6,
        out_specs=(VMEM_SPEC,) * 3,
        scratch_shapes=[
            pltpu.VMEM((3, rows, group), BF16),
            pltpu.VMEM((rows, width), F32),
            pltpu.VMEM((3, tok, width), BF16),
            pltpu.VMEM((3, tok, width), BF16),
            pltpu.SemaphoreType.DMA((6,)),
            pltpu.SemaphoreType.DMA((6,)),
            pltpu.SemaphoreType.DMA((3,)),
            pltpu.SemaphoreType.DMA((3,)),
        ]
        + owner_scratch([out_part]),
        compiler_params=params(4),
        name="dqkv_exchange",
    )(mine, wq, wk, wv, cols_t, out_part)


def branch_kernel(
    mine, wo_in, attn_in, d_attn, full_out, attn_t_out, wo, attn, full, attn_t, local, ssem, rsem
):
    r, e = lax.axis_index("dp"), lax.axis_index("expert")
    tok = mine.shape[0]
    half = tok // 2
    peers = [r ^ m for m in PEER_MASKS]
    near, far, diag = r ^ 1, r ^ 2, r ^ 3
    loads = loading(((attn_in, attn), (wo_in, wo)), local)
    greet([(p, e) for p in peers])

    def part(q, which):
        return pl.ds(pl.multiple_of(q * tok + which * half, half), half)

    low, high = pl.ds(0, half), pl.ds(half, half)
    first_near = remote(mine.at[low], full.at[part(r, 0)], ssem.at[0], rsem.at[0], (near, e))
    first_far = remote(mine.at[high], full.at[part(r, 1)], ssem.at[1], rsem.at[1], (far, e))
    second_near = remote(mine.at[high], full.at[part(r, 1)], ssem.at[2], rsem.at[2], (near, e))
    second_far = remote(mine.at[low], full.at[part(r, 0)], ssem.at[3], rsem.at[3], (far, e))
    pass_far = remote(full.at[part(near, 0)], full.at[part(near, 0)], ssem.at[4], rsem.at[4], (far, e))
    pass_near = remote(full.at[part(far, 1)], full.at[part(far, 1)], ssem.at[5], rsem.at[5], (near, e))
    for copy in (first_near, first_far, second_near, second_far):
        copy.start()
    full[aligned(r, tok), :] = mine[...]
    wait_all(loads[0])
    attn_t[...] = attn[...].T
    leaving = start_all([pltpu.make_async_copy(attn_t, attn_t_out, local.at[0])])
    wait_all(loads[1])
    heads = wo.shape[0]
    step = heads // 4

    def products(q):
        def chunk(c, carry):
            n = aligned(c, step)
            d_attn[aligned(q, tok), n] = dot_nt(full[aligned(q, tok), :], wo[n, :]).astype(BF16)
            return carry

        lax.fori_loop(0, 4, chunk, 0)

    products(r)
    first_near.wait()
    pass_far.start()
    first_far.wait()
    pass_near.start()
    second_near.wait()
    products(near)
    second_far.wait()
    products(far)
    pass_far.wait()
    pass_near.wait()
    leaving += start_all([pltpu.make_async_copy(full, full_out, local.at[1])])
    products(diag)
    wait_all(leaving)


def grad_branch(mine, wo, attn):
    tok, width = mine.shape
    return pl.pallas_call(
        branch_kernel,
        out_shape=(
            jax.ShapeDtypeStruct((4 * tok, wo.shape[0]), BF16),
            jax.ShapeDtypeStruct((4 * tok, width), BF16),
            jax.ShapeDtypeStruct((wo.shape[0], 4 * tok), BF16),
        ),
        in_specs=[VMEM_SPEC, ANY_SPEC, ANY_SPEC],
        out_specs=(VMEM_SPEC, ANY_SPEC, ANY_SPEC),
        scratch_shapes=[
            pltpu.VMEM(wo.shape, BF16),
            pltpu.VMEM(attn.shape, BF16),
            pltpu.VMEM((4 * tok, width), BF16),
            pltpu.VMEM((wo.shape[0], 4 * tok), BF16),
            pltpu.SemaphoreType.DMA((2,)),
            pltpu.SemaphoreType.DMA((6,)),
            pltpu.SemaphoreType.DMA((6,)),
        ],
        compiler_params=params(3),
        name="branch_exchange",
    )(mine, wo, attn)


def owner_order(n_z):
    order = list(range(1, n_z)) + [0]
    return order[1:2] + order[:1] + order[2:] if n_z > 2 else order


def owner_sum(arrays, outs, pair_in, send, recv, psend, precv, zsend, zrecv):
    r, e = lax.axis_index("dp"), lax.axis_index("expert")
    n_z = arrays[0].shape[0] // 2
    z, core = e // 2, e % 2
    targets = [lax.rem(z + j, n_z) for j in range(n_z)]
    order = owner_order(n_z)
    n_arrays = len(arrays)
    pair, moves = {}, []

    def begin():
        for j in order:
            for a in range(n_arrays):
                copy = remote(
                    arrays[a].at[targets[j] * 2 + (1 - core)], pair_in[a].at[j],
                    psend.at[a, j], precv.at[a, j], (r, e ^ 1),
                )
                copy.start()
                pair[a, j] = copy

    def middle():
        for j in order:
            for a in range(n_arrays):
                pair[a, j].wait()
                own = arrays[a][targets[j] * 2 + core].astype(F32) + pair_in[a][j].astype(F32)
                if j == 0:
                    outs[a][...] = own
                else:
                    send[a][j - 1] = own.astype(BF16)
                    copy = remote(
                        send[a].at[j - 1], recv[a].at[j - 1],
                        zsend.at[a, j - 1], zrecv.at[a, j - 1], (r, targets[j] * 2 + core),
                    )
                    copy.start()
                    moves.append(copy)

    def finish():
        for copy in moves:
            copy.wait()
        for a in range(n_arrays):
            value = outs[a][...]
            for j in range(n_z - 1):
                value = value + recv[a][j].astype(F32)
            outs[a][...] = value

    return begin, middle, finish


def owner_scratch(arrays):
    n_z = arrays[0].shape[0] // 2
    n = len(arrays)
    shapes = [a.shape[1:] for a in arrays]
    return (
        [pltpu.VMEM((n_z, *s), BF16) for s in shapes]
        + [pltpu.VMEM((n_z - 1, *s), BF16) for s in shapes]
        + [pltpu.VMEM((n_z - 1, *s), BF16) for s in shapes]
        + [pltpu.SemaphoreType.DMA((n, n_z))] * 2
        + [pltpu.SemaphoreType.DMA((n, n_z - 1))] * 2
    )


def owner_peers():
    r, e = lax.axis_index("dp"), lax.axis_index("expert")
    n_z = lax.axis_size("expert") // 2
    return [(r, lax.rem(e // 2 + j, n_z) * 2 + e % 2) for j in range(1, n_z)]


def last_sums_kernel(grads, small, grads_out, small_out, *scratch):
    r, e = lax.axis_index("dp"), lax.axis_index("expert")
    z, core = e // 2, e % 2
    n_z = grads.shape[0] // 2
    pair_in, send, recv, psend, precv, zsend, zrecv = scratch[:7]
    first_in, piece, line_in, s1, r1, s2, r2, s3, r3 = scratch[7:]
    begin, middle, finish = owner_sum(
        [grads], [grads_out], [pair_in], [send], [recv], psend, precv, zsend, zrecv
    )
    others = [(m // 2, m % 2) for m in range(1, 8)]
    plane = [(r ^ a, e ^ c) for a, c in others]
    greet(plane + owner_peers())
    begin()
    firsts = []
    for i, (a, c) in enumerate(others):
        copy = remote(
            small.at[(r ^ a) * 2 + (core ^ c)], first_in.at[i], s1.at[i], r1.at[i], plane[i]
        )
        copy.start()
        firsts.append(copy)
    middle()
    for copy in firsts:
        copy.wait()
    mine = r * 2 + core
    value = small[mine]
    for i in range(7):
        value = value + first_in[i]
    piece[0] = value
    seconds = []
    for j in range(1, n_z):
        copy = remote(
            piece.at[0], line_in.at[j - 1], s2.at[j - 1], r2.at[j - 1], owner_peers()[j - 1]
        )
        copy.start()
        seconds.append(copy)
    for copy in seconds:
        copy.wait()
    value = piece[0]
    for j in range(n_z - 1):
        value = value + line_in[j]
    small_out[mine] = value
    thirds = []
    for i, (a, c) in enumerate(others):
        copy = remote(small_out.at[mine], small_out.at[mine], s3.at[i], r3.at[i], plane[i])
        copy.start()
        thirds.append(copy)
    finish()
    for copy in thirds:
        copy.wait()


def last_sums(grads, small):
    n_z = grads.shape[0] // 2
    piece = small.shape[1:]
    return pl.pallas_call(
        last_sums_kernel,
        out_shape=(
            jax.ShapeDtypeStruct(grads.shape[1:], F32),
            jax.ShapeDtypeStruct(small.shape, F32),
        ),
        in_specs=[VMEM_SPEC] * 2,
        out_specs=(VMEM_SPEC,) * 2,
        scratch_shapes=owner_scratch([grads])
        + [
            pltpu.VMEM((7, *piece), F32),
            pltpu.VMEM((1, *piece), F32),
            pltpu.VMEM((n_z - 1, *piece), F32),
            pltpu.SemaphoreType.DMA((7,)),
            pltpu.SemaphoreType.DMA((7,)),
            pltpu.SemaphoreType.DMA((n_z - 1,)),
            pltpu.SemaphoreType.DMA((n_z - 1,)),
            pltpu.SemaphoreType.DMA((7,)),
            pltpu.SemaphoreType.DMA((7,)),
        ],
        compiler_params=params(5),
        name="last_sums",
    )(grads, small)


def line_sum(block, out, pair_in, work, lines, ps, pr, zs, zr):
    r, e = lax.axis_index("dp"), lax.axis_index("expert")
    z, core = e // 2, e % 2
    order = plane_order(z)[::-1]
    right = jnp.minimum(z + 1, 3) * 2 + core
    left = jnp.maximum(z - 1, 0) * 2 + core
    pairs, moves = [], []

    def begin():
        for k in range(4):
            copy = remote(
                block(order[k] * 2 + (1 - core)), pair_in.at[k], ps.at[k], pr.at[k], (r, e ^ 1)
            )
            copy.start()
            pairs.append(copy)

    def move(k, side, cond, to, add):
        b = order[k]
        copy = remote(work.at[k], lines.at[side, b], zs.at[side, k], zr.at[side, b], (r, to))
        moves.append((cond, copy))

        @pl.when(cond)
        def _():
            if add:
                copy.wait_recv()
                value = work[k].astype(F32) + lines[side, b].astype(F32)
                work[k] = value.astype(BF16)
            copy.start()

    def first():
        for k in range(4):
            pairs[k].wait_recv()
            value = block(order[k] * 2 + core)[...].astype(F32) + pair_in[k].astype(F32)
            if k == 3:
                out[...] = value
            else:
                work[k] = value.astype(BF16)
        ends(0)

    def ends(k):
        move(k, 0, z == 0, right, False)
        move(k, 1, z == 3, left, False)

    def inner(k):
        inside = (z > 0) & (z < 3)
        move(k, 0, inside & (order[k] > z), right, True)
        move(k, 1, inside & (order[k] < z), left, True)
        if k < 2:
            ends(k + 1)

    def last():
        for side, cond in ((0, z > 0), (1, z < 3)):

            @pl.when(cond)
            def _():
                at = lines.at[side, z]
                remote(at, at, zs.at[side, 3], zr.at[side, z], (r, e ^ 1)).wait_recv()
                out[...] = out[...] + lines[side, z].astype(F32)

        for copy in pairs:
            copy.wait_send()
        for cond, copy in moves:

            @pl.when(cond)
            def _():
                copy.wait_send()

    return begin, first, inner, last


LINE_SEMS = [
    pltpu.SemaphoreType.DMA((4,)),
    pltpu.SemaphoreType.DMA((4,)),
    pltpu.SemaphoreType.DMA((2, 4)),
    pltpu.SemaphoreType.DMA((2, 4)),
]


def dgrad_line_kernel(
    d_q, d_keys, d_values, key_lin, cos, sin, key_gain,
    wq_in, wk_in, wv_in, cols_t_in, cols_in, out_part_in, small, gain,
    normal, q_out, k_out, v_out, out_sum, small_out, gain_out,
    mine, prompt_sum, prompt_in, ksend, krecv, wq, wk, wv, cols_t, cols, out_part, local, qkv_sum, grads, blocks, dsum, dsend, drecv, opair, owork, olines, qpair, qwork, qlines,
    first_in, piece, line_in, gain_v, gain_in,
    ssem, rsem, bsend, brecv, s1, r1, s2, r2, s3, r3, s4, r4, s5, r5, *sems,
):
    r, e = lax.axis_index("dp"), lax.axis_index("expert")
    z, core = e // 2, e % 2
    rows = mine.shape[0]
    tok = rows // 4
    half = rows // 2
    qg = wq.shape[1] // 4
    kg = wk.shape[1] // 4
    width = wq.shape[0]
    share = width // 8
    peers = [r ^ m for m in PEER_MASKS]
    near, far, diag = r ^ 1, r ^ 2, r ^ 3
    order = (r, near, far, diag)
    out_begin, out_first, out_inner, out_last = line_sum(
        lambda o: out_part.at[o], out_sum, opair, owork, olines, *sems[:4]
    )
    units = [
        line_sum(
            lambda o, p=p: grads.at[o, p], qkv_sum.at[p], qpair.at[i], qwork.at[i], qlines.at[i],
            *(sem.at[i] for sem in sems[4:]),
        )
        for i, p in enumerate(order)
    ]
    line_peers = [(r, lax.rem(z + j, 4) * 2 + core) for j in (1, 2, 3)]
    others = [(m // 2, m % 2) for m in (6, 7, 2, 3, 4, 5, 1)]
    plane = [(r ^ a, e ^ c) for a, c in others]
    owners = [(r, e ^ m) for m in range(1, 8)]
    loads = loading(
        (
            (out_part_in, out_part), (cols_t_in, cols_t), (wq_in, wq), (wk_in, wk), (wv_in, wv),
            (cols_in, cols),
        ),
        local,
    )
    mine[:, :qg] = d_q[...]
    prompt = tok - CMAX
    column = 4 * prompt
    for n, d in enumerate((d_keys, d_values)):
        for c in range(2):
            part = slice(c * column, (c + 1) * column)
            prompt_sum[c, n] = d[0, part] + d[1, part] + d[2, part] + d[3, part]
    greet(plane + owners[1:])
    swap = remote(prompt_sum.at[1 - core], prompt_in, ksend.at[0], krecv.at[0], (r, e ^ 1))
    swap.start()
    swap.wait()
    prompt_in[...] = prompt_in[...] + prompt_sum[core]
    head = key_gain.shape[1]
    key_gain_sum = jnp.zeros((1, head), F32)
    for i in range(4):
        for at, size, dk, dv in (
            (0, prompt, prompt_in[0, i * prompt : (i + 1) * prompt], prompt_in[1, i * prompt : (i + 1) * prompt]),
            (prompt, CMAX, d_keys[i, 2 * column :], d_values[i, 2 * column :]),
        ):
            t = slice(at, at + size)
            rows_i = slice(i * tok + at, i * tok + at + size)
            turned = dk * cos[i, t] + pltpu.roll(dk * sin[i, t], head // 2, 1)
            x = key_lin[rows_i, :]
            inverse = lax.rsqrt(jnp.mean(x * x, axis=-1, keepdims=True) + norm_eps)
            unit = x * inverse
            key_gain_sum = key_gain_sum + jnp.sum(turned * unit, axis=0, keepdims=True)
            weighted = turned * key_gain[...]
            mine[rows_i, qg : qg + kg] = (
                inverse * (weighted - unit * jnp.mean(weighted * unit, axis=-1, keepdims=True))
            ).astype(BF16)
            mine[rows_i, qg + kg :] = dv.astype(BF16)
    low, high = pl.ds(0, half), pl.ds(half, half)
    first_near = remote(mine.at[low], blocks.at[0, low], ssem.at[0], rsem.at[0], (near, e))
    first_far = remote(mine.at[high], blocks.at[1, high], ssem.at[1], rsem.at[1], (far, e))
    second_near = remote(mine.at[high], blocks.at[0, high], ssem.at[2], rsem.at[2], (near, e))
    second_far = remote(mine.at[low], blocks.at[1, low], ssem.at[3], rsem.at[3], (far, e))
    pass_far = remote(blocks.at[0, low], blocks.at[2, low], ssem.at[4], rsem.at[4], (far, e))
    pass_near = remote(blocks.at[1, high], blocks.at[2, high], ssem.at[5], rsem.at[5], (near, e))
    me = r * 2 + core
    firsts = []
    for i, (a, c) in enumerate(others):
        copy = remote(small.at[(r ^ a) * 2 + (core ^ c)], first_in.at[i], s1.at[i], r1.at[i], plane[i])
        copy.start()
        firsts.append(copy)
    for copy in (first_near, first_far, second_near, second_far):
        copy.start()
    wait_all(loads[0])
    out_begin()
    seconds, thirds = [], []

    def small_second():
        for copy in firsts:
            copy.wait()
        value = small[me]
        for i in range(7):
            value = value + first_in[i]
        piece[0] = value
        for j in range(3):
            copy = remote(piece.at[0], line_in.at[j], s2.at[j], r2.at[j], line_peers[j])
            copy.start()
            seconds.append(copy)

    def small_third():
        for copy in seconds:
            copy.wait()
        small_out[me] = piece[0] + line_in[0] + line_in[1] + line_in[2]
        for i in range(7):
            copy = remote(small_out.at[me], small_out.at[me], s3.at[i], r3.at[i], plane[i])
            copy.start()
            thirds.append(copy)

    def outer(p, src):
        def step(c, carry):
            n = aligned(c, 256)
            value = dot_nn(cols_t[...], src[:, n]).astype(BF16)
            for o in range(8):
                grads[o, p, :, n] = value[o * share : (o + 1) * share]
            return carry

        lax.fori_loop(0, (qg + 2 * kg) // 256, step, 0)

    def inner(p, src, start):
        def chunk(c, carry):
            n = aligned(c, 128)
            value = (
                dot_nt(src[:, :qg], wq[n, aligned(p, qg)])
                + dot_nt(src[:, qg : qg + kg], wk[n, aligned(p, kg)])
                + dot_nt(src[:, qg + kg :], wv[n, aligned(p, kg)])
            )
            if start:
                dsum[:, n] = value
            else:
                dsum[:, n] = dsum[:, n] + value
            return carry

        lax.fori_loop(0, width // 128, chunk, 0)

    def begin(i):
        units[i][0]()

    def first(i):
        units[i][1]()

    def onward(i, k):
        units[i][2](k)

    wait_all(loads[1])
    outer(r, mine)
    begin(0)
    out_first()
    small_second()
    for copies in loads[2:5]:
        wait_all(copies)
    inner(r, mine, True)
    first_near.wait()
    pass_far.start()
    first_far.wait()
    pass_near.start()
    out_inner(0)
    first(0)
    out_inner(1)
    small_third()
    onward(0, 0)
    second_near.wait()
    outer(near, blocks.at[0])
    begin(1)
    second_far.wait()
    outer(far, blocks.at[1])
    begin(2)
    out_inner(2)
    onward(0, 1)
    first(1)
    inner(near, blocks.at[0], False)
    onward(0, 2)
    onward(1, 0)
    first(2)
    inner(far, blocks.at[1], False)
    onward(1, 1)
    pass_far.wait()
    pass_near.wait()
    outer(diag, blocks.at[2])
    begin(3)
    inner(diag, blocks.at[2], False)
    back = []
    for i, p in enumerate(peers):
        dsend[i] = dsum[aligned(p, tok), :].astype(BF16)
        copy = remote(dsend.at[i], drecv.at[i], bsend.at[i], brecv.at[i], (p, e))
        copy.start()
        back.append(copy)
    wait_all(loads[5])
    scale = 1.0 / gain[:, aligned(r, width)]
    gain_v[...] = jnp.broadcast_to(
        jnp.sum(dsum[...] * cols[...].astype(F32), axis=0, keepdims=True) * scale, gain_v.shape
    )
    gain_v[1:2, :head] = key_gain_sum
    fourths = []
    for i in range(7):
        copy = remote(gain_v, gain_in.at[i], s4.at[i], r4.at[i], owners[i])
        copy.start()
        fourths.append(copy)
    onward(1, 2)
    onward(2, 0)
    first(3)
    onward(2, 1)
    for copy in fourths:
        copy.wait()
    value = gain_v[...]
    for i in range(7):
        value = value + gain_in[i]
    gain_out[r] = value
    fifths = []
    for i, p in enumerate(peers):
        copy = remote(gain_out.at[r], gain_out.at[r], s5.at[i], r5.at[i], (p, e))
        copy.start()
        fifths.append(copy)
    onward(3, 0)
    normal[:, aligned(r, width)] = dsum[aligned(r, tok), :]
    for i, p in enumerate(peers):
        back[i].wait()
        normal[:, aligned(p, width)] = drecv[i].astype(F32)
    onward(2, 2)
    onward(3, 1)
    out_last()

    def close(i):
        p = order[i]
        units[i][3]()
        q_out[:, aligned(p, qg)] = qkv_sum[p, :, :qg]
        k_out[:, aligned(p, kg)] = qkv_sum[p, :, qg : qg + kg]
        v_out[:, aligned(p, kg)] = qkv_sum[p, :, qg + kg :]

    close(0)
    close(1)
    onward(3, 2)
    close(2)
    close(3)
    for copy in fifths + thirds:
        copy.wait()


def grad_qkv_line(
    d_q, d_keys, d_values, key_lin, cos, sin, key_gain, wq, wk, wv, cols_t, cols, out_part, small, gain
):
    rows, head = key_lin.shape
    group = d_q.shape[1] + 2 * head
    tok = rows // 4
    width = wq.shape[0]
    piece = (width // 8, group)
    out_piece = out_part.shape[1:]
    small_piece = small.shape[1:]
    return pl.pallas_call(
        dgrad_line_kernel,
        out_shape=(
            jax.ShapeDtypeStruct((tok, 4 * width), F32),
            jax.ShapeDtypeStruct((width // 8, wq.shape[1]), F32),
            jax.ShapeDtypeStruct((width // 8, wk.shape[1]), F32),
            jax.ShapeDtypeStruct((width // 8, wv.shape[1]), F32),
            jax.ShapeDtypeStruct(out_piece, F32),
            jax.ShapeDtypeStruct(small.shape, F32),
            jax.ShapeDtypeStruct((4, 8, width), F32),
        ),
        in_specs=[VMEM_SPEC] * 7 + [ANY_SPEC] * 6 + [VMEM_SPEC] * 2,
        out_specs=(VMEM_SPEC,) * 7,
        scratch_shapes=[
            pltpu.VMEM((rows, group), BF16),
            pltpu.VMEM((2, 2, 4 * (tok - CMAX), head), F32),
            pltpu.VMEM((2, 4 * (tok - CMAX), head), F32),
            pltpu.SemaphoreType.DMA((1,)),
            pltpu.SemaphoreType.DMA((1,)),
        ]
        + [pltpu.VMEM(a.shape, BF16) for a in (wq, wk, wv, cols_t, cols, out_part)]
        + [
            pltpu.SemaphoreType.DMA((6,)),
            pltpu.VMEM((4, *piece), F32),
            pltpu.VMEM((8, 4, *piece), BF16),
            pltpu.VMEM((3, rows, group), BF16),
            pltpu.VMEM((rows, width), F32),
            pltpu.VMEM((3, tok, width), BF16),
            pltpu.VMEM((3, tok, width), BF16),
            pltpu.VMEM((4, *out_piece), BF16),
            pltpu.VMEM((3, *out_piece), BF16),
            pltpu.VMEM((2, 4, *out_piece), BF16),
            pltpu.VMEM((4, 4, *piece), BF16),
            pltpu.VMEM((4, 3, *piece), BF16),
            pltpu.VMEM((4, 2, 4, *piece), BF16),
            pltpu.VMEM((7, *small_piece), F32),
            pltpu.VMEM((1, *small_piece), F32),
            pltpu.VMEM((3, *small_piece), F32),
            pltpu.VMEM((8, width), F32),
            pltpu.VMEM((7, 8, width), F32),
            pltpu.SemaphoreType.DMA((6,)),
            pltpu.SemaphoreType.DMA((6,)),
        ]
        + [pltpu.SemaphoreType.DMA((n,)) for n in (3, 3, 7, 7, 3, 3, 7, 7, 7, 7, 3, 3)]
        + LINE_SEMS
        + [
            pltpu.SemaphoreType.DMA((4, 4)),
            pltpu.SemaphoreType.DMA((4, 4)),
            pltpu.SemaphoreType.DMA((4, 2, 4)),
            pltpu.SemaphoreType.DMA((4, 2, 4)),
        ],
        compiler_params=params(10),
        name="dqkv_line_exchange",
    )(
        d_q, d_keys, d_values, key_lin, cos, sin, key_gain, wq, wk, wv, cols_t, cols, out_part, small, gain
    )


def masks_of(block, own_length, slots, prompt_block, prompt_len, column, keys):
    slot = lax.broadcasted_iota(jnp.int32, (slots, keys), 0)
    key = lax.broadcasted_iota(jnp.int32, (slots, keys), 1)
    is_prompt = slot < prompt_block
    position = (column * 4 + block) * prompt_block + slot
    sees_prompt = (key < prompt_len) & (jnp.logical_not(is_prompt) | (key <= position))
    cont = key - prompt_len
    sees_cont = (
        (key >= prompt_len)
        & jnp.logical_not(is_prompt)
        & (cont <= slot - prompt_block)
        & (cont < own_length)
    )
    return sees_prompt | sees_cont


def attention_fwd_kernel(
    prompt_len, lengths, lin, gain, cos, sin, keys, values, queries, attn, q_all, score_all, low_all
):
    block = pl.program_id(0)
    slots = lin.shape[0]
    head = gain.shape[1]
    e = lax.axis_index("expert")
    own_length = lengths[block * lax.axis_size("expert") + e]
    allowed = masks_of(block, own_length, slots, slots - CMAX, prompt_len, e % 2, keys.shape[1])
    scale = head ** (-0.5)
    k, v = keys[0], values[0]
    c, s, g = cos[0], sin[0], gain[...]
    heads = lin.shape[1] // head
    parts = [slice(h * head, (h + 1) * head) for h in range(heads)]
    rows = [slice(h * slots, (h + 1) * slots) for h in range(heads)]
    for h in range(heads):
        x = lin[:, parts[h]]
        x = x * lax.rsqrt(jnp.mean(x * x, axis=-1, keepdims=True) + norm_eps) * g
        q = (x * c + pltpu.roll(x, head // 2, 1) * s).astype(BF16)
        queries[:, parts[h]] = q
        q_all[rows[h]] = q
    score_all[...] = dot_nt(q_all[...], k)
    for h in range(heads):
        score = jnp.where(allowed, score_all[rows[h]] * scale, -jnp.inf)
        peak = jnp.max(score, axis=-1, keepdims=True)
        exponent = jnp.exp(score - peak)
        low_all[rows[h]] = (exponent * (1.0 / jnp.sum(exponent, axis=-1, keepdims=True))).astype(BF16)
    out = dot_nn(low_all[...], v)
    for h in range(heads):
        attn[:, parts[h]] = out[rows[h]].astype(BF16)


def attention_fwd(lengths, lin, gain, cos, sin, keys, values, prompt_len):
    blocks, total_keys, head = keys.shape
    slots = lin.shape[0] // blocks
    width = lin.shape[1] - 2 * head
    row = pl.BlockSpec((slots, width), lambda i, *_: (i, 0))
    table = pl.BlockSpec((1, slots, head), lambda i, *_: (i, 0, 0))
    kv = pl.BlockSpec((1, total_keys, head), lambda i, *_: (i, 0, 0))
    one = pl.BlockSpec((1, head), lambda i, *_: (0, 0))
    return pl.pallas_call(
        functools.partial(attention_fwd_kernel, prompt_len),
        grid_spec=pltpu.PrefetchScalarGridSpec(
            num_scalar_prefetch=1,
            grid=(blocks,),
            in_specs=[row, one, table, table, kv, kv],
            out_specs=[row, row],
            scratch_shapes=[
                pltpu.VMEM((slots * width // head, head), BF16),
                pltpu.VMEM((slots * width // head, total_keys), F32),
                pltpu.VMEM((slots * width // head, total_keys), BF16),
            ],
        ),
        out_shape=(
            jax.ShapeDtypeStruct((lin.shape[0], width), BF16),
            jax.ShapeDtypeStruct((lin.shape[0], width), BF16),
        ),
        compiler_params=params(),
        name="attention_fwd",
    )(lengths, lin, gain, cos, sin, keys, values)


def attention_bwd_kernel(
    prompt_len, lengths, lin, queries, d_attn, gain, cos, sin, keys, values, attn_t, d_branch,
    d_lin, d_keys, d_values, d_gain, out_part,
    q_all, d_all, score_all, d_probs_all, low_all, d_score_all, d_q_all,
):
    block = pl.program_id(0)
    slots = lin.shape[0]
    head = gain.shape[1]
    e = lax.axis_index("expert")
    own_length = lengths[block * lax.axis_size("expert") + e]
    allowed = masks_of(block, own_length, slots, slots - CMAX, prompt_len, e % 2, keys.shape[1])
    scale = head ** (-0.5)
    k, v = keys[0], values[0]
    c, s, g = cos[0], sin[0], gain[...]
    heads = lin.shape[1] // head
    parts = [slice(h * head, (h + 1) * head) for h in range(heads)]
    rows = [slice(h * slots, (h + 1) * slots) for h in range(heads)]
    for h in range(heads):
        q_all[rows[h]] = queries[:, parts[h]]
        d_all[rows[h]] = d_attn[:, parts[h]]
    score_all[...] = dot_nt(q_all[...], k)
    d_probs_all[...] = dot_nt(d_all[...], v)
    for h in range(heads):
        score = jnp.where(allowed, score_all[rows[h]] * scale, -jnp.inf)
        peak = jnp.max(score, axis=-1, keepdims=True)
        exponent = jnp.exp(score - peak)
        probs = exponent * (1.0 / jnp.sum(exponent, axis=-1, keepdims=True))
        d_probs = d_probs_all[rows[h]]
        inner = jnp.sum(probs * d_probs, axis=-1, keepdims=True)
        low_all[rows[h]] = probs.astype(BF16)
        d_score_all[rows[h]] = (probs * (d_probs - inner)).astype(BF16)
    d_q_all[...] = dot_nn(d_score_all[...], k)
    d_keys[0] = dot_tn(d_score_all[...], q_all[...]) * scale
    d_values[0] = dot_tn(low_all[...], d_all[...])
    for n in range(2):
        half = slice(n * out_part.shape[1] // 2, (n + 1) * out_part.shape[1] // 2)
        out_part[:, half] = dot_nn(attn_t[...], d_branch[:, half]).astype(BF16)
    gain_total = jnp.zeros((8, head), F32)
    for h in range(heads):
        d_q = d_q_all[rows[h]] * scale
        turned = d_q * c + pltpu.roll(d_q * s, head // 2, 1)
        x = lin[:, parts[h]]
        inverse = lax.rsqrt(jnp.mean(x * x, axis=-1, keepdims=True) + norm_eps)
        unit = x * inverse
        pairs = turned * unit
        for j in range(slots // 8):
            gain_total = gain_total + pairs[j * 8 : (j + 1) * 8]
        weighted = turned * g
        d_lin[:, parts[h]] = (
            inverse * (weighted - unit * jnp.mean(weighted * unit, axis=-1, keepdims=True))
        ).astype(BF16)
    d_gain[0] = gain_total


def attention_bwd(
    lengths, lin, queries, d_attn, gain, cos, sin, keys, values, attn_t, d_branch, prompt_len
):
    blocks, total_keys, head = keys.shape
    slots = lin.shape[0] // blocks
    width = lin.shape[1] - 2 * head
    row = pl.BlockSpec((slots, width), lambda i, *_: (i, 0))
    table = pl.BlockSpec((1, slots, head), lambda i, *_: (i, 0, 0))
    kv = pl.BlockSpec((1, total_keys, head), lambda i, *_: (i, 0, 0))
    step = d_branch.shape[1] // blocks
    one = pl.BlockSpec((1, head), lambda i, *_: (0, 0))
    return pl.pallas_call(
        functools.partial(attention_bwd_kernel, prompt_len),
        grid_spec=pltpu.PrefetchScalarGridSpec(
            num_scalar_prefetch=1,
            grid=(blocks,),
            in_specs=[row, row, row, one, table, table, kv, kv]
            + [
                pl.BlockSpec(attn_t.shape, lambda i, *_: (0, 0)),
                pl.BlockSpec((d_branch.shape[0], step), lambda i, *_: (0, i)),
            ],
            out_specs=[
                row,
                kv,
                kv,
                pl.BlockSpec((1, 8, head), lambda i, *_: (i, 0, 0)),
                pl.BlockSpec((attn_t.shape[0], step), lambda i, *_: (0, i)),
            ],
            scratch_shapes=[
                pltpu.VMEM((slots * width // head, head), BF16),
                pltpu.VMEM((slots * width // head, head), BF16),
                pltpu.VMEM((slots * width // head, total_keys), F32),
                pltpu.VMEM((slots * width // head, total_keys), F32),
                pltpu.VMEM((slots * width // head, total_keys), BF16),
                pltpu.VMEM((slots * width // head, total_keys), BF16),
                pltpu.VMEM((slots * width // head, head), F32),
            ],
        ),
        out_shape=(
            jax.ShapeDtypeStruct((lin.shape[0], width), BF16),
            jax.ShapeDtypeStruct(keys.shape, F32),
            jax.ShapeDtypeStruct(values.shape, F32),
            jax.ShapeDtypeStruct((blocks, 8, head), F32),
            jax.ShapeDtypeStruct((attn_t.shape[0], d_branch.shape[1]), BF16),
        ),
        compiler_params=params(),
        name="attention_bwd",
    )(lengths, lin, queries, d_attn, gain, cos, sin, keys, values, attn_t, d_branch)


def partner(shard, axis, bit):
    return lax.ppermute(shard, axis, [(i, i ^ 1 << bit) for i in range(lax.axis_size(axis))])


def root_mean_scale(value_rows, gain_vec):
    return (
        value_rows
        * lax.rsqrt(jnp.mean(value_rows * value_rows, axis=-1, keepdims=True) + norm_eps)
        * gain_vec
    )


def contract(left_side, right_side, left_dim, right_dim):
    return lax.dot_general(
        left_side,
        right_side,
        (((left_dim,), (right_dim,)), ((), ())),
        preferred_element_type=F32,
    )


def plane_order(z):
    upper, odd = z // 2, z % 2
    return [z, z + 1 - 2 * upper, 2 + upper - 2 * odd, 3 - 3 * upper]


def world(with_diag):
    r, e = lax.axis_index("dp"), lax.axis_index("expert")
    z, core = e // 2, e % 2
    near, far = r ^ 1, r ^ 2
    devices = [(near, e), (far, e), (r, e ^ 1)]
    devices += [(r, lax.rem(z + j, 4) * 2 + core) for j in (1, 2, 3)]
    return r, e, z, core, near, far, devices


def everyone():
    me = lax.axis_index("dp") * 8 + lax.axis_index("expert")
    return me, [lax.rem(me + j, 32) for j in range(1, 32)]


def scatter_rows(rows, rows_in, ss, rs):
    me, others = everyone()
    copies = start_all(
        [
            remote(rows.at[d], rows_in.at[me], ss.at[j], rs.at[j], (d // 8, lax.rem(d, 8)))
            for j, d in enumerate(others)
        ]
    )
    rows_in[me] = rows[me]
    return copies


def greet_everyone():
    greet([(d // 8, lax.rem(d, 8)) for d in everyone()[1]])


ROW_SEMS = [pltpu.SemaphoreType.DMA((31,)), pltpu.SemaphoreType.DMA((31,))]


def gather_world(mine, buf, zs, zr, ps, pr, ds, dr, before, group, done, greeting=None):
    r, e, z, core, near, far, greeted = world(True)
    half = mine.shape[0] // 2
    low, high = pl.ds(0, half), pl.ds(half, half)
    order = plane_order(z)
    if greeting is None:
        greet(greeted)
    else:
        greeting()

    def slot(q, b, c):
        return q * 8 + b * 2 + c

    buf[slot(r, z, core)] = mine[...]
    diag = r ^ 3
    plane, pairs, lines = {}, {}, []

    def hand(k, i, q):
        at = slot(q, order[k], core)
        copy = remote(buf.at[at], buf.at[at], ds.at[k, i], dr.at[k, i], (r, e ^ 1))
        copy.start()
        pairs[k, i] = copy

    def issue(k):
        b = order[k]
        at = slot(r, b, core)
        for side, cond, to in (
            (0, (b <= z) & (z < 3), jnp.minimum(z + 1, 3)),
            (1, (b >= z) & (z > 0), jnp.maximum(z - 1, 0)),
        ):
            copy = remote(buf.at[at], buf.at[at], zs.at[k, side], zr.at[b], (r, to * 2 + core))
            lines.append((cond, copy))

            @pl.when(cond)
            def _():
                copy.start()

        mine_at, near_at, far_at = at, slot(near, b, core), slot(far, b, core)
        for i, (src, part, p) in enumerate(
            (
                (mine_at, low, near),
                (mine_at, high, far),
                (mine_at, high, near),
                (mine_at, low, far),
                (near_at, low, far),
                (far_at, high, near),
            )
        ):
            plane[k, i] = remote(
                buf.at[src, part], buf.at[src, part], ps.at[k, i], pr.at[k, i], (p, e)
            )
        for i in range(4):
            plane[k, i].start()
        hand(k, 0, r)

    def line_wait(k):
        b = order[k]
        at = slot(r, b, core)
        remote(buf.at[at], buf.at[at], zs.at[k, 0], zr.at[b], (r, e ^ 1)).wait_recv()
        issue(k)

    def passes(k):
        plane[k, 0].wait_recv()
        plane[k, 4].start()
        plane[k, 1].wait_recv()
        plane[k, 5].start()

    def finish(k):
        plane[k, 2].wait_recv()
        hand(k, 1, near)
        plane[k, 3].wait_recv()
        hand(k, 2, far)

    def corner(k):
        plane[k, 4].wait_recv()
        plane[k, 5].wait_recv()
        hand(k, 3, diag)

    who = (r, near, far, diag)

    def ready(k):
        before(k)
        for i in range(4):
            pairs[k, i].wait_recv()
        group(k, [(k * 4 + i, who[i] * 8 + order[k] * 2) for i in range(4)])

    issue(0)
    passes(0)
    line_wait(1)
    finish(0)
    passes(1)
    line_wait(2)
    corner(0)
    finish(1)
    ready(0)
    passes(2)
    line_wait(3)
    corner(1)
    finish(2)
    ready(1)
    passes(3)
    corner(2)
    finish(3)
    ready(2)
    corner(3)
    ready(3)
    done()
    for copy in plane.values():
        copy.wait_send()
    for copy in pairs.values():
        copy.wait_send()
    for cond, copy in lines:

        @pl.when(cond)
        def _():
            copy.wait_send()


def group_rows(k, room):
    return pl.ds(k * 4 * room, 4 * room)


GATHER_SEMS = [
    pltpu.SemaphoreType.DMA((4, 2)),
    pltpu.SemaphoreType.DMA((4,)),
    pltpu.SemaphoreType.DMA((4, 6)),
    pltpu.SemaphoreType.DMA((4, 6)),
    pltpu.SemaphoreType.DMA((4, 4)),
    pltpu.SemaphoreType.DMA((4, 4)),
]


def selector(row, room):
    ids = lax.broadcasted_iota(jnp.int32, (room, row.shape[1]), 0).astype(F32)
    return jnp.where(ids == row, 1.0, 0.0).astype(BF16)


def experts_fwd_kernel(
    capacity, mine, gate_rows, wg, wu, wd, pos, x_out, y_out, g_out, u_out, o_out, hid_out, gate_out,
    buf, wg_v, wu_v, wd_v, x_v, y_v, g_v, u_v, o_v, hid_v, gate_v, gate_in, local, rs, rr, *sems,
):
    model = wg.shape[0]
    rows_in = mine.shape[0]
    room = x_v.shape[0] // 4
    loads = start_all(
        [
            pltpu.make_async_copy(a, b, local.at[0, i])
            for i, (a, b) in enumerate(((wg, wg_v), (wu, wu_v), (wd, wd_v)))
        ]
    )
    leaving = {g: [] for g in range(4)}
    scattered = []

    def greeting():
        greet_everyone()
        scattered.extend(scatter_rows(gate_rows, gate_in, rs, rr))

    def leave(g, pairs):
        kept = group_rows(g, room)
        leaving[g].extend(
            start_all(
                [
                    pltpu.make_async_copy(v, o.at[kept], local.at[g % 2, i])
                    for i, v, o in pairs
                ]
            )
        )

    def before(g):
        wait_all(loads)
        wait_all(scattered)
        if g > 0:
            wait_all(leaving[g - 1])

    upto = jnp.where(
        lax.broadcasted_iota(jnp.int32, (rows_in, rows_in), 0)
        <= lax.broadcasted_iota(jnp.int32, (rows_in, rows_in), 1),
        1.0,
        0.0,
    ).astype(BF16)
    line = lax.broadcasted_iota(jnp.int32, (16, rows_in), 0)

    def pick(at, s, start):
        rows = pl.ds(start, room)
        sels = []
        gate = jnp.zeros((room, 1), F32)
        for c in range(2):
            row = jnp.broadcast_to(gate_in[s + c], (16, rows_in))
            named = jnp.where(row > 0.0, 1.0, 0.0)
            place = (dot_nn(named.astype(BF16), upto) + (c * capacity)) * named - 1.0
            pos[at * 2 + c] = place[:1]
            sels.append(selector(place[:1], room))
            top = row.astype(BF16).astype(F32)
            parts = jnp.where(line == 0, top, jnp.where(line == 1, row - top, 0.0)).astype(BF16)
            gate = gate + jnp.sum(dot_nt(sels[c], parts), axis=-1, keepdims=True)
        for c in range(4):
            n = slice(c * model // 4, (c + 1) * model // 4)
            x_v[rows, n] = (dot_nn(sels[0], buf[s, :, n]) + dot_nn(sels[1], buf[s + 1, :, n])).astype(BF16)
        gate_v[rows, :] = jnp.broadcast_to(gate, (room, 128))

    def group(g, blocks):
        for j, (at, s) in enumerate(blocks):
            pick(at, s, j * room)
        leave(g, ((0, x_v, x_out), (1, gate_v, gate_out)))

        def first(c, carry):
            n = aligned(c, 256)
            x = x_v[...]
            gates = dot_nn(x, wg_v[:, n])
            u = dot_nn(x, wu_v[:, n])
            g_v[:, n] = gates.astype(BF16)
            u_v[:, n] = u.astype(BF16)
            hid_v[:, n] = (gates / (1.0 + jnp.exp(-gates)) * u).astype(BF16)
            return carry

        lax.fori_loop(0, wg.shape[1] // 256, first, 0)
        leave(g, ((2, g_v, g_out), (3, u_v, u_out), (4, hid_v, hid_out)))

        def second(c, carry):
            n = aligned(c, 256)
            o = dot_nn(hid_v[...], wd_v[:, n]).astype(BF16)
            o_v[:, n] = o
            y_v[:, n] = (o.astype(F32) * gate_v[:, :1]).astype(BF16)
            return carry

        lax.fori_loop(0, model // 256, second, 0)
        leave(g, ((5, o_v, o_out), (6, y_v, y_out)))

    def done():
        for copies in leaving.values():
            wait_all(copies)

    gather_world(mine, buf, *sems, before, group, done, greeting)


def experts_fwd(mine, gate_rows, wg, wu, wd, capacity, room):
    rows, width = mine.shape
    model, ff = wg.shape
    group = 4 * room
    wide = jax.ShapeDtypeStruct((16 * room, model), BF16)
    thin = jax.ShapeDtypeStruct((16 * room, ff), BF16)
    pos, x, y, g, u, o, hidden, gates = pl.pallas_call(
        functools.partial(experts_fwd_kernel, capacity),
        out_shape=(
            jax.ShapeDtypeStruct((32, 1, rows), F32),
            wide,
            wide,
            thin,
            thin,
            wide,
            thin,
            jax.ShapeDtypeStruct((16 * room, 128), F32),
        ),
        in_specs=[VMEM_SPEC, VMEM_SPEC, ANY_SPEC, ANY_SPEC, ANY_SPEC],
        out_specs=(VMEM_SPEC,) + (ANY_SPEC,) * 7,
        scratch_shapes=[
            pltpu.VMEM((32, rows, width), BF16),
            pltpu.VMEM((model, ff), BF16),
            pltpu.VMEM((model, ff), BF16),
            pltpu.VMEM((ff, model), BF16),
            pltpu.VMEM((group, model), BF16),
            pltpu.VMEM((group, model), BF16),
            pltpu.VMEM((group, ff), BF16),
            pltpu.VMEM((group, ff), BF16),
            pltpu.VMEM((group, model), BF16),
            pltpu.VMEM((group, ff), BF16),
            pltpu.VMEM((group, 128), F32),
            pltpu.VMEM((32, 1, rows), F32),
            pltpu.SemaphoreType.DMA((2, 7)),
        ]
        + ROW_SEMS
        + GATHER_SEMS,
        compiler_params=params(6),
        name="experts_fwd",
    )(mine, gate_rows, wg, wu, wd)
    return pos, x, y, (g, u, o, hidden, gates)


def experts_bwd_kernel(
    mine, pos, g_in, u_in, o_in, gate_in, wg, wu, wd, d_gates, y_out, d_copy_out, dg_out, du_out,
    buf, wg_v, wu_v, wd_v, g_v, u_v, o_v, gate_v, y_v, d_copy_v, dg_v, du_v,
    local, ins, *sems,
):
    model, ff = wg.shape
    room = d_copy_v.shape[0] // 4
    loads = start_all(
        [
            pltpu.make_async_copy(a, b, local.at[0, i])
            for i, (a, b) in enumerate(((wg, wg_v), (wu, wu_v), (wd, wd_v)))
        ]
    )
    leaving, coming = {g: [] for g in range(4)}, {}

    def fetch(g):
        kept = group_rows(g, room)
        coming[g] = start_all(
            [
                pltpu.make_async_copy(a.at[kept], v.at[g % 2], ins.at[g % 2, i])
                for i, (a, v) in enumerate(
                    ((g_in, g_v), (u_in, u_v), (o_in, o_v), (gate_in, gate_v))
                )
            ]
        )

    fetch(0)

    def leave(g, pairs):
        kept = group_rows(g, room)
        leaving[g].extend(
            start_all(
                [
                    pltpu.make_async_copy(v, o.at[kept], local.at[g % 2, i])
                    for i, v, o in pairs
                ]
            )
        )

    def before(g):
        wait_all(loads)
        wait_all(coming[g])
        if g + 1 < 4:
            fetch(g + 1)
        if g > 0:
            wait_all(leaving[g - 1])

    def pick(slot, at, s, start):
        rows = pl.ds(start, room)
        sels = [selector(pos[at * 2 + c], room) for c in range(2)]
        gate = gate_v[slot, rows, :1]
        inner = jnp.zeros((room, 1), F32)
        for c in range(4):
            n = slice(c * model // 4, (c + 1) * model // 4)
            picked = dot_nn(sels[0], buf[s, :, n]) + dot_nn(sels[1], buf[s + 1, :, n])
            d_copy_v[rows, n] = (gate * picked).astype(BF16)
            inner = inner + jnp.sum(picked * o_v[slot, rows, n].astype(F32), axis=-1, keepdims=True)
        top = inner.astype(BF16).astype(F32)
        rest = inner - top
        lane = lax.broadcasted_iota(jnp.int32, (room, 128), 1)
        parts = jnp.where(lane == 0, top, jnp.where(lane == 1, rest, 0.0)).astype(BF16)
        for c in range(2):
            both = dot_tn(parts, sels[c])
            d_gates[s + c] = both[:1] + both[1:2]

    def group(g, blocks):
        slot = g % 2
        for j, (at, s) in enumerate(blocks):
            pick(slot, at, s, j * room)
        leave(g, ((0, d_copy_v, d_copy_out),))

        def third(c, carry):
            n = aligned(c, 256)
            d_hidden = dot_nt(d_copy_v[...], wd_v[n, :])
            gates, u = g_v[slot, :, n].astype(F32), u_v[slot, :, n].astype(F32)
            s = 1.0 / (1.0 + jnp.exp(-gates))
            dg_v[:, n] = (d_hidden * u * s * (1.0 + gates * (1.0 - s))).astype(BF16)
            du_v[:, n] = (d_hidden * gates * s).astype(BF16)
            return carry

        lax.fori_loop(0, ff // 256, third, 0)
        leave(g, ((1, dg_v, dg_out), (2, du_v, du_out)))

        def fourth(c, carry):
            n = aligned(c, 256)
            y_v[:, n] = (
                dot_nt(dg_v[...], wg_v[n, :]) + dot_nt(du_v[...], wu_v[n, :])
            ).astype(BF16)
            return carry

        lax.fori_loop(0, model // 256, fourth, 0)
        leave(g, ((3, y_v, y_out),))

    def done():
        for copies in leaving.values():
            wait_all(copies)

    gather_world(mine, buf, *sems, before, group, done)


def experts_bwd(mine, pos, kept, wg, wu, wd, room):
    rows, width = mine.shape
    model, ff = wg.shape
    group = 4 * room
    return pl.pallas_call(
        experts_bwd_kernel,
        out_shape=(
            jax.ShapeDtypeStruct((32, 1, rows), F32),
            jax.ShapeDtypeStruct((16 * room, model), BF16),
            jax.ShapeDtypeStruct((16 * room, model), BF16),
            jax.ShapeDtypeStruct((16 * room, ff), BF16),
            jax.ShapeDtypeStruct((16 * room, ff), BF16),
        ),
        in_specs=[VMEM_SPEC, VMEM_SPEC] + [ANY_SPEC] * 7,
        out_specs=(VMEM_SPEC,) + (ANY_SPEC,) * 4,
        scratch_shapes=[
            pltpu.VMEM((32, rows, width), BF16),
            pltpu.VMEM((model, ff), BF16),
            pltpu.VMEM((model, ff), BF16),
            pltpu.VMEM((ff, model), BF16),
            pltpu.VMEM((2, group, ff), BF16),
            pltpu.VMEM((2, group, ff), BF16),
            pltpu.VMEM((2, group, model), BF16),
            pltpu.VMEM((2, group, 128), F32),
            pltpu.VMEM((group, model), BF16),
            pltpu.VMEM((group, model), BF16),
            pltpu.VMEM((group, ff), BF16),
            pltpu.VMEM((group, ff), BF16),
            pltpu.SemaphoreType.DMA((2, 4)),
            pltpu.SemaphoreType.DMA((2, 4)),
        ]
        + GATHER_SEMS,
        compiler_params=params(7),
        name="experts_bwd",
    )(mine, pos, *kept, wg, wu, wd)


def sum_world_kernel(with_rows, *refs):
    if with_rows:
        y_in, pos, rows_given, out, rows_out, *refs, rs, rr = refs
    else:
        y_in, pos, out, *refs = refs
    (
        y, local, psend, pair, half_near, half_far, full_near, full_far, lines,
        ds, dr, hs, hr, fs, fr, zs, zr,
    ) = refs
    r, e, z, core, near, far, greeted = world(True)
    rows, width = out.shape
    room = y.shape[1]
    half = rows // 2
    low, high = pl.ds(0, half), pl.ds(half, half)
    order = plane_order(z)[::-1]
    body_width = width // 512 * 512
    loads = loading(
        [(y_in.at[pl.ds(12 - 4 * k, 4)], y.at[pl.ds(12 - 4 * k, 4)]) for k in range(4)], local
    )
    if with_rows:
        greet_everyone()
        scattering = scatter_rows(rows_given, rows_out, rs, rr)
    else:
        greet(greeted)

    def for_columns(fn):
        def step(c, carry):
            fn(aligned(c, 512))
            return carry

        lax.fori_loop(0, body_width // 512, step, 0)
        if width > body_width:
            fn(pl.ds(body_width, width - body_width))

    def scattered(sel, k, i, n):
        return dot_tn(sel, y[(3 - k) * 4 + i, :, n])

    def select(k, i, c):
        return selector(pos[((3 - k) * 4 + i) * 2 + c], room)

    pairs, halves, fulls, moves = {}, {}, {}, []

    def stage_a(k):
        wait_all(loads[k])
        for i in (3, 1, 2, 0):
            at = k * 4 + i
            sel = select(k, i, 1 - core)

            def fill(n):
                psend[at, :, n] = scattered(sel, k, i, n).astype(BF16)

            for_columns(fill)
            copy = remote(psend.at[at], pair.at[at], ds.at[at], dr.at[at], (r, e ^ 1))
            copy.start()
            pairs[at] = copy
        for i in (3, 1, 2, 0):
            at = k * 4 + i
            sel = select(k, i, core)
            pairs[at].wait_recv()

            def add(n):
                value = scattered(sel, k, i, n) + pair[at, :, n].astype(F32)
                pair[at, :, n] = value.astype(BF16)

            for_columns(add)
            if i == 3:
                for side, (part, dst, p) in enumerate(
                    ((low, half_near, near), (high, half_far, far))
                ):
                    copy = remote(
                        pair.at[at, part], dst.at[k], hs.at[k, side], hr.at[k, side], (p, e)
                    )
                    copy.start()
                    halves[k, side] = copy

    def stage_b(k):
        for side, (i, part, src, dst, p) in enumerate(
            (
                (2, low, half_near, full_far, far),
                (1, high, half_far, full_near, near),
            )
        ):
            at = k * 4 + i
            halves[k, side].wait_recv()

            def add(n):
                value = pair[at, part, n].astype(F32) + src[k, :, n].astype(F32)
                pair[at, part, n] = value.astype(BF16)

            for_columns(add)
            copy = remote(pair.at[at], dst.at[k], fs.at[k, side], fr.at[k, side], (p, e))
            copy.start()
            fulls[k, side] = copy

    def stage_c(k):
        b = order[k]
        at = k * 4
        fulls[k, 0].wait_recv()
        fulls[k, 1].wait_recv()

        def add(n):
            out[:, n] = (
                pair[at, :, n].astype(F32)
                + full_near[k, :, n].astype(F32)
                + full_far[k, :, n].astype(F32)
            )

        for_columns(add)
        for side, cond in ((0, (b >= z) & (z > 0)), (1, (b <= z) & (z < 3))):

            @pl.when(cond)
            def _():
                remote(
                    lines.at[side, b], lines.at[side, b], zs.at[side, k], zr.at[side, b], (r, e ^ 1)
                ).wait_recv()

                def more(n):
                    out[:, n] = out[:, n] + lines[side, b, :, n].astype(F32)

                for_columns(more)

        if k < 3:

            def keep(n):
                pair[at, :, n] = out[:, n].astype(BF16)

            for_columns(keep)
            for side, cond, to in (
                (0, b > z, jnp.minimum(z + 1, 3)),
                (1, b < z, jnp.maximum(z - 1, 0)),
            ):
                copy = remote(
                    pair.at[at], lines.at[side, b], zs.at[side, k], zr.at[side, b], (r, to * 2 + core)
                )
                moves.append((cond, copy))

                @pl.when(cond)
                def _():
                    copy.start()

    stage_a(0)
    stage_a(1)
    stage_b(0)
    stage_a(2)
    stage_b(1)
    stage_c(0)
    stage_a(3)
    stage_b(2)
    stage_c(1)
    stage_b(3)
    stage_c(2)
    stage_c(3)
    for copies in (pairs, halves, fulls):
        for copy in copies.values():
            copy.wait_send()
    for cond, copy in moves:

        @pl.when(cond)
        def _():
            copy.wait_send()

    if with_rows:
        wait_all(scattering)


def sum_world(y, pos, rows, collective_id, given=None):
    width = y.shape[-1]

    def blocks(n, size):
        return pltpu.VMEM((n, size, width), BF16)

    extra = () if given is None else (given,)
    return pl.pallas_call(
        functools.partial(sum_world_kernel, len(extra) > 0),
        out_shape=(jax.ShapeDtypeStruct((rows, width), F32),)
        + tuple(jax.ShapeDtypeStruct(a.shape, F32) for a in extra),
        in_specs=[ANY_SPEC, VMEM_SPEC] + [VMEM_SPEC] * len(extra),
        out_specs=(VMEM_SPEC,) * (1 + len(extra)),
        scratch_shapes=[
            pltpu.VMEM(y.shape, BF16),
            pltpu.SemaphoreType.DMA((4,)),
            blocks(16, rows),
            blocks(16, rows),
            blocks(4, rows // 2),
            blocks(4, rows // 2),
            blocks(4, rows),
            blocks(4, rows),
            pltpu.VMEM((2, 4, rows, width), BF16),
            pltpu.SemaphoreType.DMA((16,)),
            pltpu.SemaphoreType.DMA((16,)),
            pltpu.SemaphoreType.DMA((4, 2)),
            pltpu.SemaphoreType.DMA((4, 2)),
            pltpu.SemaphoreType.DMA((4, 2)),
            pltpu.SemaphoreType.DMA((4, 2)),
            pltpu.SemaphoreType.DMA((2, 4)),
            pltpu.SemaphoreType.DMA((2, 4)),
        ]
        + (ROW_SEMS if extra else []),
        compiler_params=params(collective_id),
        name="sum_world",
    )(y, pos, *extra)


def expert_grads_kernel(x, d_gate, d_up, hidden, d_copy, gate_grad, up_grad, down_grad, hidden_t):
    @pl.when(pl.program_id(0) == 0)
    def _():
        hidden_t[...] = hidden[...].T

    rows = x[...].T
    gate_grad[...] = dot_nn(rows, d_gate[...])
    up_grad[...] = dot_nn(rows, d_up[...])
    down_grad[...] = dot_nn(hidden_t[...], d_copy[...])


def expert_grads(x, d_gate, d_up, hidden, d_copy):
    slots, model = x.shape
    ff = hidden.shape[1]
    step = 256
    whole = pl.BlockSpec((slots, ff), lambda i: (0, 0))
    columns = pl.BlockSpec((slots, step), lambda i: (0, i))
    return pl.pallas_call(
        expert_grads_kernel,
        grid=(model // step,),
        in_specs=[columns, whole, whole, whole, columns],
        out_specs=[
            pl.BlockSpec((step, ff), lambda i: (i, 0)),
            pl.BlockSpec((step, ff), lambda i: (i, 0)),
            pl.BlockSpec((ff, step), lambda i: (0, i)),
        ],
        out_shape=(
            jax.ShapeDtypeStruct((model, ff), F32),
            jax.ShapeDtypeStruct((model, ff), F32),
            jax.ShapeDtypeStruct((ff, model), F32),
        ),
        scratch_shapes=[pltpu.VMEM((ff, slots), BF16)],
        compiler_params=params(),
        name="expert_grads",
    )(x, d_gate, d_up, hidden, d_copy)


def experts_by_all_to_all(
    mixed, state, teacher, routes, valid_slot, valid_count, router_weight, gate_weight, up_weight, down_weight,
    devices, capacity, slots_all,
):
    tok_dev, model_width = mixed.shape
    top_count = routes.shape[1]
    ffn_width = gate_weight.shape[2]
    logits = jnp.dot(mixed, router_weight, preferred_element_type=jnp.float32)
    gates = jax.nn.softmax(jnp.take_along_axis(logits, routes, axis=1), axis=-1)
    rows_total = tok_dev * top_count
    expert_ids = routes.reshape(rows_total)
    live_rows = jnp.repeat(valid_slot, top_count)
    expert_range = jnp.arange(devices, dtype=jnp.int32)
    hit_table = ((expert_ids[:, None] == expert_range[None, :]) & live_rows[:, None]).astype(
        jnp.int32
    )
    earlier = jnp.cumsum(hit_table, axis=0) - hit_table
    position_in = jnp.sum(earlier * hit_table, axis=1)
    slot_index = jnp.where(live_rows, expert_ids * capacity + position_in, devices * capacity)
    row_of_slot = (
        jnp.full((devices * capacity + 1,), rows_total, jnp.int32)
        .at[slot_index]
        .set(jnp.arange(rows_total, dtype=jnp.int32))[: devices * capacity]
    )
    token_of_slot = jnp.where(row_of_slot < rows_total, row_of_slot // top_count, tok_dev)
    mixed_pad = jnp.concatenate([mixed, jnp.zeros((1, model_width), jnp.bfloat16)], axis=0)
    send_rows = mixed_pad[token_of_slot].reshape(devices, capacity, model_width)
    arrived = lax.all_to_all(send_rows, ("dp", "expert"), split_axis=0, concat_axis=0, tiled=True)
    sources = arrived.shape[0]
    items = arrived.shape[1]
    flat_in = arrived.reshape(sources * items, model_width)
    gate_pre = jnp.dot(flat_in, gate_weight[0], preferred_element_type=jnp.float32)
    up_pre = jnp.dot(flat_in, up_weight[0], preferred_element_type=jnp.float32)
    hidden_units = (jax.nn.silu(gate_pre) * up_pre).astype(jnp.bfloat16)
    produced = jnp.dot(hidden_units, down_weight[0], preferred_element_type=jnp.float32).astype(
        jnp.bfloat16
    )
    produced, gate_pre, up_pre, hidden_units, arrived = (
        produced.reshape(sources, items, model_width),
        gate_pre.reshape(sources, items, ffn_width),
        up_pre.reshape(sources, items, ffn_width),
        hidden_units.reshape(sources, items, ffn_width),
        arrived,
    )
    returned = lax.all_to_all(produced, ("dp", "expert"), split_axis=0, concat_axis=0, tiled=True)
    returned_pad = jnp.concatenate(
        [
            returned.reshape(devices * capacity, model_width),
            jnp.zeros((1, model_width), jnp.bfloat16),
        ],
        axis=0,
    )
    copies = returned_pad[slot_index].reshape(tok_dev, top_count, model_width)
    layer_out = state + jnp.sum(gates[:, :, None] * copies, axis=1)
    live_tokens = valid_slot.astype(jnp.float32)[:, None]
    diff = (layer_out - teacher.astype(jnp.float32)) * live_tokens
    local_square = jnp.sum(diff * diff)
    d_out = 2.0 * slots_all * diff / valid_count
    d_gates = jnp.sum(d_out[:, None, :] * copies, axis=-1)
    d_chosen = gates * (d_gates - jnp.sum(gates * d_gates, axis=-1, keepdims=True))
    d_logits = jnp.sum(
        jnp.where(routes[:, :, None] == expert_range[None, None, :], d_chosen[:, :, None], 0.0),
        axis=1,
    ).astype(jnp.bfloat16)
    d_copies = (
        (gates[:, :, None] * d_out[:, None, :])
        .astype(jnp.bfloat16)
        .reshape(rows_total, model_width)
    )
    d_copies_pad = jnp.concatenate([d_copies, jnp.zeros((1, model_width), jnp.bfloat16)], axis=0)
    d_send = d_copies_pad[row_of_slot].reshape(devices, capacity, model_width)
    d_arrived = lax.all_to_all(d_send, ("dp", "expert"), split_axis=0, concat_axis=0, tiled=True)
    flat_d = d_arrived.reshape(-1, model_width)
    flat_in = arrived.reshape(-1, model_width)
    flat_gate = gate_pre.reshape(-1, ffn_width)
    flat_up = up_pre.reshape(-1, ffn_width)
    flat_hidden = hidden_units.reshape(-1, ffn_width)
    d_hidden = contract(flat_d, down_weight[0], 1, 1)
    sigmoid_gate = jax.nn.sigmoid(flat_gate)
    d_gate = (d_hidden * flat_up * sigmoid_gate * (1.0 + flat_gate * (1.0 - sigmoid_gate))).astype(
        jnp.bfloat16
    )
    d_up = (d_hidden * flat_gate * sigmoid_gate).astype(jnp.bfloat16)
    down_grad = contract(flat_hidden, flat_d, 0, 0)[None]
    gate_grad = contract(flat_in, d_gate, 0, 0)[None]
    up_grad = contract(flat_in, d_up, 0, 0)[None]
    d_in = (contract(d_gate, gate_weight[0], 1, 1) + contract(d_up, up_weight[0], 1, 1)).astype(
        jnp.bfloat16
    )
    d_returned = lax.all_to_all(
        d_in.reshape(devices, capacity, model_width),
        ("dp", "expert"),
        split_axis=0,
        concat_axis=0,
        tiled=True,
    )
    d_returned_pad = jnp.concatenate(
        [
            d_returned.reshape(devices * capacity, model_width),
            jnp.zeros((1, model_width), jnp.bfloat16),
        ],
        axis=0,
    )
    d_mixed = jnp.sum(
        d_returned_pad[slot_index].reshape(tok_dev, top_count, model_width),
        axis=1,
        dtype=jnp.float32,
    )
    d_mixed = d_mixed + contract(d_logits, router_weight, 1, 1)
    router_local = contract(d_logits, mixed, 0, 0)
    return layer_out, d_out, d_mixed, local_square, router_local, (gate_grad, up_grad, down_grad)


def experts_by_gather(
    mixed, state, teacher, routes, valid_slot, valid_count, router_weight,
    gate_weight, up_weight, down_weight, devices, capacity, slots_all,
):
    tok_dev, model_width = mixed.shape
    room = -(-2 * capacity // 16) * 16
    expert_range = jnp.arange(devices, dtype=jnp.int32)
    logits = jnp.dot(mixed, router_weight, preferred_element_type=F32)
    chosen = jnp.any(routes[:, :, None] == expert_range[None, None], axis=1)
    gates = jax.nn.softmax(jnp.where(chosen, logits, -jnp.inf), axis=-1)
    live_gates = jnp.where(valid_slot[:, None], gates, 0.0)
    gate_rows = live_gates.T[:, None]
    pos, x_rows, y_rows, kept = experts_fwd(
        mixed, gate_rows, gate_weight[0], up_weight[0], down_weight[0], capacity, room
    )
    layer_out = state + sum_world(y_rows.reshape(16, room, model_width), pos, tok_dev, 8)[0]
    live_tokens = valid_slot.astype(F32)[:, None]
    diff = (layer_out - teacher.astype(F32)) * live_tokens
    local_square = jnp.sum(diff * diff)
    d_out = 2.0 * slots_all * diff / valid_count
    hidden = kept[3]
    d_gates, d_rows, d_copy, d_gate, d_up = experts_bwd(
        d_out.astype(BF16), pos, kept[:3] + kept[4:], gate_weight[0], up_weight[0], down_weight[0], room
    )
    back, d_gates = sum_world(d_rows.reshape(16, room, model_width), pos, tok_dev, 9, d_gates)
    d_gates = d_gates[:, 0].T

    grad_rows = (x_rows, d_gate, d_up, hidden, d_copy)
    d_logits = (gates * (d_gates - jnp.sum(gates * d_gates, axis=-1, keepdims=True))).astype(BF16)
    d_mixed = back + contract(d_logits, router_weight, 1, 1)
    router_local = contract(d_logits, mixed, 0, 0)
    return layer_out, d_out, d_mixed, local_square, router_local, grad_rows


def head_rope(linear, gain_vec, cos, sin):
    value = root_mean_scale(linear, gain_vec)
    half = value.shape[-1] // 2
    return value * cos + jnp.roll(value, half, axis=-1) * sin


def body(
    tokens,
    teacher,
    routes,
    cont_lengths,
    query_weight,
    key_projection,
    value_projection,
    output_weight,
    router_weight,
    gate_weight,
    up_weight,
    down_weight,
    input_gain,
    post_gain,
    query_gain,
    key_gain,
):
    n_dp = lax.axis_size("dp")
    n_owner = lax.axis_size("expert")
    devices = n_dp * n_owner
    rank_dp = lax.axis_index("dp")
    rank_owner = lax.axis_index("expert")
    flat_rank = rank_dp * n_owner + rank_owner
    column = rank_owner % 2
    first_column = column == 0
    tok_dev, model_width = tokens.shape
    top_count = routes.shape[1]
    head_dim = query_gain.shape[0]
    kv_width = key_projection.shape[1]
    query_width = query_weight.shape[1]
    query_group = query_width // n_dp
    assert n_dp == 4 and kv_width == n_dp * head_dim
    prompt_block = tok_dev - CMAX
    half_prompt = n_dp * prompt_block
    prompt_len = 2 * half_prompt
    capacity = max(2, tok_dev * top_count * 5 // (4 * devices))
    slots_all = devices * tok_dev
    slot_ids = jnp.arange(tok_dev, dtype=jnp.int32)
    is_own = jnp.arange(devices, dtype=jnp.int32) == flat_rank
    own_length = jnp.sum(jnp.where(is_own, cont_lengths, 0))
    valid_slot = (slot_ids < prompt_block) | (slot_ids - prompt_block < own_length)
    valid_count = (devices * prompt_block + jnp.sum(cont_lengths)).astype(F32)
    tokens_float = tokens.astype(F32)

    block_ids = jnp.arange(n_dp, dtype=jnp.int32)[:, None]
    positions = jnp.where(
        slot_ids[None] < prompt_block,
        (column * n_dp + block_ids) * prompt_block + slot_ids[None],
        prompt_len + slot_ids[None] - prompt_block,
    )
    half_head = head_dim // 2
    frequency = rope_base ** (-(jnp.arange(half_head, dtype=F32) * 2.0) / head_dim)
    angles = positions.astype(F32)[:, :, None] * frequency
    cos_half, sin_half = jnp.cos(angles), jnp.sin(angles)
    cos = jnp.concatenate([cos_half, cos_half], axis=-1)
    sin = jnp.concatenate([-sin_half, sin_half], axis=-1)
    lin, normed_cols_t, normed_cols, key_lin, all_keys, all_values, inverse = project_qkv(
        tokens, input_gain[None], query_weight, key_projection, value_projection, key_gain[None], cos, sin
    )
    query_gain_row = query_gain[None]
    queries, attended = attention_fwd(
        cont_lengths, lin, query_gain_row, cos, sin, all_keys, all_values, prompt_len
    )
    state = tokens_float + project_out(attended, output_weight)
    mixed_float, second_norm_back = jax.vjp(root_mean_scale, state, post_gain)
    mixed = mixed_float.astype(BF16)
    sizes = (devices, capacity, slots_all)
    weights = (router_weight, gate_weight, up_weight, down_weight)
    if n_dp == 4 and n_owner == 8:
        moe = experts_by_gather(
            mixed, state, teacher, routes, valid_slot, valid_count, *weights, *sizes
        )
    else:
        moe = experts_by_all_to_all(
            mixed, state, teacher, routes, valid_slot, valid_count, *weights, *sizes
        )
    layer_out, d_out, d_mixed, local_square, router_local, grad_rows = moe
    d_state_norm, d_post_gain = second_norm_back(d_mixed)
    d_state = d_out + d_state_norm
    d_branch = d_state.astype(BF16)
    d_attended, d_branch_all, attended_t = grad_branch(d_branch, output_weight, attended)
    d_query_lin, d_keys, d_values, gain_parts, out_part = attention_bwd(
        cont_lengths, lin, queries, d_attended, query_gain_row, cos, sin, all_keys, all_values,
        attended_t, d_branch_all, prompt_len,
    )
    d_query_gain = jnp.sum(gain_parts, axis=(0, 1))
    width = query_weight.shape[0]
    group = query_group + 2 * head_dim
    rows_here = width // n_owner
    by_line = n_dp == 4 and n_owner == 8

    def packed(parts):
        small = jnp.concatenate([a.reshape(-1) for a in parts])
        piece_rows = -(-small.shape[0] // (8 * 8 * 128)) * 8
        small = jnp.pad(small, (0, 8 * piece_rows * 128 - small.shape[0]))
        return small.reshape(8, piece_rows, 128)

    out_part = out_part.reshape(n_owner, -1, model_width)
    weights = (query_weight, key_projection, value_projection)
    if by_line:

        def line(parts):
            flat = jnp.concatenate(parts)
            return jnp.pad(flat, (0, model_width - flat.shape[0]))[None]

        small = jnp.concatenate(
            [router_local, d_post_gain[None], line([d_query_gain]), line([local_square[None]])]
        )
        small_rows = -(-small.shape[0] // 8) * 8
        small = jnp.pad(small, ((0, small_rows - small.shape[0]), (0, 0)))
        small = small.reshape(small_rows, 8, -1).transpose(1, 0, 2)
        d_normed, query_grad, key_grad, value_grad, output_grad, small, input_gain_grad = grad_qkv_line(
            d_query_lin, d_keys, d_values, key_lin, cos, sin, key_gain[None],
            *weights, normed_cols_t, normed_cols, out_part, small, input_gain[None],
        )
        key_gain_grad = jnp.sum(input_gain_grad[:, 1, :head_dim], axis=0)
        input_gain_grad = input_gain_grad[:, 0].reshape(-1)
        sums = small.transpose(1, 0, 2).reshape(small_rows, model_width)
        at = router_local.shape[0]
        router_grad, post_gain_grad = sums[:at].T, sums[at]
        query_gain_grad = sums[at + 1, :head_dim]
        total_square = sums[at + 2, :1]
    else:
        _, key_back = jax.vjp(
            lambda a, b: head_rope(a, b, cos, sin), key_lin.reshape(n_dp, tok_dev, head_dim), key_gain
        )
        prompt_grads = jnp.stack(
            [jnp.sum(d_keys[:, :prompt_len], axis=0), jnp.sum(d_values[:, :prompt_len], axis=0)]
        )
        mine_part = jnp.where(first_column, prompt_grads[:, :half_prompt], prompt_grads[:, half_prompt:])
        their_part = jnp.where(first_column, prompt_grads[:, half_prompt:], prompt_grads[:, :half_prompt])
        own_prompt = (mine_part + partner(their_part, "expert", 0)).reshape(
            2, n_dp, prompt_block, head_dim
        )
        d_key_post = jnp.concatenate([own_prompt[0], d_keys[:, prompt_len:]], axis=1)
        d_value_lin = jnp.concatenate([own_prompt[1], d_values[:, prompt_len:]], axis=1)
        d_key_float, d_key_gain = key_back(d_key_post)
        rows = n_dp * tok_dev
        d_lin = jnp.concatenate(
            [
                d_query_lin,
                d_key_float.astype(BF16).reshape(rows, head_dim),
                d_value_lin.astype(BF16).reshape(rows, head_dim),
            ],
            axis=1,
        )
        small_parts = [router_local, d_post_gain, d_query_gain, d_key_gain, local_square[None]]
        d_normed, qkv_part, output_grad = grad_qkv(d_lin, *weights, normed_cols_t, out_part)
        small_parts.append(jnp.sum(d_normed * tokens_float * inverse[:, :1], axis=0))
        by_owner = (
            qkv_part.reshape(n_dp, n_owner, rows_here, group)
            .transpose(1, 0, 2, 3)
            .reshape(n_owner, n_dp * rows_here, group)
        )
        qkv_rows, small = last_sums(by_owner, packed(small_parts))
        qkv_rows = qkv_rows.reshape(n_dp, rows_here, group)

        def columns(start, size):
            part = qkv_rows[:, :, start : start + size]
            return part.transpose(1, 0, 2).reshape(rows_here, n_dp * size)

        query_grad = columns(0, query_group)
        key_grad = columns(query_group, head_dim)
        value_grad = columns(query_group + head_dim, head_dim)
        small = small.reshape(-1)
        starts = [0]
        for a in small_parts:
            starts.append(starts[-1] + a.size)
        sums = [small[i:j].reshape(a.shape) for a, i, j in zip(small_parts, starts, starts[1:])]
        router_grad, post_gain_grad, query_gain_grad, key_gain_grad, total_square, input_gain_grad = sums
        router_grad = router_grad.T
    inverse = inverse[:, :1]
    weighted = d_normed * input_gain
    along = jnp.mean(weighted * tokens_float, axis=-1, keepdims=True) * inverse * inverse
    tokens_grad = d_state + inverse * (weighted - tokens_float * along)
    if by_line:
        gate_grad, up_grad, down_grad = expert_grads(*grad_rows)
        gate_grad, up_grad, down_grad = gate_grad[None], up_grad[None], down_grad[None]
    else:
        gate_grad, up_grad, down_grad = grad_rows
    loss = total_square[0] / (valid_count * model_width)
    return (
        layer_out,
        loss,
        tokens_grad,
        query_grad,
        key_grad,
        value_grad,
        output_grad,
        router_grad,
        gate_grad,
        up_grad,
        down_grad,
        input_gain_grad,
        post_gain_grad,
        query_gain_grad,
        key_gain_grad,
    )


def solution(mesh):
    in_specs = (
        P(("dp", "expert"), None),
        P(("dp", "expert"), None),
        P(("dp", "expert"), None),
        P(),
        P("dp", None),
        P("dp", None),
        P("dp", None),
        P("dp", None),
        P(),
        P(("dp", "expert"), None, None),
        P(("dp", "expert"), None, None),
        P(("dp", "expert"), None, None),
        P(),
        P(),
        P(),
        P(),
    )
    out_specs = (
        P(("dp", "expert"), None),
        P(),
        P(("dp", "expert"), None),
        P(("dp", "expert"), None),
        P(("dp", "expert"), None),
        P(("dp", "expert"), None),
        P(("dp", "expert"), None),
        P(),
        P(("dp", "expert"), None, None),
        P(("dp", "expert"), None, None),
        P(("dp", "expert"), None, None),
        P(),
        P(),
        P(),
        P(),
    )
    return jax.shard_map(body, mesh=mesh, in_specs=in_specs, out_specs=out_specs, check_vma=False)
```

```python
import functools

import jax
import jax.numpy as jnp
from jax import lax
from jax.experimental import pallas as pl
from jax.experimental.pallas import tpu as pltpu
from jax.sharding import PartitionSpec as P

CMAX = 128
norm_eps = 1e-06
rope_base = 1000000.0
MESH = pl.DeviceIdType.MESH
F32 = jnp.float32
BF16 = jnp.bfloat16
VMEM_SPEC = pl.BlockSpec(memory_space=pltpu.VMEM)
ANY_SPEC = pl.BlockSpec(memory_space=pl.ANY)
VMEM_LIMIT = 56 * 1024 * 1024


def params(collective_id=None):
    return pltpu.CompilerParams(
        collective_id=collective_id,
        has_side_effects=collective_id is not None,
        vmem_limit_bytes=VMEM_LIMIT,
    )


def greet(devices):
    barrier = pltpu.get_barrier_semaphore()
    for device in devices:
        pl.semaphore_signal(barrier, inc=1, device_id=device, device_id_type=MESH)
    pl.semaphore_wait(barrier, len(devices))


def remote(src, dst, send_sem, recv_sem, device):
    return pltpu.make_async_remote_copy(
        src_ref=src,
        dst_ref=dst,
        send_sem=send_sem,
        recv_sem=recv_sem,
        device_id=device,
        device_id_type=MESH,
    )


def start_all(copies):
    for copy in copies:
        copy.start()
    return copies


def wait_all(copies):
    for copy in copies:
        copy.wait()
    copies.clear()


def loading(pairs, sems):
    return [start_all([pltpu.make_async_copy(a, b, sems.at[i])]) for i, (a, b) in enumerate(pairs)]


def aligned(index, size):
    return pl.ds(pl.multiple_of(index * size, size), size)


def dot_nn(a, b):
    return lax.dot_general(a, b, (((1,), (0,)), ((), ())), preferred_element_type=F32)


def dot_nt(a, b):
    return lax.dot_general(a, b, (((1,), (1,)), ((), ())), preferred_element_type=F32)


def dot_tn(a, b):
    return lax.dot_general(a, b, (((0,), (0,)), ((), ())), preferred_element_type=F32)


PEER_MASKS = (3, 1, 2)


def relay_sum(r, e, products, own, mine, send, half_in, full_in, hs, hr, fs, fr, step):
    near, far, diag = r ^ 1, r ^ 2, r ^ 3
    rows = mine.shape[0]
    half = rows // 2
    low, high = pl.ds(0, half), pl.ds(half, half)
    products(diag, send.at[2])
    relays = [
        remote(send.at[2, low], half_in.at[0], hs.at[0], hr.at[0], (near, e)),
        remote(send.at[2, high], half_in.at[1], hs.at[1], hr.at[1], (far, e)),
    ]
    for copy in relays:
        copy.start()
    parts = ((0, low, near), (1, high, far), (0, high, near), (1, low, far))
    fulls = [
        remote(send.at[i, part], full_in.at[i, part], fs.at[n], fr.at[n], (p, e))
        for n, (i, part, p) in enumerate(parts)
    ]
    products(near, send.at[0])
    fulls[0].start()
    products(far, send.at[1])
    fulls[1].start()
    for i, start, slot, n in ((1, 0, 0, 3), (0, half, 1, 2)):
        relays[slot].wait_recv()

        def add(c, carry):
            t = pl.ds(pl.multiple_of(start + c * step, step), step)
            value = send[i, t, :].astype(F32) + half_in[slot, aligned(c, step), :].astype(F32)
            send[i, t, :] = value.astype(BF16)
            return carry

        lax.fori_loop(0, half // step, add, 0)
        fulls[n].start()
    own()
    for n, (i, start) in enumerate(((0, 0), (1, half), (0, half), (1, 0))):
        fulls[n].wait_recv()

        def total(c, carry):
            t = pl.ds(pl.multiple_of(start + c * step, step), step)
            mine[t, :] = mine[t, :] + full_in[i, t, :].astype(F32)
            return carry

        lax.fori_loop(0, half // step, total, 0)
    for copy in relays + fulls:
        copy.wait_send()


def relay_scratch(rows, width):
    return [
        pltpu.VMEM((3, rows, width), BF16),
        pltpu.VMEM((2, rows // 2, width), BF16),
        pltpu.VMEM((2, rows, width), BF16),
        pltpu.SemaphoreType.DMA((2,)),
        pltpu.SemaphoreType.DMA((2,)),
        pltpu.SemaphoreType.DMA((4,)),
        pltpu.SemaphoreType.DMA((4,)),
    ]


def qkv_kernel(
    tok, tokens, in_gain, wq_in, wk_in, wv_in, gain, cos, sin,
    lin, cols_t, cols, key_lin, keys, values, inverse_out,
    normed, wq, wk, wv, own_kv, other_kv, local, asend, arecv, ksend, krecv, *relay,
):
    r, e = lax.axis_index("dp"), lax.axis_index("expert")
    peers = [r ^ m for m in PEER_MASKS]
    width = wq.shape[0]
    qg = wq.shape[1] // 4
    kg = wk.shape[1] // 4
    rows = cols.shape[0]
    loads = loading(((wq_in, wq), (wk_in, wk), (wv_in, wv)), local)
    value = tokens[...].astype(F32)
    inverse = lax.rsqrt(jnp.mean(value * value, axis=-1, keepdims=True) + norm_eps)
    normed[...] = (value * inverse * in_gain[...]).astype(BF16)
    inverse_out[...] = jnp.broadcast_to(inverse, inverse_out.shape)
    greet([(p, e) for p in peers] + [(r, e ^ 1)])
    first = []
    for i, p in enumerate(peers):
        copy = remote(
            normed.at[:, aligned(p, width)], cols.at[aligned(r, tok), :],
            asend.at[i], arecv.at[i], (p, e),
        )
        copy.start()
        first.append(copy)
    cols[aligned(r, tok), :] = normed[:, aligned(r, width)]
    for copy in first:
        copy.wait()
    for copies in loads:
        wait_all(copies)

    def products(p, dst):
        def chunk(c, carry):
            columns = pl.ds(pl.multiple_of(p * qg + c * 256, 256), 256)
            dst[:, aligned(c, 256)] = dot_nn(cols[...], wq[:, columns]).astype(dst.dtype)
            return carry

        lax.fori_loop(0, qg // 256, chunk, 0)
        dst[:, qg : qg + kg] = dot_nn(cols[...], wk[:, aligned(p, kg)]).astype(dst.dtype)
        dst[:, qg + kg :] = dot_nn(cols[...], wv[:, aligned(p, kg)]).astype(dst.dtype)

    def own():
        products(r, lin)
        cols_t[...] = cols[...].T

    relay_sum(r, e, products, own, lin, *relay, 32)
    core = e % 2
    head = gain.shape[1]
    prompt = tok - CMAX
    column = 4 * prompt
    for i in range(4):
        rows_i = slice(i * tok, (i + 1) * tok)
        x = lin[rows_i, qg : qg + kg]
        key_lin[rows_i, :] = x
        x = x * lax.rsqrt(jnp.mean(x * x, axis=-1, keepdims=True) + norm_eps) * gain[...]
        k = (x * cos[i] + pltpu.roll(x, head // 2, 1) * sin[i]).astype(BF16)
        v = lin[rows_i, qg + kg :].astype(BF16)
        for n, (part, out) in enumerate(((k, keys), (v, values))):
            own_kv[n, i * prompt : (i + 1) * prompt] = part[:prompt]
            out[i, 2 * column :] = part[prompt:]
    copy = remote(own_kv, other_kv, ksend.at[0], krecv.at[0], (r, e ^ 1))
    copy.start()
    for n, out in enumerate((keys, values)):
        for i in range(4):
            out[i, aligned(core, column)] = own_kv[n]
    copy.wait()
    for n, out in enumerate((keys, values)):
        for i in range(4):
            out[i, aligned(1 - core, column)] = other_kv[n]


def project_qkv(tokens, in_gain, wq, wk, wv, gain, cos, sin):
    tok = tokens.shape[0]
    rows = 4 * tok
    group = (wq.shape[1] + wk.shape[1] + wv.shape[1]) // 4
    head = gain.shape[1]
    total_keys = 8 * (tok - CMAX) + CMAX
    return pl.pallas_call(
        functools.partial(qkv_kernel, tok),
        out_shape=(
            jax.ShapeDtypeStruct((rows, group), F32),
            jax.ShapeDtypeStruct((wq.shape[0], rows), BF16),
            jax.ShapeDtypeStruct((rows, wq.shape[0]), BF16),
            jax.ShapeDtypeStruct((rows, head), F32),
            jax.ShapeDtypeStruct((4, total_keys, head), BF16),
            jax.ShapeDtypeStruct((4, total_keys, head), BF16),
            jax.ShapeDtypeStruct((tok, 128), F32),
        ),
        in_specs=[VMEM_SPEC] * 2 + [ANY_SPEC] * 3 + [VMEM_SPEC] * 3,
        out_specs=(VMEM_SPEC,) * 7,
        scratch_shapes=[pltpu.VMEM(w.shape, BF16) for w in (tokens, wq, wk, wv)]
        + [pltpu.VMEM((2, 4 * (tok - CMAX), head), BF16)] * 2
        + [pltpu.SemaphoreType.DMA((3,))] * 3
        + [pltpu.SemaphoreType.DMA((1,))] * 2
        + relay_scratch(rows, group),
        compiler_params=params(1),
        name="qkv_exchange",
    )(tokens, in_gain, wq, wk, wv, gain, cos, sin)


def out_kernel(attn_in, wo_in, total, attn, wo, local, *relay):
    r, e = lax.axis_index("dp"), lax.axis_index("expert")
    tok, width = total.shape
    step = width // 4
    loads = loading(((attn_in, attn), (wo_in, wo)), local)
    greet([(r ^ m, e) for m in PEER_MASKS])
    for copies in loads:
        wait_all(copies)

    def products(p, dst):
        def chunk(c, carry):
            n = aligned(c, step)
            dst[:, n] = dot_nn(attn[aligned(p, tok), :], wo[:, n]).astype(dst.dtype)
            return carry

        lax.fori_loop(0, width // step, chunk, 0)

    relay_sum(r, e, products, lambda: products(r, total), total, *relay, 16)


def project_out(attn, wo):
    tok = attn.shape[0] // 4
    return pl.pallas_call(
        out_kernel,
        out_shape=jax.ShapeDtypeStruct((tok, wo.shape[1]), F32),
        in_specs=[ANY_SPEC] * 2,
        out_specs=VMEM_SPEC,
        scratch_shapes=[
            pltpu.VMEM(attn.shape, BF16),
            pltpu.VMEM(wo.shape, BF16),
            pltpu.SemaphoreType.DMA((2,)),
        ]
        + relay_scratch(tok, wo.shape[1]),
        compiler_params=params(2),
        name="out_exchange",
    )(attn, wo)


def dgrad_kernel(
    mine, wq, wk, wv, cols_t, out_part, normal, grads, out_grad,
    blocks, dsum, dsend, drecv, ssem, rsem, bsend, brecv, *scratch,
):
    r, e = lax.axis_index("dp"), lax.axis_index("expert")
    rows = mine.shape[0]
    tok = rows // 4
    half = rows // 2
    qg = wq.shape[1] // 4
    kg = wk.shape[1] // 4
    width = wq.shape[0]
    peers = [r ^ m for m in PEER_MASKS]
    near, far, diag = r ^ 1, r ^ 2, r ^ 3
    pair_in, send, recv, *sems = scratch
    begin, middle, finish = owner_sum([out_part], [out_grad], [pair_in], [send], [recv], *sems)
    greet([(p, e) for p in peers] + [(r, e ^ 1)] + owner_peers())
    begin()
    low, high = pl.ds(0, half), pl.ds(half, half)
    first_near = remote(mine.at[low], blocks.at[0, low], ssem.at[0], rsem.at[0], (near, e))
    first_far = remote(mine.at[high], blocks.at[1, high], ssem.at[1], rsem.at[1], (far, e))
    second_near = remote(mine.at[high], blocks.at[0, high], ssem.at[2], rsem.at[2], (near, e))
    second_far = remote(mine.at[low], blocks.at[1, low], ssem.at[3], rsem.at[3], (far, e))
    pass_far = remote(blocks.at[0, low], blocks.at[2, low], ssem.at[4], rsem.at[4], (far, e))
    pass_near = remote(blocks.at[1, high], blocks.at[2, high], ssem.at[5], rsem.at[5], (near, e))
    for copy in (first_near, first_far, second_near, second_far):
        copy.start()

    def products(p, src, start):
        def chunk(c, carry):
            t = aligned(c, tok)
            x = src[t, :]
            value = (
                dot_nt(x[:, :qg], wq[:, aligned(p, qg)])
                + dot_nt(x[:, qg : qg + kg], wk[:, aligned(p, kg)])
                + dot_nt(x[:, qg + kg :], wv[:, aligned(p, kg)])
            )
            if start:
                dsum[t, :] = value
            else:
                dsum[t, :] = dsum[t, :] + value
            return carry

        lax.fori_loop(0, 4, chunk, 0)

        def outer(c, carry):
            n = aligned(c, 128)
            grads[aligned(p, width), n] = dot_nn(cols_t[...], src[:, n]).astype(BF16)
            return carry

        lax.fori_loop(0, (qg + 2 * kg) // 128, outer, 0)

    middle()
    products(r, mine, True)
    first_near.wait()
    pass_far.start()
    first_far.wait()
    pass_near.start()
    second_near.wait()
    products(near, blocks.at[0], False)
    second_far.wait()
    products(far, blocks.at[1], False)
    pass_far.wait()
    pass_near.wait()
    products(diag, blocks.at[2], False)
    back = []
    for i, p in enumerate(peers):
        dsend[i] = dsum[aligned(p, tok), :].astype(BF16)
        copy = remote(dsend.at[i], drecv.at[i], bsend.at[i], brecv.at[i], (p, e))
        copy.start()
        back.append(copy)
    normal[:, aligned(r, width)] = dsum[aligned(r, tok), :]
    for i, p in enumerate(peers):
        back[i].wait()
        normal[:, aligned(p, width)] = drecv[i].astype(F32)
    finish()


def grad_qkv(mine, wq, wk, wv, cols_t, out_part):
    rows, group = mine.shape
    tok = rows // 4
    width = wq.shape[0]
    return pl.pallas_call(
        dgrad_kernel,
        out_shape=(
            jax.ShapeDtypeStruct((tok, 4 * width), F32),
            jax.ShapeDtypeStruct((4 * width, group), BF16),
            jax.ShapeDtypeStruct(out_part.shape[1:], F32),
        ),
        in_specs=[VMEM_SPEC] * 6,
        out_specs=(VMEM_SPEC,) * 3,
        scratch_shapes=[
            pltpu.VMEM((3, rows, group), BF16),
            pltpu.VMEM((rows, width), F32),
            pltpu.VMEM((3, tok, width), BF16),
            pltpu.VMEM((3, tok, width), BF16),
            pltpu.SemaphoreType.DMA((6,)),
            pltpu.SemaphoreType.DMA((6,)),
            pltpu.SemaphoreType.DMA((3,)),
            pltpu.SemaphoreType.DMA((3,)),
        ]
        + owner_scratch([out_part]),
        compiler_params=params(4),
        name="dqkv_exchange",
    )(mine, wq, wk, wv, cols_t, out_part)


def branch_kernel(
    mine, wo_in, attn_in, d_attn, full_out, attn_t_out, wo, attn, full, attn_t, local, ssem, rsem
):
    r, e = lax.axis_index("dp"), lax.axis_index("expert")
    tok = mine.shape[0]
    half = tok // 2
    peers = [r ^ m for m in PEER_MASKS]
    near, far, diag = r ^ 1, r ^ 2, r ^ 3
    loads = loading(((attn_in, attn), (wo_in, wo)), local)
    greet([(p, e) for p in peers])

    def part(q, which):
        return pl.ds(pl.multiple_of(q * tok + which * half, half), half)

    low, high = pl.ds(0, half), pl.ds(half, half)
    first_near = remote(mine.at[low], full.at[part(r, 0)], ssem.at[0], rsem.at[0], (near, e))
    first_far = remote(mine.at[high], full.at[part(r, 1)], ssem.at[1], rsem.at[1], (far, e))
    second_near = remote(mine.at[high], full.at[part(r, 1)], ssem.at[2], rsem.at[2], (near, e))
    second_far = remote(mine.at[low], full.at[part(r, 0)], ssem.at[3], rsem.at[3], (far, e))
    pass_far = remote(full.at[part(near, 0)], full.at[part(near, 0)], ssem.at[4], rsem.at[4], (far, e))
    pass_near = remote(full.at[part(far, 1)], full.at[part(far, 1)], ssem.at[5], rsem.at[5], (near, e))
    for copy in (first_near, first_far, second_near, second_far):
        copy.start()
    full[aligned(r, tok), :] = mine[...]
    wait_all(loads[0])
    attn_t[...] = attn[...].T
    leaving = start_all([pltpu.make_async_copy(attn_t, attn_t_out, local.at[0])])
    wait_all(loads[1])
    heads = wo.shape[0]
    step = heads // 4

    def products(q):
        def chunk(c, carry):
            n = aligned(c, step)
            d_attn[aligned(q, tok), n] = dot_nt(full[aligned(q, tok), :], wo[n, :]).astype(BF16)
            return carry

        lax.fori_loop(0, 4, chunk, 0)

    products(r)
    first_near.wait()
    pass_far.start()
    first_far.wait()
    pass_near.start()
    second_near.wait()
    products(near)
    second_far.wait()
    products(far)
    pass_far.wait()
    pass_near.wait()
    leaving += start_all([pltpu.make_async_copy(full, full_out, local.at[1])])
    products(diag)
    wait_all(leaving)


def grad_branch(mine, wo, attn):
    tok, width = mine.shape
    return pl.pallas_call(
        branch_kernel,
        out_shape=(
            jax.ShapeDtypeStruct((4 * tok, wo.shape[0]), BF16),
            jax.ShapeDtypeStruct((4 * tok, width), BF16),
            jax.ShapeDtypeStruct((wo.shape[0], 4 * tok), BF16),
        ),
        in_specs=[VMEM_SPEC, ANY_SPEC, ANY_SPEC],
        out_specs=(VMEM_SPEC, ANY_SPEC, ANY_SPEC),
        scratch_shapes=[
            pltpu.VMEM(wo.shape, BF16),
            pltpu.VMEM(attn.shape, BF16),
            pltpu.VMEM((4 * tok, width), BF16),
            pltpu.VMEM((wo.shape[0], 4 * tok), BF16),
            pltpu.SemaphoreType.DMA((2,)),
            pltpu.SemaphoreType.DMA((6,)),
            pltpu.SemaphoreType.DMA((6,)),
        ],
        compiler_params=params(3),
        name="branch_exchange",
    )(mine, wo, attn)


def owner_order(n_z):
    order = list(range(1, n_z)) + [0]
    return order[1:2] + order[:1] + order[2:] if n_z > 2 else order


def owner_sum(arrays, outs, pair_in, send, recv, psend, precv, zsend, zrecv):
    r, e = lax.axis_index("dp"), lax.axis_index("expert")
    n_z = arrays[0].shape[0] // 2
    z, core = e // 2, e % 2
    targets = [lax.rem(z + j, n_z) for j in range(n_z)]
    order = owner_order(n_z)
    n_arrays = len(arrays)
    pair, moves = {}, []

    def begin():
        for j in order:
            for a in range(n_arrays):
                copy = remote(
                    arrays[a].at[targets[j] * 2 + (1 - core)], pair_in[a].at[j],
                    psend.at[a, j], precv.at[a, j], (r, e ^ 1),
                )
                copy.start()
                pair[a, j] = copy

    def middle():
        for j in order:
            for a in range(n_arrays):
                pair[a, j].wait()
                own = arrays[a][targets[j] * 2 + core].astype(F32) + pair_in[a][j].astype(F32)
                if j == 0:
                    outs[a][...] = own
                else:
                    send[a][j - 1] = own.astype(BF16)
                    copy = remote(
                        send[a].at[j - 1], recv[a].at[j - 1],
                        zsend.at[a, j - 1], zrecv.at[a, j - 1], (r, targets[j] * 2 + core),
                    )
                    copy.start()
                    moves.append(copy)

    def finish():
        for copy in moves:
            copy.wait()
        for a in range(n_arrays):
            value = outs[a][...]
            for j in range(n_z - 1):
                value = value + recv[a][j].astype(F32)
            outs[a][...] = value

    return begin, middle, finish


def owner_scratch(arrays):
    n_z = arrays[0].shape[0] // 2
    n = len(arrays)
    shapes = [a.shape[1:] for a in arrays]
    return (
        [pltpu.VMEM((n_z, *s), BF16) for s in shapes]
        + [pltpu.VMEM((n_z - 1, *s), BF16) for s in shapes]
        + [pltpu.VMEM((n_z - 1, *s), BF16) for s in shapes]
        + [pltpu.SemaphoreType.DMA((n, n_z))] * 2
        + [pltpu.SemaphoreType.DMA((n, n_z - 1))] * 2
    )


def owner_peers():
    r, e = lax.axis_index("dp"), lax.axis_index("expert")
    n_z = lax.axis_size("expert") // 2
    return [(r, lax.rem(e // 2 + j, n_z) * 2 + e % 2) for j in range(1, n_z)]


def last_sums_kernel(grads, small, grads_out, small_out, *scratch):
    r, e = lax.axis_index("dp"), lax.axis_index("expert")
    z, core = e // 2, e % 2
    n_z = grads.shape[0] // 2
    pair_in, send, recv, psend, precv, zsend, zrecv = scratch[:7]
    first_in, piece, line_in, s1, r1, s2, r2, s3, r3 = scratch[7:]
    begin, middle, finish = owner_sum(
        [grads], [grads_out], [pair_in], [send], [recv], psend, precv, zsend, zrecv
    )
    others = [(m // 2, m % 2) for m in range(1, 8)]
    plane = [(r ^ a, e ^ c) for a, c in others]
    greet(plane + owner_peers())
    begin()
    firsts = []
    for i, (a, c) in enumerate(others):
        copy = remote(
            small.at[(r ^ a) * 2 + (core ^ c)], first_in.at[i], s1.at[i], r1.at[i], plane[i]
        )
        copy.start()
        firsts.append(copy)
    middle()
    for copy in firsts:
        copy.wait()
    mine = r * 2 + core
    value = small[mine]
    for i in range(7):
        value = value + first_in[i]
    piece[0] = value
    seconds = []
    for j in range(1, n_z):
        copy = remote(
            piece.at[0], line_in.at[j - 1], s2.at[j - 1], r2.at[j - 1], owner_peers()[j - 1]
        )
        copy.start()
        seconds.append(copy)
    for copy in seconds:
        copy.wait()
    value = piece[0]
    for j in range(n_z - 1):
        value = value + line_in[j]
    small_out[mine] = value
    thirds = []
    for i, (a, c) in enumerate(others):
        copy = remote(small_out.at[mine], small_out.at[mine], s3.at[i], r3.at[i], plane[i])
        copy.start()
        thirds.append(copy)
    finish()
    for copy in thirds:
        copy.wait()


def last_sums(grads, small):
    n_z = grads.shape[0] // 2
    piece = small.shape[1:]
    return pl.pallas_call(
        last_sums_kernel,
        out_shape=(
            jax.ShapeDtypeStruct(grads.shape[1:], F32),
            jax.ShapeDtypeStruct(small.shape, F32),
        ),
        in_specs=[VMEM_SPEC] * 2,
        out_specs=(VMEM_SPEC,) * 2,
        scratch_shapes=owner_scratch([grads])
        + [
            pltpu.VMEM((7, *piece), F32),
            pltpu.VMEM((1, *piece), F32),
            pltpu.VMEM((n_z - 1, *piece), F32),
            pltpu.SemaphoreType.DMA((7,)),
            pltpu.SemaphoreType.DMA((7,)),
            pltpu.SemaphoreType.DMA((n_z - 1,)),
            pltpu.SemaphoreType.DMA((n_z - 1,)),
            pltpu.SemaphoreType.DMA((7,)),
            pltpu.SemaphoreType.DMA((7,)),
        ],
        compiler_params=params(5),
        name="last_sums",
    )(grads, small)


def line_sum(block, out, pair_in, work, lines, ps, pr, zs, zr):
    r, e = lax.axis_index("dp"), lax.axis_index("expert")
    z, core = e // 2, e % 2
    order = plane_order(z)[::-1]
    right = jnp.minimum(z + 1, 3) * 2 + core
    left = jnp.maximum(z - 1, 0) * 2 + core
    pairs, moves = [], []

    def begin():
        for k in range(4):
            copy = remote(
                block(order[k] * 2 + (1 - core)), pair_in.at[k], ps.at[k], pr.at[k], (r, e ^ 1)
            )
            copy.start()
            pairs.append(copy)

    def move(k, side, cond, to, add):
        b = order[k]
        copy = remote(work.at[k], lines.at[side, b], zs.at[side, k], zr.at[side, b], (r, to))
        moves.append((cond, copy))

        @pl.when(cond)
        def _():
            if add:
                copy.wait_recv()
                value = work[k].astype(F32) + lines[side, b].astype(F32)
                work[k] = value.astype(BF16)
            copy.start()

    def first():
        for k in range(4):
            pairs[k].wait_recv()
            value = block(order[k] * 2 + core)[...].astype(F32) + pair_in[k].astype(F32)
            if k == 3:
                out[...] = value
            else:
                work[k] = value.astype(BF16)
        ends(0)

    def ends(k):
        move(k, 0, z == 0, right, False)
        move(k, 1, z == 3, left, False)

    def inner(k):
        inside = (z > 0) & (z < 3)
        move(k, 0, inside & (order[k] > z), right, True)
        move(k, 1, inside & (order[k] < z), left, True)
        if k < 2:
            ends(k + 1)

    def last():
        for side, cond in ((0, z > 0), (1, z < 3)):

            @pl.when(cond)
            def _():
                at = lines.at[side, z]
                remote(at, at, zs.at[side, 3], zr.at[side, z], (r, e ^ 1)).wait_recv()
                out[...] = out[...] + lines[side, z].astype(F32)

        for copy in pairs:
            copy.wait_send()
        for cond, copy in moves:

            @pl.when(cond)
            def _():
                copy.wait_send()

    return begin, first, inner, last


LINE_SEMS = [
    pltpu.SemaphoreType.DMA((4,)),
    pltpu.SemaphoreType.DMA((4,)),
    pltpu.SemaphoreType.DMA((2, 4)),
    pltpu.SemaphoreType.DMA((2, 4)),
]


def dgrad_line_kernel(
    d_q, d_keys, d_values, key_lin, cos, sin, key_gain,
    wq_in, wk_in, wv_in, cols_t_in, cols_in, out_part_in, small, gain,
    normal, q_out, k_out, v_out, out_sum, small_out, gain_out,
    mine, prompt_sum, prompt_in, ksend, krecv, wq, wk, wv, cols_t, cols, out_part, local, qkv_sum, grads, blocks, dsum, dsend, drecv, opair, owork, olines, qpair, qwork, qlines,
    first_in, piece, line_in, gain_v, gain_in,
    ssem, rsem, bsend, brecv, s1, r1, s2, r2, s3, r3, s4, r4, s5, r5, *sems,
):
    r, e = lax.axis_index("dp"), lax.axis_index("expert")
    z, core = e // 2, e % 2
    rows = mine.shape[0]
    tok = rows // 4
    half = rows // 2
    qg = wq.shape[1] // 4
    kg = wk.shape[1] // 4
    width = wq.shape[0]
    share = width // 8
    peers = [r ^ m for m in PEER_MASKS]
    near, far, diag = r ^ 1, r ^ 2, r ^ 3
    order = (r, near, far, diag)
    out_begin, out_first, out_inner, out_last = line_sum(
        lambda o: out_part.at[o], out_sum, opair, owork, olines, *sems[:4]
    )
    units = [
        line_sum(
            lambda o, p=p: grads.at[o, p], qkv_sum.at[p], qpair.at[i], qwork.at[i], qlines.at[i],
            *(sem.at[i] for sem in sems[4:]),
        )
        for i, p in enumerate(order)
    ]
    line_peers = [(r, lax.rem(z + j, 4) * 2 + core) for j in (1, 2, 3)]
    others = [(m // 2, m % 2) for m in (6, 7, 2, 3, 4, 5, 1)]
    plane = [(r ^ a, e ^ c) for a, c in others]
    owners = [(r, e ^ m) for m in range(1, 8)]
    loads = loading(
        (
            (out_part_in, out_part), (cols_t_in, cols_t), (wq_in, wq), (wk_in, wk), (wv_in, wv),
            (cols_in, cols),
        ),
        local,
    )
    mine[:, :qg] = d_q[...]
    prompt = tok - CMAX
    column = 4 * prompt
    for n, d in enumerate((d_keys, d_values)):
        for c in range(2):
            part = slice(c * column, (c + 1) * column)
            prompt_sum[c, n] = d[0, part] + d[1, part] + d[2, part] + d[3, part]
    greet(plane + owners[1:])
    swap = remote(prompt_sum.at[1 - core], prompt_in, ksend.at[0], krecv.at[0], (r, e ^ 1))
    swap.start()
    swap.wait()
    prompt_in[...] = prompt_in[...] + prompt_sum[core]
    head = key_gain.shape[1]
    key_gain_sum = jnp.zeros((1, head), F32)
    for i in range(4):
        for at, size, dk, dv in (
            (0, prompt, prompt_in[0, i * prompt : (i + 1) * prompt], prompt_in[1, i * prompt : (i + 1) * prompt]),
            (prompt, CMAX, d_keys[i, 2 * column :], d_values[i, 2 * column :]),
        ):
            t = slice(at, at + size)
            rows_i = slice(i * tok + at, i * tok + at + size)
            turned = dk * cos[i, t] + pltpu.roll(dk * sin[i, t], head // 2, 1)
            x = key_lin[rows_i, :]
            inverse = lax.rsqrt(jnp.mean(x * x, axis=-1, keepdims=True) + norm_eps)
            unit = x * inverse
            key_gain_sum = key_gain_sum + jnp.sum(turned * unit, axis=0, keepdims=True)
            weighted = turned * key_gain[...]
            mine[rows_i, qg : qg + kg] = (
                inverse * (weighted - unit * jnp.mean(weighted * unit, axis=-1, keepdims=True))
            ).astype(BF16)
            mine[rows_i, qg + kg :] = dv.astype(BF16)
    low, high = pl.ds(0, half), pl.ds(half, half)
    first_near = remote(mine.at[low], blocks.at[0, low], ssem.at[0], rsem.at[0], (near, e))
    first_far = remote(mine.at[high], blocks.at[1, high], ssem.at[1], rsem.at[1], (far, e))
    second_near = remote(mine.at[high], blocks.at[0, high], ssem.at[2], rsem.at[2], (near, e))
    second_far = remote(mine.at[low], blocks.at[1, low], ssem.at[3], rsem.at[3], (far, e))
    pass_far = remote(blocks.at[0, low], blocks.at[2, low], ssem.at[4], rsem.at[4], (far, e))
    pass_near = remote(blocks.at[1, high], blocks.at[2, high], ssem.at[5], rsem.at[5], (near, e))
    me = r * 2 + core
    firsts = []
    for i, (a, c) in enumerate(others):
        copy = remote(small.at[(r ^ a) * 2 + (core ^ c)], first_in.at[i], s1.at[i], r1.at[i], plane[i])
        copy.start()
        firsts.append(copy)
    for copy in (first_near, first_far, second_near, second_far):
        copy.start()
    wait_all(loads[0])
    out_begin()
    seconds, thirds = [], []

    def small_second():
        for copy in firsts:
            copy.wait()
        value = small[me]
        for i in range(7):
            value = value + first_in[i]
        piece[0] = value
        for j in range(3):
            copy = remote(piece.at[0], line_in.at[j], s2.at[j], r2.at[j], line_peers[j])
            copy.start()
            seconds.append(copy)

    def small_third():
        for copy in seconds:
            copy.wait()
        small_out[me] = piece[0] + line_in[0] + line_in[1] + line_in[2]
        for i in range(7):
            copy = remote(small_out.at[me], small_out.at[me], s3.at[i], r3.at[i], plane[i])
            copy.start()
            thirds.append(copy)

    def outer(p, src):
        def step(c, carry):
            n = aligned(c, 256)
            value = dot_nn(cols_t[...], src[:, n]).astype(BF16)
            for o in range(8):
                grads[o, p, :, n] = value[o * share : (o + 1) * share]
            return carry

        lax.fori_loop(0, (qg + 2 * kg) // 256, step, 0)

    def inner(p, src, start):
        def chunk(c, carry):
            n = aligned(c, 128)
            value = (
                dot_nt(src[:, :qg], wq[n, aligned(p, qg)])
                + dot_nt(src[:, qg : qg + kg], wk[n, aligned(p, kg)])
                + dot_nt(src[:, qg + kg :], wv[n, aligned(p, kg)])
            )
            if start:
                dsum[:, n] = value
            else:
                dsum[:, n] = dsum[:, n] + value
            return carry

        lax.fori_loop(0, width // 128, chunk, 0)

    def begin(i):
        units[i][0]()

    def first(i):
        units[i][1]()

    def onward(i, k):
        units[i][2](k)

    wait_all(loads[1])
    outer(r, mine)
    begin(0)
    out_first()
    small_second()
    for copies in loads[2:5]:
        wait_all(copies)
    inner(r, mine, True)
    first_near.wait()
    pass_far.start()
    first_far.wait()
    pass_near.start()
    out_inner(0)
    first(0)
    out_inner(1)
    small_third()
    onward(0, 0)
    second_near.wait()
    outer(near, blocks.at[0])
    begin(1)
    second_far.wait()
    outer(far, blocks.at[1])
    begin(2)
    out_inner(2)
    onward(0, 1)
    first(1)
    inner(near, blocks.at[0], False)
    onward(0, 2)
    onward(1, 0)
    first(2)
    inner(far, blocks.at[1], False)
    onward(1, 1)
    pass_far.wait()
    pass_near.wait()
    outer(diag, blocks.at[2])
    begin(3)
    inner(diag, blocks.at[2], False)
    back = []
    for i, p in enumerate(peers):
        dsend[i] = dsum[aligned(p, tok), :].astype(BF16)
        copy = remote(dsend.at[i], drecv.at[i], bsend.at[i], brecv.at[i], (p, e))
        copy.start()
        back.append(copy)
    wait_all(loads[5])
    scale = 1.0 / gain[:, aligned(r, width)]
    gain_v[...] = jnp.broadcast_to(
        jnp.sum(dsum[...] * cols[...].astype(F32), axis=0, keepdims=True) * scale, gain_v.shape
    )
    gain_v[1:2, :head] = key_gain_sum
    fourths = []
    for i in range(7):
        copy = remote(gain_v, gain_in.at[i], s4.at[i], r4.at[i], owners[i])
        copy.start()
        fourths.append(copy)
    onward(1, 2)
    onward(2, 0)
    first(3)
    onward(2, 1)
    for copy in fourths:
        copy.wait()
    value = gain_v[...]
    for i in range(7):
        value = value + gain_in[i]
    gain_out[r] = value
    fifths = []
    for i, p in enumerate(peers):
        copy = remote(gain_out.at[r], gain_out.at[r], s5.at[i], r5.at[i], (p, e))
        copy.start()
        fifths.append(copy)
    onward(3, 0)
    normal[:, aligned(r, width)] = dsum[aligned(r, tok), :]
    for i, p in enumerate(peers):
        back[i].wait()
        normal[:, aligned(p, width)] = drecv[i].astype(F32)
    onward(2, 2)
    onward(3, 1)
    out_last()

    def close(i):
        p = order[i]
        units[i][3]()
        q_out[:, aligned(p, qg)] = qkv_sum[p, :, :qg]
        k_out[:, aligned(p, kg)] = qkv_sum[p, :, qg : qg + kg]
        v_out[:, aligned(p, kg)] = qkv_sum[p, :, qg + kg :]

    close(0)
    close(1)
    onward(3, 2)
    close(2)
    close(3)
    for copy in fifths + thirds:
        copy.wait()


def grad_qkv_line(
    d_q, d_keys, d_values, key_lin, cos, sin, key_gain, wq, wk, wv, cols_t, cols, out_part, small, gain
):
    rows, head = key_lin.shape
    group = d_q.shape[1] + 2 * head
    tok = rows // 4
    width = wq.shape[0]
    piece = (width // 8, group)
    out_piece = out_part.shape[1:]
    small_piece = small.shape[1:]
    return pl.pallas_call(
        dgrad_line_kernel,
        out_shape=(
            jax.ShapeDtypeStruct((tok, 4 * width), F32),
            jax.ShapeDtypeStruct((width // 8, wq.shape[1]), F32),
            jax.ShapeDtypeStruct((width // 8, wk.shape[1]), F32),
            jax.ShapeDtypeStruct((width // 8, wv.shape[1]), F32),
            jax.ShapeDtypeStruct(out_piece, F32),
            jax.ShapeDtypeStruct(small.shape, F32),
            jax.ShapeDtypeStruct((4, 8, width), F32),
        ),
        in_specs=[VMEM_SPEC] * 7 + [ANY_SPEC] * 6 + [VMEM_SPEC] * 2,
        out_specs=(VMEM_SPEC,) * 7,
        scratch_shapes=[
            pltpu.VMEM((rows, group), BF16),
            pltpu.VMEM((2, 2, 4 * (tok - CMAX), head), F32),
            pltpu.VMEM((2, 4 * (tok - CMAX), head), F32),
            pltpu.SemaphoreType.DMA((1,)),
            pltpu.SemaphoreType.DMA((1,)),
        ]
        + [pltpu.VMEM(a.shape, BF16) for a in (wq, wk, wv, cols_t, cols, out_part)]
        + [
            pltpu.SemaphoreType.DMA((6,)),
            pltpu.VMEM((4, *piece), F32),
            pltpu.VMEM((8, 4, *piece), BF16),
            pltpu.VMEM((3, rows, group), BF16),
            pltpu.VMEM((rows, width), F32),
            pltpu.VMEM((3, tok, width), BF16),
            pltpu.VMEM((3, tok, width), BF16),
            pltpu.VMEM((4, *out_piece), BF16),
            pltpu.VMEM((3, *out_piece), BF16),
            pltpu.VMEM((2, 4, *out_piece), BF16),
            pltpu.VMEM((4, 4, *piece), BF16),
            pltpu.VMEM((4, 3, *piece), BF16),
            pltpu.VMEM((4, 2, 4, *piece), BF16),
            pltpu.VMEM((7, *small_piece), F32),
            pltpu.VMEM((1, *small_piece), F32),
            pltpu.VMEM((3, *small_piece), F32),
            pltpu.VMEM((8, width), F32),
            pltpu.VMEM((7, 8, width), F32),
            pltpu.SemaphoreType.DMA((6,)),
            pltpu.SemaphoreType.DMA((6,)),
        ]
        + [pltpu.SemaphoreType.DMA((n,)) for n in (3, 3, 7, 7, 3, 3, 7, 7, 7, 7, 3, 3)]
        + LINE_SEMS
        + [
            pltpu.SemaphoreType.DMA((4, 4)),
            pltpu.SemaphoreType.DMA((4, 4)),
            pltpu.SemaphoreType.DMA((4, 2, 4)),
            pltpu.SemaphoreType.DMA((4, 2, 4)),
        ],
        compiler_params=params(10),
        name="dqkv_line_exchange",
    )(
        d_q, d_keys, d_values, key_lin, cos, sin, key_gain, wq, wk, wv, cols_t, cols, out_part, small, gain
    )


def masks_of(block, own_length, slots, prompt_block, prompt_len, column, keys):
    slot = lax.broadcasted_iota(jnp.int32, (slots, keys), 0)
    key = lax.broadcasted_iota(jnp.int32, (slots, keys), 1)
    is_prompt = slot < prompt_block
    position = (column * 4 + block) * prompt_block + slot
    sees_prompt = (key < prompt_len) & (jnp.logical_not(is_prompt) | (key <= position))
    cont = key - prompt_len
    sees_cont = (
        (key >= prompt_len)
        & jnp.logical_not(is_prompt)
        & (cont <= slot - prompt_block)
        & (cont < own_length)
    )
    return sees_prompt | sees_cont


def attention_fwd_kernel(
    prompt_len, lengths, lin, gain, cos, sin, keys, values, queries, attn, q_all, score_all, low_all
):
    block = pl.program_id(0)
    slots = lin.shape[0]
    head = gain.shape[1]
    e = lax.axis_index("expert")
    own_length = lengths[block * lax.axis_size("expert") + e]
    allowed = masks_of(block, own_length, slots, slots - CMAX, prompt_len, e % 2, keys.shape[1])
    scale = head ** (-0.5)
    k, v = keys[0], values[0]
    c, s, g = cos[0], sin[0], gain[...]
    heads = lin.shape[1] // head
    parts = [slice(h * head, (h + 1) * head) for h in range(heads)]
    rows = [slice(h * slots, (h + 1) * slots) for h in range(heads)]
    for h in range(heads):
        x = lin[:, parts[h]]
        x = x * lax.rsqrt(jnp.mean(x * x, axis=-1, keepdims=True) + norm_eps) * g
        q = (x * c + pltpu.roll(x, head // 2, 1) * s).astype(BF16)
        queries[:, parts[h]] = q
        q_all[rows[h]] = q
    score_all[...] = dot_nt(q_all[...], k)
    for h in range(heads):
        score = jnp.where(allowed, score_all[rows[h]] * scale, -jnp.inf)
        peak = jnp.max(score, axis=-1, keepdims=True)
        exponent = jnp.exp(score - peak)
        low_all[rows[h]] = (exponent * (1.0 / jnp.sum(exponent, axis=-1, keepdims=True))).astype(BF16)
    out = dot_nn(low_all[...], v)
    for h in range(heads):
        attn[:, parts[h]] = out[rows[h]].astype(BF16)


def attention_fwd(lengths, lin, gain, cos, sin, keys, values, prompt_len):
    blocks, total_keys, head = keys.shape
    slots = lin.shape[0] // blocks
    width = lin.shape[1] - 2 * head
    row = pl.BlockSpec((slots, width), lambda i, *_: (i, 0))
    table = pl.BlockSpec((1, slots, head), lambda i, *_: (i, 0, 0))
    kv = pl.BlockSpec((1, total_keys, head), lambda i, *_: (i, 0, 0))
    one = pl.BlockSpec((1, head), lambda i, *_: (0, 0))
    return pl.pallas_call(
        functools.partial(attention_fwd_kernel, prompt_len),
        grid_spec=pltpu.PrefetchScalarGridSpec(
            num_scalar_prefetch=1,
            grid=(blocks,),
            in_specs=[row, one, table, table, kv, kv],
            out_specs=[row, row],
            scratch_shapes=[
                pltpu.VMEM((slots * width // head, head), BF16),
                pltpu.VMEM((slots * width // head, total_keys), F32),
                pltpu.VMEM((slots * width // head, total_keys), BF16),
            ],
        ),
        out_shape=(
            jax.ShapeDtypeStruct((lin.shape[0], width), BF16),
            jax.ShapeDtypeStruct((lin.shape[0], width), BF16),
        ),
        compiler_params=params(),
        name="attention_fwd",
    )(lengths, lin, gain, cos, sin, keys, values)


def attention_bwd_kernel(
    prompt_len, lengths, lin, queries, d_attn, gain, cos, sin, keys, values, attn_t, d_branch,
    d_lin, d_keys, d_values, d_gain, out_part,
    q_all, d_all, score_all, d_probs_all, low_all, d_score_all, d_q_all,
):
    block = pl.program_id(0)
    slots = lin.shape[0]
    head = gain.shape[1]
    e = lax.axis_index("expert")
    own_length = lengths[block * lax.axis_size("expert") + e]
    allowed = masks_of(block, own_length, slots, slots - CMAX, prompt_len, e % 2, keys.shape[1])
    scale = head ** (-0.5)
    k, v = keys[0], values[0]
    c, s, g = cos[0], sin[0], gain[...]
    heads = lin.shape[1] // head
    parts = [slice(h * head, (h + 1) * head) for h in range(heads)]
    rows = [slice(h * slots, (h + 1) * slots) for h in range(heads)]
    for h in range(heads):
        q_all[rows[h]] = queries[:, parts[h]]
        d_all[rows[h]] = d_attn[:, parts[h]]
    score_all[...] = dot_nt(q_all[...], k)
    d_probs_all[...] = dot_nt(d_all[...], v)
    for h in range(heads):
        score = jnp.where(allowed, score_all[rows[h]] * scale, -jnp.inf)
        peak = jnp.max(score, axis=-1, keepdims=True)
        exponent = jnp.exp(score - peak)
        probs = exponent * (1.0 / jnp.sum(exponent, axis=-1, keepdims=True))
        d_probs = d_probs_all[rows[h]]
        inner = jnp.sum(probs * d_probs, axis=-1, keepdims=True)
        low_all[rows[h]] = probs.astype(BF16)
        d_score_all[rows[h]] = (probs * (d_probs - inner)).astype(BF16)
    d_q_all[...] = dot_nn(d_score_all[...], k)
    d_keys[0] = dot_tn(d_score_all[...], q_all[...]) * scale
    d_values[0] = dot_tn(low_all[...], d_all[...])
    for n in range(2):
        half = slice(n * out_part.shape[1] // 2, (n + 1) * out_part.shape[1] // 2)
        out_part[:, half] = dot_nn(attn_t[...], d_branch[:, half]).astype(BF16)
    gain_total = jnp.zeros((8, head), F32)
    for h in range(heads):
        d_q = d_q_all[rows[h]] * scale
        turned = d_q * c + pltpu.roll(d_q * s, head // 2, 1)
        x = lin[:, parts[h]]
        inverse = lax.rsqrt(jnp.mean(x * x, axis=-1, keepdims=True) + norm_eps)
        unit = x * inverse
        pairs = turned * unit
        for j in range(slots // 8):
            gain_total = gain_total + pairs[j * 8 : (j + 1) * 8]
        weighted = turned * g
        d_lin[:, parts[h]] = (
            inverse * (weighted - unit * jnp.mean(weighted * unit, axis=-1, keepdims=True))
        ).astype(BF16)
    d_gain[0] = gain_total


def attention_bwd(
    lengths, lin, queries, d_attn, gain, cos, sin, keys, values, attn_t, d_branch, prompt_len
):
    blocks, total_keys, head = keys.shape
    slots = lin.shape[0] // blocks
    width = lin.shape[1] - 2 * head
    row = pl.BlockSpec((slots, width), lambda i, *_: (i, 0))
    table = pl.BlockSpec((1, slots, head), lambda i, *_: (i, 0, 0))
    kv = pl.BlockSpec((1, total_keys, head), lambda i, *_: (i, 0, 0))
    step = d_branch.shape[1] // blocks
    one = pl.BlockSpec((1, head), lambda i, *_: (0, 0))
    return pl.pallas_call(
        functools.partial(attention_bwd_kernel, prompt_len),
        grid_spec=pltpu.PrefetchScalarGridSpec(
            num_scalar_prefetch=1,
            grid=(blocks,),
            in_specs=[row, row, row, one, table, table, kv, kv]
            + [
                pl.BlockSpec(attn_t.shape, lambda i, *_: (0, 0)),
                pl.BlockSpec((d_branch.shape[0], step), lambda i, *_: (0, i)),
            ],
            out_specs=[
                row,
                kv,
                kv,
                pl.BlockSpec((1, 8, head), lambda i, *_: (i, 0, 0)),
                pl.BlockSpec((attn_t.shape[0], step), lambda i, *_: (0, i)),
            ],
            scratch_shapes=[
                pltpu.VMEM((slots * width // head, head), BF16),
                pltpu.VMEM((slots * width // head, head), BF16),
                pltpu.VMEM((slots * width // head, total_keys), F32),
                pltpu.VMEM((slots * width // head, total_keys), F32),
                pltpu.VMEM((slots * width // head, total_keys), BF16),
                pltpu.VMEM((slots * width // head, total_keys), BF16),
                pltpu.VMEM((slots * width // head, head), F32),
            ],
        ),
        out_shape=(
            jax.ShapeDtypeStruct((lin.shape[0], width), BF16),
            jax.ShapeDtypeStruct(keys.shape, F32),
            jax.ShapeDtypeStruct(values.shape, F32),
            jax.ShapeDtypeStruct((blocks, 8, head), F32),
            jax.ShapeDtypeStruct((attn_t.shape[0], d_branch.shape[1]), BF16),
        ),
        compiler_params=params(),
        name="attention_bwd",
    )(lengths, lin, queries, d_attn, gain, cos, sin, keys, values, attn_t, d_branch)


def partner(shard, axis, bit):
    return lax.ppermute(shard, axis, [(i, i ^ 1 << bit) for i in range(lax.axis_size(axis))])


def root_mean_scale(value_rows, gain_vec):
    return (
        value_rows
        * lax.rsqrt(jnp.mean(value_rows * value_rows, axis=-1, keepdims=True) + norm_eps)
        * gain_vec
    )


def contract(left_side, right_side, left_dim, right_dim):
    return lax.dot_general(
        left_side,
        right_side,
        (((left_dim,), (right_dim,)), ((), ())),
        preferred_element_type=F32,
    )


def plane_order(z):
    upper, odd = z // 2, z % 2
    return [z, z + 1 - 2 * upper, 2 + upper - 2 * odd, 3 - 3 * upper]


def world(with_diag):
    r, e = lax.axis_index("dp"), lax.axis_index("expert")
    z, core = e // 2, e % 2
    near, far = r ^ 1, r ^ 2
    devices = [(near, e), (far, e), (r, e ^ 1)]
    devices += [(r, lax.rem(z + j, 4) * 2 + core) for j in (1, 2, 3)]
    return r, e, z, core, near, far, devices


def everyone():
    me = lax.axis_index("dp") * 8 + lax.axis_index("expert")
    return me, [lax.rem(me + j, 32) for j in range(1, 32)]


def scatter_rows(rows, rows_in, ss, rs):
    me, others = everyone()
    copies = start_all(
        [
            remote(rows.at[d], rows_in.at[me], ss.at[j], rs.at[j], (d // 8, lax.rem(d, 8)))
            for j, d in enumerate(others)
        ]
    )
    rows_in[me] = rows[me]
    return copies


def greet_everyone():
    greet([(d // 8, lax.rem(d, 8)) for d in everyone()[1]])


ROW_SEMS = [pltpu.SemaphoreType.DMA((31,)), pltpu.SemaphoreType.DMA((31,))]


def gather_world(mine, buf, zs, zr, ps, pr, ds, dr, before, group, done, greeting=None):
    r, e, z, core, near, far, greeted = world(True)
    half = mine.shape[0] // 2
    low, high = pl.ds(0, half), pl.ds(half, half)
    order = plane_order(z)
    if greeting is None:
        greet(greeted)
    else:
        greeting()

    def slot(q, b, c):
        return q * 8 + b * 2 + c

    buf[slot(r, z, core)] = mine[...]
    diag = r ^ 3
    plane, pairs, lines = {}, {}, []

    def hand(k, i, q):
        at = slot(q, order[k], core)
        copy = remote(buf.at[at], buf.at[at], ds.at[k, i], dr.at[k, i], (r, e ^ 1))
        copy.start()
        pairs[k, i] = copy

    def issue(k):
        b = order[k]
        at = slot(r, b, core)
        for side, cond, to in (
            (0, (b <= z) & (z < 3), jnp.minimum(z + 1, 3)),
            (1, (b >= z) & (z > 0), jnp.maximum(z - 1, 0)),
        ):
            copy = remote(buf.at[at], buf.at[at], zs.at[k, side], zr.at[b], (r, to * 2 + core))
            lines.append((cond, copy))

            @pl.when(cond)
            def _():
                copy.start()

        mine_at, near_at, far_at = at, slot(near, b, core), slot(far, b, core)
        for i, (src, part, p) in enumerate(
            (
                (mine_at, low, near),
                (mine_at, high, far),
                (mine_at, high, near),
                (mine_at, low, far),
                (near_at, low, far),
                (far_at, high, near),
            )
        ):
            plane[k, i] = remote(
                buf.at[src, part], buf.at[src, part], ps.at[k, i], pr.at[k, i], (p, e)
            )
        for i in range(4):
            plane[k, i].start()
        hand(k, 0, r)

    def line_wait(k):
        b = order[k]
        at = slot(r, b, core)
        remote(buf.at[at], buf.at[at], zs.at[k, 0], zr.at[b], (r, e ^ 1)).wait_recv()
        issue(k)

    def passes(k):
        plane[k, 0].wait_recv()
        plane[k, 4].start()
        plane[k, 1].wait_recv()
        plane[k, 5].start()

    def finish(k):
        plane[k, 2].wait_recv()
        hand(k, 1, near)
        plane[k, 3].wait_recv()
        hand(k, 2, far)

    def corner(k):
        plane[k, 4].wait_recv()
        plane[k, 5].wait_recv()
        hand(k, 3, diag)

    who = (r, near, far, diag)

    def ready(k):
        before(k)
        for i in range(4):
            pairs[k, i].wait_recv()
        group(k, [(k * 4 + i, who[i] * 8 + order[k] * 2) for i in range(4)])

    issue(0)
    passes(0)
    line_wait(1)
    finish(0)
    passes(1)
    line_wait(2)
    corner(0)
    finish(1)
    ready(0)
    passes(2)
    line_wait(3)
    corner(1)
    finish(2)
    ready(1)
    passes(3)
    corner(2)
    finish(3)
    ready(2)
    corner(3)
    ready(3)
    done()
    for copy in plane.values():
        copy.wait_send()
    for copy in pairs.values():
        copy.wait_send()
    for cond, copy in lines:

        @pl.when(cond)
        def _():
            copy.wait_send()


def group_rows(k, room):
    return pl.ds(k * 4 * room, 4 * room)


GATHER_SEMS = [
    pltpu.SemaphoreType.DMA((4, 2)),
    pltpu.SemaphoreType.DMA((4,)),
    pltpu.SemaphoreType.DMA((4, 6)),
    pltpu.SemaphoreType.DMA((4, 6)),
    pltpu.SemaphoreType.DMA((4, 4)),
    pltpu.SemaphoreType.DMA((4, 4)),
]


def selector(row, room):
    ids = lax.broadcasted_iota(jnp.int32, (room, row.shape[1]), 0).astype(F32)
    return jnp.where(ids == row, 1.0, 0.0).astype(BF16)


def experts_fwd_kernel(
    capacity, mine, gate_rows, wg, wu, wd, pos, x_out, y_out, g_out, u_out, o_out, hid_out, gate_out,
    buf, wg_v, wu_v, wd_v, x_v, y_v, g_v, u_v, o_v, hid_v, gate_v, gate_in, local, rs, rr, *sems,
):
    model = wg.shape[0]
    rows_in = mine.shape[0]
    room = x_v.shape[0] // 4
    loads = start_all(
        [
            pltpu.make_async_copy(a, b, local.at[0, i])
            for i, (a, b) in enumerate(((wg, wg_v), (wu, wu_v), (wd, wd_v)))
        ]
    )
    leaving = {g: [] for g in range(4)}
    scattered = []

    def greeting():
        greet_everyone()
        scattered.extend(scatter_rows(gate_rows, gate_in, rs, rr))

    def leave(g, pairs):
        kept = group_rows(g, room)
        leaving[g].extend(
            start_all(
                [
                    pltpu.make_async_copy(v, o.at[kept], local.at[g % 2, i])
                    for i, v, o in pairs
                ]
            )
        )

    def before(g):
        wait_all(loads)
        wait_all(scattered)
        if g > 0:
            wait_all(leaving[g - 1])

    upto = jnp.where(
        lax.broadcasted_iota(jnp.int32, (rows_in, rows_in), 0)
        <= lax.broadcasted_iota(jnp.int32, (rows_in, rows_in), 1),
        1.0,
        0.0,
    ).astype(BF16)
    line = lax.broadcasted_iota(jnp.int32, (16, rows_in), 0)

    def pick(at, s, start):
        rows = pl.ds(start, room)
        sels = []
        gate = jnp.zeros((room, 1), F32)
        for c in range(2):
            row = jnp.broadcast_to(gate_in[s + c], (16, rows_in))
            named = jnp.where(row > 0.0, 1.0, 0.0)
            place = (dot_nn(named.astype(BF16), upto) + (c * capacity)) * named - 1.0
            pos[at * 2 + c] = place[:1]
            sels.append(selector(place[:1], room))
            top = row.astype(BF16).astype(F32)
            parts = jnp.where(line == 0, top, jnp.where(line == 1, row - top, 0.0)).astype(BF16)
            gate = gate + jnp.sum(dot_nt(sels[c], parts), axis=-1, keepdims=True)
        for c in range(4):
            n = slice(c * model // 4, (c + 1) * model // 4)
            x_v[rows, n] = (dot_nn(sels[0], buf[s, :, n]) + dot_nn(sels[1], buf[s + 1, :, n])).astype(BF16)
        gate_v[rows, :] = jnp.broadcast_to(gate, (room, 128))

    def group(g, blocks):
        for j, (at, s) in enumerate(blocks):
            pick(at, s, j * room)
        leave(g, ((0, x_v, x_out), (1, gate_v, gate_out)))

        def first(c, carry):
            n = aligned(c, 256)
            x = x_v[...]
            gates = dot_nn(x, wg_v[:, n])
            u = dot_nn(x, wu_v[:, n])
            g_v[:, n] = gates.astype(BF16)
            u_v[:, n] = u.astype(BF16)
            hid_v[:, n] = (gates / (1.0 + jnp.exp(-gates)) * u).astype(BF16)
            return carry

        lax.fori_loop(0, wg.shape[1] // 256, first, 0)
        leave(g, ((2, g_v, g_out), (3, u_v, u_out), (4, hid_v, hid_out)))

        def second(c, carry):
            n = aligned(c, 256)
            o = dot_nn(hid_v[...], wd_v[:, n]).astype(BF16)
            o_v[:, n] = o
            y_v[:, n] = (o.astype(F32) * gate_v[:, :1]).astype(BF16)
            return carry

        lax.fori_loop(0, model // 256, second, 0)
        leave(g, ((5, o_v, o_out), (6, y_v, y_out)))

    def done():
        for copies in leaving.values():
            wait_all(copies)

    gather_world(mine, buf, *sems, before, group, done, greeting)


def experts_fwd(mine, gate_rows, wg, wu, wd, capacity, room):
    rows, width = mine.shape
    model, ff = wg.shape
    group = 4 * room
    wide = jax.ShapeDtypeStruct((16 * room, model), BF16)
    thin = jax.ShapeDtypeStruct((16 * room, ff), BF16)
    pos, x, y, g, u, o, hidden, gates = pl.pallas_call(
        functools.partial(experts_fwd_kernel, capacity),
        out_shape=(
            jax.ShapeDtypeStruct((32, 1, rows), F32),
            wide,
            wide,
            thin,
            thin,
            wide,
            thin,
            jax.ShapeDtypeStruct((16 * room, 128), F32),
        ),
        in_specs=[VMEM_SPEC, VMEM_SPEC, ANY_SPEC, ANY_SPEC, ANY_SPEC],
        out_specs=(VMEM_SPEC,) + (ANY_SPEC,) * 7,
        scratch_shapes=[
            pltpu.VMEM((32, rows, width), BF16),
            pltpu.VMEM((model, ff), BF16),
            pltpu.VMEM((model, ff), BF16),
            pltpu.VMEM((ff, model), BF16),
            pltpu.VMEM((group, model), BF16),
            pltpu.VMEM((group, model), BF16),
            pltpu.VMEM((group, ff), BF16),
            pltpu.VMEM((group, ff), BF16),
            pltpu.VMEM((group, model), BF16),
            pltpu.VMEM((group, ff), BF16),
            pltpu.VMEM((group, 128), F32),
            pltpu.VMEM((32, 1, rows), F32),
            pltpu.SemaphoreType.DMA((2, 7)),
        ]
        + ROW_SEMS
        + GATHER_SEMS,
        compiler_params=params(6),
        name="experts_fwd",
    )(mine, gate_rows, wg, wu, wd)
    return pos, x, y, (g, u, o, hidden, gates)


def experts_bwd_kernel(
    mine, pos, g_in, u_in, o_in, gate_in, wg, wu, wd, d_gates, y_out, d_copy_out, dg_out, du_out,
    buf, wg_v, wu_v, wd_v, g_v, u_v, o_v, gate_v, y_v, d_copy_v, dg_v, du_v,
    local, ins, *sems,
):
    model, ff = wg.shape
    room = d_copy_v.shape[0] // 4
    loads = start_all(
        [
            pltpu.make_async_copy(a, b, local.at[0, i])
            for i, (a, b) in enumerate(((wg, wg_v), (wu, wu_v), (wd, wd_v)))
        ]
    )
    leaving, coming = {g: [] for g in range(4)}, {}

    def fetch(g):
        kept = group_rows(g, room)
        coming[g] = start_all(
            [
                pltpu.make_async_copy(a.at[kept], v.at[g % 2], ins.at[g % 2, i])
                for i, (a, v) in enumerate(
                    ((g_in, g_v), (u_in, u_v), (o_in, o_v), (gate_in, gate_v))
                )
            ]
        )

    fetch(0)

    def leave(g, pairs):
        kept = group_rows(g, room)
        leaving[g].extend(
            start_all(
                [
                    pltpu.make_async_copy(v, o.at[kept], local.at[g % 2, i])
                    for i, v, o in pairs
                ]
            )
        )

    def before(g):
        wait_all(loads)
        wait_all(coming[g])
        if g + 1 < 4:
            fetch(g + 1)
        if g > 0:
            wait_all(leaving[g - 1])

    def pick(slot, at, s, start):
        rows = pl.ds(start, room)
        sels = [selector(pos[at * 2 + c], room) for c in range(2)]
        gate = gate_v[slot, rows, :1]
        inner = jnp.zeros((room, 1), F32)
        for c in range(4):
            n = slice(c * model // 4, (c + 1) * model // 4)
            picked = dot_nn(sels[0], buf[s, :, n]) + dot_nn(sels[1], buf[s + 1, :, n])
            d_copy_v[rows, n] = (gate * picked).astype(BF16)
            inner = inner + jnp.sum(picked * o_v[slot, rows, n].astype(F32), axis=-1, keepdims=True)
        top = inner.astype(BF16).astype(F32)
        rest = inner - top
        lane = lax.broadcasted_iota(jnp.int32, (room, 128), 1)
        parts = jnp.where(lane == 0, top, jnp.where(lane == 1, rest, 0.0)).astype(BF16)
        for c in range(2):
            both = dot_tn(parts, sels[c])
            d_gates[s + c] = both[:1] + both[1:2]

    def group(g, blocks):
        slot = g % 2
        for j, (at, s) in enumerate(blocks):
            pick(slot, at, s, j * room)
        leave(g, ((0, d_copy_v, d_copy_out),))

        def third(c, carry):
            n = aligned(c, 256)
            d_hidden = dot_nt(d_copy_v[...], wd_v[n, :])
            gates, u = g_v[slot, :, n].astype(F32), u_v[slot, :, n].astype(F32)
            s = 1.0 / (1.0 + jnp.exp(-gates))
            dg_v[:, n] = (d_hidden * u * s * (1.0 + gates * (1.0 - s))).astype(BF16)
            du_v[:, n] = (d_hidden * gates * s).astype(BF16)
            return carry

        lax.fori_loop(0, ff // 256, third, 0)
        leave(g, ((1, dg_v, dg_out), (2, du_v, du_out)))

        def fourth(c, carry):
            n = aligned(c, 256)
            y_v[:, n] = (
                dot_nt(dg_v[...], wg_v[n, :]) + dot_nt(du_v[...], wu_v[n, :])
            ).astype(BF16)
            return carry

        lax.fori_loop(0, model // 256, fourth, 0)
        leave(g, ((3, y_v, y_out),))

    def done():
        for copies in leaving.values():
            wait_all(copies)

    gather_world(mine, buf, *sems, before, group, done)


def experts_bwd(mine, pos, kept, wg, wu, wd, room):
    rows, width = mine.shape
    model, ff = wg.shape
    group = 4 * room
    return pl.pallas_call(
        experts_bwd_kernel,
        out_shape=(
            jax.ShapeDtypeStruct((32, 1, rows), F32),
            jax.ShapeDtypeStruct((16 * room, model), BF16),
            jax.ShapeDtypeStruct((16 * room, model), BF16),
            jax.ShapeDtypeStruct((16 * room, ff), BF16),
            jax.ShapeDtypeStruct((16 * room, ff), BF16),
        ),
        in_specs=[VMEM_SPEC, VMEM_SPEC] + [ANY_SPEC] * 7,
        out_specs=(VMEM_SPEC,) + (ANY_SPEC,) * 4,
        scratch_shapes=[
            pltpu.VMEM((32, rows, width), BF16),
            pltpu.VMEM((model, ff), BF16),
            pltpu.VMEM((model, ff), BF16),
            pltpu.VMEM((ff, model), BF16),
            pltpu.VMEM((2, group, ff), BF16),
            pltpu.VMEM((2, group, ff), BF16),
            pltpu.VMEM((2, group, model), BF16),
            pltpu.VMEM((2, group, 128), F32),
            pltpu.VMEM((group, model), BF16),
            pltpu.VMEM((group, model), BF16),
            pltpu.VMEM((group, ff), BF16),
            pltpu.VMEM((group, ff), BF16),
            pltpu.SemaphoreType.DMA((2, 4)),
            pltpu.SemaphoreType.DMA((2, 4)),
        ]
        + GATHER_SEMS,
        compiler_params=params(7),
        name="experts_bwd",
    )(mine, pos, *kept, wg, wu, wd)


def sum_world_kernel(with_rows, *refs):
    if with_rows:
        y_in, pos, rows_given, out, rows_out, *refs, rs, rr = refs
    else:
        y_in, pos, out, *refs = refs
    (
        y, local, psend, pair, half_near, half_far, full_near, full_far, lines,
        ds, dr, hs, hr, fs, fr, zs, zr,
    ) = refs
    r, e, z, core, near, far, greeted = world(True)
    rows, width = out.shape
    room = y.shape[1]
    half = rows // 2
    low, high = pl.ds(0, half), pl.ds(half, half)
    order = plane_order(z)[::-1]
    body_width = width // 512 * 512
    loads = loading(
        [(y_in.at[pl.ds(12 - 4 * k, 4)], y.at[pl.ds(12 - 4 * k, 4)]) for k in range(4)], local
    )
    if with_rows:
        greet_everyone()
        scattering = scatter_rows(rows_given, rows_out, rs, rr)
    else:
        greet(greeted)

    def for_columns(fn):
        def step(c, carry):
            fn(aligned(c, 512))
            return carry

        lax.fori_loop(0, body_width // 512, step, 0)
        if width > body_width:
            fn(pl.ds(body_width, width - body_width))

    def scattered(sel, k, i, n):
        return dot_tn(sel, y[(3 - k) * 4 + i, :, n])

    def select(k, i, c):
        return selector(pos[((3 - k) * 4 + i) * 2 + c], room)

    pairs, halves, fulls, moves = {}, {}, {}, []

    def stage_a(k):
        wait_all(loads[k])
        for i in (3, 1, 2, 0):
            at = k * 4 + i
            sel = select(k, i, 1 - core)

            def fill(n):
                psend[at, :, n] = scattered(sel, k, i, n).astype(BF16)

            for_columns(fill)
            copy = remote(psend.at[at], pair.at[at], ds.at[at], dr.at[at], (r, e ^ 1))
            copy.start()
            pairs[at] = copy
        for i in (3, 1, 2, 0):
            at = k * 4 + i
            sel = select(k, i, core)
            pairs[at].wait_recv()

            def add(n):
                value = scattered(sel, k, i, n) + pair[at, :, n].astype(F32)
                pair[at, :, n] = value.astype(BF16)

            for_columns(add)
            if i == 3:
                for side, (part, dst, p) in enumerate(
                    ((low, half_near, near), (high, half_far, far))
                ):
                    copy = remote(
                        pair.at[at, part], dst.at[k], hs.at[k, side], hr.at[k, side], (p, e)
                    )
                    copy.start()
                    halves[k, side] = copy

    def stage_b(k):
        for side, (i, part, src, dst, p) in enumerate(
            (
                (2, low, half_near, full_far, far),
                (1, high, half_far, full_near, near),
            )
        ):
            at = k * 4 + i
            halves[k, side].wait_recv()

            def add(n):
                value = pair[at, part, n].astype(F32) + src[k, :, n].astype(F32)
                pair[at, part, n] = value.astype(BF16)

            for_columns(add)
            copy = remote(pair.at[at], dst.at[k], fs.at[k, side], fr.at[k, side], (p, e))
            copy.start()
            fulls[k, side] = copy

    def stage_c(k):
        b = order[k]
        at = k * 4
        fulls[k, 0].wait_recv()
        fulls[k, 1].wait_recv()

        def add(n):
            out[:, n] = (
                pair[at, :, n].astype(F32)
                + full_near[k, :, n].astype(F32)
                + full_far[k, :, n].astype(F32)
            )

        for_columns(add)
        for side, cond in ((0, (b >= z) & (z > 0)), (1, (b <= z) & (z < 3))):

            @pl.when(cond)
            def _():
                remote(
                    lines.at[side, b], lines.at[side, b], zs.at[side, k], zr.at[side, b], (r, e ^ 1)
                ).wait_recv()

                def more(n):
                    out[:, n] = out[:, n] + lines[side, b, :, n].astype(F32)

                for_columns(more)

        if k < 3:

            def keep(n):
                pair[at, :, n] = out[:, n].astype(BF16)

            for_columns(keep)
            for side, cond, to in (
                (0, b > z, jnp.minimum(z + 1, 3)),
                (1, b < z, jnp.maximum(z - 1, 0)),
            ):
                copy = remote(
                    pair.at[at], lines.at[side, b], zs.at[side, k], zr.at[side, b], (r, to * 2 + core)
                )
                moves.append((cond, copy))

                @pl.when(cond)
                def _():
                    copy.start()

    stage_a(0)
    stage_a(1)
    stage_b(0)
    stage_a(2)
    stage_b(1)
    stage_c(0)
    stage_a(3)
    stage_b(2)
    stage_c(1)
    stage_b(3)
    stage_c(2)
    stage_c(3)
    for copies in (pairs, halves, fulls):
        for copy in copies.values():
            copy.wait_send()
    for cond, copy in moves:

        @pl.when(cond)
        def _():
            copy.wait_send()

    if with_rows:
        wait_all(scattering)


def sum_world(y, pos, rows, collective_id, given=None):
    width = y.shape[-1]

    def blocks(n, size):
        return pltpu.VMEM((n, size, width), BF16)

    extra = () if given is None else (given,)
    return pl.pallas_call(
        functools.partial(sum_world_kernel, len(extra) > 0),
        out_shape=(jax.ShapeDtypeStruct((rows, width), F32),)
        + tuple(jax.ShapeDtypeStruct(a.shape, F32) for a in extra),
        in_specs=[ANY_SPEC, VMEM_SPEC] + [VMEM_SPEC] * len(extra),
        out_specs=(VMEM_SPEC,) * (1 + len(extra)),
        scratch_shapes=[
            pltpu.VMEM(y.shape, BF16),
            pltpu.SemaphoreType.DMA((4,)),
            blocks(16, rows),
            blocks(16, rows),
            blocks(4, rows // 2),
            blocks(4, rows // 2),
            blocks(4, rows),
            blocks(4, rows),
            pltpu.VMEM((2, 4, rows, width), BF16),
            pltpu.SemaphoreType.DMA((16,)),
            pltpu.SemaphoreType.DMA((16,)),
            pltpu.SemaphoreType.DMA((4, 2)),
            pltpu.SemaphoreType.DMA((4, 2)),
            pltpu.SemaphoreType.DMA((4, 2)),
            pltpu.SemaphoreType.DMA((4, 2)),
            pltpu.SemaphoreType.DMA((2, 4)),
            pltpu.SemaphoreType.DMA((2, 4)),
        ]
        + (ROW_SEMS if extra else []),
        compiler_params=params(collective_id),
        name="sum_world",
    )(y, pos, *extra)


def expert_grads_kernel(x, d_gate, d_up, hidden, d_copy, gate_grad, up_grad, down_grad, hidden_t):
    @pl.when(pl.program_id(0) == 0)
    def _():
        hidden_t[...] = hidden[...].T

    rows = x[...].T
    gate_grad[...] = dot_nn(rows, d_gate[...])
    up_grad[...] = dot_nn(rows, d_up[...])
    down_grad[...] = dot_nn(hidden_t[...], d_copy[...])


def expert_grads(x, d_gate, d_up, hidden, d_copy):
    slots, model = x.shape
    ff = hidden.shape[1]
    step = 256
    whole = pl.BlockSpec((slots, ff), lambda i: (0, 0))
    columns = pl.BlockSpec((slots, step), lambda i: (0, i))
    return pl.pallas_call(
        expert_grads_kernel,
        grid=(model // step,),
        in_specs=[columns, whole, whole, whole, columns],
        out_specs=[
            pl.BlockSpec((step, ff), lambda i: (i, 0)),
            pl.BlockSpec((step, ff), lambda i: (i, 0)),
            pl.BlockSpec((ff, step), lambda i: (0, i)),
        ],
        out_shape=(
            jax.ShapeDtypeStruct((model, ff), F32),
            jax.ShapeDtypeStruct((model, ff), F32),
            jax.ShapeDtypeStruct((ff, model), F32),
        ),
        scratch_shapes=[pltpu.VMEM((ff, slots), BF16)],
        compiler_params=params(),
        name="expert_grads",
    )(x, d_gate, d_up, hidden, d_copy)


def experts_by_all_to_all(
    mixed, state, teacher, routes, valid_slot, valid_count, router_weight, gate_weight, up_weight, down_weight,
    devices, capacity, slots_all,
):
    tok_dev, model_width = mixed.shape
    top_count = routes.shape[1]
    ffn_width = gate_weight.shape[2]
    logits = jnp.dot(mixed, router_weight, preferred_element_type=jnp.float32)
    gates = jax.nn.softmax(jnp.take_along_axis(logits, routes, axis=1), axis=-1)
    rows_total = tok_dev * top_count
    expert_ids = routes.reshape(rows_total)
    live_rows = jnp.repeat(valid_slot, top_count)
    expert_range = jnp.arange(devices, dtype=jnp.int32)
    hit_table = ((expert_ids[:, None] == expert_range[None, :]) & live_rows[:, None]).astype(
        jnp.int32
    )
    earlier = jnp.cumsum(hit_table, axis=0) - hit_table
    position_in = jnp.sum(earlier * hit_table, axis=1)
    slot_index = jnp.where(live_rows, expert_ids * capacity + position_in, devices * capacity)
    row_of_slot = (
        jnp.full((devices * capacity + 1,), rows_total, jnp.int32)
        .at[slot_index]
        .set(jnp.arange(rows_total, dtype=jnp.int32))[: devices * capacity]
    )
    token_of_slot = jnp.where(row_of_slot < rows_total, row_of_slot // top_count, tok_dev)
    mixed_pad = jnp.concatenate([mixed, jnp.zeros((1, model_width), jnp.bfloat16)], axis=0)
    send_rows = mixed_pad[token_of_slot].reshape(devices, capacity, model_width)
    arrived = lax.all_to_all(send_rows, ("dp", "expert"), split_axis=0, concat_axis=0, tiled=True)
    sources = arrived.shape[0]
    items = arrived.shape[1]
    flat_in = arrived.reshape(sources * items, model_width)
    gate_pre = jnp.dot(flat_in, gate_weight[0], preferred_element_type=jnp.float32)
    up_pre = jnp.dot(flat_in, up_weight[0], preferred_element_type=jnp.float32)
    hidden_units = (jax.nn.silu(gate_pre) * up_pre).astype(jnp.bfloat16)
    produced = jnp.dot(hidden_units, down_weight[0], preferred_element_type=jnp.float32).astype(
        jnp.bfloat16
    )
    produced, gate_pre, up_pre, hidden_units, arrived = (
        produced.reshape(sources, items, model_width),
        gate_pre.reshape(sources, items, ffn_width),
        up_pre.reshape(sources, items, ffn_width),
        hidden_units.reshape(sources, items, ffn_width),
        arrived,
    )
    returned = lax.all_to_all(produced, ("dp", "expert"), split_axis=0, concat_axis=0, tiled=True)
    returned_pad = jnp.concatenate(
        [
            returned.reshape(devices * capacity, model_width),
            jnp.zeros((1, model_width), jnp.bfloat16),
        ],
        axis=0,
    )
    copies = returned_pad[slot_index].reshape(tok_dev, top_count, model_width)
    layer_out = state + jnp.sum(gates[:, :, None] * copies, axis=1)
    live_tokens = valid_slot.astype(jnp.float32)[:, None]
    diff = (layer_out - teacher.astype(jnp.float32)) * live_tokens
    local_square = jnp.sum(diff * diff)
    d_out = 2.0 * slots_all * diff / valid_count
    d_gates = jnp.sum(d_out[:, None, :] * copies, axis=-1)
    d_chosen = gates * (d_gates - jnp.sum(gates * d_gates, axis=-1, keepdims=True))
    d_logits = jnp.sum(
        jnp.where(routes[:, :, None] == expert_range[None, None, :], d_chosen[:, :, None], 0.0),
        axis=1,
    ).astype(jnp.bfloat16)
    d_copies = (
        (gates[:, :, None] * d_out[:, None, :])
        .astype(jnp.bfloat16)
        .reshape(rows_total, model_width)
    )
    d_copies_pad = jnp.concatenate([d_copies, jnp.zeros((1, model_width), jnp.bfloat16)], axis=0)
    d_send = d_copies_pad[row_of_slot].reshape(devices, capacity, model_width)
    d_arrived = lax.all_to_all(d_send, ("dp", "expert"), split_axis=0, concat_axis=0, tiled=True)
    flat_d = d_arrived.reshape(-1, model_width)
    flat_in = arrived.reshape(-1, model_width)
    flat_gate = gate_pre.reshape(-1, ffn_width)
    flat_up = up_pre.reshape(-1, ffn_width)
    flat_hidden = hidden_units.reshape(-1, ffn_width)
    d_hidden = contract(flat_d, down_weight[0], 1, 1)
    sigmoid_gate = jax.nn.sigmoid(flat_gate)
    d_gate = (d_hidden * flat_up * sigmoid_gate * (1.0 + flat_gate * (1.0 - sigmoid_gate))).astype(
        jnp.bfloat16
    )
    d_up = (d_hidden * flat_gate * sigmoid_gate).astype(jnp.bfloat16)
    down_grad = contract(flat_hidden, flat_d, 0, 0)[None]
    gate_grad = contract(flat_in, d_gate, 0, 0)[None]
    up_grad = contract(flat_in, d_up, 0, 0)[None]
    d_in = (contract(d_gate, gate_weight[0], 1, 1) + contract(d_up, up_weight[0], 1, 1)).astype(
        jnp.bfloat16
    )
    d_returned = lax.all_to_all(
        d_in.reshape(devices, capacity, model_width),
        ("dp", "expert"),
        split_axis=0,
        concat_axis=0,
        tiled=True,
    )
    d_returned_pad = jnp.concatenate(
        [
            d_returned.reshape(devices * capacity, model_width),
            jnp.zeros((1, model_width), jnp.bfloat16),
        ],
        axis=0,
    )
    d_mixed = jnp.sum(
        d_returned_pad[slot_index].reshape(tok_dev, top_count, model_width),
        axis=1,
        dtype=jnp.float32,
    )
    d_mixed = d_mixed + contract(d_logits, router_weight, 1, 1)
    router_local = contract(d_logits, mixed, 0, 0)
    return layer_out, d_out, d_mixed, local_square, router_local, (gate_grad, up_grad, down_grad)


def experts_by_gather(
    mixed, state, teacher, routes, valid_slot, valid_count, router_weight,
    gate_weight, up_weight, down_weight, devices, capacity, slots_all,
):
    tok_dev, model_width = mixed.shape
    room = -(-2 * capacity // 16) * 16
    expert_range = jnp.arange(devices, dtype=jnp.int32)
    logits = jnp.dot(mixed, router_weight, preferred_element_type=F32)
    chosen = jnp.any(routes[:, :, None] == expert_range[None, None], axis=1)
    gates = jax.nn.softmax(jnp.where(chosen, logits, -jnp.inf), axis=-1)
    live_gates = jnp.where(valid_slot[:, None], gates, 0.0)
    gate_rows = live_gates.T[:, None]
    pos, x_rows, y_rows, kept = experts_fwd(
        mixed, gate_rows, gate_weight[0], up_weight[0], down_weight[0], capacity, room
    )
    layer_out = state + sum_world(y_rows.reshape(16, room, model_width), pos, tok_dev, 8)[0]
    live_tokens = valid_slot.astype(F32)[:, None]
    diff = (layer_out - teacher.astype(F32)) * live_tokens
    local_square = jnp.sum(diff * diff)
    d_out = 2.0 * slots_all * diff / valid_count
    hidden = kept[3]
    d_gates, d_rows, d_copy, d_gate, d_up = experts_bwd(
        d_out.astype(BF16), pos, kept[:3] + kept[4:], gate_weight[0], up_weight[0], down_weight[0], room
    )
    back, d_gates = sum_world(d_rows.reshape(16, room, model_width), pos, tok_dev, 9, d_gates)
    d_gates = d_gates[:, 0].T

    grad_rows = (x_rows, d_gate, d_up, hidden, d_copy)
    d_logits = (gates * (d_gates - jnp.sum(gates * d_gates, axis=-1, keepdims=True))).astype(BF16)
    d_mixed = back + contract(d_logits, router_weight, 1, 1)
    router_local = contract(d_logits, mixed, 0, 0)
    return layer_out, d_out, d_mixed, local_square, router_local, grad_rows


def head_rope(linear, gain_vec, cos, sin):
    value = root_mean_scale(linear, gain_vec)
    half = value.shape[-1] // 2
    return value * cos + jnp.roll(value, half, axis=-1) * sin


def body(
    tokens,
    teacher,
    routes,
    cont_lengths,
    query_weight,
    key_projection,
    value_projection,
    output_weight,
    router_weight,
    gate_weight,
    up_weight,
    down_weight,
    input_gain,
    post_gain,
    query_gain,
    key_gain,
):
    n_dp = lax.axis_size("dp")
    n_owner = lax.axis_size("expert")
    devices = n_dp * n_owner
    rank_dp = lax.axis_index("dp")
    rank_owner = lax.axis_index("expert")
    flat_rank = rank_dp * n_owner + rank_owner
    column = rank_owner % 2
    first_column = column == 0
    tok_dev, model_width = tokens.shape
    top_count = routes.shape[1]
    head_dim = query_gain.shape[0]
    kv_width = key_projection.shape[1]
    query_width = query_weight.shape[1]
    query_group = query_width // n_dp
    assert n_dp == 4 and kv_width == n_dp * head_dim
    prompt_block = tok_dev - CMAX
    half_prompt = n_dp * prompt_block
    prompt_len = 2 * half_prompt
    capacity = max(2, tok_dev * top_count * 5 // (4 * devices))
    slots_all = devices * tok_dev
    slot_ids = jnp.arange(tok_dev, dtype=jnp.int32)
    is_own = jnp.arange(devices, dtype=jnp.int32) == flat_rank
    own_length = jnp.sum(jnp.where(is_own, cont_lengths, 0))
    valid_slot = (slot_ids < prompt_block) | (slot_ids - prompt_block < own_length)
    valid_count = (devices * prompt_block + jnp.sum(cont_lengths)).astype(F32)
    tokens_float = tokens.astype(F32)

    block_ids = jnp.arange(n_dp, dtype=jnp.int32)[:, None]
    positions = jnp.where(
        slot_ids[None] < prompt_block,
        (column * n_dp + block_ids) * prompt_block + slot_ids[None],
        prompt_len + slot_ids[None] - prompt_block,
    )
    half_head = head_dim // 2
    frequency = rope_base ** (-(jnp.arange(half_head, dtype=F32) * 2.0) / head_dim)
    angles = positions.astype(F32)[:, :, None] * frequency
    cos_half, sin_half = jnp.cos(angles), jnp.sin(angles)
    cos = jnp.concatenate([cos_half, cos_half], axis=-1)
    sin = jnp.concatenate([-sin_half, sin_half], axis=-1)
    lin, normed_cols_t, normed_cols, key_lin, all_keys, all_values, inverse = project_qkv(
        tokens, input_gain[None], query_weight, key_projection, value_projection, key_gain[None], cos, sin
    )
    query_gain_row = query_gain[None]
    queries, attended = attention_fwd(
        cont_lengths, lin, query_gain_row, cos, sin, all_keys, all_values, prompt_len
    )
    state = tokens_float + project_out(attended, output_weight)
    mixed_float, second_norm_back = jax.vjp(root_mean_scale, state, post_gain)
    mixed = mixed_float.astype(BF16)
    sizes = (devices, capacity, slots_all)
    weights = (router_weight, gate_weight, up_weight, down_weight)
    if n_dp == 4 and n_owner == 8:
        moe = experts_by_gather(
            mixed, state, teacher, routes, valid_slot, valid_count, *weights, *sizes
        )
    else:
        moe = experts_by_all_to_all(
            mixed, state, teacher, routes, valid_slot, valid_count, *weights, *sizes
        )
    layer_out, d_out, d_mixed, local_square, router_local, grad_rows = moe
    d_state_norm, d_post_gain = second_norm_back(d_mixed)
    d_state = d_out + d_state_norm
    d_branch = d_state.astype(BF16)
    d_attended, d_branch_all, attended_t = grad_branch(d_branch, output_weight, attended)
    d_query_lin, d_keys, d_values, gain_parts, out_part = attention_bwd(
        cont_lengths, lin, queries, d_attended, query_gain_row, cos, sin, all_keys, all_values,
        attended_t, d_branch_all, prompt_len,
    )
    d_query_gain = jnp.sum(gain_parts, axis=(0, 1))
    width = query_weight.shape[0]
    group = query_group + 2 * head_dim
    rows_here = width // n_owner
    by_line = n_dp == 4 and n_owner == 8

    def packed(parts):
        small = jnp.concatenate([a.reshape(-1) for a in parts])
        piece_rows = -(-small.shape[0] // (8 * 8 * 128)) * 8
        small = jnp.pad(small, (0, 8 * piece_rows * 128 - small.shape[0]))
        return small.reshape(8, piece_rows, 128)

    out_part = out_part.reshape(n_owner, -1, model_width)
    weights = (query_weight, key_projection, value_projection)
    if by_line:

        def line(parts):
            flat = jnp.concatenate(parts)
            return jnp.pad(flat, (0, model_width - flat.shape[0]))[None]

        small = jnp.concatenate(
            [router_local, d_post_gain[None], line([d_query_gain]), line([local_square[None]])]
        )
        small_rows = -(-small.shape[0] // 8) * 8
        small = jnp.pad(small, ((0, small_rows - small.shape[0]), (0, 0)))
        small = small.reshape(small_rows, 8, -1).transpose(1, 0, 2)
        d_normed, query_grad, key_grad, value_grad, output_grad, small, input_gain_grad = grad_qkv_line(
            d_query_lin, d_keys, d_values, key_lin, cos, sin, key_gain[None],
            *weights, normed_cols_t, normed_cols, out_part, small, input_gain[None],
        )
        key_gain_grad = jnp.sum(input_gain_grad[:, 1, :head_dim], axis=0)
        input_gain_grad = input_gain_grad[:, 0].reshape(-1)
        sums = small.transpose(1, 0, 2).reshape(small_rows, model_width)
        at = router_local.shape[0]
        router_grad, post_gain_grad = sums[:at].T, sums[at]
        query_gain_grad = sums[at + 1, :head_dim]
        total_square = sums[at + 2, :1]
    else:
        _, key_back = jax.vjp(
            lambda a, b: head_rope(a, b, cos, sin), key_lin.reshape(n_dp, tok_dev, head_dim), key_gain
        )
        prompt_grads = jnp.stack(
            [jnp.sum(d_keys[:, :prompt_len], axis=0), jnp.sum(d_values[:, :prompt_len], axis=0)]
        )
        mine_part = jnp.where(first_column, prompt_grads[:, :half_prompt], prompt_grads[:, half_prompt:])
        their_part = jnp.where(first_column, prompt_grads[:, half_prompt:], prompt_grads[:, :half_prompt])
        own_prompt = (mine_part + partner(their_part, "expert", 0)).reshape(
            2, n_dp, prompt_block, head_dim
        )
        d_key_post = jnp.concatenate([own_prompt[0], d_keys[:, prompt_len:]], axis=1)
        d_value_lin = jnp.concatenate([own_prompt[1], d_values[:, prompt_len:]], axis=1)
        d_key_float, d_key_gain = key_back(d_key_post)
        rows = n_dp * tok_dev
        d_lin = jnp.concatenate(
            [
                d_query_lin,
                d_key_float.astype(BF16).reshape(rows, head_dim),
                d_value_lin.astype(BF16).reshape(rows, head_dim),
            ],
            axis=1,
        )
        small_parts = [router_local, d_post_gain, d_query_gain, d_key_gain, local_square[None]]
        d_normed, qkv_part, output_grad = grad_qkv(d_lin, *weights, normed_cols_t, out_part)
        small_parts.append(jnp.sum(d_normed * tokens_float * inverse[:, :1], axis=0))
        by_owner = (
            qkv_part.reshape(n_dp, n_owner, rows_here, group)
            .transpose(1, 0, 2, 3)
            .reshape(n_owner, n_dp * rows_here, group)
        )
        qkv_rows, small = last_sums(by_owner, packed(small_parts))
        qkv_rows = qkv_rows.reshape(n_dp, rows_here, group)

        def columns(start, size):
            part = qkv_rows[:, :, start : start + size]
            return part.transpose(1, 0, 2).reshape(rows_here, n_dp * size)

        query_grad = columns(0, query_group)
        key_grad = columns(query_group, head_dim)
        value_grad = columns(query_group + head_dim, head_dim)
        small = small.reshape(-1)
        starts = [0]
        for a in small_parts:
            starts.append(starts[-1] + a.size)
        sums = [small[i:j].reshape(a.shape) for a, i, j in zip(small_parts, starts, starts[1:])]
        router_grad, post_gain_grad, query_gain_grad, key_gain_grad, total_square, input_gain_grad = sums
        router_grad = router_grad.T
    inverse = inverse[:, :1]
    weighted = d_normed * input_gain
    along = jnp.mean(weighted * tokens_float, axis=-1, keepdims=True) * inverse * inverse
    tokens_grad = d_state + inverse * (weighted - tokens_float * along)
    if by_line:
        gate_grad, up_grad, down_grad = expert_grads(*grad_rows)
        gate_grad, up_grad, down_grad = gate_grad[None], up_grad[None], down_grad[None]
    else:
        gate_grad, up_grad, down_grad = grad_rows
    loss = total_square[0] / (valid_count * model_width)
    return (
        layer_out,
        loss,
        tokens_grad,
        query_grad,
        key_grad,
        value_grad,
        output_grad,
        router_grad,
        gate_grad,
        up_grad,
        down_grad,
        input_gain_grad,
        post_gain_grad,
        query_gain_grad,
        key_gain_grad,
    )


def solution(mesh):
    in_specs = (
        P(("dp", "expert"), None),
        P(("dp", "expert"), None),
        P(("dp", "expert"), None),
        P(),
        P("dp", None),
        P("dp", None),
        P("dp", None),
        P("dp", None),
        P(),
        P(("dp", "expert"), None, None),
        P(("dp", "expert"), None, None),
        P(("dp", "expert"), None, None),
        P(),
        P(),
        P(),
        P(),
    )
    out_specs = (
        P(("dp", "expert"), None),
        P(),
        P(("dp", "expert"), None),
        P(("dp", "expert"), None),
        P(("dp", "expert"), None),
        P(("dp", "expert"), None),
        P(("dp", "expert"), None),
        P(),
        P(("dp", "expert"), None, None),
        P(("dp", "expert"), None, None),
        P(("dp", "expert"), None, None),
        P(),
        P(),
        P(),
        P(),
    )
    return jax.shard_map(body, mesh=mesh, in_specs=in_specs, out_specs=out_specs, check_vma=False)
```
